32 devices in a mesh: wide: 8 (over z, x), narrow: 4 (over y, core).
Axes of the slice: x: 2, y: 2, z: 4, core: 2. Of those that a mesh axis runs over, the one named last changes fastest.
Arguments:
- tokens: bfloat16 [8, 512, 1152], P('wide', 'narrow'), may hold values from -3 to 3
- cond: bfloat16 [8, 4, 1152], P('wide'), may hold values from -3 to 3
- seg_ids: int32 [8, 512], P('wide'), may hold values from 0 to 3, as said below
- cond_index: int32 [8, 4], P('wide'), may hold values from 0 to 3
- cotangent: bfloat16 [8, 512, 1152], P('wide', 'narrow'), may hold values from -3 to 3
- ada_weight: bfloat16 [2, 1152, 6912], P(None, 'wide'), may hold values from -0.1875 to 0.1875
- ada_bias: bfloat16 [2, 6912], P(None, 'wide'), may hold values from -0.5 to 0.5
- qkv_weight: bfloat16 [2, 1152, 3456], P(None, 'wide'), may hold values from -0.1875 to 0.1875
- qkv_bias: bfloat16 [2, 3456], P(None, 'wide'), may hold values from -0.5 to 0.5
- out_weight: bfloat16 [2, 1152, 1152], P(None, 'wide'), may hold values from -0.375 to 0.375
- out_bias: bfloat16 [2, 1152], P(None, 'wide'), may hold values from -0.5 to 0.5
- up_weight: bfloat16 [2, 1152, 4608], P(None, 'wide'), may hold values from -0.1875 to 0.1875
- up_bias: bfloat16 [2, 4608], P(None, 'wide'), may hold values from -0.5 to 0.5
- down_weight: bfloat16 [2, 4608, 1152], P(None, 'wide'), may hold values from -0.09375 to 0.09375
- down_bias: bfloat16 [2, 1152], P(None, 'wide'), may hold values from -0.5 to 0.5
Outputs:
- mixed: bfloat16 [8, 512, 1152], P('wide', 'narrow')
- token_grad: float32 [8, 512, 1152], P('wide', 'narrow')
- cond_grad: float32 [8, 4, 1152], P('wide')
- ada_weight_grad: float32 [2, 1152, 6912], P(None, 'wide')
- ada_bias_grad: float32 [2, 6912], P(None, 'wide')
- qkv_weight_grad: float32 [2, 1152, 3456], P(None, 'wide')
- qkv_bias_grad: float32 [2, 3456], P(None, 'wide')
- out_weight_grad: float32 [2, 1152, 1152], P(None, 'wide')
- out_bias_grad: float32 [2, 1152], P(None, 'wide')
- up_weight_grad: float32 [2, 1152, 4608], P(None, 'wide')
- up_bias_grad: float32 [2, 4608], P(None, 'wide')
- down_weight_grad: float32 [2, 4608, 1152], P(None, 'wide')
- down_bias_grad: float32 [2, 1152], P(None, 'wide')
The draws below stay inside these ranges and needn't reach their ends.
Inputs may be any that keep to these rules, and one draw needn't show every extreme that they name: `seg_ids`: within a row the ids never fall and each of 0 to 3 occurs; segment 1 of every row begins among the row's first 128 tokens and ends among its last 128.
All inputs are finite; a program needn't handle non-finite values.
Results may differ from the reference program's by a relative error of at most 0.02.
Values may be sent and summed in bfloat16 or wider, within the bound.
A program may use at most 384 MiB of HBM per device.

```python
import math
import jax
import jax.numpy as jnp
from jax import lax

D = 1152
HEADS = 16
HEAD = 72
FF = 4608
LAYERS = 2
ROW_LEN = 512
SEGS = 4
ROWS_DEV = 1
ROWS = 8
TL = 128


def draw_seg_ids(key, part):
    key = jax.random.fold_in(key, 11)
    keys = jax.random.split(key, 3)
    first_end = jax.random.randint(keys[0], (ROWS, 1), 1, TL)
    long_end = jax.random.randint(keys[1], (ROWS, 1), ROW_LEN - TL + 1, ROW_LEN - 1)
    third_end = jax.random.randint(keys[2], (ROWS, 1), long_end + 1, ROW_LEN)
    position = jnp.arange(ROW_LEN, dtype=jnp.int32)[None, :]
    return (position >= first_end).astype(jnp.int32) + (position >= long_end).astype(jnp.int32) + (position >= third_end).astype(jnp.int32)


def plant(array, key, least, high):
    longest = array.shape.index(max(array.shape))
    spots = []
    for shift in (0, 1):
        where = [jax.random.randint(jax.random.fold_in(key, axis), (), 0, length) for axis, length in enumerate(array.shape)]
        where[longest] = (where[longest] + shift) % array.shape[longest]
        spots.append(tuple(where))
    return array.at[spots[0]].set(least).at[spots[1]].set(high)


def levels(key, shape, shards, smallest, top_value):
    level = 1.0
    for dim, blocks in shards:
        steps = jax.random.uniform(jax.random.fold_in(jax.random.fold_in(key, 6), dim), (blocks,), jnp.float32, smallest / len(shards), top_value / len(shards))
        level = level * jnp.repeat(jnp.exp(steps), shape[dim] // blocks).reshape((-1,) + (1,) * (len(shape) - 1 - dim))
    return level


def scatter_about(own_key, dims, spread, bound, shards=(), kind=jnp.bfloat16):
    entries = jax.random.normal(own_key, dims, jnp.float32) * spread
    if len(shards) > 0:
        entries = levels(own_key, dims, shards, -0.22, 0.18) * entries
    return jnp.clip(entries, min=-bound, max=bound).astype(kind)


def setup_inputs(seed: int = 0) -> dict:
    key_of = jax.random.split(jax.random.key(seed), 16)
    return {
        "tokens": scatter_about(key_of[0], (ROWS, ROW_LEN, D), 1.0, 3.0, ((0, 8), (1, 4))),
        "cond": scatter_about(key_of[1], (ROWS, SEGS, D), 1.0, 3.0, ((0, 8),)),
        "seg_ids": draw_seg_ids(jax.random.fold_in(key_of[15], 71), 0),
        "cond_index": plant(jax.random.randint(key_of[3], (ROWS, SEGS), 0, SEGS), jax.random.fold_in(key_of[3], 1), 0, SEGS - 1).astype(jnp.int32),
        "cotangent": scatter_about(key_of[4], (ROWS, ROW_LEN, D), 1.0, 3.0, ((0, 8), (1, 4))),
        "ada_weight": scatter_about(key_of[5], (LAYERS, D, 6 * D), D ** -0.5, 0.1875, ((1, 8),)),
        "ada_bias": jnp.clip(jax.random.uniform(key_of[6], (LAYERS, 6 * D), jnp.float32, -0.5, 0.5) * levels(key_of[6], (LAYERS, 6 * D), ((1, 8),), -0.4, 0.0), -0.5, 0.5).astype(jnp.bfloat16),
        "qkv_weight": scatter_about(key_of[7], (LAYERS, D, 3 * D), D ** -0.5, 0.1875, ((1, 8),)),
        "qkv_bias": jnp.clip(jax.random.uniform(key_of[8], (LAYERS, 3 * D), jnp.float32, -0.5, 0.5) * levels(key_of[8], (LAYERS, 3 * D), ((1, 8),), -0.4, 0.0), -0.5, 0.5).astype(jnp.bfloat16),
        "out_weight": scatter_about(key_of[9], (LAYERS, D, D), (D // 4) ** -0.5, 0.375, ((1, 8),)),
        "out_bias": jnp.clip(jax.random.uniform(key_of[10], (LAYERS, D), jnp.float32, -0.5, 0.5) * levels(key_of[10], (LAYERS, D), ((1, 8),), -0.4, 0.0), -0.5, 0.5).astype(jnp.bfloat16),
        "up_weight": scatter_about(key_of[11], (LAYERS, D, FF), D ** -0.5, 0.1875, ((1, 8),)),
        "up_bias": jnp.clip(jax.random.uniform(key_of[12], (LAYERS, FF), jnp.float32, -0.5, 0.5) * levels(key_of[12], (LAYERS, FF), ((1, 8),), -0.4, 0.0), -0.5, 0.5).astype(jnp.bfloat16),
        "down_weight": scatter_about(key_of[13], (LAYERS, FF, D), FF ** -0.5, 0.09375, ((1, 8),)),
        "down_bias": jnp.clip(jax.random.uniform(key_of[14], (LAYERS, D), jnp.float32, -0.5, 0.5) * levels(key_of[14], (LAYERS, D), ((1, 8),), -0.4, 0.0), -0.5, 0.5).astype(jnp.bfloat16),
    }


EXACT = lax.Precision.HIGHEST

@jax.custom_vjp
def low(v):
    return lax.optimization_barrier(v.astype(jnp.bfloat16)).astype(jnp.float32)

@jax.custom_vjp
def low_back(v):
    return v

def low_keep(v):
    return (low(v), None)

def low_pass(kept, grad):
    return (grad,)

def back_keep(v):
    return (v, None)

def back_low(kept, grad):
    return (low(grad),)
low.defvjp(low_keep, low_pass)
low_back.defvjp(back_keep, back_low)

def layer_norm(values):
    row_mean = lax.optimization_barrier(jnp.mean(values, -1, keepdims=True))
    centred = values - row_mean
    return centred * lax.rsqrt(lax.optimization_barrier(jnp.mean(centred * centred, -1, keepdims=True)) + 1e-06)

def attend(parts):
    queries, keys, values, segments = parts
    scores = jnp.einsum('qhe,khe->hqk', queries, keys, precision=EXACT) * (1.0 / math.sqrt(HEAD))
    scores = low_back(scores)
    same_seg = segments[:, None] == segments[None, :]
    attn_probs = jax.nn.softmax(jnp.where(same_seg[None], scores, -1e+30), axis=-1)
    return jnp.einsum('hqk,khe->qhe', low(attn_probs), values, precision=EXACT)

def forward(tok_value, cond_value, seg_block, index_block, params):
    row_count, length = (tok_value.shape[0], tok_value.shape[1])
    cond_hot = (index_block[:, :, None] == jnp.arange(SEGS, dtype=jnp.int32)[None, None, :]).astype(jnp.float32)
    chosen = jnp.einsum('rsk,rkd->rsd', cond_hot, cond_value, precision=EXACT)
    lead = low(chosen * jax.nn.sigmoid(chosen))
    token_hot = (seg_block[:, :, None] == jnp.arange(SEGS, dtype=jnp.int32)[None, None, :]).astype(jnp.float32)
    state = tok_value
    for layer_idx in range(LAYERS):
        ada_weight, ada_bias, qkv_weight, qkv_bias, out_weight, out_bias, up_weight, up_bias, down_weight, down_bias = [stack_item[layer_idx] for stack_item in params]
        modulation = low_back(jnp.einsum('rsd,de->rse', lead, ada_weight, precision=EXACT) + ada_bias)
        per_token = jnp.einsum('rls,rse->rle', token_hot, modulation, precision=EXACT)
        shift_attn, scale_attn, gate_attn, shift_mlp, scale_mlp, gate_mlp = jnp.split(per_token, 6, axis=-1)
        hidden_attn = low(layer_norm(state) * (1.0 + scale_attn) + shift_attn)
        qkv_rows = low(low_back(jnp.einsum('rld,de->rle', hidden_attn, qkv_weight, precision=EXACT) + qkv_bias))
        heads_view = qkv_rows.reshape(row_count, length, 3, HEADS, HEAD)
        attn_out = lax.map(jax.checkpoint(attend), (heads_view[:, :, 0], heads_view[:, :, 1], heads_view[:, :, 2], seg_block))
        attn_mixed = low(low_back(attn_out.reshape(row_count, length, D)))
        branch = low_back(jnp.einsum('rld,de->rle', attn_mixed, out_weight, precision=EXACT) + out_bias)
        middle = state + gate_attn * branch
        hidden_mlp = low(layer_norm(middle) * (1.0 + scale_mlp) + shift_mlp)
        up_proj = low_back(jnp.einsum('rld,df->rlf', hidden_mlp, up_weight, precision=EXACT) + up_bias)
        activated = low(jax.nn.gelu(up_proj, approximate=True))
        down_proj = low_back(jnp.einsum('rlf,fd->rld', activated, down_weight, precision=EXACT) + down_bias)
        state = middle + gate_mlp * down_proj
    return state

def reference(tokens, cond, seg_ids, cond_index, cotangent, ada_weight, ada_bias, qkv_weight, qkv_bias, out_weight, out_bias, up_weight, up_bias, down_weight, down_bias):
    weights = tuple((stack_item.astype(jnp.float32) for stack_item in (ada_weight, ada_bias, qkv_weight, qkv_bias, out_weight, out_bias, up_weight, up_bias, down_weight, down_bias)))
    block_count = ROWS // ROWS_DEV

    def shaped(array_in):
        return array_in.reshape((block_count, ROWS_DEV) + array_in.shape[1:])

    def block_step(totals, block):
        tok_block, cond_block, seg_block, index_block, cot_block = block

        def run_block(tok_value, cond_value, *params):
            return forward(tok_value, cond_value, seg_block, index_block, params)
        out_value, pull_back = jax.vjp(run_block, tok_block.astype(jnp.float32), cond_block.astype(jnp.float32), *weights)
        pulled = pull_back(cot_block.astype(jnp.float32))
        totals = tuple((total_item + grad_item for total_item, grad_item in zip(totals, pulled[2:])))
        return (totals, (out_value.astype(jnp.bfloat16), pulled[0], pulled[1]))
    zeros = tuple((jnp.zeros_like(stack_item) for stack_item in weights))
    totals, (outputs, token_grads, cond_grads) = lax.scan(block_step, zeros, (shaped(tokens), shaped(cond), shaped(seg_ids), shaped(cond_index), shaped(cotangent)))
    mixed = outputs.reshape(ROWS, ROW_LEN, D)
    token_grad = token_grads.reshape(ROWS, ROW_LEN, D)
    cond_grad = cond_grads.reshape(ROWS, SEGS, D)
    return (mixed, token_grad, cond_grad, totals[0], totals[1], totals[2], totals[3], totals[4], totals[5], totals[6], totals[7], totals[8], totals[9])
```

```python
from functools import partial
import math

import jax
import jax.numpy as jnp
from jax import lax
from jax.sharding import PartitionSpec as P

HEADS = 16
HEAD = 72
LAYERS = 2
SEGS = 4
EPS = 1e-06
EXACT = lax.Precision.HIGHEST
F32 = jnp.float32
BF16 = jnp.bfloat16


def dot(left, right, dims):
    return lax.dot_general(left, right, (dims, ((), ())), preferred_element_type=F32)


def norm(values):
    centred = values - jnp.mean(values, -1, keepdims=True)
    inv = lax.rsqrt(jnp.mean(centred * centred, -1, keepdims=True) + EPS)
    return centred * inv, inv


def norm_back(grad, unit, inv):
    return inv * (
        grad
        - jnp.mean(grad, -1, keepdims=True)
        - unit * jnp.mean(grad * unit, -1, keepdims=True)
    )


def gather_tokens(values):
    return lax.all_gather(values, "narrow", axis=0, tiled=True)


def scatter_tokens(values):
    return lax.psum_scatter(
        values.astype(BF16), "narrow", scatter_dimension=0, tiled=True
    ).astype(F32)


def gelu(values):
    return jax.nn.gelu(values, approximate=True)


def layer_forward(state, mods, same_seg, weights):
    qkv_w, qkv_b, out_w, out_b, up_w, up_b, down_w, down_b = weights
    shift_attn, scale_attn, gate_attn, shift_mlp, scale_mlp, gate_mlp = mods
    own_heads = out_w.shape[0] // HEAD
    unit_attn, inv_attn = norm(state)
    hidden_attn = gather_tokens((unit_attn * (1.0 + scale_attn) + shift_attn).astype(BF16))
    full_len = hidden_attn.shape[0]
    qkv = (dot(hidden_attn, qkv_w, ((1,), (0,))) + qkv_b).astype(BF16)
    queries, keys, values = [
        part.reshape(full_len, own_heads, HEAD) for part in jnp.split(qkv, 3, axis=-1)
    ]
    scores = jnp.einsum("qhe,khe->hqk", queries, keys, preferred_element_type=F32) * (
        1.0 / math.sqrt(HEAD)
    )
    probs = jax.nn.softmax(jnp.where(same_seg[None], scores, -1e30), axis=-1)
    mixed = jnp.einsum("hqk,khe->qhe", probs.astype(BF16), values, preferred_element_type=F32)
    mixed = mixed.reshape(full_len, own_heads * HEAD).astype(BF16)
    branch = scatter_tokens(dot(mixed, out_w, ((1,), (0,)))) + out_b
    middle = state + gate_attn * branch
    unit_mlp, inv_mlp = norm(middle)
    hidden_mlp = gather_tokens((unit_mlp * (1.0 + scale_mlp) + shift_mlp).astype(BF16))
    up_proj = dot(hidden_mlp, up_w, ((1,), (0,))) + up_b
    activated = gelu(up_proj).astype(BF16)
    down_proj = scatter_tokens(dot(activated, down_w, ((1,), (0,)))) + down_b
    result = middle + gate_mlp * down_proj
    kept = (
        unit_attn, inv_attn, hidden_attn, queries, keys, values, probs, mixed, branch,
        unit_mlp, inv_mlp, hidden_mlp, up_proj, activated, down_proj,
    )
    return result, kept


def layer_backward(grad_out, kept, mods, weights):
    qkv_w, qkv_b, out_w, out_b, up_w, up_b, down_w, down_b = weights
    shift_attn, scale_attn, gate_attn, shift_mlp, scale_mlp, gate_mlp = mods
    (
        unit_attn, inv_attn, hidden_attn, queries, keys, values, probs, mixed, branch,
        unit_mlp, inv_mlp, hidden_mlp, up_proj, activated, down_proj,
    ) = kept
    scale_inv = 1.0 / math.sqrt(HEAD)
    full_len = hidden_attn.shape[0]
    own_down = (gate_mlp * grad_out).astype(BF16)
    grad_gate_mlp = down_proj * grad_out
    grad_down = gather_tokens(own_down)
    grad_act = dot(grad_down, down_w, ((1,), (1,)))
    grad_up = jax.vjp(gelu, up_proj)[1](grad_act)[0].astype(BF16)
    grad_hidden_mlp = scatter_tokens(dot(grad_up, up_w, ((1,), (1,))))
    grad_down_w = dot(activated, grad_down, ((0,), (0,)))
    grad_up_w = dot(hidden_mlp, grad_up, ((0,), (0,)))
    grad_middle = grad_out + norm_back(grad_hidden_mlp * (1.0 + scale_mlp), unit_mlp, inv_mlp)
    own_branch = (gate_attn * grad_middle).astype(BF16)
    grad_gate_attn = branch * grad_middle
    grad_branch = gather_tokens(own_branch)
    grad_attn = dot(grad_branch, out_w, ((1,), (1,))).astype(BF16).reshape(queries.shape)
    grad_probs = jnp.einsum("qhe,khe->hqk", grad_attn, values, preferred_element_type=F32)
    grad_scores = probs * (grad_probs - jnp.sum(probs * grad_probs, -1, keepdims=True))
    grad_scores = grad_scores.astype(BF16)
    grad_q = jnp.einsum("hqk,khe->qhe", grad_scores, keys, preferred_element_type=F32) * scale_inv
    grad_k = jnp.einsum("hqk,qhe->khe", grad_scores, queries, preferred_element_type=F32) * scale_inv
    grad_v = jnp.einsum("hqk,qhe->khe", probs.astype(BF16), grad_attn, preferred_element_type=F32)
    grad_qkv = jnp.concatenate(
        [part.astype(BF16).reshape(full_len, -1) for part in (grad_q, grad_k, grad_v)], axis=-1
    )
    grad_hidden_attn = scatter_tokens(dot(grad_qkv, qkv_w, ((1,), (1,))))
    grad_out_w = dot(mixed, grad_branch, ((0,), (0,)))
    grad_qkv_w = dot(hidden_attn, grad_qkv, ((0,), (0,)))
    grad_state = grad_middle + norm_back(grad_hidden_attn * (1.0 + scale_attn), unit_attn, inv_attn)
    token_mod = jnp.concatenate(
        [
            grad_hidden_attn, grad_hidden_attn * unit_attn, grad_gate_attn,
            grad_hidden_mlp, grad_hidden_mlp * unit_mlp, grad_gate_mlp,
        ],
        axis=-1,
    )
    bias_grads = (
        jnp.sum(grad_qkv.astype(F32), 0),
        jnp.sum(own_branch.astype(F32), 0),
        jnp.sum(grad_up.astype(F32), 0),
        jnp.sum(own_down.astype(F32), 0),
    )
    return grad_state, token_mod, (grad_qkv_w, grad_out_w, grad_up_w, grad_down_w), bias_grads


def per_device(
    wide, narrow,
    tokens, cond, seg_ids, cond_index, cotangent,
    ada_weight, ada_bias, qkv_weight, qkv_bias, out_weight, out_bias,
    up_weight, up_bias, down_weight, down_bias,
):
    w = lax.axis_index("wide")
    n = lax.axis_index("narrow")
    local_len, width = tokens.shape[1:]
    depth = width // wide
    cols = width // narrow
    hidden_own = up_weight.shape[-1] // wide // narrow
    mod_cols = ada_weight.shape[-1] // narrow

    def own(values, axis):
        return lax.dynamic_index_in_dim(values, n, axis, keepdims=False)

    bias_parts = (ada_bias, qkv_bias, out_bias, up_bias, down_bias)
    sizes = [part.shape[1] for part in bias_parts]
    packed = lax.all_gather(jnp.concatenate(bias_parts, axis=1), "wide", axis=1, tiled=False)
    biases = []
    at = 0
    for size in sizes:
        biases.append(packed[:, :, at : at + size].reshape(LAYERS, -1).astype(F32))
        at += size
    ada_b, qkv_b, out_b, up_b, down_b = biases
    qkv_b = own(qkv_b.reshape(LAYERS, 3, narrow, cols), 2).reshape(LAYERS, 3 * cols)
    up_b = own(up_b.reshape(LAYERS, wide, narrow, hidden_own), 2).reshape(LAYERS, -1)

    cond_hot = (cond_index[0, :, None] == jnp.arange(SEGS, dtype=jnp.int32)[None, :]).astype(F32)
    chosen = jnp.dot(cond_hot, cond[0].astype(F32), precision=EXACT)
    lead = (chosen * jax.nn.sigmoid(chosen)).astype(BF16)
    lead_all = lax.all_gather(lead, "wide", axis=0, tiled=True)
    lead_own = lax.dynamic_slice_in_dim(lead_all, w * depth, depth, 1)
    ada_quarter = lax.dynamic_slice_in_dim(ada_weight, n * mod_cols, mod_cols, 2)
    mod_part = jnp.einsum("nd,lde->nle", lead_own, ada_quarter, preferred_element_type=F32)
    mod_part = lax.psum_scatter(mod_part, "wide", scatter_dimension=0, tiled=True)
    modulation = lax.all_gather(mod_part, "narrow", axis=2, tiled=True)
    modulation = modulation.transpose(1, 0, 2) + ada_b[:, None, :]

    seg_row = seg_ids[0]
    seg_query = lax.dynamic_slice_in_dim(seg_row, n * local_len, local_len, 0)
    token_hot = (seg_query[:, None] == jnp.arange(SEGS, dtype=jnp.int32)[None, :]).astype(F32)
    same_seg = seg_row[:, None] == seg_row[None, :]

    qkv_own = own(qkv_weight.reshape(LAYERS, depth, 3, narrow, cols), 3).reshape(LAYERS, depth, 3 * cols)
    up_own = own(up_weight.reshape(LAYERS, depth, wide, narrow, hidden_own), 3).reshape(LAYERS, depth, -1)
    down_own = own(down_weight.reshape(LAYERS, narrow, hidden_own, width), 1)

    def fetch(idx):
        out_full = lax.all_gather(out_weight[idx], "wide", axis=0, tiled=True)
        return (
            lax.all_gather(qkv_own[idx], "wide", axis=0, tiled=True),
            qkv_b[idx],
            lax.dynamic_slice_in_dim(out_full, n * cols, cols, 0),
            out_b[idx],
            lax.all_gather(up_own[idx], "wide", axis=0, tiled=True),
            up_b[idx],
            lax.all_gather(down_own[idx], "wide", axis=0, tiled=True),
            down_b[idx],
        )

    state = tokens[0].astype(F32)
    weights, mods, kept = [], [], []
    for idx in range(LAYERS):
        weights.append(fetch(idx))
        per_token = jnp.dot(token_hot, modulation[idx], precision=EXACT)
        mods.append(jnp.split(per_token, 6, axis=-1))
        state, saved = layer_forward(state, mods[idx], same_seg, weights[idx])
        kept.append(saved)
    result = state.astype(BF16)

    grad_state = cotangent[0].astype(F32)
    token_hot_t = token_hot.T
    reduced, bias_sums, mod_grads = [None] * LAYERS, [None] * LAYERS, [None] * LAYERS
    for idx in reversed(range(LAYERS)):
        grad_state, token_mod, grads, bias_grads = layer_backward(
            grad_state, kept[idx], mods[idx], weights[idx]
        )
        mod_grads[idx] = jnp.dot(token_hot_t, token_mod, precision=EXACT)
        qkv_g, out_g, up_g, down_g = [item.astype(BF16) for item in grads]
        qkv_g, up_g, down_g = [
            lax.psum_scatter(item, "wide", scatter_dimension=0, tiled=True)
            for item in (qkv_g, up_g, down_g)
        ]
        out_g = lax.psum(out_g, "wide")
        qkv_g = lax.all_gather(qkv_g.reshape(depth, 3, 1, cols), "narrow", axis=2, tiled=True)
        up_g = lax.all_gather(up_g.reshape(depth, wide, 1, hidden_own), "narrow", axis=2, tiled=True)
        down_g = lax.all_gather(down_g, "narrow", axis=0, tiled=True)
        out_g = lax.all_gather(out_g, "narrow", axis=0, tiled=True)
        out_g = lax.dynamic_slice_in_dim(out_g, w * depth, depth, 0)
        reduced[idx] = (
            qkv_g.reshape(depth, 3 * width),
            out_g,
            up_g.reshape(depth, -1),
            down_g,
        )
        spot = lax.broadcasted_iota(jnp.int32, (1, narrow, 1), 1) == n
        qkv_s = jnp.where(spot, bias_grads[0].reshape(3, 1, cols), 0.0).reshape(-1)
        up_s = jnp.where(spot, bias_grads[2].reshape(wide, 1, hidden_own), 0.0).reshape(-1)
        bias_sums[idx] = [
            item.reshape(wide, -1) for item in (qkv_s, bias_grads[1], up_s, bias_grads[3])
        ]
    sizes = [item.shape[1] for item in bias_sums[0]]
    bias_sum = jnp.stack([jnp.concatenate(item, axis=1) for item in bias_sums], axis=1)
    bias_sum = lax.psum_scatter(lax.psum(bias_sum, "narrow"), "wide", scatter_dimension=0, tiled=True)[0]
    bias_out = []
    at = 0
    for size in sizes:
        bias_out.append(bias_sum[:, at : at + size])
        at += size

    mod_grad = lax.psum(jnp.stack(mod_grads), "narrow").astype(BF16)
    mod_all = lax.all_gather(mod_grad, "wide", axis=1, tiled=True)
    ada_grad = jnp.einsum("nd,lne->lde", lead_own, mod_all, preferred_element_type=F32)
    ada_size = ada_bias.shape[1]
    ada_bias_grad = jnp.sum(
        lax.dynamic_slice_in_dim(mod_all, w * ada_size, ada_size, 2).astype(F32), axis=1
    )
    lead_grad = jnp.einsum("lne,lde->nd", mod_all, ada_weight, preferred_element_type=F32)
    lead_grad = lax.all_to_all(lead_grad.reshape(wide, SEGS, depth), "wide", 0, 0, tiled=False)
    lead_grad = lead_grad.transpose(1, 0, 2).reshape(SEGS, width)
    gate = jax.nn.sigmoid(chosen)
    chosen_grad = lead_grad * (gate * (1.0 + chosen * (1.0 - gate)))
    cond_grad = jnp.dot(cond_hot.T, chosen_grad, precision=EXACT)

    stacked = [
        jnp.stack([reduced[idx][pos].astype(F32) for idx in range(LAYERS)]) for pos in range(4)
    ]
    return (
        result[None], grad_state[None], cond_grad[None],
        ada_grad, ada_bias_grad,
        stacked[0], bias_out[0], stacked[1], bias_out[1],
        stacked[2], bias_out[2], stacked[3], bias_out[3],
    )


def solution(mesh):
    matrix, vector = P(None, "wide", None), P(None, "wide")
    rows, cond_rows = P("wide", "narrow", None), P("wide", None, None)
    return jax.shard_map(
        partial(per_device, mesh.shape["wide"], mesh.shape["narrow"]),
        mesh=mesh,
        in_specs=(rows, cond_rows, P("wide", None), P("wide", None), rows) + (matrix, vector) * 5,
        out_specs=(rows, rows, cond_rows) + (matrix, vector) * 5,
        check_vma=False,
    )
```

```python
from functools import partial
import math
from types import SimpleNamespace

import jax
import jax.numpy as jnp
from jax import lax
from jax.experimental import pallas as pl
from jax.experimental.pallas import tpu as pltpu
from jax.sharding import PartitionSpec as P

HEADS = 16
HEAD = 72
LAYERS = 2
SEGS = 4
EPS = 1e-06
EXACT = lax.Precision.HIGHEST
F32 = jnp.float32
BF16 = jnp.bfloat16


def dot(left, right, dims):
    return lax.dot_general(left, right, (dims, ((), ())), preferred_element_type=F32)


def norm(values):
    centred = values - jnp.mean(values, -1, keepdims=True)
    inv = lax.rsqrt(jnp.mean(centred * centred, -1, keepdims=True) + EPS)
    return centred * inv, inv


def norm_back(grad, unit, inv):
    return inv * (
        grad
        - jnp.mean(grad, -1, keepdims=True)
        - unit * jnp.mean(grad * unit, -1, keepdims=True)
    )


def gather_tokens(values):
    return lax.all_gather(values, "narrow", axis=0, tiled=True)


def scatter_tokens(values):
    return lax.psum_scatter(
        values.astype(BF16), "narrow", scatter_dimension=0, tiled=True
    ).astype(F32)


def gelu(values):
    return jax.nn.gelu(values, approximate=True)


def layer_forward(state, mods, same_seg, weights):
    qkv_w, qkv_b, out_w, out_b, up_w, up_b, down_w, down_b = weights
    shift_attn, scale_attn, gate_attn, shift_mlp, scale_mlp, gate_mlp = mods
    own_heads = out_w.shape[0] // HEAD
    unit_attn, inv_attn = norm(state)
    hidden_attn = gather_tokens((unit_attn * (1.0 + scale_attn) + shift_attn).astype(BF16))
    full_len = hidden_attn.shape[0]
    qkv = (dot(hidden_attn, qkv_w, ((1,), (0,))) + qkv_b).astype(BF16)
    queries, keys, values = [
        part.reshape(full_len, own_heads, HEAD) for part in jnp.split(qkv, 3, axis=-1)
    ]
    scores = jnp.einsum("qhe,khe->hqk", queries, keys, preferred_element_type=F32) * (
        1.0 / math.sqrt(HEAD)
    )
    probs = jax.nn.softmax(jnp.where(same_seg[None], scores, -1e30), axis=-1)
    mixed = jnp.einsum("hqk,khe->qhe", probs.astype(BF16), values, preferred_element_type=F32)
    mixed = mixed.reshape(full_len, own_heads * HEAD).astype(BF16)
    branch = scatter_tokens(dot(mixed, out_w, ((1,), (0,)))) + out_b
    middle = state + gate_attn * branch
    unit_mlp, inv_mlp = norm(middle)
    hidden_mlp = gather_tokens((unit_mlp * (1.0 + scale_mlp) + shift_mlp).astype(BF16))
    up_proj = dot(hidden_mlp, up_w, ((1,), (0,))) + up_b
    activated = gelu(up_proj).astype(BF16)
    down_proj = scatter_tokens(dot(activated, down_w, ((1,), (0,)))) + down_b
    result = middle + gate_mlp * down_proj
    kept = (
        unit_attn, inv_attn, hidden_attn, queries, keys, values, probs, mixed, branch,
        unit_mlp, inv_mlp, hidden_mlp, up_proj, activated, down_proj,
    )
    return result, kept


def layer_backward(grad_out, kept, mods, weights):
    qkv_w, qkv_b, out_w, out_b, up_w, up_b, down_w, down_b = weights
    shift_attn, scale_attn, gate_attn, shift_mlp, scale_mlp, gate_mlp = mods
    (
        unit_attn, inv_attn, hidden_attn, queries, keys, values, probs, mixed, branch,
        unit_mlp, inv_mlp, hidden_mlp, up_proj, activated, down_proj,
    ) = kept
    scale_inv = 1.0 / math.sqrt(HEAD)
    full_len = hidden_attn.shape[0]
    own_down = (gate_mlp * grad_out).astype(BF16)
    grad_gate_mlp = down_proj * grad_out
    grad_down = gather_tokens(own_down)
    grad_act = dot(grad_down, down_w, ((1,), (1,)))
    grad_up = jax.vjp(gelu, up_proj)[1](grad_act)[0].astype(BF16)
    grad_hidden_mlp = scatter_tokens(dot(grad_up, up_w, ((1,), (1,))))
    grad_down_w = dot(activated, grad_down, ((0,), (0,)))
    grad_up_w = dot(hidden_mlp, grad_up, ((0,), (0,)))
    grad_middle = grad_out + norm_back(grad_hidden_mlp * (1.0 + scale_mlp), unit_mlp, inv_mlp)
    own_branch = (gate_attn * grad_middle).astype(BF16)
    grad_gate_attn = branch * grad_middle
    grad_branch = gather_tokens(own_branch)
    grad_attn = dot(grad_branch, out_w, ((1,), (1,))).astype(BF16).reshape(queries.shape)
    grad_probs = jnp.einsum("qhe,khe->hqk", grad_attn, values, preferred_element_type=F32)
    grad_scores = probs * (grad_probs - jnp.sum(probs * grad_probs, -1, keepdims=True))
    grad_scores = grad_scores.astype(BF16)
    grad_q = jnp.einsum("hqk,khe->qhe", grad_scores, keys, preferred_element_type=F32) * scale_inv
    grad_k = jnp.einsum("hqk,qhe->khe", grad_scores, queries, preferred_element_type=F32) * scale_inv
    grad_v = jnp.einsum("hqk,qhe->khe", probs.astype(BF16), grad_attn, preferred_element_type=F32)
    grad_qkv = jnp.concatenate(
        [part.astype(BF16).reshape(full_len, -1) for part in (grad_q, grad_k, grad_v)], axis=-1
    )
    grad_hidden_attn = scatter_tokens(dot(grad_qkv, qkv_w, ((1,), (1,))))
    grad_out_w = dot(mixed, grad_branch, ((0,), (0,)))
    grad_qkv_w = dot(hidden_attn, grad_qkv, ((0,), (0,)))
    grad_state = grad_middle + norm_back(grad_hidden_attn * (1.0 + scale_attn), unit_attn, inv_attn)
    token_mod = jnp.concatenate(
        [
            grad_hidden_attn, grad_hidden_attn * unit_attn, grad_gate_attn,
            grad_hidden_mlp, grad_hidden_mlp * unit_mlp, grad_gate_mlp,
        ],
        axis=-1,
    )
    bias_grads = (
        jnp.sum(grad_qkv.astype(F32), 0),
        jnp.sum(own_branch.astype(F32), 0),
        jnp.sum(grad_up.astype(F32), 0),
        jnp.sum(own_down.astype(F32), 0),
    )
    return grad_state, token_mod, (grad_qkv_w, grad_out_w, grad_up_w, grad_down_w), bias_grads


def plain_device(
    wide, narrow,
    tokens, cond, seg_ids, cond_index, cotangent,
    ada_weight, ada_bias, qkv_weight, qkv_bias, out_weight, out_bias,
    up_weight, up_bias, down_weight, down_bias,
):
    w = lax.axis_index("wide")
    n = lax.axis_index("narrow")
    local_len, width = tokens.shape[1:]
    depth = width // wide
    cols = width // narrow
    hidden_own = up_weight.shape[-1] // wide // narrow
    mod_cols = ada_weight.shape[-1] // narrow

    def own(values, axis):
        return lax.dynamic_index_in_dim(values, n, axis, keepdims=False)

    bias_parts = (ada_bias, qkv_bias, out_bias, up_bias, down_bias)
    sizes = [part.shape[1] for part in bias_parts]
    packed = lax.all_gather(jnp.concatenate(bias_parts, axis=1), "wide", axis=1, tiled=False)
    biases = []
    at = 0
    for size in sizes:
        biases.append(packed[:, :, at : at + size].reshape(LAYERS, -1).astype(F32))
        at += size
    ada_b, qkv_b, out_b, up_b, down_b = biases
    qkv_b = own(qkv_b.reshape(LAYERS, 3, narrow, cols), 2).reshape(LAYERS, 3 * cols)
    up_b = own(up_b.reshape(LAYERS, wide, narrow, hidden_own), 2).reshape(LAYERS, -1)

    cond_hot = (cond_index[0, :, None] == jnp.arange(SEGS, dtype=jnp.int32)[None, :]).astype(F32)
    chosen = jnp.dot(cond_hot, cond[0].astype(F32), precision=EXACT)
    lead = (chosen * jax.nn.sigmoid(chosen)).astype(BF16)
    lead_all = lax.all_gather(lead, "wide", axis=0, tiled=True)
    lead_own = lax.dynamic_slice_in_dim(lead_all, w * depth, depth, 1)
    ada_quarter = lax.dynamic_slice_in_dim(ada_weight, n * mod_cols, mod_cols, 2)
    mod_part = jnp.einsum("nd,lde->nle", lead_own, ada_quarter, preferred_element_type=F32)
    mod_part = lax.psum_scatter(mod_part, "wide", scatter_dimension=0, tiled=True)
    modulation = lax.all_gather(mod_part, "narrow", axis=2, tiled=True)
    modulation = modulation.transpose(1, 0, 2) + ada_b[:, None, :]

    seg_row = seg_ids[0]
    seg_query = lax.dynamic_slice_in_dim(seg_row, n * local_len, local_len, 0)
    token_hot = (seg_query[:, None] == jnp.arange(SEGS, dtype=jnp.int32)[None, :]).astype(F32)
    same_seg = seg_row[:, None] == seg_row[None, :]

    qkv_own = own(qkv_weight.reshape(LAYERS, depth, 3, narrow, cols), 3).reshape(LAYERS, depth, 3 * cols)
    up_own = own(up_weight.reshape(LAYERS, depth, wide, narrow, hidden_own), 3).reshape(LAYERS, depth, -1)
    down_own = own(down_weight.reshape(LAYERS, narrow, hidden_own, width), 1)

    def fetch(idx):
        out_full = lax.all_gather(out_weight[idx], "wide", axis=0, tiled=True)
        return (
            lax.all_gather(qkv_own[idx], "wide", axis=0, tiled=True),
            qkv_b[idx],
            lax.dynamic_slice_in_dim(out_full, n * cols, cols, 0),
            out_b[idx],
            lax.all_gather(up_own[idx], "wide", axis=0, tiled=True),
            up_b[idx],
            lax.all_gather(down_own[idx], "wide", axis=0, tiled=True),
            down_b[idx],
        )

    state = tokens[0].astype(F32)
    weights, mods, kept = [], [], []
    for idx in range(LAYERS):
        weights.append(fetch(idx))
        per_token = jnp.dot(token_hot, modulation[idx], precision=EXACT)
        mods.append(jnp.split(per_token, 6, axis=-1))
        state, saved = layer_forward(state, mods[idx], same_seg, weights[idx])
        kept.append(saved)
    result = state.astype(BF16)

    grad_state = cotangent[0].astype(F32)
    token_hot_t = token_hot.T
    reduced, bias_sums, mod_grads = [None] * LAYERS, [None] * LAYERS, [None] * LAYERS
    for idx in reversed(range(LAYERS)):
        grad_state, token_mod, grads, bias_grads = layer_backward(
            grad_state, kept[idx], mods[idx], weights[idx]
        )
        mod_grads[idx] = jnp.dot(token_hot_t, token_mod, precision=EXACT)
        qkv_g, out_g, up_g, down_g = [item.astype(BF16) for item in grads]
        qkv_g, up_g, down_g = [
            lax.psum_scatter(item, "wide", scatter_dimension=0, tiled=True)
            for item in (qkv_g, up_g, down_g)
        ]
        out_g = lax.psum(out_g, "wide")
        qkv_g = lax.all_gather(qkv_g.reshape(depth, 3, 1, cols), "narrow", axis=2, tiled=True)
        up_g = lax.all_gather(up_g.reshape(depth, wide, 1, hidden_own), "narrow", axis=2, tiled=True)
        down_g = lax.all_gather(down_g, "narrow", axis=0, tiled=True)
        out_g = lax.all_gather(out_g, "narrow", axis=0, tiled=True)
        out_g = lax.dynamic_slice_in_dim(out_g, w * depth, depth, 0)
        reduced[idx] = (
            qkv_g.reshape(depth, 3 * width),
            out_g,
            up_g.reshape(depth, -1),
            down_g,
        )
        spot = lax.broadcasted_iota(jnp.int32, (1, narrow, 1), 1) == n
        qkv_s = jnp.where(spot, bias_grads[0].reshape(3, 1, cols), 0.0).reshape(-1)
        up_s = jnp.where(spot, bias_grads[2].reshape(wide, 1, hidden_own), 0.0).reshape(-1)
        bias_sums[idx] = [
            item.reshape(wide, -1) for item in (qkv_s, bias_grads[1], up_s, bias_grads[3])
        ]
    sizes = [item.shape[1] for item in bias_sums[0]]
    bias_sum = jnp.stack([jnp.concatenate(item, axis=1) for item in bias_sums], axis=1)
    bias_sum = lax.psum_scatter(lax.psum(bias_sum, "narrow"), "wide", scatter_dimension=0, tiled=True)[0]
    bias_out = []
    at = 0
    for size in sizes:
        bias_out.append(bias_sum[:, at : at + size])
        at += size

    mod_grad = lax.psum(jnp.stack(mod_grads), "narrow").astype(BF16)
    mod_all = lax.all_gather(mod_grad, "wide", axis=1, tiled=True)
    ada_grad = jnp.einsum("nd,lne->lde", lead_own, mod_all, preferred_element_type=F32)
    ada_size = ada_bias.shape[1]
    ada_bias_grad = jnp.sum(
        lax.dynamic_slice_in_dim(mod_all, w * ada_size, ada_size, 2).astype(F32), axis=1
    )
    lead_grad = jnp.einsum("lne,lde->nd", mod_all, ada_weight, preferred_element_type=F32)
    lead_grad = lax.all_to_all(lead_grad.reshape(wide, SEGS, depth), "wide", 0, 0, tiled=False)
    lead_grad = lead_grad.transpose(1, 0, 2).reshape(SEGS, width)
    gate = jax.nn.sigmoid(chosen)
    chosen_grad = lead_grad * (gate * (1.0 + chosen * (1.0 - gate)))
    cond_grad = jnp.dot(cond_hot.T, chosen_grad, precision=EXACT)

    stacked = [
        jnp.stack([reduced[idx][pos].astype(F32) for idx in range(LAYERS)]) for pos in range(4)
    ]
    return (
        result[None], grad_state[None], cond_grad[None],
        ada_grad, ada_bias_grad,
        stacked[0], bias_out[0], stacked[1], bias_out[1],
        stacked[2], bias_out[2], stacked[3], bias_out[3],
    )


QKV, OUT, UP, DOWN = range(4)
PLANES = 4
PAIR = 2
LANES = 128
STEP = 32
MESH = pl.DeviceIdType.MESH


def mod_start(tiles, parts, part):
    return tiles * part // parts


def block_kernel(cfg, *refs):
    r = SimpleNamespace(**dict(zip(cfg.names, refs)))
    wide, narrow, width, depth = cfg.wide, cfg.narrow, cfg.width, cfg.depth
    local, cols, mod_cols, tiles = cfg.local, cfg.cols, cfg.mod_cols, cfg.tiles
    half = local // 2
    own_heads = cols // HEAD
    scale_inv = 1.0 / math.sqrt(HEAD)
    w = lax.axis_index("wide")
    n = lax.axis_index("narrow")
    z, x = w // PAIR, w % PAIR
    y, c = n // 2, n % 2
    n_core = n + 1 - 2 * c
    n_side = n + 2 - 4 * y
    n_far = 3 - n
    core, side, far = (w, n_core), (w, n_side), (w, n_far)
    beside = (w + 1 - 2 * x, n)

    def plane_of(j):
        return (z + j) % PLANES

    def plane(j):
        return (plane_of(j) * PAIR + x, n)

    def wide_peer(j):
        return ((w + j) % wide, n)

    def remote(src, dst, sems, device):
        return pltpu.make_async_remote_copy(
            src_ref=src, dst_ref=dst, send_sem=sems[0], recv_sem=sems[1],
            device_id=device, device_id_type=MESH,
        )

    def span(start, size, step=16):
        return pl.ds(pl.multiple_of(start, step), size)

    barrier = pltpu.get_barrier_semaphore()
    partners = [core, side, far] + [wide_peer(j) for j in range(1, wide)]
    for partner in partners:
        pl.semaphore_signal(barrier, inc=1, device_id=partner, device_id_type=MESH)
    pl.semaphore_wait(barrier, len(partners))

    shards = (r.qkv_s, r.out_s, r.up_s, r.down_s)
    full = (r.qkv_h, r.out_h, r.up_h, r.down_h)
    loaded = (r.qkv_v, r.out_v, r.up_v, r.down_v)

    def w_rows(which, plane_idx, col):
        if which == OUT:
            return span(col * depth, depth)
        return span((plane_idx * PAIR + col) * depth, depth)

    def w_block(which, layer, plane_idx, col):
        return full[which].at[layer, w_rows(which, plane_idx, col)]

    def w_z(which, layer, j):
        slot = layer * 4 + which
        k = 0 if which == OUT else j - 1
        return remote(
            shards[which].at[layer], w_block(which, layer, z, x),
            (r.wz_s.at[slot, j - 1], r.wz_r.at[slot, k]), plane(j),
        )

    def w_z_in(which, layer, j):
        slot = layer * 4 + which
        src_plane = n if which == OUT else (z - j + PLANES) % PLANES
        k = 0 if which == OUT else j - 1
        block = w_block(which, layer, src_plane, x)
        return remote(block, block, (r.wz_s.at[slot, k], r.wz_r.at[slot, k]), plane(j)), src_plane

    def w_x(which, layer, j, src, plane_idx, col):
        slot = layer * 4 + which
        return remote(
            src, w_block(which, layer, plane_idx, col),
            (r.wx_s.at[slot, j], r.wx_r.at[slot, j]), beside,
        )

    def w_own(which, layer):
        return pltpu.make_async_copy(
            shards[which].at[layer], w_block(which, layer, z, x), r.w_own.at[layer * 4 + which]
        )

    def weights_start(which, layer):
        def go():
            w_own(which, layer).start()
            for j in range(1, PLANES):
                w_z(which, layer, j).start()

        if which == OUT:
            pl.when(z == n)(go)
        else:
            go()

    def weights_forward(which, layer):
        def own():
            w_x(which, layer, 0, shards[which].at[layer], z, x).start()

        def passed(j):
            arrived, src_plane = w_z_in(which, layer, j)
            arrived.wait_recv()
            k = 0 if which == OUT else j
            w_x(which, layer, k, w_block(which, layer, src_plane, x), src_plane, x).start()

        if which == OUT:
            pl.when(z == n)(own)
            pl.when(z != n)(lambda: passed(1))
        else:
            own()
            for j in range(1, PLANES):
                passed(j)

    def weights_finish(which, layer):
        if which == OUT:
            block = w_block(which, layer, n, 1 - x)
            w_x(which, layer, 0, block, n, 1 - x).wait_recv()
            pl.when(z == n)(lambda: w_own(which, layer).wait())
        else:
            for j in range(PLANES):
                src_plane = (z - j + PLANES) % PLANES
                block = w_block(which, layer, src_plane, 1 - x)
                w_x(which, layer, j, block, src_plane, 1 - x).wait_recv()
            w_own(which, layer).wait()

    def weights_drain(which, layer):
        if which == OUT:
            w_x(which, layer, 0, shards[which].at[layer], z, x).wait_send()

            @pl.when(z == n)
            def _():
                for j in range(1, PLANES):
                    w_z(which, layer, j).wait_send()
        else:
            for j in range(PLANES):
                w_x(which, layer, j, shards[which].at[layer], z, x).wait_send()
            for j in range(1, PLANES):
                w_z(which, layer, j).wait_send()

    def load(which, layer):
        return pltpu.make_async_copy(full[which].at[layer], loaded[which], r.load_sem.at[which])

    def weights_ready(which, layer):
        weights_finish(which, layer)
        load(which, layer).start()
        load(which, layer).wait()

    def tok_rows(chunk, part):
        return span(local * chunk + half * part, half)

    def tok_copy(ref, kind, part, incoming=False):
        chunk = ((n_core, n_side, n_far) if incoming else (n, n, n_side))[kind]
        rows = ref.at[tok_rows(chunk, part)]
        k = 2 * kind + part
        return remote(rows, rows, (r.tok_s.at[k], r.tok_r.at[k]), side if kind == 1 else core)

    def tok_send(ref, part):
        tok_copy(ref, 1, part).start()
        tok_copy(ref, 0, part).start()

    def tok_own(ref):
        for part in range(2):
            tok_copy(ref, 0, part, True).wait_recv()

    def tok_other(ref):
        for part in range(2):
            tok_copy(ref, 1, part, True).wait_recv()
            tok_copy(ref, 2, part).start()
        for part in range(2):
            tok_copy(ref, 2, part, True).wait_recv()

    def tok_drain(ref):
        for kind in range(3):
            for part in range(2):
                tok_copy(ref, kind, part).wait_send()

    def block_rows(block):
        return span(2 * local * (y if block else 1 - y), 2 * local)

    def sum_core(block):
        return remote(
            r.core_tx.at[block], r.core_rx.at[block], (r.sum_s.at[block], r.sum_r.at[block]), core
        )

    def sum_side(part):
        rows = span(half * part, half)
        return remote(
            r.side_tx.at[rows], r.side_rx.at[rows], (r.sum_s.at[2 + part], r.sum_r.at[2 + part]), side
        )

    def sum_block(block):
        r.core_tx[block] = r.part[block, span(local * (1 - c), local), :].astype(BF16)
        sum_core(block).start()

    def sum_cross():
        sum_core(0).wait_recv()
        for part in range(2):
            rows = span(half * part, half)
            mine = r.part[0, span(local * c + half * part, half), :]
            r.side_tx[rows, :] = (mine + r.core_rx[0, rows, :].astype(F32)).astype(BF16)
            sum_side(part).start()

    def sum_wait(part):
        if part == 0:
            sum_core(1).wait_recv()
        sum_side(part).wait_recv()
        if part == 1:
            for block in range(2):
                sum_core(block).wait_send()
                sum_side(block).wait_send()

    def sum_take(start):
        rows = span(start, STEP)
        return (
            r.part[1, span(local * c + start, STEP), :]
            + r.core_rx[1, rows, :].astype(F32)
            + r.side_rx[rows, :].astype(F32)
        )

    def each_step(part, body):
        @pl.loop(0, half // STEP)
        def _(i):
            body(half * part + STEP * i)

    def seg_of(start):
        return r.seg_own[span(start, STEP), :]

    def mod(layer, block, seg):
        rows = r.mods[SEGS * layer : SEGS * layer + SEGS, width * block : width * (block + 1)]
        out = rows[SEGS - 1 : SEGS]
        for s in range(SEGS - 1):
            out = jnp.where(seg == s, rows[s : s + 1], out)
        return out

    def mod_sum(layer, block, seg, values):
        sums = [jnp.sum(jnp.where(seg == s, values, 0.0), 0, keepdims=True) for s in range(SEGS)]
        at = (slice(SEGS * layer, SEGS * layer + SEGS), slice(width * block, width * (block + 1)))
        r.mod_grad[at] += jnp.concatenate(sums, 0)

    def lead_copy(j, incoming=False):
        return remote(
            r.lead.at[(w + j) % wide], r.lead_rx.at[(w - j + wide) % wide if incoming else w],
            (r.lead_sem_s.at[j - 1], r.lead_sem_r.at[j - 1]), wide_peer(j),
        )

    def bias_copy(j, incoming=False):
        return remote(
            r.bias, r.bias_rx.at[(w - j + wide) % wide if incoming else w],
            (r.bias_sem_s.at[j - 1], r.bias_sem_r.at[j - 1]), wide_peer(j),
        )

    def mod_copy(j, incoming=False):
        return remote(
            r.mod_tx.at[(w + j) % wide], r.mod_rx.at[(w - j + wide) % wide if incoming else w],
            (r.mod_sem_s.at[j - 1], r.mod_sem_r.at[j - 1]), wide_peer(j),
        )

    narrow_peers = ((core, n_core), (side, n_side), (far, n_far))

    def quarter_copy(k, incoming=False):
        device, idx = narrow_peers[k]
        return remote(
            r.mod_q.at[n], r.mod_q.at[idx if incoming else n],
            (r.quarter_s.at[k], r.quarter_r.at[k]), device,
        )

    ada_load = pltpu.make_async_copy(
        r.ada.at[:, :, span(LANES * mod_start(tiles, narrow, n), mod_cols, LANES)], r.ada_v, r.ada_sem
    )
    ada_load.start()
    for j in range(1, wide):
        lead_copy(j).start()
    weights_start(QKV, 0)
    for j in range(1, wide):
        bias_copy(j).start()
    r.lead_rx[pl.ds(w, 1)] = r.lead[pl.ds(w, 1)]
    r.bias_rx[pl.ds(w, 1)] = r.bias[...][None]
    r.mod_grad[...] = jnp.zeros_like(r.mod_grad)
    ada_load.wait()
    for j in range(1, wide):
        lead_copy(j, True).wait_recv()
    lead_all = r.lead_rx[...].reshape(wide * 16, depth)
    for layer in range(LAYERS):
        product = dot(lead_all, r.ada_v[layer], ((1,), (0,)))
        at = slice(SEGS * layer, SEGS * layer + SEGS)
        for row in range(wide):
            r.mod_tx[row, at, :] = product[16 * row : 16 * row + SEGS] + r.ada_bias[at, :]
    for j in range(1, wide):
        mod_copy(j).start()
    r.mod_rx[pl.ds(w, 1)] = r.mod_tx[pl.ds(w, 1)]
    for layer in range(LAYERS):
        for which in (QKV, OUT, UP, DOWN):
            if (which, layer) != (QKV, 0):
                weights_start(which, layer)
    weights_forward(QKV, 0)
    for j in range(1, wide):
        mod_copy(j, True).wait_recv()
    r.mod_q[pl.ds(n, 1)] = jnp.sum(r.mod_rx[...], 0, keepdims=True)
    for k in range(3):
        quarter_copy(k).start()
    weights_forward(OUT, 0)
    for j in range(1, wide):
        bias_copy(j, True).wait_recv()
    r.bias_sum[...] = jnp.sum(r.bias_rx[...], 0)
    for k in range(3):
        quarter_copy(k, True).wait_recv()
    for part in range(narrow):
        at = LANES * mod_start(tiles, narrow, part)
        r.mods[:, at : at + mod_cols] = r.mod_q[part]

    def bias_row(layer, which, size):
        return r.bias_sum[4 * layer + which : 4 * layer + which + 1, :size]

    def gather_norm(layer, hid, shift, scale, take, before):
        for part in range(2):
            before(part)

            def step(start):
                seg = seg_of(start)
                unit, _ = norm(take(start, seg))
                hidden = unit * (1.0 + mod(layer, scale, seg)) + mod(layer, shift, seg)
                hid[span(local * n + start, STEP), :] = hidden.astype(BF16)

            each_step(part, step)
            tok_send(hid, part)

    def qkv_block(layer, block):
        rows = block_rows(block)
        out = dot(r.hid_attn[layer, rows, :], r.qkv_v[...], ((1,), (0,)))
        out = (out + bias_row(layer, QKV, 3 * cols)).astype(BF16)
        for j in range(3 * own_heads):
            r.heads[layer, j, rows, :HEAD] = out[:, HEAD * j : HEAD * (j + 1)]

    def attend(layer):
        for head in range(own_heads):

            @pl.loop(0, narrow)
            def _(i):
                rows = span(local * i, local)
                query = r.heads[layer, head, rows, :HEAD]
                key = r.heads[layer, own_heads + head, :, :HEAD]
                value = r.heads[layer, 2 * own_heads + head, :, :HEAD]
                scores = dot(query, key, ((1,), (1,))) * scale_inv
                scores = jnp.where(r.seg_col[rows, :] == r.seg_row[...], scores, -1e30)
                top = jnp.max(scores, -1, keepdims=True)
                power = jnp.exp(scores - top)
                total = jnp.sum(power, -1, keepdims=True)
                probs = (power / total).astype(BF16)
                mixed = dot(probs, value, ((1,), (0,)))
                r.mixed[layer, rows, HEAD * head : HEAD * (head + 1)] = mixed.astype(BF16)
                r.log_sum[layer, rows, head : head + 1] = top + jnp.log(total)

    def mlp_block(layer, block):
        rows = block_rows(block)
        hidden = r.hid_mlp[layer, rows, :]
        for at in range(0, width, 3 * LANES):
            tile = slice(at, at + 3 * LANES)
            up = dot(hidden, r.up_v[:, tile], ((1,), (0,)))
            up = up + r.bias_sum[4 * layer + UP : 4 * layer + UP + 1, tile]
            r.up[layer, rows, tile] = up.astype(BF16)
            r.act[layer, rows, tile] = gelu(up).astype(BF16)
        r.part[block] = dot(r.act[layer, rows, :], r.down_v[...], ((1,), (0,)))

    def state_of(layer, start):
        rows = span(start, STEP)
        return r.tok[rows, :].astype(F32) if layer == 0 else r.state[rows, :]

    def after_attn(layer):
        def take(start, seg):
            rows = span(start, STEP)
            branch = sum_take(start) + bias_row(layer, OUT, width)
            r.branch[layer, rows, :] = branch
            middle = state_of(layer, start) + mod(layer, 2, seg) * branch
            r.middle[layer, rows, :] = middle
            return middle

        return take

    def after_mlp(layer):
        def take(start, seg):
            rows = span(start, STEP)
            down = sum_take(start) + bias_row(layer, DOWN, width)
            r.down[layer, rows, :] = down
            result = r.middle[layer, rows, :] + mod(layer, 5, seg) * down
            if layer == 0:
                r.state[rows, :] = result
            else:
                r.mixed_o[rows, :] = result.astype(BF16)
            return result

        return take

    for layer in range(LAYERS):
        hid = r.hid_attn.at[layer]
        if layer == 0:
            gather_norm(0, hid, 0, 1, lambda start, seg: state_of(0, start), lambda part: None)
        else:
            gather_norm(layer, hid, 0, 1, after_mlp(layer - 1), sum_wait)
        weights_ready(QKV, layer)
        tok_own(hid)
        qkv_block(layer, 1)
        tok_other(hid)
        qkv_block(layer, 0)
        if layer == 1:
            weights_forward(OUT, 1)
        attend(layer)
        weights_ready(OUT, layer)
        tok_drain(hid)
        for block in range(2):
            r.part[block] = dot(r.mixed[layer, block_rows(block), :], r.out_v[...], ((1,), (0,)))
            sum_block(block)
            if block == 0:
                sum_cross()
        weights_forward(UP, layer)
        hid = r.hid_mlp.at[layer]
        gather_norm(layer, hid, 3, 4, after_attn(layer), sum_wait)
        weights_ready(UP, layer)
        weights_forward(DOWN, layer)
        weights_ready(DOWN, layer)
        tok_own(hid)
        mlp_block(layer, 1)
        sum_block(1)
        tok_other(hid)
        mlp_block(layer, 0)
        sum_block(0)
        sum_cross()
        tok_drain(hid)
        if layer == 0:
            weights_forward(QKV, 1)
    for part in range(2):
        sum_wait(part)
        finish = after_mlp(LAYERS - 1)

        def last(start):
            finish(start, seg_of(start))

        each_step(part, last)

    sums = (r.qkv_d, r.out_d, r.up_d, r.down_d)
    from_x = (r.qkv_xr, r.out_xr, r.up_xr, r.down_xr)
    from_z = (r.qkv_zr, r.out_zr, r.up_zr, r.down_zr)
    final = (r.qkv_f, r.out_f, r.up_f, r.down_f)
    grads_o = (r.qkv_o, r.out_o, r.up_o, r.down_o)
    same_y, same_c = y == z // 2, c == z % 2

    def d_rows(which, plane_idx, col):
        return w_rows(which, plane_idx, col)

    def d_x(which, plane_idx, incoming=False):
        k = 0 if which == OUT else plane_idx
        src = sums[which].at[d_rows(which, plane_idx, 1 - x)]
        return remote(
            src, from_x[which].at[k], (r.dx_s.at[which, k], r.dx_r.at[which, k]), beside
        )

    def d_z(which, j):
        dest = n if which == OUT else plane_of(j)
        k = 0 if which == OUT else j - 1
        src = sums[which].at[d_rows(which, dest, x)]
        return remote(
            src, from_z[which].at[j - 1], (r.dz_s.at[which, k], r.dz_r.at[which, j - 1]), plane(j)
        )

    def grad_product(which, layer):
        left, right = (
            (r.hid_attn, r.grad_qkv), (r.mixed, r.grad_branch),
            (r.hid_mlp, r.grad_up), (r.act, r.grad_down),
        )[which]
        if which == OUT:
            product = dot(left[layer], right[...], ((0,), (0,)))
            sums[which][...] = product.astype(BF16)
        else:

            @pl.loop(0, width // (3 * LANES))
            def _(i):
                tile = span(3 * LANES * i, 3 * LANES, LANES)
                product = dot(left[layer, :, tile], right[...], ((0,), (0,)))
                sums[which][tile, :] = product.astype(BF16)

        if layer == 0:
            pl.semaphore_wait(r.credit_x.at[which], 1)
        for plane_idx in range(1 if which == OUT else PLANES):
            d_x(which, plane_idx).start()

    def grad_beside(which, layer):
        if which == OUT:
            d_x(which, 0).wait_recv()
            rows = d_rows(which, n, x)
            total = sums[which][rows, :].astype(F32) + from_x[which][0].astype(F32)
            sums[which][rows, :] = total.astype(BF16)

            @pl.when(z != n)
            def _():
                if layer == 0:
                    pl.semaphore_wait(r.credit_z.at[which], 1)
                d_z(which, (n - z + PLANES) % PLANES).start()

            d_x(which, 0).wait_send()
        else:
            for j in (1, 2, 3, 0):
                idx = plane_of(j)
                d_x(which, idx).wait_recv()
                rows = d_rows(which, idx, x)
                total = sums[which][rows, :].astype(F32) + from_x[which][idx].astype(F32)
                sums[which][rows, :] = total.astype(BF16)
                if layer == 0 and j == 1:
                    pl.semaphore_wait(r.credit_z.at[which], PLANES - 1)
                if j:
                    d_z(which, j).start()
            for idx in range(PLANES):
                d_x(which, idx).wait_send()
        if layer == 1:
            pl.semaphore_signal(
                r.credit_x.at[which], inc=1, device_id=beside, device_id_type=MESH
            )

    def grad_planes(which, layer):
        def add():
            for j in range(1, PLANES):
                d_z(which, j).wait_recv()
            rows = d_rows(which, z, x)
            total = sums[which][rows, :].astype(F32)
            for j in range(PLANES - 1):
                total = total + from_z[which][j].astype(F32)
            final[which][layer] = total.astype(BF16)
            if layer == 1:
                for j in range(1, PLANES):
                    pl.semaphore_signal(
                        r.credit_z.at[which], inc=1, device_id=plane(j), device_id_type=MESH
                    )

        if which == OUT:
            pl.when(z == n)(add)

            @pl.when(z != n)
            def _():
                d_z(which, (n - z + PLANES) % PLANES).wait_send()
        else:
            add()
            for j in range(1, PLANES):
                d_z(which, j).wait_send()

    def spread(which, layer, kind, source=None):
        slot = layer * 4 + which
        if which == OUT:
            dst = grads_o[which].at[layer]
        else:
            dst = grads_o[which].at[layer, n if source is None else source]
        src = final[which].at[layer] if kind < 2 else dst
        return remote(
            src, dst, (r.spread_s.at[slot, kind], r.spread_r.at[slot, kind]), side if kind == 1 else core
        )

    def spread_own(which, layer):
        dst = grads_o[which].at[layer] if which == OUT else grads_o[which].at[layer, n]
        return pltpu.make_async_copy(final[which].at[layer], dst, r.spread_l.at[layer * 4 + which])

    def grad_spread(which, layer):
        def go():
            spread(which, layer, 1).start()
            spread(which, layer, 0).start()
            spread_own(which, layer).start()

        if which == OUT:
            pl.when(jnp.logical_and(same_y, same_c))(go)
        else:
            go()

    def grad_pass(which, layer):
        def go():
            spread(which, layer, 1, n_side).wait_recv()
            spread(which, layer, 2, n_side).start()

        if which == OUT:
            pl.when(jnp.logical_and(jnp.logical_not(same_y), same_c))(go)
        else:
            go()

    def grad_end(which, layer):
        if which == OUT:

            @pl.when(jnp.logical_and(same_y, same_c))
            def _():
                spread(which, layer, 1).wait_send()
                spread(which, layer, 0).wait_send()
                spread_own(which, layer).wait()

            @pl.when(jnp.logical_and(jnp.logical_not(same_y), same_c))
            def _():
                spread(which, layer, 2).wait_send()

            @pl.when(jnp.logical_and(same_y, jnp.logical_not(same_c)))
            def _():
                spread(which, layer, 0).wait_recv()

            @pl.when(jnp.logical_and(jnp.logical_not(same_y), jnp.logical_not(same_c)))
            def _():
                spread(which, layer, 2).wait_recv()
        else:
            spread(which, layer, 0, n_core).wait_recv()
            spread(which, layer, 2, n_far).wait_recv()
            spread(which, layer, 2, n_side).wait_send()
            spread(which, layer, 1).wait_send()
            spread(which, layer, 0).wait_send()
            spread_own(which, layer).wait()

    def bias_grad(layer, which, values):
        at = 4 * layer + which
        r.bias_grad[at : at + 1, : values.shape[1]] = jnp.sum(
            values.astype(F32), 0, keepdims=True
        )

    def back_mlp_block(layer, block):
        rows = block_rows(block)
        grad_down = r.grad_down[rows, :]
        for at in range(0, width, 3 * LANES):
            tile = slice(at, at + 3 * LANES)
            grad_act = dot(grad_down, r.down_v[tile, :], ((1,), (1,)))
            up = r.up[layer, rows, tile].astype(F32)
            r.grad_up[rows, tile] = (grad_act * gelu_slope(up)).astype(BF16)
        r.part[block] = dot(r.grad_up[rows, :], r.up_v[...], ((1,), (1,)))

    def back_attn_block(layer, block):
        rows = block_rows(block)
        out = dot(r.grad_branch[rows, :], r.out_v[...], ((1,), (1,))).astype(BF16)
        for j in range(own_heads):
            r.grad_heads[j, rows, :HEAD] = out[:, HEAD * j : HEAD * (j + 1)]

    def back_attend(layer, head):
        @pl.loop(0, narrow)
        def _(i):
            rows = span(local * i, local)
            query = r.heads[layer, head, rows, :HEAD]
            key = r.heads[layer, own_heads + head, :, :HEAD]
            value = r.heads[layer, 2 * own_heads + head, :, :HEAD]
            grad = r.grad_heads[head, rows, :HEAD]
            scores = dot(query, key, ((1,), (1,))) * scale_inv
            probs = jnp.exp(scores - r.log_sum[layer, rows, head : head + 1])
            probs = jnp.where(r.seg_col[rows, :] == r.seg_row[...], probs, 0.0)
            grad_probs = dot(grad, value, ((1,), (1,)))
            inner = jnp.sum(probs * grad_probs, -1, keepdims=True)
            grad_scores = (probs * (grad_probs - inner)).astype(BF16)
            grad_query = dot(grad_scores, key, ((1,), (0,))) * scale_inv
            r.grad_qkv[rows, HEAD * head : HEAD * (head + 1)] = grad_query.astype(BF16)
            grad_key = dot(grad_scores, query, ((0,), (0,)))
            grad_value = dot(probs.astype(BF16), grad, ((0,), (0,)))

            @pl.when(i == 0)
            def _():
                r.key_sum[:, :HEAD] = grad_key
                r.value_sum[:, :HEAD] = grad_value

            @pl.when(i > 0)
            def _():
                r.key_sum[:, :HEAD] += grad_key
                r.value_sum[:, :HEAD] += grad_value

        at = cols + HEAD * head
        r.grad_qkv[:, at : at + HEAD] = (r.key_sum[:, :HEAD] * scale_inv).astype(BF16)
        r.grad_qkv[:, cols + at : cols + at + HEAD] = r.value_sum[:, :HEAD].astype(BF16)

    for part in range(2):
        def first(start):
            rows = span(start, STEP)
            r.grad[rows, :] = r.cot[rows, :].astype(F32)

        each_step(part, first)

    def both(body):
        for part in range(2):
            each_step(part, body)

    for layer in reversed(range(LAYERS)):
        older = layer + 1
        for part in range(2):
            if layer < LAYERS - 1:
                sum_wait(part)

            def start_down(start):
                rows = span(start, STEP)
                seg = seg_of(start)
                if layer < LAYERS - 1:
                    grad_hidden = sum_take(start)
                    unit, inv = norm(state_of(older, start))
                    r.grad_hid[rows, :] = grad_hidden
                    r.grad[rows, :] += norm_back(
                        grad_hidden * (1.0 + mod(older, 1, seg)), unit, inv
                    )
                grad_down = (mod(layer, 5, seg) * r.grad[rows, :]).astype(BF16)
                r.grad_down[span(local * n + start, STEP), :] = grad_down

            each_step(part, start_down)
            tok_send(r.grad_down, part)

        def sums_attn(idx):
            def body(start):
                rows = span(start, STEP)
                seg = seg_of(start)
                unit, _ = norm(state_of(idx, start))
                grad_hidden = r.grad_hid[rows, :]
                mod_sum(idx, 0, seg, grad_hidden)
                mod_sum(idx, 1, seg, grad_hidden * unit)

            return body

        if layer < LAYERS - 1:
            both(sums_attn(older))
            load(DOWN, layer).wait()
            load(UP, layer).wait()

        def sums_gate_mlp(start):
            rows = span(start, STEP)
            mod_sum(layer, 5, seg_of(start), r.down[layer, rows, :] * r.grad[rows, :])

        both(sums_gate_mlp)
        bias_grad(layer, DOWN, r.grad_down[span(local * n, local), :])
        tok_own(r.grad_down)
        back_mlp_block(layer, 1)
        sum_block(1)
        tok_other(r.grad_down)
        back_mlp_block(layer, 0)
        sum_block(0)
        sum_cross()
        if layer > 0:
            load(DOWN, layer - 1).start()
            load(UP, layer - 1).start()
        if layer == 1:
            grad_product(DOWN, 1)
            grad_product(UP, 1)
        else:
            grad_beside(UP, 1)
            grad_beside(OUT, 1)
            grad_planes(DOWN, 1)
            grad_product(DOWN, 0)
        bias_grad(layer, UP, r.grad_up[...])
        tok_drain(r.grad_down)
        for part in range(2):
            sum_wait(part)

            def start_branch(start):
                rows = span(start, STEP)
                seg = seg_of(start)
                grad_hidden = sum_take(start)
                unit, inv = norm(r.middle[layer, rows, :])
                r.grad_hid[rows, :] = grad_hidden
                grad = r.grad[rows, :] + norm_back(
                    grad_hidden * (1.0 + mod(layer, 4, seg)), unit, inv
                )
                r.grad[rows, :] = grad
                grad_branch = (mod(layer, 2, seg) * grad).astype(BF16)
                r.grad_branch[span(local * n + start, STEP), :] = grad_branch

            each_step(part, start_branch)
            tok_send(r.grad_branch, part)

        def sums_mlp(start):
            rows = span(start, STEP)
            seg = seg_of(start)
            unit, _ = norm(r.middle[layer, rows, :])
            grad_hidden = r.grad_hid[rows, :]
            mod_sum(layer, 3, seg, grad_hidden)
            mod_sum(layer, 4, seg, grad_hidden * unit)
            mod_sum(layer, 2, seg, r.branch[layer, rows, :] * r.grad[rows, :])

        both(sums_mlp)
        bias_grad(layer, OUT, r.grad_branch[span(local * n, local), :])
        if layer < LAYERS - 1:
            load(OUT, layer).wait()
            load(QKV, layer).wait()
        tok_own(r.grad_branch)
        back_attn_block(layer, 1)
        tok_other(r.grad_branch)
        back_attn_block(layer, 0)
        if layer > 0:
            load(OUT, layer - 1).start()
        if layer == 0:
            grad_spread(DOWN, 1)
            grad_beside(QKV, 1)
        for head in range(own_heads):
            back_attend(layer, head)
        for block in range(2):
            rows = block_rows(block)
            r.part[block] = dot(r.grad_qkv[rows, :], r.qkv_v[...], ((1,), (1,)))
            sum_block(block)
            if block == 0:
                sum_cross()
        tok_drain(r.grad_branch)
        if layer > 0:
            load(QKV, layer - 1).start()
        if layer == 1:
            grad_product(OUT, 1)
            grad_product(QKV, 1)
            grad_beside(DOWN, 1)
        else:
            grad_planes(UP, 1)
            grad_product(UP, 0)
            grad_planes(OUT, 1)
            grad_product(OUT, 0)
            grad_planes(QKV, 1)
            grad_product(QKV, 0)
        bias_grad(layer, QKV, r.grad_qkv[...])
    for part in range(2):
        sum_wait(part)

        def finish_grad(start):
            rows = span(start, STEP)
            seg = seg_of(start)
            grad_hidden = sum_take(start)
            unit, inv = norm(state_of(0, start))
            grad = r.grad[rows, :] + norm_back(grad_hidden * (1.0 + mod(0, 1, seg)), unit, inv)
            r.token_o[rows, :] = grad
            mod_sum(0, 0, seg, grad_hidden)
            mod_sum(0, 1, seg, grad_hidden * unit)

        each_step(part, finish_grad)

    def quarter_back(k, incoming=False):
        device, idx = narrow_peers[k]
        at = span(LANES * mod_start(tiles, narrow, idx), mod_cols, LANES)
        return remote(
            r.mod_grad.at[:, at], r.quarter_rx.at[k], (r.back_s.at[k], r.back_r.at[k]), device
        )

    def wide_back(j, incoming=False):
        return remote(
            r.quarter_sum, r.quarter_all.at[(w - j + wide) % wide if incoming else w],
            (r.wide_s.at[j - 1], r.wide_r.at[j - 1]), wide_peer(j),
        )

    def bias_wide(j, incoming=False):
        return remote(
            r.bias_grad, r.bias_all.at[(w - j + wide) % wide if incoming else w],
            (r.bias_wide_s.at[j - 1], r.bias_wide_r.at[j - 1]), wide_peer(j),
        )

    def bias_narrow(k, incoming=False):
        device, idx = narrow_peers[k]
        return remote(
            r.bias_row, r.bias_o.at[idx if incoming else n],
            (r.bias_narrow_s.at[k], r.bias_narrow_r.at[k]), device,
        )

    def mod_narrow(k, incoming=False):
        device, idx = narrow_peers[k]
        return remote(
            r.mod_all, r.mod_o.at[idx if incoming else n],
            (r.mod_narrow_s.at[k], r.mod_narrow_r.at[k]), device,
        )

    for k in range(3):
        quarter_back(k).start()
    grad_beside(DOWN, 0)
    grad_spread(UP, 1)
    grad_spread(OUT, 1)
    own_at = span(LANES * mod_start(tiles, narrow, n), mod_cols, LANES)
    total = r.mod_grad[:, own_at]
    for k in range(3):
        quarter_back(k, True).wait_recv()
        total = total + r.quarter_rx[k]
    r.quarter_sum[...] = total
    for j in range(1, wide):
        wide_back(j).start()
    for j in range(1, wide):
        bias_wide(j).start()
    r.quarter_all[pl.ds(w, 1)] = total[None]
    r.bias_all[pl.ds(w, 1)] = r.bias_grad[...][None]
    grad_spread(QKV, 1)
    grad_beside(UP, 0)
    grad_beside(OUT, 0)
    for which in (DOWN, UP, OUT, QKV):
        grad_pass(which, 1)
    grad_planes(DOWN, 0)
    grad_spread(DOWN, 0)
    grad_beside(QKV, 0)
    for j in range(1, wide):
        wide_back(j, True).wait_recv()
    r.mod_all[...] = r.quarter_all[...].reshape(wide * 2 * SEGS, mod_cols).astype(BF16)
    mod_own = pltpu.make_async_copy(r.mod_all, r.mod_o.at[n], r.mod_own_sem)
    mod_own.start()
    for k in range(3):
        mod_narrow(k).start()
    for j in range(1, wide):
        bias_wide(j, True).wait_recv()
    r.bias_row[...] = jnp.sum(r.bias_all[...], 0)
    bias_own = pltpu.make_async_copy(r.bias_row, r.bias_o.at[n], r.bias_own_sem)
    bias_own.start()
    for k in range(3):
        bias_narrow(k).start()
    grad_planes(UP, 0)
    grad_spread(UP, 0)
    grad_planes(OUT, 0)
    grad_spread(OUT, 0)
    grad_pass(DOWN, 0)
    grad_planes(QKV, 0)
    grad_spread(QKV, 0)
    for which in (UP, OUT, QKV):
        grad_pass(which, 0)

    for layer in range(LAYERS):
        for which in range(4):
            weights_drain(which, layer)
            grad_end(which, layer)
    for j in range(1, wide):
        for copy in (lead_copy, bias_copy, mod_copy, wide_back, bias_wide):
            copy(j).wait_send()
    for k in range(3):
        for copy in (quarter_copy, quarter_back, mod_narrow, bias_narrow):
            copy(k).wait_send()
        mod_narrow(k, True).wait_recv()
        bias_narrow(k, True).wait_recv()
    mod_own.wait()
    bias_own.wait()


def gelu_slope(values):
    rate = math.sqrt(2.0 / math.pi)
    bent = jnp.tanh(rate * (values + 0.044715 * values * values * values))
    inner = rate * (1.0 + 3.0 * 0.044715 * values * values)
    return 0.5 * (1.0 + bent) + 0.5 * values * (1.0 - bent * bent) * inner


def fused_device(
    wide, narrow,
    tokens, cond, seg_ids, cond_index, cotangent,
    ada_weight, ada_bias, qkv_weight, qkv_bias, out_weight, out_bias,
    up_weight, up_bias, down_weight, down_bias,
):
    w = lax.axis_index("wide")
    n = lax.axis_index("narrow")
    local, width = tokens.shape[1:]
    row_len = seg_ids.shape[1]
    depth, cols = width // wide, width // narrow
    hidden_own = up_weight.shape[-1] // wide // narrow
    hidden = wide * hidden_own
    tiles = ada_weight.shape[-1] // LANES
    mod_cols = LANES * -(-tiles // narrow)

    def own(values, axis):
        return lax.dynamic_index_in_dim(values, n, axis, keepdims=False)

    def placed(values):
        spot = jnp.arange(wide)[None, :, None] == w
        return jnp.where(spot, values.astype(F32)[:, None, :], 0.0).reshape(LAYERS, -1)

    ada_b = lax.dynamic_slice_in_dim(
        placed(ada_bias), LANES * mod_start(tiles, narrow, n), mod_cols, 1
    )
    ada_b = jnp.repeat(ada_b, SEGS, axis=0)
    qkv_b = own(placed(qkv_bias).reshape(LAYERS, 3, narrow, cols), 2).reshape(LAYERS, -1)
    qkv_b = jnp.pad(qkv_b, ((0, 0), (0, width - 3 * cols)))
    up_b = own(placed(up_bias).reshape(LAYERS, wide, narrow, hidden_own), 2).reshape(LAYERS, -1)
    bias = jnp.stack([qkv_b, placed(out_bias), up_b, placed(down_bias)], 1).reshape(-1, width)

    cond_hot = (cond_index[0, :, None] == jnp.arange(SEGS, dtype=jnp.int32)[None, :]).astype(F32)
    chosen = jnp.dot(cond_hot, cond[0].astype(F32), precision=EXACT)
    lead = (chosen * jax.nn.sigmoid(chosen)).astype(BF16)
    lead = lead.reshape(SEGS, wide, depth).transpose(1, 0, 2)
    lead = jnp.pad(lead, ((0, 0), (0, 16 - SEGS), (0, 0)))

    seg_row = seg_ids[0]
    seg_own = lax.dynamic_slice_in_dim(seg_row, n * local, local, 0)

    qkv_own = jnp.concatenate(
        [
            lax.dynamic_slice_in_dim(qkv_weight, width * j + n * cols, cols, 2) for j in range(3)
        ],
        axis=2,
    )
    up_own = jnp.concatenate(
        [
            lax.dynamic_slice_in_dim(up_weight, (j * narrow + n) * hidden_own, hidden_own, 2)
            for j in range(wide)
        ],
        axis=2,
    )
    down_own = lax.dynamic_slice_in_dim(down_weight, n * hidden_own, hidden_own, 1)

    inputs = dict(
        tok=tokens[0], lead=lead, bias=bias, ada_bias=ada_b,
        seg_own=seg_own[:, None], seg_col=seg_row[:, None], seg_row=seg_row[None, :],
        cot=cotangent[0], ada=ada_weight, qkv_s=qkv_own, out_s=out_weight, up_s=up_own, down_s=down_own,
    )
    in_hbm = ("ada", "qkv_s", "out_s", "up_s", "down_s")
    shape = jax.ShapeDtypeStruct
    outputs = dict(
        mixed_o=shape((local, width), BF16), token_o=shape((local, width), F32),
        qkv_o=shape((LAYERS, narrow, depth, 3 * cols), BF16),
        out_o=shape((LAYERS, depth, width), BF16),
        up_o=shape((LAYERS, narrow, depth, hidden), BF16),
        down_o=shape((LAYERS, narrow, hidden_own, width), BF16),
        bias_o=shape((narrow, 4 * LAYERS, width), F32),
        mod_o=shape((narrow, wide * LAYERS * SEGS, mod_cols), BF16),
        qkv_h=shape((LAYERS, width, 3 * cols), BF16), out_h=shape((LAYERS, cols, width), BF16),
        up_h=shape((LAYERS, width, hidden), BF16), down_h=shape((LAYERS, hidden, width), BF16),
    )
    out_vmem = ("mixed_o", "token_o")
    vmem, dma = pltpu.VMEM, pltpu.SemaphoreType.DMA
    heads = cols // HEAD
    scratch = dict(
        qkv_v=vmem((width, 3 * cols), BF16), out_v=vmem((cols, width), BF16),
        up_v=vmem((width, hidden), BF16), down_v=vmem((hidden, width), BF16),
        hid_attn=vmem((LAYERS, row_len, width), BF16), hid_mlp=vmem((LAYERS, row_len, width), BF16),
        heads=vmem((LAYERS, 3 * heads, row_len, LANES), BF16),
        mixed=vmem((LAYERS, row_len, cols), BF16), log_sum=vmem((LAYERS, row_len, heads), F32),
        up=vmem((LAYERS, row_len, hidden), BF16), act=vmem((LAYERS, row_len, hidden), BF16),
        state=vmem((local, width), F32), middle=vmem((LAYERS, local, width), F32),
        branch=vmem((LAYERS, local, width), F32), down=vmem((LAYERS, local, width), F32),
        grad=vmem((local, width), F32), grad_hid=vmem((local, width), F32),
        grad_down=vmem((row_len, width), BF16), grad_branch=vmem((row_len, width), BF16),
        grad_up=vmem((row_len, hidden), BF16), grad_qkv=vmem((row_len, 3 * cols), BF16),
        grad_heads=vmem((heads, row_len, LANES), BF16),
        key_sum=vmem((row_len, LANES), F32), value_sum=vmem((row_len, LANES), F32),
        part=vmem((2, 2 * local, width), F32),
        core_tx=vmem((2, local, width), BF16), core_rx=vmem((2, local, width), BF16),
        side_tx=vmem((local, width), BF16), side_rx=vmem((local, width), BF16),
        ada_v=vmem((LAYERS, depth, mod_cols), BF16),
        lead_rx=vmem((wide, 16, depth), BF16), bias_rx=vmem((wide, 4 * LAYERS, width), F32),
        bias_sum=vmem((4 * LAYERS, width), F32),
        mod_tx=vmem((wide, LAYERS * SEGS, mod_cols), F32), mod_rx=vmem((wide, LAYERS * SEGS, mod_cols), F32),
        mod_q=vmem((narrow, LAYERS * SEGS, mod_cols), F32),
        mods=vmem((LAYERS * SEGS, tiles * LANES), F32),
        mod_grad=vmem((LAYERS * SEGS, tiles * LANES), F32),
        quarter_rx=vmem((3, LAYERS * SEGS, mod_cols), F32),
        quarter_sum=vmem((LAYERS * SEGS, mod_cols), F32),
        quarter_all=vmem((wide, LAYERS * SEGS, mod_cols), F32),
        mod_all=vmem((wide * LAYERS * SEGS, mod_cols), BF16),
        bias_grad=vmem((4 * LAYERS, width), F32), bias_all=vmem((wide, 4 * LAYERS, width), F32),
        bias_row=vmem((4 * LAYERS, width), F32),
        qkv_d=vmem((width, 3 * cols), BF16), out_d=vmem((cols, width), BF16),
        up_d=vmem((width, hidden), BF16), down_d=vmem((hidden, width), BF16),
        qkv_xr=vmem((PLANES, depth, 3 * cols), BF16), out_xr=vmem((1, depth, width), BF16),
        up_xr=vmem((PLANES, depth, hidden), BF16), down_xr=vmem((PLANES, hidden_own, width), BF16),
        qkv_zr=vmem((PLANES - 1, depth, 3 * cols), BF16), out_zr=vmem((PLANES - 1, depth, width), BF16),
        up_zr=vmem((PLANES - 1, depth, hidden), BF16), down_zr=vmem((PLANES - 1, hidden_own, width), BF16),
        qkv_f=vmem((LAYERS, depth, 3 * cols), BF16), out_f=vmem((LAYERS, depth, width), BF16),
        up_f=vmem((LAYERS, depth, hidden), BF16), down_f=vmem((LAYERS, hidden_own, width), BF16),
        wz_s=dma((8, 3)), wz_r=dma((8, 3)), wx_s=dma((8, 4)), wx_r=dma((8, 4)), w_own=dma((8,)),
        load_sem=dma((4,)), tok_s=dma((6,)), tok_r=dma((6,)), sum_s=dma((4,)), sum_r=dma((4,)),
        lead_sem_s=dma((wide - 1,)), lead_sem_r=dma((wide - 1,)),
        bias_sem_s=dma((wide - 1,)), bias_sem_r=dma((wide - 1,)),
        mod_sem_s=dma((wide - 1,)), mod_sem_r=dma((wide - 1,)),
        quarter_s=dma((3,)), quarter_r=dma((3,)), ada_sem=dma,
        dx_s=dma((4, 4)), dx_r=dma((4, 4)), dz_s=dma((4, 3)), dz_r=dma((4, 3)),
        spread_s=dma((8, 3)), spread_r=dma((8, 3)), spread_l=dma((8,)),
        back_s=dma((3,)), back_r=dma((3,)),
        wide_s=dma((wide - 1,)), wide_r=dma((wide - 1,)),
        bias_wide_s=dma((wide - 1,)), bias_wide_r=dma((wide - 1,)),
        bias_narrow_s=dma((3,)), bias_narrow_r=dma((3,)),
        mod_narrow_s=dma((3,)), mod_narrow_r=dma((3,)), mod_own_sem=dma, bias_own_sem=dma,
        credit_x=pltpu.SemaphoreType.REGULAR((4,)), credit_z=pltpu.SemaphoreType.REGULAR((4,)),
    )
    cfg = SimpleNamespace(
        names=[*inputs, *outputs, *scratch], wide=wide, narrow=narrow, width=width, depth=depth,
        local=local, cols=cols, mod_cols=mod_cols, tiles=tiles,
    )

    def place(name, vmem_ok):
        return pl.BlockSpec(memory_space=pltpu.VMEM if vmem_ok else pl.ANY)

    results = pl.pallas_call(
        partial(block_kernel, cfg),
        out_shape=list(outputs.values()),
        in_specs=[place(name, name not in in_hbm) for name in inputs],
        out_specs=[place(name, name in out_vmem) for name in outputs],
        scratch_shapes=list(scratch.values()),
        compiler_params=pltpu.CompilerParams(
            collective_id=0, has_side_effects=True, vmem_limit_bytes=62 * 2**20
        ),
    )(*inputs.values())
    got = dict(zip(outputs, results))

    qkv_g = got["qkv_o"].reshape(LAYERS, narrow, depth, 3, cols).transpose(0, 2, 3, 1, 4)
    up_g = got["up_o"].reshape(LAYERS, narrow, depth, wide, hidden_own).transpose(0, 2, 3, 1, 4)
    weight_grads = (
        qkv_g.reshape(LAYERS, depth, -1).astype(F32),
        got["out_o"].astype(F32),
        up_g.reshape(LAYERS, depth, -1).astype(F32),
        got["down_o"].reshape(LAYERS, -1, width).astype(F32),
    )

    bias_g = got["bias_o"].reshape(narrow, LAYERS, 4, width)
    qkv_bg = bias_g[:, :, QKV, : 3 * cols].reshape(narrow, LAYERS, 3, cols).transpose(1, 2, 0, 3)
    up_bg = bias_g[:, :, UP].reshape(narrow, LAYERS, wide, hidden_own).transpose(1, 2, 0, 3)
    full_biases = (
        qkv_bg.reshape(LAYERS, -1), jnp.sum(bias_g[:, :, OUT], 0),
        up_bg.reshape(LAYERS, -1), jnp.sum(bias_g[:, :, DOWN], 0),
    )
    bias_grads = [
        lax.dynamic_slice_in_dim(item, w * (item.shape[1] // wide), item.shape[1] // wide, 1)
        for item in full_biases
    ]

    mod_parts = []
    for part in range(narrow):
        size = mod_start(tiles, narrow, part + 1) - mod_start(tiles, narrow, part)
        mod_parts.append(got["mod_o"][part, :, : LANES * size])
    mod_all = jnp.concatenate(mod_parts, axis=1).reshape(wide, LAYERS, SEGS, -1)
    mod_all = mod_all.transpose(1, 0, 2, 3).reshape(LAYERS, wide * SEGS, -1)
    return weight_grads, bias_grads, mod_all, got["mixed_o"], got["token_o"], chosen, cond_hot


def fused_program(wide, narrow, *args):
    tokens, cond, seg_ids, cond_index, cotangent, ada_weight, ada_bias = args[:7]
    w = lax.axis_index("wide")
    width = tokens.shape[-1]
    depth = width // wide
    weight_grads, bias_grads, mod_all, mixed, token_grad, chosen, cond_hot = fused_device(
        wide, narrow, *args
    )
    lead = (chosen * jax.nn.sigmoid(chosen)).astype(BF16)
    lead_own = lax.all_to_all(
        lead.reshape(SEGS, wide, depth).transpose(1, 0, 2), "wide", 0, 0, tiled=False
    ).reshape(wide * SEGS, depth)
    ada_grad = jnp.einsum("nd,lne->lde", lead_own, mod_all, preferred_element_type=F32)
    ada_size = ada_bias.shape[1]
    ada_bias_grad = jnp.sum(
        lax.dynamic_slice_in_dim(mod_all, w * ada_size, ada_size, 2).astype(F32), axis=1
    )
    lead_grad = jnp.einsum("lne,lde->nd", mod_all, ada_weight, preferred_element_type=F32)
    lead_grad = lax.all_to_all(lead_grad.reshape(wide, SEGS, depth), "wide", 0, 0, tiled=False)
    lead_grad = lead_grad.transpose(1, 0, 2).reshape(SEGS, width)
    gate = jax.nn.sigmoid(chosen)
    chosen_grad = lead_grad * (gate * (1.0 + chosen * (1.0 - gate)))
    cond_grad = jnp.dot(cond_hot.T, chosen_grad, precision=EXACT)
    out = [mixed[None], token_grad[None], cond_grad[None], ada_grad, ada_bias_grad]
    for weight, bias in zip(weight_grads, bias_grads):
        out += [weight, bias]
    return tuple(out)


def solution(mesh):
    matrix, vector = P(None, "wide", None), P(None, "wide")
    rows, cond_rows = P("wide", "narrow", None), P("wide", None, None)
    wide, narrow = mesh.shape["wide"], mesh.shape["narrow"]
    fused = wide == PLANES * PAIR and narrow == PLANES
    return jax.shard_map(
        partial(fused_program if fused else plain_device, wide, narrow),
        mesh=mesh,
        in_specs=(rows, cond_rows, P("wide", None), P("wide", None), rows) + (matrix, vector) * 5,
        out_specs=(rows, rows, cond_rows) + (matrix, vector) * 5,
        check_vma=False,
    )
```

```python
from functools import partial
import math
from types import SimpleNamespace

import jax
import jax.numpy as jnp
from jax import lax
from jax.experimental import pallas as pl
from jax.experimental.pallas import tpu as pltpu
from jax.sharding import PartitionSpec as P

HEADS = 16
HEAD = 72
LAYERS = 2
SEGS = 4
EPS = 1e-06
EXACT = lax.Precision.HIGHEST
F32 = jnp.float32
BF16 = jnp.bfloat16


def dot(left, right, dims):
    return lax.dot_general(left, right, (dims, ((), ())), preferred_element_type=F32)


def norm(values):
    centred = values - jnp.mean(values, -1, keepdims=True)
    inv = lax.rsqrt(jnp.mean(centred * centred, -1, keepdims=True) + EPS)
    return centred * inv, inv


def norm_back(grad, unit, inv):
    return inv * (
        grad
        - jnp.mean(grad, -1, keepdims=True)
        - unit * jnp.mean(grad * unit, -1, keepdims=True)
    )


def gather_tokens(values):
    return lax.all_gather(values, "narrow", axis=0, tiled=True)


def scatter_tokens(values):
    return lax.psum_scatter(
        values.astype(BF16), "narrow", scatter_dimension=0, tiled=True
    ).astype(F32)


def gelu(values):
    return jax.nn.gelu(values, approximate=True)


def layer_forward(state, mods, same_seg, weights):
    qkv_w, qkv_b, out_w, out_b, up_w, up_b, down_w, down_b = weights
    shift_attn, scale_attn, gate_attn, shift_mlp, scale_mlp, gate_mlp = mods
    own_heads = out_w.shape[0] // HEAD
    unit_attn, inv_attn = norm(state)
    hidden_attn = gather_tokens((unit_attn * (1.0 + scale_attn) + shift_attn).astype(BF16))
    full_len = hidden_attn.shape[0]
    qkv = (dot(hidden_attn, qkv_w, ((1,), (0,))) + qkv_b).astype(BF16)
    queries, keys, values = [
        part.reshape(full_len, own_heads, HEAD) for part in jnp.split(qkv, 3, axis=-1)
    ]
    scores = jnp.einsum("qhe,khe->hqk", queries, keys, preferred_element_type=F32) * (
        1.0 / math.sqrt(HEAD)
    )
    probs = jax.nn.softmax(jnp.where(same_seg[None], scores, -1e30), axis=-1)
    mixed = jnp.einsum("hqk,khe->qhe", probs.astype(BF16), values, preferred_element_type=F32)
    mixed = mixed.reshape(full_len, own_heads * HEAD).astype(BF16)
    branch = scatter_tokens(dot(mixed, out_w, ((1,), (0,)))) + out_b
    middle = state + gate_attn * branch
    unit_mlp, inv_mlp = norm(middle)
    hidden_mlp = gather_tokens((unit_mlp * (1.0 + scale_mlp) + shift_mlp).astype(BF16))
    up_proj = dot(hidden_mlp, up_w, ((1,), (0,))) + up_b
    activated = gelu(up_proj).astype(BF16)
    down_proj = scatter_tokens(dot(activated, down_w, ((1,), (0,)))) + down_b
    result = middle + gate_mlp * down_proj
    kept = (
        unit_attn, inv_attn, hidden_attn, queries, keys, values, probs, mixed, branch,
        unit_mlp, inv_mlp, hidden_mlp, up_proj, activated, down_proj,
    )
    return result, kept


def layer_backward(grad_out, kept, mods, weights):
    qkv_w, qkv_b, out_w, out_b, up_w, up_b, down_w, down_b = weights
    shift_attn, scale_attn, gate_attn, shift_mlp, scale_mlp, gate_mlp = mods
    (
        unit_attn, inv_attn, hidden_attn, queries, keys, values, probs, mixed, branch,
        unit_mlp, inv_mlp, hidden_mlp, up_proj, activated, down_proj,
    ) = kept
    scale_inv = 1.0 / math.sqrt(HEAD)
    full_len = hidden_attn.shape[0]
    own_down = (gate_mlp * grad_out).astype(BF16)
    grad_gate_mlp = down_proj * grad_out
    grad_down = gather_tokens(own_down)
    grad_act = dot(grad_down, down_w, ((1,), (1,)))
    grad_up = jax.vjp(gelu, up_proj)[1](grad_act)[0].astype(BF16)
    grad_hidden_mlp = scatter_tokens(dot(grad_up, up_w, ((1,), (1,))))
    grad_down_w = dot(activated, grad_down, ((0,), (0,)))
    grad_up_w = dot(hidden_mlp, grad_up, ((0,), (0,)))
    grad_middle = grad_out + norm_back(grad_hidden_mlp * (1.0 + scale_mlp), unit_mlp, inv_mlp)
    own_branch = (gate_attn * grad_middle).astype(BF16)
    grad_gate_attn = branch * grad_middle
    grad_branch = gather_tokens(own_branch)
    grad_attn = dot(grad_branch, out_w, ((1,), (1,))).astype(BF16).reshape(queries.shape)
    grad_probs = jnp.einsum("qhe,khe->hqk", grad_attn, values, preferred_element_type=F32)
    grad_scores = probs * (grad_probs - jnp.sum(probs * grad_probs, -1, keepdims=True))
    grad_scores = grad_scores.astype(BF16)
    grad_q = jnp.einsum("hqk,khe->qhe", grad_scores, keys, preferred_element_type=F32) * scale_inv
    grad_k = jnp.einsum("hqk,qhe->khe", grad_scores, queries, preferred_element_type=F32) * scale_inv
    grad_v = jnp.einsum("hqk,qhe->khe", probs.astype(BF16), grad_attn, preferred_element_type=F32)
    grad_qkv = jnp.concatenate(
        [part.astype(BF16).reshape(full_len, -1) for part in (grad_q, grad_k, grad_v)], axis=-1
    )
    grad_hidden_attn = scatter_tokens(dot(grad_qkv, qkv_w, ((1,), (1,))))
    grad_out_w = dot(mixed, grad_branch, ((0,), (0,)))
    grad_qkv_w = dot(hidden_attn, grad_qkv, ((0,), (0,)))
    grad_state = grad_middle + norm_back(grad_hidden_attn * (1.0 + scale_attn), unit_attn, inv_attn)
    token_mod = jnp.concatenate(
        [
            grad_hidden_attn, grad_hidden_attn * unit_attn, grad_gate_attn,
            grad_hidden_mlp, grad_hidden_mlp * unit_mlp, grad_gate_mlp,
        ],
        axis=-1,
    )
    bias_grads = (
        jnp.sum(grad_qkv.astype(F32), 0),
        jnp.sum(own_branch.astype(F32), 0),
        jnp.sum(grad_up.astype(F32), 0),
        jnp.sum(own_down.astype(F32), 0),
    )
    return grad_state, token_mod, (grad_qkv_w, grad_out_w, grad_up_w, grad_down_w), bias_grads


def plain_device(
    wide, narrow,
    tokens, cond, seg_ids, cond_index, cotangent,
    ada_weight, ada_bias, qkv_weight, qkv_bias, out_weight, out_bias,
    up_weight, up_bias, down_weight, down_bias,
):
    w = lax.axis_index("wide")
    n = lax.axis_index("narrow")
    local_len, width = tokens.shape[1:]
    depth = width // wide
    cols = width // narrow
    hidden_own = up_weight.shape[-1] // wide // narrow
    mod_cols = ada_weight.shape[-1] // narrow

    def own(values, axis):
        return lax.dynamic_index_in_dim(values, n, axis, keepdims=False)

    bias_parts = (ada_bias, qkv_bias, out_bias, up_bias, down_bias)
    sizes = [part.shape[1] for part in bias_parts]
    packed = lax.all_gather(jnp.concatenate(bias_parts, axis=1), "wide", axis=1, tiled=False)
    biases = []
    at = 0
    for size in sizes:
        biases.append(packed[:, :, at : at + size].reshape(LAYERS, -1).astype(F32))
        at += size
    ada_b, qkv_b, out_b, up_b, down_b = biases
    qkv_b = own(qkv_b.reshape(LAYERS, 3, narrow, cols), 2).reshape(LAYERS, 3 * cols)
    up_b = own(up_b.reshape(LAYERS, wide, narrow, hidden_own), 2).reshape(LAYERS, -1)

    cond_hot = (cond_index[0, :, None] == jnp.arange(SEGS, dtype=jnp.int32)[None, :]).astype(F32)
    chosen = jnp.dot(cond_hot, cond[0].astype(F32), precision=EXACT)
    lead = (chosen * jax.nn.sigmoid(chosen)).astype(BF16)
    lead_all = lax.all_gather(lead, "wide", axis=0, tiled=True)
    lead_own = lax.dynamic_slice_in_dim(lead_all, w * depth, depth, 1)
    ada_quarter = lax.dynamic_slice_in_dim(ada_weight, n * mod_cols, mod_cols, 2)
    mod_part = jnp.einsum("nd,lde->nle", lead_own, ada_quarter, preferred_element_type=F32)
    mod_part = lax.psum_scatter(mod_part, "wide", scatter_dimension=0, tiled=True)
    modulation = lax.all_gather(mod_part, "narrow", axis=2, tiled=True)
    modulation = modulation.transpose(1, 0, 2) + ada_b[:, None, :]

    seg_row = seg_ids[0]
    seg_query = lax.dynamic_slice_in_dim(seg_row, n * local_len, local_len, 0)
    token_hot = (seg_query[:, None] == jnp.arange(SEGS, dtype=jnp.int32)[None, :]).astype(F32)
    same_seg = seg_row[:, None] == seg_row[None, :]

    qkv_own = own(qkv_weight.reshape(LAYERS, depth, 3, narrow, cols), 3).reshape(LAYERS, depth, 3 * cols)
    up_own = own(up_weight.reshape(LAYERS, depth, wide, narrow, hidden_own), 3).reshape(LAYERS, depth, -1)
    down_own = own(down_weight.reshape(LAYERS, narrow, hidden_own, width), 1)

    def fetch(idx):
        out_full = lax.all_gather(out_weight[idx], "wide", axis=0, tiled=True)
        return (
            lax.all_gather(qkv_own[idx], "wide", axis=0, tiled=True),
            qkv_b[idx],
            lax.dynamic_slice_in_dim(out_full, n * cols, cols, 0),
            out_b[idx],
            lax.all_gather(up_own[idx], "wide", axis=0, tiled=True),
            up_b[idx],
            lax.all_gather(down_own[idx], "wide", axis=0, tiled=True),
            down_b[idx],
        )

    state = tokens[0].astype(F32)
    weights, mods, kept = [], [], []
    for idx in range(LAYERS):
        weights.append(fetch(idx))
        per_token = jnp.dot(token_hot, modulation[idx], precision=EXACT)
        mods.append(jnp.split(per_token, 6, axis=-1))
        state, saved = layer_forward(state, mods[idx], same_seg, weights[idx])
        kept.append(saved)
    result = state.astype(BF16)

    grad_state = cotangent[0].astype(F32)
    token_hot_t = token_hot.T
    reduced, bias_sums, mod_grads = [None] * LAYERS, [None] * LAYERS, [None] * LAYERS
    for idx in reversed(range(LAYERS)):
        grad_state, token_mod, grads, bias_grads = layer_backward(
            grad_state, kept[idx], mods[idx], weights[idx]
        )
        mod_grads[idx] = jnp.dot(token_hot_t, token_mod, precision=EXACT)
        qkv_g, out_g, up_g, down_g = [item.astype(BF16) for item in grads]
        qkv_g, up_g, down_g = [
            lax.psum_scatter(item, "wide", scatter_dimension=0, tiled=True)
            for item in (qkv_g, up_g, down_g)
        ]
        out_g = lax.psum(out_g, "wide")
        qkv_g = lax.all_gather(qkv_g.reshape(depth, 3, 1, cols), "narrow", axis=2, tiled=True)
        up_g = lax.all_gather(up_g.reshape(depth, wide, 1, hidden_own), "narrow", axis=2, tiled=True)
        down_g = lax.all_gather(down_g, "narrow", axis=0, tiled=True)
        out_g = lax.all_gather(out_g, "narrow", axis=0, tiled=True)
        out_g = lax.dynamic_slice_in_dim(out_g, w * depth, depth, 0)
        reduced[idx] = (
            qkv_g.reshape(depth, 3 * width),
            out_g,
            up_g.reshape(depth, -1),
            down_g,
        )
        spot = lax.broadcasted_iota(jnp.int32, (1, narrow, 1), 1) == n
        qkv_s = jnp.where(spot, bias_grads[0].reshape(3, 1, cols), 0.0).reshape(-1)
        up_s = jnp.where(spot, bias_grads[2].reshape(wide, 1, hidden_own), 0.0).reshape(-1)
        bias_sums[idx] = [
            item.reshape(wide, -1) for item in (qkv_s, bias_grads[1], up_s, bias_grads[3])
        ]
    sizes = [item.shape[1] for item in bias_sums[0]]
    bias_sum = jnp.stack([jnp.concatenate(item, axis=1) for item in bias_sums], axis=1)
    bias_sum = lax.psum_scatter(lax.psum(bias_sum, "narrow"), "wide", scatter_dimension=0, tiled=True)[0]
    bias_out = []
    at = 0
    for size in sizes:
        bias_out.append(bias_sum[:, at : at + size])
        at += size

    mod_grad = lax.psum(jnp.stack(mod_grads), "narrow").astype(BF16)
    mod_all = lax.all_gather(mod_grad, "wide", axis=1, tiled=True)
    ada_grad = jnp.einsum("nd,lne->lde", lead_own, mod_all, preferred_element_type=F32)
    ada_size = ada_bias.shape[1]
    ada_bias_grad = jnp.sum(
        lax.dynamic_slice_in_dim(mod_all, w * ada_size, ada_size, 2).astype(F32), axis=1
    )
    lead_grad = jnp.einsum("lne,lde->nd", mod_all, ada_weight, preferred_element_type=F32)
    lead_grad = lax.all_to_all(lead_grad.reshape(wide, SEGS, depth), "wide", 0, 0, tiled=False)
    lead_grad = lead_grad.transpose(1, 0, 2).reshape(SEGS, width)
    gate = jax.nn.sigmoid(chosen)
    chosen_grad = lead_grad * (gate * (1.0 + chosen * (1.0 - gate)))
    cond_grad = jnp.dot(cond_hot.T, chosen_grad, precision=EXACT)

    stacked = [
        jnp.stack([reduced[idx][pos].astype(F32) for idx in range(LAYERS)]) for pos in range(4)
    ]
    return (
        result[None], grad_state[None], cond_grad[None],
        ada_grad, ada_bias_grad,
        stacked[0], bias_out[0], stacked[1], bias_out[1],
        stacked[2], bias_out[2], stacked[3], bias_out[3],
    )


QKV, OUT, UP, DOWN = range(4)
PLANES = 4
PAIR = 2
LANES = 128
STEP = 32
MESH = pl.DeviceIdType.MESH


def mod_start(tiles, parts, part):
    return tiles * part // parts


def block_kernel(cfg, *refs):
    r = SimpleNamespace(**dict(zip(cfg.names, refs)))
    wide, narrow, width, depth = cfg.wide, cfg.narrow, cfg.width, cfg.depth
    local, cols, mod_cols, tiles = cfg.local, cfg.cols, cfg.mod_cols, cfg.tiles
    half = local // 2
    own_heads = cols // HEAD
    scale_inv = 1.0 / math.sqrt(HEAD)
    w = lax.axis_index("wide")
    n = lax.axis_index("narrow")
    z, x = w // PAIR, w % PAIR
    y, c = n // 2, n % 2
    n_core = n + 1 - 2 * c
    n_side = n + 2 - 4 * y
    n_far = 3 - n
    core, side, far = (w, n_core), (w, n_side), (w, n_far)
    beside = (w + 1 - 2 * x, n)

    def plane_of(j):
        return (z + j) % PLANES

    def plane(j):
        return (plane_of(j) * PAIR + x, n)

    def wide_peer(j):
        return ((w + j) % wide, n)

    def remote(src, dst, sems, device):
        return pltpu.make_async_remote_copy(
            src_ref=src, dst_ref=dst, send_sem=sems[0], recv_sem=sems[1],
            device_id=device, device_id_type=MESH,
        )

    def span(start, size, step=16):
        return pl.ds(pl.multiple_of(start, step), size)

    ada_load = pltpu.make_async_copy(
        r.ada.at[:, :, span(LANES * mod_start(tiles, narrow, n), mod_cols, LANES)], r.ada_v, r.ada_sem
    )
    hidden_own = r.up_w.shape[-1] // wide // narrow

    def windows(which):
        if which == QKV:
            return [(width * j + cols * n, cols, 3 * LANES) for j in range(3)]
        return [((j * narrow + n) * hidden_own, hidden_own, 2 * LANES) for j in range(wide)]

    def raw(which, layer, k):
        src, dst = ((r.qkv_w, r.qkv_raw), (r.up_w, r.up_raw))[which == UP]
        start, _, window = windows(which)[k]
        at = span(LANES * (start // LANES), window, LANES)
        return pltpu.make_async_copy(
            src.at[layer, :, at], dst.at[layer, k], r.raw_sem.at[layer, k + 3 * (which == UP)]
        )

    for layer in range(LAYERS):
        for which in (QKV, UP):
            for k in range(len(windows(which))):
                raw(which, layer, k).start()
        if layer == 0:
            ada_load.start()
    chosen = chosen_of(r.cond, r.cond_index)
    lead = (chosen * jax.nn.sigmoid(chosen)).astype(BF16).astype(F32)
    r.lead[...] = jnp.zeros_like(r.lead)
    for row in range(wide):
        tile = jnp.concatenate(
            [lead[:, depth * row : depth * (row + 1)], jnp.zeros((16 - SEGS, depth), F32)], 0
        )
        r.lead[row] = tile.astype(BF16)
    r.bias_tx[...] = jnp.zeros_like(r.bias_tx)
    for layer in range(LAYERS):
        for line, at, ref in (
            (0, 0, r.ada_b), (1, 0, r.qkv_b), (1, 4 * LANES, r.out_b),
            (2, 0, r.up_b), (2, 5 * LANES, r.down_b),
        ):
            size = ref.shape[1]
            row = 3 * layer + line
            r.bias_tx[row : row + 1, at : at + size] = ref[...].astype(F32)[layer : layer + 1]

    barrier = pltpu.get_barrier_semaphore()
    partners = [core, side, far] + [wide_peer(j) for j in range(1, wide)]
    for partner in partners:
        pl.semaphore_signal(barrier, inc=1, device_id=partner, device_id_type=MESH)
    pl.semaphore_wait(barrier, len(partners))

    full = (r.qkv_h, r.out_h, r.up_h, r.down_h)
    loaded = (r.qkv_v, r.out_v, r.up_v, r.down_v)

    def shard(which, layer):
        if which == DOWN:
            return r.down_w.at[layer, span(depth * n, depth)]
        return (r.qkv_s, r.out_w, r.up_s)[which].at[layer]

    def w_rows(which, plane_idx, col):
        if which == OUT:
            return span(col * depth, depth)
        return span((plane_idx * PAIR + col) * depth, depth)

    def w_block(which, layer, plane_idx, col):
        return full[which].at[layer, w_rows(which, plane_idx, col)]

    def w_hop(which, layer, plane_idx, right, own=False):
        slot = layer * 4 + which
        block = w_block(which, layer, plane_idx, x)
        k = PLANES if own and not right else plane_idx
        return remote(
            shard(which, layer) if own else block, block,
            (r.wz_s.at[slot, k], r.wz_r.at[slot, plane_idx]), plane(1 if right else PLANES - 1),
        )

    def w_x(which, layer, plane_idx, col, own=False):
        slot = layer * 4 + which
        block = w_block(which, layer, plane_idx, col)
        return remote(
            shard(which, layer) if own else block, block,
            (r.wx_s.at[slot, plane_idx], r.wx_r.at[slot, plane_idx]), beside,
        )

    def w_own(which, layer):
        return pltpu.make_async_copy(
            shard(which, layer), w_block(which, layer, z, x), r.w_own.at[layer * 4 + which]
        )

    last_plane = PLANES - 1

    def weights_start(which, layer):
        def go():
            pl.when(z < last_plane)(lambda: w_hop(which, layer, z, True, True).start())
            pl.when(z > 0)(lambda: w_hop(which, layer, z, False, True).start())
            w_own(which, layer).start()

        if which == OUT:
            pl.when(z == n)(go)
        else:
            go()

    def weights_steps(which, layer):
        def own():
            w_x(which, layer, z, x, True).start()

        def passed(plane_idx, right):
            w_hop(which, layer, plane_idx, right).wait_recv()
            onward = z < last_plane if right else z > 0
            pl.when(onward)(lambda: w_hop(which, layer, plane_idx, right).start())
            w_x(which, layer, plane_idx, x).start()

        def first():
            slot = layer * 4 + which + 1
            if slot < 4 * LAYERS:
                weights_start(slot % 4, slot // 4)
            if which == OUT:
                pl.when(z == n)(own)
                pl.when(z > n)(lambda: passed(n, True))
                pl.when(z < n)(lambda: passed(n, False))
            else:
                own()

        def further(j):
            pl.when(z >= j)(lambda: passed(z - j, True))
            pl.when(z + j <= last_plane)(lambda: passed(z + j, False))

        if which == OUT:
            return [first]
        return [first] + [partial(further, j) for j in range(1, PLANES)]

    steps = [
        (layer * 4 + which, step)
        for layer in range(LAYERS)
        for which in (QKV, OUT, UP, DOWN)
        for step in weights_steps(which, layer)
    ]

    def pump(count):
        for _ in range(min(count, len(steps))):
            steps.pop(0)[1]()

    def pump_through(which, layer):
        while steps and steps[0][0] <= layer * 4 + which:
            pump(1)

    def weights_finish(which, layer):
        if which == OUT:
            w_x(which, layer, n, 1 - x).wait_recv()
            pl.when(z == n)(lambda: w_own(which, layer).wait())
        else:
            for j in range(PLANES):
                w_x(which, layer, plane_of(j), 1 - x).wait_recv()
            w_own(which, layer).wait()

    def weights_drain(which, layer):
        def own():
            pl.when(z < last_plane)(lambda: w_hop(which, layer, z, True, True).wait_send())
            pl.when(z > 0)(lambda: w_hop(which, layer, z, False, True).wait_send())

        def passed(plane_idx, right):
            onward = z < last_plane if right else z > 0
            pl.when(onward)(lambda: w_hop(which, layer, plane_idx, right).wait_send())

        if which == OUT:
            w_x(which, layer, n, x).wait_send()
            pl.when(z == n)(own)
            pl.when(z > n)(lambda: passed(n, True))
            pl.when(z < n)(lambda: passed(n, False))
        else:
            own()
            for j in range(1, PLANES):
                pl.when(z >= j)(lambda: passed(z - j, True))
                pl.when(z + j <= last_plane)(lambda: passed(z + j, False))
            for j in range(PLANES):
                w_x(which, layer, plane_of(j), x).wait_send()

    def load(which, layer):
        return pltpu.make_async_copy(full[which].at[layer], loaded[which], r.load_sem.at[which])

    def weights_ready(which, layer):
        pump_through(which, layer)
        weights_finish(which, layer)
        load(which, layer).start()
        load(which, layer).wait()

    def tok_rows(chunk, part):
        return span(local * chunk + half * part, half)

    def tok_copy(ref, kind, part, incoming=False):
        chunk = ((n_core, n_side, n_far) if incoming else (n, n, n_side))[kind]
        rows = ref.at[tok_rows(chunk, part)]
        k = 2 * kind + part
        return remote(rows, rows, (r.tok_s.at[k], r.tok_r.at[k]), side if kind == 1 else core)

    def tok_send(ref, part):
        tok_copy(ref, 1, part).start()
        tok_copy(ref, 0, part).start()

    def tok_own(ref):
        for part in range(2):
            tok_copy(ref, 0, part, True).wait_recv()

    def tok_other(ref):
        for part in range(2):
            tok_copy(ref, 1, part, True).wait_recv()
            tok_copy(ref, 2, part).start()
        for part in range(2):
            tok_copy(ref, 2, part, True).wait_recv()

    def tok_drain(ref):
        for kind in range(3):
            for part in range(2):
                tok_copy(ref, kind, part).wait_send()

    def block_rows(block):
        return span(2 * local * (y if block else 1 - y), 2 * local)

    def sum_core(block):
        return remote(
            r.core_tx.at[block], r.core_rx.at[block], (r.sum_s.at[block], r.sum_r.at[block]), core
        )

    def sum_side(part):
        rows = span(half * part, half)
        return remote(
            r.side_tx.at[rows], r.side_rx.at[rows], (r.sum_s.at[2 + part], r.sum_r.at[2 + part]), side
        )

    def sum_block(block):
        r.core_tx[block] = r.part[block, span(local * (1 - c), local), :].astype(BF16)
        sum_core(block).start()

    def sum_cross():
        sum_core(0).wait_recv()
        for part in range(2):
            rows = span(half * part, half)
            mine = r.part[0, span(local * c + half * part, half), :]
            r.side_tx[rows, :] = (mine + r.core_rx[0, rows, :].astype(F32)).astype(BF16)
            sum_side(part).start()

    def sum_wait(part):
        if part == 0:
            sum_core(1).wait_recv()
        sum_side(part).wait_recv()
        if part == 1:
            for block in range(2):
                sum_core(block).wait_send()
                sum_side(block).wait_send()

    def sum_take(start):
        rows = span(start, STEP)
        return (
            r.part[1, span(local * c + start, STEP), :]
            + r.core_rx[1, rows, :].astype(F32)
            + r.side_rx[rows, :].astype(F32)
        )

    def each_step(part, body):
        @pl.loop(0, half // STEP)
        def _(i):
            body(half * part + STEP * i)

    def seg_of(start):
        return r.seg_col[span(local * n + start, STEP), :]

    def mod(layer, block, seg):
        rows = r.mods[SEGS * layer : SEGS * layer + SEGS, width * block : width * (block + 1)]
        out = rows[SEGS - 1 : SEGS]
        for s in range(SEGS - 1):
            out = jnp.where(seg == s, rows[s : s + 1], out)
        return out

    def mod_sum(layer, block, seg, values):
        sums = [jnp.sum(jnp.where(seg == s, values, 0.0), 0, keepdims=True) for s in range(SEGS)]
        at = (slice(SEGS * layer, SEGS * layer + SEGS), slice(width * block, width * (block + 1)))
        r.mod_grad[at] += jnp.concatenate(sums, 0)

    seg_cols = jnp.transpose(jnp.broadcast_to(r.seg_row[...].astype(F32), (8, narrow * local)))
    r.seg_col[...] = seg_cols[:, :1].astype(jnp.int32)

    def shifted(values, rest, size):
        window = values.shape[1]
        return pltpu.roll(values.astype(F32), (window - rest) % window, 1)[:, :size]

    def pick(ref, start, size, window):
        return shifted(ref[0, :, span(LANES * (start // LANES), window, LANES)], start % LANES, size)

    def pack(dst, pieces):
        at = 0
        for piece in pieces:
            size = piece.shape[1]
            dst[..., at : at + size] = piece.astype(dst.dtype)
            at += size

    def pack_shard(which, layer):
        dst, pieces = (r.qkv_s if which == QKV else r.up_s).at[layer], []
        for k, (start, size, _) in enumerate(windows(which)):
            raw(which, layer, k).wait()
            buffer = r.qkv_raw if which == QKV else r.up_raw
            pieces.append(shifted(buffer[layer, k], start % LANES, size))
        pack(dst, pieces)

    def lead_copy(j, incoming=False):
        return remote(
            r.lead.at[(w + j) % wide], r.lead_rx.at[(w - j + wide) % wide if incoming else w],
            (r.lead_sem_s.at[j - 1], r.lead_sem_r.at[j - 1]), wide_peer(j),
        )

    def bias_copy(j, incoming=False):
        return remote(
            r.bias_tx, r.bias_rx.at[(w - j + wide) % wide if incoming else w],
            (r.bias_sem_s.at[j - 1], r.bias_sem_r.at[j - 1]), wide_peer(j),
        )

    def mod_copy(j, incoming=False):
        return remote(
            r.mod_tx.at[(w + j) % wide], r.mod_rx.at[(w - j + wide) % wide if incoming else w],
            (r.mod_sem_s.at[j - 1], r.mod_sem_r.at[j - 1]), wide_peer(j),
        )

    narrow_peers = ((core, n_core), (side, n_side), (far, n_far))

    def quarter_copy(k, incoming=False):
        device, idx = narrow_peers[k]
        return remote(
            r.mod_q.at[n], r.mod_q.at[idx if incoming else n],
            (r.quarter_s.at[k], r.quarter_r.at[k]), device,
        )

    for j in range(1, wide):
        lead_copy(j).start()
    pack_shard(QKV, 0)
    weights_start(QKV, 0)
    for j in range(1, wide):
        bias_copy(j).start()
    r.lead_rx[pl.ds(w, 1)] = r.lead[pl.ds(w, 1)]
    r.bias_rx[pl.ds(w, 1)] = r.bias_tx[...][None]
    ada_load.wait()
    for j in range(1, wide):
        lead_copy(j, True).wait_recv()
    lead_all = r.lead_rx[...].reshape(wide * 16, depth)
    for layer in range(LAYERS):
        product = dot(lead_all, r.ada_v[layer], ((1,), (0,)))
        for row in range(wide):
            at = slice(SEGS * layer, SEGS * layer + SEGS)
            r.mod_tx[row, at, :] = product[16 * row : 16 * row + SEGS]
    for j in range(1, wide):
        mod_copy(j).start()
    r.mod_rx[pl.ds(w, 1)] = r.mod_tx[pl.ds(w, 1)]
    for which, layer in ((UP, 0), (QKV, 1), (UP, 1)):
        pack_shard(which, layer)
    pump_through(QKV, 0)
    r.mod_grad[...] = jnp.zeros_like(r.mod_grad)
    r.lead_t[...] = jnp.zeros_like(r.lead_t)
    for layer in range(LAYERS):
        for row in range(wide):
            at = (row * LAYERS + layer) * SEGS
            r.lead_t[layer, at : at + SEGS, :] = r.lead_rx[row].astype(F32)[:SEGS]
        r.lead_o[layer] = jnp.transpose(r.lead_t[layer]).astype(BF16)

    for j in range(1, wide):
        bias_copy(j, True).wait_recv()
    for row in range(wide):
        for line, at, ref in (
            (0, 0, r.ada_full), (1, 0, r.qkv_full), (1, 4 * LANES, r.out_full),
            (2, 0, r.up_full), (2, 5 * LANES, r.down_full),
        ):
            size = ref.shape[-1] // wide
            for layer in range(LAYERS):
                piece = r.bias_rx[row, 3 * layer + line : 3 * layer + line + 1, at : at + size]
                ref[0, layer : layer + 1, size * row : size * (row + 1)] = piece
    for which, ref in ((QKV, r.qkv_full), (UP, r.up_full)):
        pieces = [pick(ref, *window) for window in windows(which)]
        for layer in range(LAYERS):
            at = 4 * layer + which
            pack(r.bias_sum.at[at : at + 1], [piece[layer : layer + 1] for piece in pieces])
    for layer in range(LAYERS):
        at = 4 * layer
        r.bias_sum[at + OUT : at + OUT + 1] = r.out_full[0, layer : layer + 1]
        r.bias_sum[at + DOWN : at + DOWN + 1] = r.down_full[0, layer : layer + 1]

    for j in range(1, wide):
        mod_copy(j, True).wait_recv()
    ada_own = r.ada_full[0, :, span(LANES * mod_start(tiles, narrow, n), mod_cols, LANES)]
    total = jnp.sum(r.mod_rx[...], 0)
    for layer in range(LAYERS):
        at = slice(SEGS * layer, SEGS * layer + SEGS)
        r.mod_q[pl.ds(n, 1), at, :] = (total[at] + ada_own[layer : layer + 1])[None]
    for k in range(3):
        quarter_copy(k).start()
    pump(2)
    for k in range(3):
        quarter_copy(k, True).wait_recv()
    for part in range(narrow):
        at = LANES * mod_start(tiles, narrow, part)
        r.mods[:, at : at + mod_cols] = r.mod_q[part]

    def bias_row(layer, which, size):
        return r.bias_sum[4 * layer + which : 4 * layer + which + 1, :size]

    def gather_norm(layer, hid, shift, scale, take, before):
        for part in range(2):
            before(part)

            def step(start):
                seg = seg_of(start)
                unit, _ = norm(take(start, seg))
                hidden = unit * (1.0 + mod(layer, scale, seg)) + mod(layer, shift, seg)
                hid[span(local * n + start, STEP), :] = hidden.astype(BF16)

            each_step(part, step)
            tok_send(hid, part)

    def qkv_block(layer, block):
        rows = block_rows(block)
        out = dot(r.hid_attn[layer, rows, :], r.qkv_v[...], ((1,), (0,)))
        out = (out + bias_row(layer, QKV, 3 * cols)).astype(BF16)
        for j in range(3 * own_heads):
            r.heads[layer, j, rows, :HEAD] = out[:, HEAD * j : HEAD * (j + 1)]

    def attend(layer):
        for head in range(own_heads):

            @pl.loop(0, narrow)
            def _(i):
                rows = span(local * i, local)
                query = r.heads[layer, head, rows, :HEAD]
                key = r.heads[layer, own_heads + head, :, :HEAD]
                value = r.heads[layer, 2 * own_heads + head, :, :HEAD]
                scores = dot(query, key, ((1,), (1,))) * scale_inv
                scores = jnp.where(r.seg_col[rows, :] == r.seg_row[...], scores, -1e30)
                top = jnp.max(scores, -1, keepdims=True)
                power = jnp.exp(scores - top)
                total = jnp.sum(power, -1, keepdims=True)
                probs = (power / total).astype(BF16)
                mixed = dot(probs, value, ((1,), (0,)))
                r.mixed[layer, rows, HEAD * head : HEAD * (head + 1)] = mixed.astype(BF16)
                r.log_sum[layer, rows, head : head + 1] = top + jnp.log(total)

            if head % 2:
                pump(1)

    def mlp_block(layer, block):
        rows = block_rows(block)
        hidden = r.hid_mlp[layer, rows, :]
        for at in range(0, width, 3 * LANES):
            tile = slice(at, at + 3 * LANES)
            up = dot(hidden, r.up_v[:, tile], ((1,), (0,)))
            up = up + r.bias_sum[4 * layer + UP : 4 * layer + UP + 1, tile]
            r.up[layer, rows, tile] = up.astype(BF16)
            r.act[layer, rows, tile] = gelu(up).astype(BF16)
        r.part[block] = dot(r.act[layer, rows, :], r.down_v[...], ((1,), (0,)))

    def state_of(layer, start):
        rows = span(start, STEP)
        return r.tok[rows, :].astype(F32) if layer == 0 else r.state[rows, :]

    def after_attn(layer):
        def take(start, seg):
            rows = span(start, STEP)
            branch = sum_take(start) + bias_row(layer, OUT, width)
            r.branch[layer, rows, :] = branch.astype(BF16)
            middle = state_of(layer, start) + mod(layer, 2, seg) * branch
            r.middle[layer, rows, :] = middle
            return middle

        return take

    def after_mlp(layer):
        def take(start, seg):
            rows = span(start, STEP)
            down = sum_take(start) + bias_row(layer, DOWN, width)
            r.down[layer, rows, :] = down.astype(BF16)
            result = r.middle[layer, rows, :] + mod(layer, 5, seg) * down
            if layer == 0:
                r.state[rows, :] = result
            else:
                r.mixed_o[rows, :] = result.astype(BF16)
            return result

        return take

    for layer in range(LAYERS):
        hid = r.hid_attn.at[layer]
        if layer == 0:
            gather_norm(0, hid, 0, 1, lambda start, seg: state_of(0, start), lambda part: None)
        else:
            gather_norm(layer, hid, 0, 1, after_mlp(layer - 1), sum_wait)
        pump(1)
        weights_ready(QKV, layer)
        tok_own(hid)
        qkv_block(layer, 1)
        tok_other(hid)
        qkv_block(layer, 0)
        pump(1)
        attend(layer)
        weights_ready(OUT, layer)
        tok_drain(hid)
        for block in range(2):
            r.part[block] = dot(r.mixed[layer, block_rows(block), :], r.out_v[...], ((1,), (0,)))
            sum_block(block)
            if block == 0:
                sum_cross()
        pump(1)
        hid = r.hid_mlp.at[layer]
        gather_norm(layer, hid, 3, 4, after_attn(layer), sum_wait)
        pump(1)
        weights_ready(UP, layer)
        weights_ready(DOWN, layer)
        tok_own(hid)
        mlp_block(layer, 1)
        sum_block(1)
        pump(1)
        tok_other(hid)
        mlp_block(layer, 0)
        sum_block(0)
        sum_cross()
        tok_drain(hid)
        pump(1)
    for part in range(2):
        sum_wait(part)
        finish = after_mlp(LAYERS - 1)

        def last(start):
            finish(start, seg_of(start))

        each_step(part, last)

    sums = (r.qkv_d, r.out_d, r.up_d, r.down_d)
    from_x = (r.qkv_xr, r.out_xr, r.up_xr, r.down_xr)
    from_z = (r.qkv_zr, r.out_zr, r.up_zr, r.down_zr)
    final = (r.qkv_f, r.out_f, r.up_f, r.down_f)
    grads_o = (r.qkv_o, r.out_o, r.up_o, r.down_o)
    same_y, same_c = y == z // 2, c == z % 2

    def d_rows(which, plane_idx, col):
        return w_rows(which, plane_idx, col)

    def d_x(which, plane_idx, incoming=False):
        k = 0 if which == OUT else plane_idx
        src = sums[which].at[d_rows(which, plane_idx, 1 - x)]
        return remote(
            src, from_x[which].at[k], (r.dx_s.at[which, k], r.dx_r.at[which, k]), beside
        )

    def d_z(which, j):
        dest = n if which == OUT else plane_of(j)
        k = 0 if which == OUT else j - 1
        src = sums[which].at[d_rows(which, dest, x)]
        return remote(
            src, from_z[which].at[j - 1], (r.dz_s.at[which, k], r.dz_r.at[which, j - 1]), plane(j)
        )

    def grad_product(which, layer):
        left, right = (
            (r.hid_attn, r.grad_qkv), (r.mixed, r.grad_branch),
            (r.hid_mlp, r.grad_up), (r.act, r.grad_down),
        )[which]
        if which == OUT:
            product = dot(left[layer], right[...], ((0,), (0,)))
            sums[which][...] = product.astype(BF16)
        else:

            @pl.loop(0, width // (3 * LANES))
            def _(i):
                tile = span(3 * LANES * i, 3 * LANES, LANES)
                product = dot(left[layer, :, tile], right[...], ((0,), (0,)))
                sums[which][tile, :] = product.astype(BF16)

        if layer == 0:
            pl.semaphore_wait(r.credit_x.at[which], 1)
        for plane_idx in range(1 if which == OUT else PLANES):
            d_x(which, plane_idx).start()

    def grad_beside(which, layer):
        if which == OUT:
            d_x(which, 0).wait_recv()
            rows = d_rows(which, n, x)
            total = sums[which][rows, :].astype(F32) + from_x[which][0].astype(F32)
            sums[which][rows, :] = total.astype(BF16)

            @pl.when(z != n)
            def _():
                if layer == 0:
                    pl.semaphore_wait(r.credit_z.at[which], 1)
                d_z(which, (n - z + PLANES) % PLANES).start()

            d_x(which, 0).wait_send()
        else:
            for j in (1, 2, 3, 0):
                idx = plane_of(j)
                d_x(which, idx).wait_recv()
                rows = d_rows(which, idx, x)
                total = sums[which][rows, :].astype(F32) + from_x[which][idx].astype(F32)
                sums[which][rows, :] = total.astype(BF16)
                if layer == 0 and j == 1:
                    pl.semaphore_wait(r.credit_z.at[which], PLANES - 1)
                if j:
                    d_z(which, j).start()
            for idx in range(PLANES):
                d_x(which, idx).wait_send()
        if layer == 1:
            pl.semaphore_signal(
                r.credit_x.at[which], inc=1, device_id=beside, device_id_type=MESH
            )

    def grad_planes(which, layer):
        def add():
            for j in range(1, PLANES):
                d_z(which, j).wait_recv()
            rows = d_rows(which, z, x)
            total = sums[which][rows, :].astype(F32)
            for j in range(PLANES - 1):
                total = total + from_z[which][j].astype(F32)
            if layer == 0:
                spread_sent(which, 1)
            final[which][...] = total.astype(BF16)
            if layer == 1:
                for j in range(1, PLANES):
                    pl.semaphore_signal(
                        r.credit_z.at[which], inc=1, device_id=plane(j), device_id_type=MESH
                    )

        if which == OUT:
            pl.when(z == n)(add)

            @pl.when(z != n)
            def _():
                d_z(which, (n - z + PLANES) % PLANES).wait_send()
        else:
            add()
            for j in range(1, PLANES):
                d_z(which, j).wait_send()

    def spread(which, layer, kind, source=None):
        slot = layer * 4 + which
        if which == OUT:
            dst = grads_o[which].at[layer]
        else:
            dst = grads_o[which].at[layer, n if source is None else source]
        src = final[which] if kind < 2 else dst
        return remote(
            src, dst, (r.spread_s.at[slot, kind], r.spread_r.at[slot, kind]), side if kind == 1 else core
        )

    def spread_own(which, layer):
        dst = grads_o[which].at[layer] if which == OUT else grads_o[which].at[layer, n]
        return pltpu.make_async_copy(final[which], dst, r.spread_l.at[layer * 4 + which])

    def spread_sent(which, layer):
        spread(which, layer, 1).wait_send()
        spread(which, layer, 0).wait_send()
        spread_own(which, layer).wait()

    def grad_spread(which, layer):
        def go():
            spread(which, layer, 1).start()
            spread(which, layer, 0).start()
            spread_own(which, layer).start()

        if which == OUT:
            pl.when(jnp.logical_and(same_y, same_c))(go)
        else:
            go()

    def grad_pass(which, layer):
        def go():
            spread(which, layer, 1, n_side).wait_recv()
            spread(which, layer, 2, n_side).start()

        if which == OUT:
            pl.when(jnp.logical_and(jnp.logical_not(same_y), same_c))(go)
        else:
            go()

    def grad_end(which, layer):
        if which == OUT:
            if layer == 0:
                pl.when(jnp.logical_and(same_y, same_c))(lambda: spread_sent(which, layer))

            @pl.when(jnp.logical_and(jnp.logical_not(same_y), same_c))
            def _():
                spread(which, layer, 2).wait_send()

            @pl.when(jnp.logical_and(same_y, jnp.logical_not(same_c)))
            def _():
                spread(which, layer, 0).wait_recv()

            @pl.when(jnp.logical_and(jnp.logical_not(same_y), jnp.logical_not(same_c)))
            def _():
                spread(which, layer, 2).wait_recv()
        else:
            spread(which, layer, 0, n_core).wait_recv()
            spread(which, layer, 2, n_far).wait_recv()
            spread(which, layer, 2, n_side).wait_send()
            if layer == 0:
                spread_sent(which, layer)

    def bias_grad(layer, which, values):
        at = 4 * layer + which
        r.bias_grad[at : at + 1, : values.shape[1]] = jnp.sum(
            values.astype(F32), 0, keepdims=True
        )

    def back_mlp_block(layer, block):
        rows = block_rows(block)
        grad_down = r.grad_down[rows, :]
        for at in range(0, width, 3 * LANES):
            tile = slice(at, at + 3 * LANES)
            grad_act = dot(grad_down, r.down_v[tile, :], ((1,), (1,)))
            up = r.up[layer, rows, tile].astype(F32)
            r.grad_up[rows, tile] = (grad_act * gelu_slope(up)).astype(BF16)
        r.part[block] = dot(r.grad_up[rows, :], r.up_v[...], ((1,), (1,)))

    def back_attn_block(layer, block):
        rows = block_rows(block)
        out = dot(r.grad_branch[rows, :], r.out_v[...], ((1,), (1,))).astype(BF16)
        for j in range(own_heads):
            r.grad_heads[j, rows, :HEAD] = out[:, HEAD * j : HEAD * (j + 1)]

    def back_attend(layer, head):
        @pl.loop(0, narrow)
        def _(i):
            rows = span(local * i, local)
            query = r.heads[layer, head, rows, :HEAD]
            key = r.heads[layer, own_heads + head, :, :HEAD]
            value = r.heads[layer, 2 * own_heads + head, :, :HEAD]
            grad = r.grad_heads[head, rows, :HEAD]
            scores = dot(query, key, ((1,), (1,))) * scale_inv
            probs = jnp.exp(scores - r.log_sum[layer, rows, head : head + 1])
            probs = jnp.where(r.seg_col[rows, :] == r.seg_row[...], probs, 0.0)
            grad_probs = dot(grad, value, ((1,), (1,)))
            inner = jnp.sum(probs * grad_probs, -1, keepdims=True)
            grad_scores = (probs * (grad_probs - inner)).astype(BF16)
            grad_query = dot(grad_scores, key, ((1,), (0,))) * scale_inv
            r.grad_qkv[rows, HEAD * head : HEAD * (head + 1)] = grad_query.astype(BF16)
            grad_key = dot(grad_scores, query, ((0,), (0,)))
            grad_value = dot(probs.astype(BF16), grad, ((0,), (0,)))

            @pl.when(i == 0)
            def _():
                r.key_sum[:, :HEAD] = grad_key
                r.value_sum[:, :HEAD] = grad_value

            @pl.when(i > 0)
            def _():
                r.key_sum[:, :HEAD] += grad_key
                r.value_sum[:, :HEAD] += grad_value

        at = cols + HEAD * head
        r.grad_qkv[:, at : at + HEAD] = (r.key_sum[:, :HEAD] * scale_inv).astype(BF16)
        r.grad_qkv[:, cols + at : cols + at + HEAD] = r.value_sum[:, :HEAD].astype(BF16)

    for part in range(2):
        def first(start):
            rows = span(start, STEP)
            r.token_o[rows, :] = r.cot[rows, :].astype(F32)

        each_step(part, first)

    def both(body):
        for part in range(2):
            each_step(part, body)

    for layer in reversed(range(LAYERS)):
        older = layer + 1
        for part in range(2):
            if layer < LAYERS - 1:
                sum_wait(part)

            def start_down(start):
                rows = span(start, STEP)
                seg = seg_of(start)
                if layer < LAYERS - 1:
                    grad_hidden = sum_take(start)
                    unit, inv = norm(state_of(older, start))
                    r.grad_hid[rows, :] = grad_hidden
                    r.token_o[rows, :] += norm_back(
                        grad_hidden * (1.0 + mod(older, 1, seg)), unit, inv
                    )
                grad_down = (mod(layer, 5, seg) * r.token_o[rows, :]).astype(BF16)
                r.grad_down[span(local * n + start, STEP), :] = grad_down

            each_step(part, start_down)
            tok_send(r.grad_down, part)

        def sums_attn(idx):
            def body(start):
                rows = span(start, STEP)
                seg = seg_of(start)
                unit, _ = norm(state_of(idx, start))
                grad_hidden = r.grad_hid[rows, :]
                mod_sum(idx, 0, seg, grad_hidden)
                mod_sum(idx, 1, seg, grad_hidden * unit)

            return body

        if layer < LAYERS - 1:
            both(sums_attn(older))
            load(DOWN, layer).wait()
            load(UP, layer).wait()

        def sums_gate_mlp(start):
            rows = span(start, STEP)
            mod_sum(layer, 5, seg_of(start), r.down[layer, rows, :].astype(F32) * r.token_o[rows, :])

        both(sums_gate_mlp)
        bias_grad(layer, DOWN, r.grad_down[span(local * n, local), :])
        tok_own(r.grad_down)
        back_mlp_block(layer, 1)
        sum_block(1)
        tok_other(r.grad_down)
        back_mlp_block(layer, 0)
        sum_block(0)
        sum_cross()
        if layer > 0:
            load(DOWN, layer - 1).start()
            load(UP, layer - 1).start()
        if layer == 1:
            grad_product(DOWN, 1)
            grad_product(UP, 1)
        else:
            grad_beside(UP, 1)
            grad_beside(OUT, 1)
            grad_planes(DOWN, 1)
            grad_product(DOWN, 0)
        bias_grad(layer, UP, r.grad_up[...])
        tok_drain(r.grad_down)
        for part in range(2):
            sum_wait(part)

            def start_branch(start):
                rows = span(start, STEP)
                seg = seg_of(start)
                grad_hidden = sum_take(start)
                unit, inv = norm(r.middle[layer, rows, :])
                r.grad_hid[rows, :] = grad_hidden
                grad = r.token_o[rows, :] + norm_back(
                    grad_hidden * (1.0 + mod(layer, 4, seg)), unit, inv
                )
                r.token_o[rows, :] = grad
                grad_branch = (mod(layer, 2, seg) * grad).astype(BF16)
                r.grad_branch[span(local * n + start, STEP), :] = grad_branch

            each_step(part, start_branch)
            tok_send(r.grad_branch, part)

        def sums_mlp(start):
            rows = span(start, STEP)
            seg = seg_of(start)
            unit, _ = norm(r.middle[layer, rows, :])
            grad_hidden = r.grad_hid[rows, :]
            mod_sum(layer, 3, seg, grad_hidden)
            mod_sum(layer, 4, seg, grad_hidden * unit)
            mod_sum(layer, 2, seg, r.branch[layer, rows, :].astype(F32) * r.token_o[rows, :])

        both(sums_mlp)
        bias_grad(layer, OUT, r.grad_branch[span(local * n, local), :])
        if layer < LAYERS - 1:
            load(OUT, layer).wait()
            load(QKV, layer).wait()
        tok_own(r.grad_branch)
        back_attn_block(layer, 1)
        tok_other(r.grad_branch)
        back_attn_block(layer, 0)
        if layer > 0:
            load(OUT, layer - 1).start()
        if layer == 0:
            grad_spread(DOWN, 1)
            grad_beside(QKV, 1)
        for head in range(own_heads):
            back_attend(layer, head)
        for block in range(2):
            rows = block_rows(block)
            r.part[block] = dot(r.grad_qkv[rows, :], r.qkv_v[...], ((1,), (1,)))
            sum_block(block)
            if block == 0:
                sum_cross()
        tok_drain(r.grad_branch)
        if layer > 0:
            load(QKV, layer - 1).start()
        if layer == 1:
            grad_product(OUT, 1)
            grad_product(QKV, 1)
            grad_beside(DOWN, 1)
        else:
            grad_planes(UP, 1)
            grad_product(UP, 0)
            grad_planes(OUT, 1)
            grad_product(OUT, 0)
            grad_planes(QKV, 1)
            grad_product(QKV, 0)
        bias_grad(layer, QKV, r.grad_qkv[...])
    for part in range(2):
        sum_wait(part)

        def finish_grad(start):
            rows = span(start, STEP)
            seg = seg_of(start)
            grad_hidden = sum_take(start)
            unit, inv = norm(state_of(0, start))
            grad = r.token_o[rows, :] + norm_back(grad_hidden * (1.0 + mod(0, 1, seg)), unit, inv)
            r.token_o[rows, :] = grad
            mod_sum(0, 0, seg, grad_hidden)
            mod_sum(0, 1, seg, grad_hidden * unit)

        each_step(part, finish_grad)

    def quarter_back(k, incoming=False):
        device, idx = narrow_peers[k]
        at = span(LANES * mod_start(tiles, narrow, idx), mod_cols, LANES)
        return remote(
            r.mod_grad.at[:, at], r.quarter_rx.at[k], (r.back_s.at[k], r.back_r.at[k]), device
        )

    def wide_back(j, incoming=False):
        return remote(
            r.quarter_sum, r.quarter_all.at[(w - j + wide) % wide if incoming else w],
            (r.wide_s.at[j - 1], r.wide_r.at[j - 1]), wide_peer(j),
        )

    def bias_wide(j, incoming=False):
        return remote(
            r.bias_grad, r.bias_all.at[(w - j + wide) % wide if incoming else w],
            (r.bias_wide_s.at[j - 1], r.bias_wide_r.at[j - 1]), wide_peer(j),
        )

    def bias_narrow(k, incoming=False):
        device, idx = narrow_peers[k]
        return remote(
            r.bias_row, r.bias_o.at[idx if incoming else n],
            (r.bias_narrow_s.at[k], r.bias_narrow_r.at[k]), device,
        )

    def mod_narrow(k, incoming=False):
        device, idx = narrow_peers[k]
        return remote(
            r.mod_all, r.mod_o.at[idx if incoming else n],
            (r.mod_narrow_s.at[k], r.mod_narrow_r.at[k]), device,
        )

    def lead_back(j, incoming=False):
        return remote(
            r.lead_tx.at[(w + j) % wide], r.lead_back.at[(w - j + wide) % wide if incoming else w],
            (r.lead_back_s.at[j - 1], r.lead_back_r.at[j - 1]), wide_peer(j),
        )

    def lead_narrow(k, incoming=False):
        device, idx = narrow_peers[k]
        return remote(
            r.lead_back, r.lead_g.at[idx if incoming else n],
            (r.lead_narrow_s.at[k], r.lead_narrow_r.at[k]), device,
        )

    for k in range(3):
        quarter_back(k).start()
    grad_beside(DOWN, 0)
    grad_spread(UP, 1)
    grad_spread(OUT, 1)
    own_at = span(LANES * mod_start(tiles, narrow, n), mod_cols, LANES)
    total = r.mod_grad[:, own_at]
    for k in range(3):
        quarter_back(k, True).wait_recv()
        total = total + r.quarter_rx[k]
    r.quarter_sum[...] = total
    for j in range(1, wide):
        wide_back(j).start()
    for j in range(1, wide):
        bias_wide(j).start()
    r.quarter_all[pl.ds(w, 1)] = total[None]
    r.bias_all[pl.ds(w, 1)] = r.bias_grad[...][None]
    grad_spread(QKV, 1)
    grad_beside(UP, 0)
    grad_beside(OUT, 0)
    for which in (DOWN, UP, OUT, QKV):
        grad_pass(which, 1)
    grad_planes(DOWN, 0)
    grad_spread(DOWN, 0)
    grad_beside(QKV, 0)
    for j in range(1, wide):
        wide_back(j, True).wait_recv()
    r.mod_all[...] = r.quarter_all[...].reshape(wide * LAYERS * SEGS, mod_cols).astype(BF16)
    mod_own = pltpu.make_async_copy(r.mod_all, r.mod_o.at[n], r.mod_own_sem)
    mod_own.start()
    for k in range(3):
        mod_narrow(k).start()
    owned = LANES * (mod_start(tiles, narrow, n + 1) - mod_start(tiles, narrow, n))
    lane = lax.broadcasted_iota(jnp.int32, r.mod_all.shape, 1)
    own_grads = jnp.where(lane < owned, r.mod_all[...].astype(F32), 0.0).astype(BF16)
    lead_parts = [dot(own_grads, r.ada_v[layer], ((1,), (1,))) for layer in range(LAYERS)]
    for row in range(wide):
        at = row * LAYERS * SEGS
        r.lead_tx[row] = lead_parts[0][at : at + SEGS] + lead_parts[1][at + SEGS : at + 2 * SEGS]
    for j in range(1, wide):
        lead_back(j).start()
    r.lead_back[pl.ds(w, 1)] = r.lead_tx[pl.ds(w, 1)]
    for j in range(1, wide):
        bias_wide(j, True).wait_recv()
    r.bias_row[...] = jnp.sum(r.bias_all[...], 0)
    bias_own = pltpu.make_async_copy(r.bias_row, r.bias_o.at[n], r.bias_own_sem)
    bias_own.start()
    for k in range(3):
        bias_narrow(k).start()
    for j in range(1, wide):
        lead_back(j, True).wait_recv()
    lead_own = pltpu.make_async_copy(r.lead_back, r.lead_g.at[n], r.lead_own_sem)
    lead_own.start()
    for k in range(3):
        lead_narrow(k).start()
    grad_planes(UP, 0)
    grad_spread(UP, 0)
    grad_planes(OUT, 0)
    grad_spread(OUT, 0)
    grad_pass(DOWN, 0)
    grad_planes(QKV, 0)
    grad_spread(QKV, 0)
    for which in (UP, OUT, QKV):
        grad_pass(which, 0)

    for layer in range(LAYERS):
        for which in range(4):
            weights_drain(which, layer)
            grad_end(which, layer)
    for j in range(1, wide):
        for copy in (lead_copy, bias_copy, mod_copy, wide_back, bias_wide, lead_back):
            copy(j).wait_send()
    for k in range(3):
        for copy in (quarter_copy, quarter_back, mod_narrow, bias_narrow, lead_narrow):
            copy(k).wait_send()
        mod_narrow(k, True).wait_recv()
        bias_narrow(k, True).wait_recv()
        lead_narrow(k, True).wait_recv()
    mod_own.wait()
    lead_own.wait()
    bias_own.wait()


def gelu_slope(values):
    rate = math.sqrt(2.0 / math.pi)
    bent = jnp.tanh(rate * (values + 0.044715 * values * values * values))
    inner = rate * (1.0 + 3.0 * 0.044715 * values * values)
    return 0.5 * (1.0 + bent) + 0.5 * values * (1.0 - bent * bent) * inner


def chosen_of(cond, index):
    values = cond[...].astype(F32)
    rows = index[...]
    chosen = jnp.zeros(values.shape, F32)
    for k in range(SEGS):
        chosen = jnp.where(rows == k, values[k : k + 1], chosen)
    return chosen


def finish_kernel(cfg, *refs):
    r = SimpleNamespace(**dict(zip(cfg.names, refs)))
    wide, narrow, width, depth, cols = cfg.wide, cfg.narrow, cfg.width, cfg.depth, cfg.cols
    tiles, hidden_own = cfg.tiles, cfg.hidden_own
    w = lax.axis_index("wide")

    for part in range(narrow):
        values = r.qkv_i[0, part].astype(F32)
        for j in range(3):
            at = width * j + cols * part
            r.qkv_g[0, :, at : at + cols] = values[:, cols * j : cols * (j + 1)]
        values = r.up_i[0, part].astype(F32)
        for j in range(wide):
            at = (j * narrow + part) * hidden_own
            r.up_g[0, :, at : at + hidden_own] = values[:, hidden_own * j : hidden_own * (j + 1)]
        at, end = [LANES * mod_start(tiles, narrow, part + k) for k in range(2)]
        r.ada_g[0, :, at:end] = dot(r.lead_i[0], r.mod_i[part, :, : end - at], ((1,), (0,)))
    r.out_g[...] = r.out_i[...].astype(F32)
    r.down_g[...] = r.down_i[...].astype(F32)

    def pick(ref, size):
        start = size * w
        window = LANES * (-(-size // LANES) + 1)
        tile, rest = start // LANES, start % LANES
        values = ref[:, pl.ds(pl.multiple_of(LANES * tile, LANES), window)]
        return pltpu.roll(values, (window - rest) % window, 1)[:, :size]

    @pl.when(pl.program_id(0) + pl.program_id(1) == 0)
    def _():
        for part in range(narrow):
            values = r.bias_i[part]
            for j in range(3):
                at = width * j + cols * part
                r.qkv_t[:, at : at + cols] = values[:, cols * j : cols * (j + 1)]
            for j in range(wide):
                at = (j * narrow + part) * hidden_own
                r.up_t[:, at : at + hidden_own] = values[:, hidden_own * j : hidden_own * (j + 1)]
            at, end = [LANES * mod_start(tiles, narrow, part + k) for k in range(2)]
            values = r.mod_i[part, :, : end - at].astype(F32)
            layer_of = lax.broadcasted_iota(jnp.int32, values.shape, 0) // SEGS % LAYERS
            for layer in range(LAYERS):
                sums = jnp.sum(jnp.where(layer_of == layer, values, 0.0), 0, keepdims=True)
                r.ada_t[layer : layer + 1, at:end] = sums
        r.row_t[:, :width] = jnp.sum(r.bias_i[...], 0)
        for dst, ref, line, step in (
            (r.ada_bg, r.ada_t, 0, 1), (r.qkv_bg, r.qkv_t, QKV, 4), (r.out_bg, r.row_t, OUT, 4),
            (r.up_bg, r.up_t, UP, 4), (r.down_bg, r.row_t, DOWN, 4),
        ):
            values = pick(ref, dst.shape[1])
            for layer in range(LAYERS):
                at = step * layer + line
                dst[layer : layer + 1, :] = values[at : at + 1]
        chosen = chosen_of(r.cond, r.cond_index)
        gate = jax.nn.sigmoid(chosen)
        slope = gate * (1.0 + chosen * (1.0 - gate))
        lead_grad = jnp.sum(r.lead_i2[...], 0)
        for row in range(wide):
            at = slice(depth * row, depth * (row + 1))
            grad = lead_grad[row] * slope[:, at]
            for k in range(SEGS):
                r.cond_g[k : k + 1, at] = jnp.sum(
                    jnp.where(r.cond_index[...] == k, grad, 0.0), 0, keepdims=True
                )


def finish(wide, narrow, got, cond, cond_index, tiles, mod_cols, w):
    width = cond.shape[1]
    depth, cols = width // wide, width // narrow
    hidden_own = got["up_o"].shape[-1] // wide
    hidden_all = got["up_o"].shape[-1] * narrow
    down_rows = narrow * hidden_own
    bands = depth // 16
    shape, vmem = jax.ShapeDtypeStruct, pltpu.VMEM

    def whole(values):
        return pl.BlockSpec(values.shape, lambda i, j: (0,) * values.ndim)

    def band(*dims):
        return pl.BlockSpec(
            (1, *dims), lambda i, j: (i, 0, j, 0) if len(dims) == 3 else (i, j, 0)
        )

    down_i = got["down_o"].reshape(LAYERS, down_rows, width)
    inputs = dict(
        qkv_i=got["qkv_o"], up_i=got["up_o"], out_i=got["out_o"], down_i=down_i,
        lead_i=got["lead_o"], mod_i=got["mod_o"], bias_i=got["bias_o"], lead_i2=got["lead_g"],
        cond=cond, cond_index=cond_index,
    )
    in_specs = [
        band(narrow, 16, 3 * cols), band(narrow, 16, wide * hidden_own), band(16, width),
        band(down_rows // bands, width), band(16, got["lead_o"].shape[-1]),
        *[whole(inputs[name]) for name in ("mod_i", "bias_i", "lead_i2", "cond", "cond_index")],
    ]
    outputs = dict(
        ada_g=shape((LAYERS, depth, tiles * LANES), F32), qkv_g=shape((LAYERS, depth, 3 * width), F32),
        out_g=shape((LAYERS, depth, width), F32), up_g=shape((LAYERS, depth, hidden_all), F32),
        down_g=shape((LAYERS, down_rows, width), F32),
        ada_bg=shape((LAYERS, tiles * LANES // wide), F32), qkv_bg=shape((LAYERS, 3 * width // wide), F32),
        out_bg=shape((LAYERS, depth), F32), up_bg=shape((LAYERS, hidden_all // wide), F32),
        down_bg=shape((LAYERS, depth), F32), cond_g=shape((SEGS, width), F32),
    )
    out_specs = [
        band(16, tiles * LANES), band(16, 3 * width), band(16, width), band(16, hidden_all),
        band(down_rows // bands, width),
        *[whole(outputs[name]) for name in ("ada_bg", "qkv_bg", "out_bg", "up_bg", "down_bg", "cond_g")],
    ]
    scratch = dict(
        ada_t=vmem((8, (tiles + 2) * LANES), F32), qkv_t=vmem((8, 3 * width + 2 * LANES), F32),
        up_t=vmem((8, hidden_all + 2 * LANES), F32), row_t=vmem((8, width + 2 * LANES), F32),
    )
    cfg = SimpleNamespace(
        names=[*inputs, *outputs, *scratch], wide=wide, narrow=narrow, width=width, depth=depth,
        cols=cols, tiles=tiles, hidden_own=hidden_own,
    )
    results = pl.pallas_call(
        partial(finish_kernel, cfg),
        grid=(LAYERS, bands),
        out_shape=list(outputs.values()), in_specs=in_specs, out_specs=out_specs,
        scratch_shapes=list(scratch.values()),
        compiler_params=pltpu.CompilerParams(vmem_limit_bytes=48 * 2**20),
    )(*inputs.values())
    done = dict(zip(outputs, results))
    out = [got["mixed_o"][None], got["token_o"][None], done["cond_g"][None]]
    for name in ("ada", "qkv", "out", "up", "down"):
        out += [done[name + "_g"], done[name + "_bg"]]
    return tuple(out)


def fused_device(
    wide, narrow,
    tokens, cond, seg_ids, cond_index, cotangent,
    ada_weight, ada_bias, qkv_weight, qkv_bias, out_weight, out_bias,
    up_weight, up_bias, down_weight, down_bias,
):
    w = lax.axis_index("wide")
    n = lax.axis_index("narrow")
    local, width = tokens.shape[1:]
    row_len = seg_ids.shape[1]
    depth, cols = width // wide, width // narrow
    hidden_own = up_weight.shape[-1] // wide // narrow
    hidden = wide * hidden_own
    tiles = ada_weight.shape[-1] // LANES
    mod_cols = LANES * -(-tiles // narrow)

    inputs = dict(
        tok=tokens[0], cond=cond[0], cond_index=cond_index.reshape(SEGS, 1), seg_row=seg_ids,
        cot=cotangent[0], ada_b=ada_bias, qkv_b=qkv_bias, out_b=out_bias, up_b=up_bias, down_b=down_bias,
        ada=ada_weight, qkv_w=qkv_weight, out_w=out_weight, up_w=up_weight, down_w=down_weight,
    )
    in_hbm = ("ada", "qkv_w", "out_w", "up_w", "down_w")
    shape = jax.ShapeDtypeStruct
    outputs = dict(
        mixed_o=shape((local, width), BF16), token_o=shape((local, width), F32),
        qkv_o=shape((LAYERS, narrow, depth, 3 * cols), BF16),
        out_o=shape((LAYERS, depth, width), BF16),
        up_o=shape((LAYERS, narrow, depth, hidden), BF16),
        down_o=shape((LAYERS, narrow, hidden_own, width), BF16),
        bias_o=shape((narrow, 4 * LAYERS, width), F32),
        mod_o=shape((narrow, wide * LAYERS * SEGS, mod_cols), BF16),
        lead_o=shape((LAYERS, depth, wide * LAYERS * SEGS), BF16),
        lead_g=shape((narrow, wide, SEGS, depth), F32),
        qkv_h=shape((LAYERS, width, 3 * cols), BF16), out_h=shape((LAYERS, cols, width), BF16),
        up_h=shape((LAYERS, width, hidden), BF16), down_h=shape((LAYERS, hidden, width), BF16),
    )
    out_vmem = ("mixed_o", "token_o", "lead_o")
    vmem, dma = pltpu.VMEM, pltpu.SemaphoreType.DMA
    heads = cols // HEAD
    scratch = dict(
        qkv_v=vmem((width, 3 * cols), BF16), out_v=vmem((cols, width), BF16),
        up_v=vmem((width, hidden), BF16), down_v=vmem((hidden, width), BF16),
        hid_attn=vmem((LAYERS, row_len, width), BF16), hid_mlp=vmem((LAYERS, row_len, width), BF16),
        heads=vmem((LAYERS, 3 * heads, row_len, LANES), BF16),
        mixed=vmem((LAYERS, row_len, cols), BF16), log_sum=vmem((LAYERS, row_len, heads), F32),
        up=vmem((LAYERS, row_len, hidden), BF16), act=vmem((LAYERS, row_len, hidden), BF16),
        state=vmem((local, width), F32), middle=vmem((LAYERS, local, width), F32),
        branch=vmem((LAYERS, local, width), BF16), down=vmem((LAYERS, local, width), BF16),
        grad_hid=vmem((local, width), F32),
        grad_down=vmem((row_len, width), BF16), grad_branch=vmem((row_len, width), BF16),
        grad_up=vmem((row_len, hidden), BF16), grad_qkv=vmem((row_len, 3 * cols), BF16),
        grad_heads=vmem((heads, row_len, LANES), BF16),
        key_sum=vmem((row_len, LANES), F32), value_sum=vmem((row_len, LANES), F32),
        part=vmem((2, 2 * local, width), F32),
        core_tx=vmem((2, local, width), BF16), core_rx=vmem((2, local, width), BF16),
        side_tx=vmem((local, width), BF16), side_rx=vmem((local, width), BF16),
        ada_v=vmem((LAYERS, depth, mod_cols), BF16),
        lead=vmem((wide, 16, depth), BF16), lead_rx=vmem((wide, 16, depth), BF16),
        bias_tx=vmem((8, 7 * LANES), F32), bias_rx=vmem((wide, 8, 7 * LANES), F32),
        ada_full=vmem((1, LAYERS, tiles * LANES), F32), qkv_full=vmem((1, LAYERS, 3 * width), F32),
        out_full=vmem((1, LAYERS, width), F32), up_full=vmem((1, LAYERS, narrow * hidden), F32),
        down_full=vmem((1, LAYERS, width), F32), seg_col=vmem((row_len, 1), jnp.int32),
        qkv_raw=vmem((LAYERS, 3, depth, 3 * LANES), BF16), up_raw=vmem((LAYERS, wide, depth, 2 * LANES), BF16),
        qkv_s=vmem((LAYERS, depth, 3 * cols), BF16), up_s=vmem((LAYERS, depth, hidden), BF16),
        lead_t=vmem((LAYERS, wide * LAYERS * SEGS, depth), F32),
        lead_tx=vmem((wide, SEGS, depth), F32), lead_back=vmem((wide, SEGS, depth), F32),
        bias_sum=vmem((4 * LAYERS, width), F32),
        mod_tx=vmem((wide, LAYERS * SEGS, mod_cols), F32), mod_rx=vmem((wide, LAYERS * SEGS, mod_cols), F32),
        mod_q=vmem((narrow, LAYERS * SEGS, mod_cols), F32),
        mods=vmem((LAYERS * SEGS, tiles * LANES), F32),
        mod_grad=vmem((LAYERS * SEGS, tiles * LANES), F32),
        quarter_rx=vmem((3, LAYERS * SEGS, mod_cols), F32),
        quarter_sum=vmem((LAYERS * SEGS, mod_cols), F32),
        quarter_all=vmem((wide, LAYERS * SEGS, mod_cols), F32),
        mod_all=vmem((wide * LAYERS * SEGS, mod_cols), BF16),
        bias_grad=vmem((4 * LAYERS, width), F32), bias_all=vmem((wide, 4 * LAYERS, width), F32),
        bias_row=vmem((4 * LAYERS, width), F32),
        qkv_d=vmem((width, 3 * cols), BF16), out_d=vmem((cols, width), BF16),
        up_d=vmem((width, hidden), BF16), down_d=vmem((hidden, width), BF16),
        qkv_xr=vmem((PLANES, depth, 3 * cols), BF16), out_xr=vmem((1, depth, width), BF16),
        up_xr=vmem((PLANES, depth, hidden), BF16), down_xr=vmem((PLANES, hidden_own, width), BF16),
        qkv_zr=vmem((PLANES - 1, depth, 3 * cols), BF16), out_zr=vmem((PLANES - 1, depth, width), BF16),
        up_zr=vmem((PLANES - 1, depth, hidden), BF16), down_zr=vmem((PLANES - 1, hidden_own, width), BF16),
        qkv_f=vmem((depth, 3 * cols), BF16), out_f=vmem((depth, width), BF16),
        up_f=vmem((depth, hidden), BF16), down_f=vmem((hidden_own, width), BF16),
        wz_s=dma((8, 5)), wz_r=dma((8, 4)), wx_s=dma((8, 4)), wx_r=dma((8, 4)), w_own=dma((8,)),
        load_sem=dma((4,)), tok_s=dma((6,)), tok_r=dma((6,)), sum_s=dma((4,)), sum_r=dma((4,)),
        lead_sem_s=dma((wide - 1,)), lead_sem_r=dma((wide - 1,)),
        bias_sem_s=dma((wide - 1,)), bias_sem_r=dma((wide - 1,)),
        mod_sem_s=dma((wide - 1,)), mod_sem_r=dma((wide - 1,)),
        quarter_s=dma((3,)), quarter_r=dma((3,)), ada_sem=dma, raw_sem=dma((LAYERS, 3 + wide)), lead_own_sem=dma,
        lead_back_s=dma((wide - 1,)), lead_back_r=dma((wide - 1,)),
        lead_narrow_s=dma((3,)), lead_narrow_r=dma((3,)),
        dx_s=dma((4, 4)), dx_r=dma((4, 4)), dz_s=dma((4, 3)), dz_r=dma((4, 3)),
        spread_s=dma((8, 3)), spread_r=dma((8, 3)), spread_l=dma((8,)),
        back_s=dma((3,)), back_r=dma((3,)),
        wide_s=dma((wide - 1,)), wide_r=dma((wide - 1,)),
        bias_wide_s=dma((wide - 1,)), bias_wide_r=dma((wide - 1,)),
        bias_narrow_s=dma((3,)), bias_narrow_r=dma((3,)),
        mod_narrow_s=dma((3,)), mod_narrow_r=dma((3,)), mod_own_sem=dma, bias_own_sem=dma,
        credit_x=pltpu.SemaphoreType.REGULAR((4,)), credit_z=pltpu.SemaphoreType.REGULAR((4,)),
    )
    cfg = SimpleNamespace(
        names=[*inputs, *outputs, *scratch], wide=wide, narrow=narrow, width=width, depth=depth,
        local=local, cols=cols, mod_cols=mod_cols, tiles=tiles,
    )

    def place(name, vmem_ok):
        return pl.BlockSpec(memory_space=pltpu.VMEM if vmem_ok else pl.ANY)

    results = pl.pallas_call(
        partial(block_kernel, cfg),
        out_shape=list(outputs.values()),
        in_specs=[place(name, name not in in_hbm) for name in inputs],
        out_specs=[place(name, name in out_vmem) for name in outputs],
        scratch_shapes=list(scratch.values()),
        compiler_params=pltpu.CompilerParams(
            collective_id=0, has_side_effects=True, vmem_limit_bytes=63 * 2**20
        ),
    )(*inputs.values())
    got = dict(zip(outputs, results))

    return finish(wide, narrow, got, cond[0], inputs["cond_index"], tiles, mod_cols, w)


def solution(mesh):
    matrix, vector = P(None, "wide", None), P(None, "wide")
    rows, cond_rows = P("wide", "narrow", None), P("wide", None, None)
    wide, narrow = mesh.shape["wide"], mesh.shape["narrow"]
    fused = wide == PLANES * PAIR and narrow == PLANES
    return jax.shard_map(
        partial(fused_device if fused else plain_device, wide, narrow),
        mesh=mesh,
        in_specs=(rows, cond_rows, P("wide", None), P("wide", None), rows) + (matrix, vector) * 5,
        out_specs=(rows, rows, cond_rows) + (matrix, vector) * 5,
        check_vma=False,
    )
```

```python
from functools import partial
import math
from types import SimpleNamespace

import jax
import jax.numpy as jnp
from jax import lax
from jax.experimental import pallas as pl
from jax.experimental.pallas import tpu as pltpu
from jax.sharding import PartitionSpec as P

HEADS = 16
HEAD = 72
LAYERS = 2
SEGS = 4
EPS = 1e-06
EXACT = lax.Precision.HIGHEST
F32 = jnp.float32
BF16 = jnp.bfloat16


def dot(left, right, dims):
    return lax.dot_general(left, right, (dims, ((), ())), preferred_element_type=F32)


def norm(values):
    centred = values - jnp.mean(values, -1, keepdims=True)
    inv = lax.rsqrt(jnp.mean(centred * centred, -1, keepdims=True) + EPS)
    return centred * inv, inv


def norm_back(grad, unit, inv):
    return inv * (
        grad
        - jnp.mean(grad, -1, keepdims=True)
        - unit * jnp.mean(grad * unit, -1, keepdims=True)
    )


def gather_tokens(values):
    return lax.all_gather(values, "narrow", axis=0, tiled=True)


def scatter_tokens(values):
    return lax.psum_scatter(
        values.astype(BF16), "narrow", scatter_dimension=0, tiled=True
    ).astype(F32)


def gelu(values):
    return jax.nn.gelu(values, approximate=True)


def layer_forward(state, mods, same_seg, weights):
    qkv_w, qkv_b, out_w, out_b, up_w, up_b, down_w, down_b = weights
    shift_attn, scale_attn, gate_attn, shift_mlp, scale_mlp, gate_mlp = mods
    own_heads = out_w.shape[0] // HEAD
    unit_attn, inv_attn = norm(state)
    hidden_attn = gather_tokens((unit_attn * (1.0 + scale_attn) + shift_attn).astype(BF16))
    full_len = hidden_attn.shape[0]
    qkv = (dot(hidden_attn, qkv_w, ((1,), (0,))) + qkv_b).astype(BF16)
    queries, keys, values = [
        part.reshape(full_len, own_heads, HEAD) for part in jnp.split(qkv, 3, axis=-1)
    ]
    scores = jnp.einsum("qhe,khe->hqk", queries, keys, preferred_element_type=F32) * (
        1.0 / math.sqrt(HEAD)
    )
    probs = jax.nn.softmax(jnp.where(same_seg[None], scores, -1e30), axis=-1)
    mixed = jnp.einsum("hqk,khe->qhe", probs.astype(BF16), values, preferred_element_type=F32)
    mixed = mixed.reshape(full_len, own_heads * HEAD).astype(BF16)
    branch = scatter_tokens(dot(mixed, out_w, ((1,), (0,)))) + out_b
    middle = state + gate_attn * branch
    unit_mlp, inv_mlp = norm(middle)
    hidden_mlp = gather_tokens((unit_mlp * (1.0 + scale_mlp) + shift_mlp).astype(BF16))
    up_proj = dot(hidden_mlp, up_w, ((1,), (0,))) + up_b
    activated = gelu(up_proj).astype(BF16)
    down_proj = scatter_tokens(dot(activated, down_w, ((1,), (0,)))) + down_b
    result = middle + gate_mlp * down_proj
    kept = (
        unit_attn, inv_attn, hidden_attn, queries, keys, values, probs, mixed, branch,
        unit_mlp, inv_mlp, hidden_mlp, up_proj, activated, down_proj,
    )
    return result, kept


def layer_backward(grad_out, kept, mods, weights):
    qkv_w, qkv_b, out_w, out_b, up_w, up_b, down_w, down_b = weights
    shift_attn, scale_attn, gate_attn, shift_mlp, scale_mlp, gate_mlp = mods
    (
        unit_attn, inv_attn, hidden_attn, queries, keys, values, probs, mixed, branch,
        unit_mlp, inv_mlp, hidden_mlp, up_proj, activated, down_proj,
    ) = kept
    scale_inv = 1.0 / math.sqrt(HEAD)
    full_len = hidden_attn.shape[0]
    own_down = (gate_mlp * grad_out).astype(BF16)
    grad_gate_mlp = down_proj * grad_out
    grad_down = gather_tokens(own_down)
    grad_act = dot(grad_down, down_w, ((1,), (1,)))
    grad_up = jax.vjp(gelu, up_proj)[1](grad_act)[0].astype(BF16)
    grad_hidden_mlp = scatter_tokens(dot(grad_up, up_w, ((1,), (1,))))
    grad_down_w = dot(activated, grad_down, ((0,), (0,)))
    grad_up_w = dot(hidden_mlp, grad_up, ((0,), (0,)))
    grad_middle = grad_out + norm_back(grad_hidden_mlp * (1.0 + scale_mlp), unit_mlp, inv_mlp)
    own_branch = (gate_attn * grad_middle).astype(BF16)
    grad_gate_attn = branch * grad_middle
    grad_branch = gather_tokens(own_branch)
    grad_attn = dot(grad_branch, out_w, ((1,), (1,))).astype(BF16).reshape(queries.shape)
    grad_probs = jnp.einsum("qhe,khe->hqk", grad_attn, values, preferred_element_type=F32)
    grad_scores = probs * (grad_probs - jnp.sum(probs * grad_probs, -1, keepdims=True))
    grad_scores = grad_scores.astype(BF16)
    grad_q = jnp.einsum("hqk,khe->qhe", grad_scores, keys, preferred_element_type=F32) * scale_inv
    grad_k = jnp.einsum("hqk,qhe->khe", grad_scores, queries, preferred_element_type=F32) * scale_inv
    grad_v = jnp.einsum("hqk,qhe->khe", probs.astype(BF16), grad_attn, preferred_element_type=F32)
    grad_qkv = jnp.concatenate(
        [part.astype(BF16).reshape(full_len, -1) for part in (grad_q, grad_k, grad_v)], axis=-1
    )
    grad_hidden_attn = scatter_tokens(dot(grad_qkv, qkv_w, ((1,), (1,))))
    grad_out_w = dot(mixed, grad_branch, ((0,), (0,)))
    grad_qkv_w = dot(hidden_attn, grad_qkv, ((0,), (0,)))
    grad_state = grad_middle + norm_back(grad_hidden_attn * (1.0 + scale_attn), unit_attn, inv_attn)
    token_mod = jnp.concatenate(
        [
            grad_hidden_attn, grad_hidden_attn * unit_attn, grad_gate_attn,
            grad_hidden_mlp, grad_hidden_mlp * unit_mlp, grad_gate_mlp,
        ],
        axis=-1,
    )
    bias_grads = (
        jnp.sum(grad_qkv.astype(F32), 0),
        jnp.sum(own_branch.astype(F32), 0),
        jnp.sum(grad_up.astype(F32), 0),
        jnp.sum(own_down.astype(F32), 0),
    )
    return grad_state, token_mod, (grad_qkv_w, grad_out_w, grad_up_w, grad_down_w), bias_grads


def plain_device(
    wide, narrow,
    tokens, cond, seg_ids, cond_index, cotangent,
    ada_weight, ada_bias, qkv_weight, qkv_bias, out_weight, out_bias,
    up_weight, up_bias, down_weight, down_bias,
):
    w = lax.axis_index("wide")
    n = lax.axis_index("narrow")
    local_len, width = tokens.shape[1:]
    depth = width // wide
    cols = width // narrow
    hidden_own = up_weight.shape[-1] // wide // narrow
    mod_cols = ada_weight.shape[-1] // narrow

    def own(values, axis):
        return lax.dynamic_index_in_dim(values, n, axis, keepdims=False)

    bias_parts = (ada_bias, qkv_bias, out_bias, up_bias, down_bias)
    sizes = [part.shape[1] for part in bias_parts]
    packed = lax.all_gather(jnp.concatenate(bias_parts, axis=1), "wide", axis=1, tiled=False)
    biases = []
    at = 0
    for size in sizes:
        biases.append(packed[:, :, at : at + size].reshape(LAYERS, -1).astype(F32))
        at += size
    ada_b, qkv_b, out_b, up_b, down_b = biases
    qkv_b = own(qkv_b.reshape(LAYERS, 3, narrow, cols), 2).reshape(LAYERS, 3 * cols)
    up_b = own(up_b.reshape(LAYERS, wide, narrow, hidden_own), 2).reshape(LAYERS, -1)

    cond_hot = (cond_index[0, :, None] == jnp.arange(SEGS, dtype=jnp.int32)[None, :]).astype(F32)
    chosen = jnp.dot(cond_hot, cond[0].astype(F32), precision=EXACT)
    lead = (chosen * jax.nn.sigmoid(chosen)).astype(BF16)
    lead_all = lax.all_gather(lead, "wide", axis=0, tiled=True)
    lead_own = lax.dynamic_slice_in_dim(lead_all, w * depth, depth, 1)
    ada_quarter = lax.dynamic_slice_in_dim(ada_weight, n * mod_cols, mod_cols, 2)
    mod_part = jnp.einsum("nd,lde->nle", lead_own, ada_quarter, preferred_element_type=F32)
    mod_part = lax.psum_scatter(mod_part, "wide", scatter_dimension=0, tiled=True)
    modulation = lax.all_gather(mod_part, "narrow", axis=2, tiled=True)
    modulation = modulation.transpose(1, 0, 2) + ada_b[:, None, :]

    seg_row = seg_ids[0]
    seg_query = lax.dynamic_slice_in_dim(seg_row, n * local_len, local_len, 0)
    token_hot = (seg_query[:, None] == jnp.arange(SEGS, dtype=jnp.int32)[None, :]).astype(F32)
    same_seg = seg_row[:, None] == seg_row[None, :]

    qkv_own = own(qkv_weight.reshape(LAYERS, depth, 3, narrow, cols), 3).reshape(LAYERS, depth, 3 * cols)
    up_own = own(up_weight.reshape(LAYERS, depth, wide, narrow, hidden_own), 3).reshape(LAYERS, depth, -1)
    down_own = own(down_weight.reshape(LAYERS, narrow, hidden_own, width), 1)

    def fetch(idx):
        out_full = lax.all_gather(out_weight[idx], "wide", axis=0, tiled=True)
        return (
            lax.all_gather(qkv_own[idx], "wide", axis=0, tiled=True),
            qkv_b[idx],
            lax.dynamic_slice_in_dim(out_full, n * cols, cols, 0),
            out_b[idx],
            lax.all_gather(up_own[idx], "wide", axis=0, tiled=True),
            up_b[idx],
            lax.all_gather(down_own[idx], "wide", axis=0, tiled=True),
            down_b[idx],
        )

    state = tokens[0].astype(F32)
    weights, mods, kept = [], [], []
    for idx in range(LAYERS):
        weights.append(fetch(idx))
        per_token = jnp.dot(token_hot, modulation[idx], precision=EXACT)
        mods.append(jnp.split(per_token, 6, axis=-1))
        state, saved = layer_forward(state, mods[idx], same_seg, weights[idx])
        kept.append(saved)
    result = state.astype(BF16)

    grad_state = cotangent[0].astype(F32)
    token_hot_t = token_hot.T
    reduced, bias_sums, mod_grads = [None] * LAYERS, [None] * LAYERS, [None] * LAYERS
    for idx in reversed(range(LAYERS)):
        grad_state, token_mod, grads, bias_grads = layer_backward(
            grad_state, kept[idx], mods[idx], weights[idx]
        )
        mod_grads[idx] = jnp.dot(token_hot_t, token_mod, precision=EXACT)
        qkv_g, out_g, up_g, down_g = [item.astype(BF16) for item in grads]
        qkv_g, up_g, down_g = [
            lax.psum_scatter(item, "wide", scatter_dimension=0, tiled=True)
            for item in (qkv_g, up_g, down_g)
        ]
        out_g = lax.psum(out_g, "wide")
        qkv_g = lax.all_gather(qkv_g.reshape(depth, 3, 1, cols), "narrow", axis=2, tiled=True)
        up_g = lax.all_gather(up_g.reshape(depth, wide, 1, hidden_own), "narrow", axis=2, tiled=True)
        down_g = lax.all_gather(down_g, "narrow", axis=0, tiled=True)
        out_g = lax.all_gather(out_g, "narrow", axis=0, tiled=True)
        out_g = lax.dynamic_slice_in_dim(out_g, w * depth, depth, 0)
        reduced[idx] = (
            qkv_g.reshape(depth, 3 * width),
            out_g,
            up_g.reshape(depth, -1),
            down_g,
        )
        spot = lax.broadcasted_iota(jnp.int32, (1, narrow, 1), 1) == n
        qkv_s = jnp.where(spot, bias_grads[0].reshape(3, 1, cols), 0.0).reshape(-1)
        up_s = jnp.where(spot, bias_grads[2].reshape(wide, 1, hidden_own), 0.0).reshape(-1)
        bias_sums[idx] = [
            item.reshape(wide, -1) for item in (qkv_s, bias_grads[1], up_s, bias_grads[3])
        ]
    sizes = [item.shape[1] for item in bias_sums[0]]
    bias_sum = jnp.stack([jnp.concatenate(item, axis=1) for item in bias_sums], axis=1)
    bias_sum = lax.psum_scatter(lax.psum(bias_sum, "narrow"), "wide", scatter_dimension=0, tiled=True)[0]
    bias_out = []
    at = 0
    for size in sizes:
        bias_out.append(bias_sum[:, at : at + size])
        at += size

    mod_grad = lax.psum(jnp.stack(mod_grads), "narrow").astype(BF16)
    mod_all = lax.all_gather(mod_grad, "wide", axis=1, tiled=True)
    ada_grad = jnp.einsum("nd,lne->lde", lead_own, mod_all, preferred_element_type=F32)
    ada_size = ada_bias.shape[1]
    ada_bias_grad = jnp.sum(
        lax.dynamic_slice_in_dim(mod_all, w * ada_size, ada_size, 2).astype(F32), axis=1
    )
    lead_grad = jnp.einsum("lne,lde->nd", mod_all, ada_weight, preferred_element_type=F32)
    lead_grad = lax.all_to_all(lead_grad.reshape(wide, SEGS, depth), "wide", 0, 0, tiled=False)
    lead_grad = lead_grad.transpose(1, 0, 2).reshape(SEGS, width)
    gate = jax.nn.sigmoid(chosen)
    chosen_grad = lead_grad * (gate * (1.0 + chosen * (1.0 - gate)))
    cond_grad = jnp.dot(cond_hot.T, chosen_grad, precision=EXACT)

    stacked = [
        jnp.stack([reduced[idx][pos].astype(F32) for idx in range(LAYERS)]) for pos in range(4)
    ]
    return (
        result[None], grad_state[None], cond_grad[None],
        ada_grad, ada_bias_grad,
        stacked[0], bias_out[0], stacked[1], bias_out[1],
        stacked[2], bias_out[2], stacked[3], bias_out[3],
    )


QKV, OUT, UP, DOWN = range(4)
PLANES = 4
PAIR = 2
LANES = 128
STEP = 32
MESH = pl.DeviceIdType.MESH


def mod_start(tiles, parts, part):
    return tiles * part // parts


def block_kernel(cfg, *refs):
    r = SimpleNamespace(**dict(zip(cfg.names, refs)))
    wide, narrow, width, depth = cfg.wide, cfg.narrow, cfg.width, cfg.depth
    local, cols, mod_cols, tiles = cfg.local, cfg.cols, cfg.mod_cols, cfg.tiles
    half = local // 2
    own_heads = cols // HEAD
    scale_inv = 1.0 / math.sqrt(HEAD)
    w = lax.axis_index("wide")
    n = lax.axis_index("narrow")
    z, x = w // PAIR, w % PAIR
    y, c = n // 2, n % 2
    n_core = n + 1 - 2 * c
    n_side = n + 2 - 4 * y
    n_far = 3 - n
    core, side, far = (w, n_core), (w, n_side), (w, n_far)
    beside = (w + 1 - 2 * x, n)

    z_half = z // 2
    z_partner, z_inner, z_outer = z + 1 - 2 * (z % 2), 2 - z_half, 3 - 3 * z_half
    is_inner = jnp.logical_or(z == 1, z == 2)

    def at_plane(idx):
        return (idx * PAIR + x, n)

    def wide_peer(j):
        return ((w + j) % wide, n)

    def remote(src, dst, sems, device):
        return pltpu.make_async_remote_copy(
            src_ref=src, dst_ref=dst, send_sem=sems[0], recv_sem=sems[1],
            device_id=device, device_id_type=MESH,
        )

    def span(start, size, step=16):
        return pl.ds(pl.multiple_of(start, step), size)

    ada_load = pltpu.make_async_copy(
        r.ada.at[:, :, span(LANES * mod_start(tiles, narrow, n), mod_cols, LANES)], r.ada_v, r.ada_sem
    )
    hidden_own = r.up_w.shape[-1] // wide // narrow

    def windows(which):
        if which == QKV:
            return [(width * j + cols * n, cols, 3 * LANES) for j in range(3)]
        return [((j * narrow + n) * hidden_own, hidden_own, 2 * LANES) for j in range(wide)]

    def raw(which, layer, k):
        src, dst = ((r.qkv_w, r.qkv_raw), (r.up_w, r.up_raw))[which == UP]
        start, _, window = windows(which)[k]
        at = span(LANES * (start // LANES), window, LANES)
        return pltpu.make_async_copy(
            src.at[layer, :, at], dst.at[layer, k], r.raw_sem.at[layer, k + 3 * (which == UP)]
        )

    for layer in range(LAYERS):
        for which in (QKV, UP):
            for k in range(len(windows(which))):
                raw(which, layer, k).start()
        if layer == 0:
            ada_load.start()
    chosen = chosen_of(r.cond, r.cond_index)
    lead = (chosen * jax.nn.sigmoid(chosen)).astype(BF16).astype(F32)
    r.lead[...] = jnp.zeros_like(r.lead)
    for row in range(wide):
        tile = jnp.concatenate(
            [lead[:, depth * row : depth * (row + 1)], jnp.zeros((16 - SEGS, depth), F32)], 0
        )
        r.lead[row] = tile.astype(BF16)
    bias_refs = (r.ada_b, r.qkv_b, r.out_b, r.up_b, r.down_b)
    bias_places, row = [], 0
    for k, ref in enumerate(bias_refs):
        for start in range(0, ref.shape[1], 3 * LANES):
            size = min(3 * LANES, ref.shape[1] - start)
            bias_places.append((k, row, start, size))
            row += 1
    r.bias_rows[...] = jnp.zeros_like(r.bias_rows)
    for layer in range(LAYERS):
        for k, row, start, size in bias_places:
            line = r.bias_rows.shape[0] // LAYERS * layer + row
            values = bias_refs[k][...].astype(F32)[layer : layer + 1, start : start + size]
            r.bias_rows[line : line + 1, :size] = values
    r.bias_tx[...] = r.bias_rows[...].astype(BF16)

    barrier = pltpu.get_barrier_semaphore()
    partners = [core, side, far] + [wide_peer(j) for j in range(1, wide)]
    for partner in partners:
        pl.semaphore_signal(barrier, inc=1, device_id=partner, device_id_type=MESH)
    pl.semaphore_wait(barrier, len(partners))

    full = (r.qkv_h, r.out_h, r.up_h, r.down_h)
    loaded = (r.qkv_v, r.out_v, r.up_v, r.down_v)

    def shard(which, layer):
        if which == DOWN:
            return r.down_w.at[layer, span(depth * n, depth)]
        return (r.qkv_s, r.out_w, r.up_s)[which].at[layer]

    def w_rows(which, plane_idx, col):
        if which == OUT:
            return span(col * depth, depth)
        return span((plane_idx * PAIR + col) * depth, depth)

    def w_block(which, layer, plane_idx, col):
        return full[which].at[layer, w_rows(which, plane_idx, col)]

    def w_z(which, layer, kind, plane_idx, own=False):
        slot = layer * 4 + which
        block = w_block(which, layer, plane_idx, x)
        return remote(
            shard(which, layer) if own else block, block,
            (r.wz_s.at[slot, kind], r.wz_r.at[slot, plane_idx]),
            at_plane(z_inner if kind == 1 else z_partner),
        )

    def w_x(which, layer, plane_idx, col, own=False):
        slot = layer * 4 + which
        block = w_block(which, layer, plane_idx, col)
        return remote(
            shard(which, layer) if own else block, block,
            (r.wx_s.at[slot, plane_idx], r.wx_r.at[slot, plane_idx]), beside,
        )

    def w_own(which, layer):
        return pltpu.make_async_copy(
            shard(which, layer), w_block(which, layer, z, x), r.w_own.at[layer * 4 + which]
        )

    def weights_start(which, layer):
        def go():
            w_z(which, layer, 1, z, True).start()
            w_z(which, layer, 0, z, True).start()
            w_x(which, layer, z, x, True).start()
            w_own(which, layer).start()

        if which == OUT:
            pl.when(z == n)(go)
        else:
            go()

    passes_out = jnp.logical_and(is_inner, z_half != n // 2)

    def weights_steps(which, layer):
        def passed(plane_idx, kind):
            w_z(which, layer, 0, plane_idx).wait_recv()
            if kind:
                onward = passes_out if which == OUT else is_inner
                pl.when(onward)(lambda: w_z(which, layer, kind, plane_idx).start())
            w_x(which, layer, plane_idx, x).start()

        def step(plane_idx, kind):
            passed(plane_idx, kind)
            slot = layer * 4 + which + 2
            if kind == 2 and 2 < slot < 4 * LAYERS:
                weights_start(slot % 4, slot // 4)

        def only():
            pl.when(z != n)(lambda: passed(n, 2))
            slot = layer * 4 + which + 2
            weights_start(slot % 4, slot // 4)

        if which == OUT:
            return [only]
        return [
            partial(step, idx, kind) for idx, kind in ((z_partner, 0), (z_inner, 2), (z_outer, 3))
        ]

    steps = [
        (layer * 4 + which, step)
        for layer in range(LAYERS)
        for which in (QKV, OUT, UP, DOWN)
        for step in weights_steps(which, layer)
    ]

    def pump(count):
        for _ in range(min(count, len(steps))):
            steps.pop(0)[1]()

    def pump_through(which, layer):
        while steps and steps[0][0] <= layer * 4 + which:
            pump(1)

    def weights_finish(which, layer):
        if which == OUT:
            w_x(which, layer, n, 1 - x).wait_recv()
            pl.when(z == n)(lambda: w_own(which, layer).wait())
        else:
            for idx in range(PLANES):
                w_x(which, layer, idx, 1 - x).wait_recv()
            w_own(which, layer).wait()

    def weights_drain(which, layer):
        def own():
            for kind in range(2):
                w_z(which, layer, kind, z, True).wait_send()

        if which == OUT:
            w_x(which, layer, n, x).wait_send()
            pl.when(z == n)(own)
            pl.when(passes_out)(lambda: w_z(which, layer, 2, n).wait_send())
        else:
            own()
            for idx in range(PLANES):
                w_x(which, layer, idx, x).wait_send()

            @pl.when(is_inner)
            def _():
                w_z(which, layer, 2, z_inner).wait_send()
                w_z(which, layer, 3, z_outer).wait_send()

    def load(which, layer):
        return pltpu.make_async_copy(full[which].at[layer], loaded[which], r.load_sem.at[which])

    def weights_ready(which, layer):
        pump_through(which, layer)
        weights_finish(which, layer)
        load(which, layer).start()
        load(which, layer).wait()

    def tok_rows(chunk, part):
        return span(local * chunk + half * part, half)

    def tok_copy(ref, kind, part, incoming=False, early=False):
        chunk = ((n_core, n_side, n_far) if incoming else (n, n, n_side))[kind]
        rows = ref.at[tok_rows(chunk, part)]
        k = 2 * kind + part + 6 * early
        return remote(rows, rows, (r.tok_s.at[k], r.tok_r.at[k]), side if kind == 1 else core)

    def tok_send(ref, part, early=False):
        tok_copy(ref, 1, part, early=early).start()
        tok_copy(ref, 0, part, early=early).start()

    def tok_own(ref, early=False):
        for part in range(2):
            tok_copy(ref, 0, part, True, early).wait_recv()

    def tok_other(ref, early=False):
        for part in range(2):
            tok_copy(ref, 1, part, True, early).wait_recv()
            tok_copy(ref, 2, part, early=early).start()
        for part in range(2):
            tok_copy(ref, 2, part, True, early).wait_recv()

    def tok_drain(ref, early=False):
        for kind in range(3):
            for part in range(2):
                tok_copy(ref, kind, part, early=early).wait_send()

    def block_rows(block):
        return span(2 * local * (y if block else 1 - y), 2 * local)

    def sum_core(block):
        return remote(
            r.core_tx.at[block], r.core_rx.at[block], (r.sum_s.at[block], r.sum_r.at[block]), core
        )

    def sum_side(part):
        rows = span(half * part, half)
        return remote(
            r.side_tx.at[rows], r.side_rx.at[rows], (r.sum_s.at[2 + part], r.sum_r.at[2 + part]), side
        )

    def sum_block(block):
        r.core_tx[block] = r.part[block, span(local * (1 - c), local), :].astype(BF16)
        sum_core(block).start()

    def sum_cross():
        sum_core(0).wait_recv()
        for part in range(2):
            rows = span(half * part, half)
            mine = r.part[0, span(local * c + half * part, half), :]
            r.side_tx[rows, :] = (mine + r.core_rx[0, rows, :].astype(F32)).astype(BF16)
            sum_side(part).start()

    def sum_wait(part):
        if part == 0:
            sum_core(1).wait_recv()
        sum_side(part).wait_recv()
        if part == 1:
            for block in range(2):
                sum_core(block).wait_send()
                sum_side(block).wait_send()

    def sum_take(start):
        rows = span(start, STEP)
        return (
            r.part[1, span(local * c + start, STEP), :]
            + r.core_rx[1, rows, :].astype(F32)
            + r.side_rx[rows, :].astype(F32)
        )

    def each_step(part, body):
        @pl.loop(0, half // STEP)
        def _(i):
            body(half * part + STEP * i)

    def seg_of(start):
        return r.seg_col[span(local * n + start, STEP), :]

    def mod(layer, block, seg):
        rows = r.mods[SEGS * layer : SEGS * layer + SEGS, width * block : width * (block + 1)]
        out = rows[SEGS - 1 : SEGS]
        for s in range(SEGS - 1):
            out = jnp.where(seg == s, rows[s : s + 1], out)
        return out

    def mod_sum(layer, block, seg, values):
        sums = [jnp.sum(jnp.where(seg == s, values, 0.0), 0, keepdims=True) for s in range(SEGS)]
        at = (slice(SEGS * layer, SEGS * layer + SEGS), slice(width * block, width * (block + 1)))
        r.mod_grad[at] += jnp.concatenate(sums, 0)

    seg_cols = jnp.transpose(jnp.broadcast_to(r.seg_row[...].astype(F32), (8, narrow * local)))
    r.seg_col[...] = seg_cols[:, :1].astype(jnp.int32)

    def shifted(values, rest, size):
        window = values.shape[1]
        return pltpu.roll(values.astype(F32), (window - rest) % window, 1)[:, :size]

    def pick(ref, start, size, window):
        return shifted(ref[0, :, span(LANES * (start // LANES), window, LANES)], start % LANES, size)

    def pack(dst, pieces):
        at = 0
        for piece in pieces:
            size = piece.shape[1]
            dst[..., at : at + size] = piece.astype(dst.dtype)
            at += size

    def pack_shard(which, layer):
        dst, pieces = (r.qkv_s if which == QKV else r.up_s).at[layer], []
        for k, (start, size, _) in enumerate(windows(which)):
            raw(which, layer, k).wait()
            buffer = r.qkv_raw if which == QKV else r.up_raw
            pieces.append(shifted(buffer[layer, k], start % LANES, size))
        pack(dst, pieces)

    def folded(values, size):
        rest = values[:, size:]
        if rest.shape[1] < size:
            rest = jnp.concatenate([rest, jnp.zeros((8, size - rest.shape[1]), F32)], 1)
        return jnp.concatenate([values[:, :size], rest], 0).astype(BF16)

    def unfolded(values, size):
        values = values.astype(F32)
        return jnp.concatenate([values[:8], values[8:]], 1)[:, :size]

    def lead_copy(j, incoming=False):
        return remote(
            r.lead.at[(w + j) % wide], r.lead_rx.at[(w - j + wide) % wide if incoming else w],
            (r.lead_sem_s.at[j - 1], r.lead_sem_r.at[j - 1]), wide_peer(j),
        )

    def bias_copy(j, incoming=False):
        return remote(
            r.bias_tx, r.bias_rx.at[(w - j + wide) % wide if incoming else w],
            (r.bias_sem_s.at[j - 1], r.bias_sem_r.at[j - 1]), wide_peer(j),
        )

    def mod_copy(j, incoming=False):
        return remote(
            r.mod_part.at[(w + j) % wide], r.mod_rx.at[(w - j + wide) % wide if incoming else w],
            (r.mod_sem_s.at[j - 1], r.mod_sem_r.at[j - 1]), wide_peer(j),
        )

    def wait_all(copy, count=wide):
        for j in range(1, count):
            copy(j, True).wait_recv()

    narrow_peers = ((core, n_core), (side, n_side), (far, n_far))

    def quarter_copy(k, incoming=False):
        device, idx = narrow_peers[k]
        return remote(
            r.mod_q.at[n], r.mod_q.at[idx if incoming else n],
            (r.quarter_s.at[k], r.quarter_r.at[k]), device,
        )

    for j in range(1, wide):
        lead_copy(j).start()
    for j in range(1, wide):
        bias_copy(j).start()
    r.bias_rx[pl.ds(w, 1)] = r.bias_tx[...][None]
    pack_shard(QKV, 0)
    weights_start(QKV, 0)
    r.lead_rx[pl.ds(w, 1)] = r.lead[pl.ds(w, 1)]
    ada_load.wait()
    wait_all(lead_copy)
    lead_all = r.lead_rx[...].reshape(wide * 16, depth)
    for layer in range(LAYERS):
        product = dot(lead_all, r.ada_v[layer], ((1,), (0,)))
        for row in range(wide):
            at = slice(SEGS * layer, SEGS * layer + SEGS)
            r.mod_part[row, at, :] = product[16 * row : 16 * row + SEGS]
    for j in range(1, wide):
        mod_copy(j).start()
    weights_start(OUT, 0)
    r.mod_rx[pl.ds(w, 1)] = r.mod_part[pl.ds(w, 1)]
    for which, layer in ((UP, 0), (QKV, 1), (UP, 1)):
        pack_shard(which, layer)
    pump_through(QKV, 0)
    weights_start(UP, 0)
    r.mod_grad[...] = jnp.zeros_like(r.mod_grad)
    r.lead_t[...] = jnp.zeros_like(r.lead_t)
    for layer in range(LAYERS):
        for row in range(wide):
            at = (row * LAYERS + layer) * SEGS
            r.lead_t[layer, at : at + SEGS, :] = r.lead_rx[row].astype(F32)[:SEGS]
        r.lead_o[layer] = jnp.transpose(r.lead_t[layer]).astype(BF16)

    wait_all(bias_copy)
    bias_full = (r.ada_full, r.qkv_full, r.out_full, r.up_full, r.down_full)
    for peer in range(wide):
        values = r.bias_rx[peer].astype(F32)
        for layer in range(LAYERS):
            for k, row, start, size in bias_places:
                line = values.shape[0] // LAYERS * layer + row
                at = bias_refs[k].shape[1] * peer + start
                bias_full[k][0, layer : layer + 1, at : at + size] = values[line : line + 1, :size]
    for which, ref in ((QKV, r.qkv_full), (UP, r.up_full)):
        pieces = [pick(ref, *window) for window in windows(which)]
        for layer in range(LAYERS):
            at = 4 * layer + which
            pack(r.bias_sum.at[at : at + 1], [piece[layer : layer + 1] for piece in pieces])
    for layer in range(LAYERS):
        at = 4 * layer
        r.bias_sum[at + OUT : at + OUT + 1] = r.out_full[0, layer : layer + 1]
        r.bias_sum[at + DOWN : at + DOWN + 1] = r.down_full[0, layer : layer + 1]

    wait_all(mod_copy)
    ada_own = r.ada_full[0, :, span(LANES * mod_start(tiles, narrow, n), mod_cols, LANES)]
    total = jnp.sum(r.mod_rx[...], 0)
    for layer in range(LAYERS):
        at = slice(SEGS * layer, SEGS * layer + SEGS)
        r.mod_q[pl.ds(n, 1), at, :] = (total[at] + ada_own[layer : layer + 1])[None]
    for k in range(3):
        quarter_copy(k).start()
    for k in range(3):
        quarter_copy(k, True).wait_recv()
    for part in range(narrow):
        at = LANES * mod_start(tiles, narrow, part)
        r.mods[:, at : at + mod_cols] = r.mod_q[part]

    def bias_row(layer, which, size):
        return r.bias_sum[4 * layer + which : 4 * layer + which + 1, :size]

    def gather_norm(layer, hid, shift, scale, take, before):
        for part in range(2):
            before(part)

            def step(start):
                seg = seg_of(start)
                unit, _ = norm(take(start, seg))
                hidden = unit * (1.0 + mod(layer, scale, seg)) + mod(layer, shift, seg)
                hid[span(local * n + start, STEP), :] = hidden.astype(BF16)

            each_step(part, step)
            tok_send(hid, part)

    def qkv_block(layer, block):
        rows = block_rows(block)
        out = dot(r.hid_attn[layer, rows, :], r.qkv_v[...], ((1,), (0,)))
        out = (out + bias_row(layer, QKV, 3 * cols)).astype(BF16)
        for j in range(3 * own_heads):
            r.heads[layer, j, rows, :HEAD] = out[:, HEAD * j : HEAD * (j + 1)]

    def attend(layer):
        for head in range(own_heads):

            @pl.loop(0, narrow)
            def _(i):
                rows = span(local * i, local)
                query = r.heads[layer, head, rows, :HEAD]
                key = r.heads[layer, own_heads + head, :, :HEAD]
                value = r.heads[layer, 2 * own_heads + head, :, :HEAD]
                scores = dot(query, key, ((1,), (1,))) * scale_inv
                scores = jnp.where(r.seg_col[rows, :] == r.seg_row[...], scores, -1e30)
                top = jnp.max(scores, -1, keepdims=True)
                power = jnp.exp(scores - top)
                total = jnp.sum(power, -1, keepdims=True)
                probs = (power / total).astype(BF16)
                mixed = dot(probs, value, ((1,), (0,)))
                r.mixed[layer, rows, HEAD * head : HEAD * (head + 1)] = mixed.astype(BF16)
                r.log_sum[layer, rows, head : head + 1] = top + jnp.log(total)

            if head % 2:
                pump(1)

    def up_block(layer, block):
        rows = block_rows(block)
        hidden = r.hid_mlp[layer, rows, :]
        for at in range(0, width, 3 * LANES):
            tile = slice(at, at + 3 * LANES)
            up = dot(hidden, r.up_v[:, tile], ((1,), (0,)))
            up = up + r.bias_sum[4 * layer + UP : 4 * layer + UP + 1, tile]
            r.up[layer, rows, tile] = up.astype(BF16)
            r.act[layer, rows, tile] = gelu(up).astype(BF16)

    def down_block(layer, block):
        r.part[block] = dot(r.act[layer, block_rows(block), :], r.down_v[...], ((1,), (0,)))

    def state_of(layer, start):
        rows = span(start, STEP)
        return r.tok[rows, :].astype(F32) if layer == 0 else r.state[rows, :]

    def after_attn(layer):
        def take(start, seg):
            rows = span(start, STEP)
            branch = sum_take(start) + bias_row(layer, OUT, width)
            r.branch[layer, rows, :] = branch.astype(BF16)
            middle = state_of(layer, start) + mod(layer, 2, seg) * branch
            r.middle[layer, rows, :] = middle
            return middle

        return take

    def after_mlp(layer):
        def take(start, seg):
            rows = span(start, STEP)
            down = sum_take(start) + bias_row(layer, DOWN, width)
            r.down[layer, rows, :] = down.astype(BF16)
            result = r.middle[layer, rows, :] + mod(layer, 5, seg) * down
            if layer == 0:
                r.state[rows, :] = result
            else:
                r.mixed_o[rows, :] = result.astype(BF16)
            return result

        return take

    def attn_forward(layer, take, before):
        hid = r.hid_attn.at[layer]
        gather_norm(layer, hid, 0, 1, take, before)
        if layer == 0:
            early_grad()
        pump(1)
        weights_ready(QKV, layer)
        tok_own(hid)
        qkv_block(layer, 1)
        pump(1)
        tok_other(hid)
        qkv_block(layer, 0)
        pump(1)
        if layer == 0:
            tok_own(r.grad_down, True)
            tok_other(r.grad_down, True)
        attend(layer)
        weights_ready(OUT, layer)
        tok_drain(hid)
        for block in range(2):
            r.part[block] = dot(r.mixed[layer, block_rows(block), :], r.out_v[...], ((1,), (0,)))
            sum_block(block)
            if block == 0:
                sum_cross()
        pump(1)
        gather_norm(layer, r.hid_mlp.at[layer], 3, 4, after_attn(layer), sum_wait)
        pump(1)
        weights_ready(UP, layer)

    def early_grad():
        for part in range(2):

            def step(start):
                rows = span(start, STEP)
                grad = r.cot[rows, :].astype(F32)
                r.token_o[rows, :] = grad
                grad_down = (mod(LAYERS - 1, 5, seg_of(start)) * grad).astype(BF16)
                r.grad_down[span(local * n + start, STEP), :] = grad_down

            each_step(part, step)
            tok_send(r.grad_down, part, True)

    attn_forward(0, lambda start, seg: state_of(0, start), lambda part: None)
    weights_ready(DOWN, 0)
    hid = r.hid_mlp.at[0]
    tok_own(hid)
    up_block(0, 1)
    down_block(0, 1)
    sum_block(1)
    pump(1)
    tok_other(hid)
    up_block(0, 0)
    down_block(0, 0)
    sum_block(0)
    sum_cross()
    tok_drain(hid)
    pump(2)
    attn_forward(1, after_mlp(0), sum_wait)

    sums = (r.qkv_d, r.out_d, r.up_d, r.down_d)
    from_x = (r.qkv_xr, r.out_xr, r.up_xr, r.down_xr)
    from_z = (r.qkv_zr, r.out_zr, r.up_zr, r.down_zr)
    final = (r.qkv_f, r.out_f, r.up_f, r.down_f)
    grads_o = (r.qkv_o, r.out_o, r.up_o, r.down_o)
    same_y, same_c = y == z // 2, c == z % 2

    def d_rows(which, plane_idx, col):
        return w_rows(which, plane_idx, col)

    def d_x(which, plane_idx, incoming=False):
        k = 0 if which == OUT else plane_idx
        src = sums[which].at[d_rows(which, plane_idx, 1 - x)]
        return remote(
            src, from_x[which].at[k], (r.dx_s.at[which, k], r.dx_r.at[which, k]), beside
        )

    def d_z(which, kind):
        idx = 0 if which == OUT else (z_partner, z_inner, z_outer)[kind]
        src = from_x[which].at[idx]

        def send(slot, plane_idx):
            return remote(
                src, from_z[which].at[slot], (r.dz_s.at[which, kind], r.dz_r.at[which, slot]),
                at_plane(plane_idx),
            )

        return send

    def d_z_in(which, slot):
        ref = from_z[which].at[slot]
        return remote(ref, ref, (r.dz_s.at[which, 0], r.dz_r.at[which, slot]), at_plane(z_partner))

    def grad_product(which, layer):
        left, right = (
            (r.hid_attn, r.grad_qkv), (r.mixed, r.grad_branch),
            (r.hid_mlp, r.grad_up), (r.act, r.grad_down),
        )[which]
        if which == OUT:
            product = dot(left[layer], right[...], ((0,), (0,)))
            sums[which][...] = product.astype(BF16)
        else:

            @pl.loop(0, width // (3 * LANES))
            def _(i):
                tile = span(3 * LANES * i, 3 * LANES, LANES)
                product = dot(left[layer, :, tile], right[...], ((0,), (0,)))
                sums[which][tile, :] = product.astype(BF16)

    def grad_send(which, layer):
        if layer == 0:
            pl.semaphore_wait(r.credit_x.at[which], 1)
        if which == OUT:
            d_x(which, 0).start()
        else:
            for idx in (z_outer, z_inner, z_partner, z):
                d_x(which, idx).start()

    out_home = z == n
    out_near = z_partner == n
    out_far = z_half != n // 2

    def credit(sem, device):
        pl.semaphore_signal(sem, inc=1, device_id=device, device_id_type=MESH)

    def grad_beside(which, layer):
        def add(slot, rows):
            total = sums[which][rows, :].astype(F32) + from_x[which][slot].astype(F32)
            from_x[which][slot] = total.astype(BF16)

        if which == OUT:
            d_x(which, 0).wait_recv()
            add(0, d_rows(which, n, x))
            outer_far = jnp.logical_and(out_far, jnp.logical_not(is_inner))

            @pl.when(jnp.logical_or(out_near, outer_far))
            def _():
                if layer == 0:
                    pl.semaphore_wait(r.credit_z.at[which, 0], 1)

            pl.when(out_near)(lambda: d_z(which, 0)(0, z_partner).start())
            pl.when(outer_far)(lambda: d_z(which, 0)(2, z_partner).start())
            d_x(which, 0).wait_send()
        else:
            for k, idx in ((2, z_outer), (1, z_inner), (0, z_partner), (None, z)):
                d_x(which, idx).wait_recv()
                add(idx, d_rows(which, idx, x))
                if k == 0:
                    if layer == 0:
                        pl.semaphore_wait(r.credit_z.at[which, 0], 1)

                    @pl.when(jnp.logical_not(is_inner))
                    def _():
                        d_z(which, 2)(3, z_partner).start()
                        d_z(which, 1)(2, z_partner).start()

                    d_z(which, 0)(0, z_partner).start()
            for idx in range(PLANES):
                d_x(which, idx).wait_send()

    def grad_join(which, layer):
        def add(slot, idx):
            d_z_in(which, slot).wait_recv()
            total = from_x[which][idx].astype(F32) + from_z[which][slot].astype(F32)
            from_x[which][idx] = total.astype(BF16)

        if which == OUT:

            @pl.when(jnp.logical_and(out_far, is_inner))
            def _():
                add(2, 0)
                if layer == 0:
                    pl.semaphore_wait(r.credit_z.at[which, 1], 1)
                else:
                    credit(r.credit_z.at[which, 0], at_plane(z_partner))
                d_z(which, 0)(1, n).start()
        else:

            @pl.when(is_inner)
            def _():
                if layer == 0:
                    pl.semaphore_wait(r.credit_z.at[which, 1], 2)
                add(3, z_outer)
                d_z(which, 2)(1, z_outer).start()
                add(2, z_inner)
                d_z(which, 1)(1, z_inner).start()

    def grad_planes(which, layer):
        def add():
            d_z_in(which, 0).wait_recv()
            d_z_in(which, 1).wait_recv()
            total = from_x[which][0 if which == OUT else z].astype(F32)
            total = total + from_z[which][0].astype(F32) + from_z[which][1].astype(F32)
            if layer == 0:
                spread_sent(which, 1)
            final[which][...] = total.astype(BF16)
            if layer == 1:
                credit(r.credit_z.at[which, 0], at_plane(z_partner))
                credit(r.credit_z.at[which, 1], at_plane(z_inner))

        if which == OUT:
            pl.when(out_home)(add)
            pl.when(jnp.logical_not(out_home))(lambda: d_z(which, 0)(0, z_partner).wait_send())
        else:
            add()
            for kind in range(3):
                d_z(which, kind)(0, z_partner).wait_send()
        if layer == 1:
            credit(r.credit_x.at[which], beside)

    def spread(which, layer, kind, source=None):
        slot = layer * 4 + which
        if which == OUT:
            dst = grads_o[which].at[layer]
        else:
            dst = grads_o[which].at[layer, n if source is None else source]
        src = final[which] if kind < 2 else dst
        return remote(
            src, dst, (r.spread_s.at[slot, kind], r.spread_r.at[slot, kind]), side if kind == 1 else core
        )

    def spread_own(which, layer):
        dst = grads_o[which].at[layer] if which == OUT else grads_o[which].at[layer, n]
        return pltpu.make_async_copy(final[which], dst, r.spread_l.at[layer * 4 + which])

    def spread_sent(which, layer):
        spread(which, layer, 1).wait_send()
        spread(which, layer, 0).wait_send()
        spread_own(which, layer).wait()

    def grad_spread(which, layer):
        def go():
            spread(which, layer, 1).start()
            spread(which, layer, 0).start()
            spread_own(which, layer).start()

        if which == OUT:
            pl.when(jnp.logical_and(same_y, same_c))(go)
        else:
            go()

    def grad_pass(which, layer):
        def go():
            spread(which, layer, 1, n_side).wait_recv()
            spread(which, layer, 2, n_side).start()

        if which == OUT:
            pl.when(jnp.logical_and(jnp.logical_not(same_y), same_c))(go)
        else:
            go()

    def grad_end(which, layer):
        if which == OUT:
            if layer == 0:
                pl.when(jnp.logical_and(same_y, same_c))(lambda: spread_sent(which, layer))

            @pl.when(jnp.logical_and(jnp.logical_not(same_y), same_c))
            def _():
                spread(which, layer, 2).wait_send()

            @pl.when(jnp.logical_and(same_y, jnp.logical_not(same_c)))
            def _():
                spread(which, layer, 0).wait_recv()

            @pl.when(jnp.logical_and(jnp.logical_not(same_y), jnp.logical_not(same_c)))
            def _():
                spread(which, layer, 2).wait_recv()
        else:
            spread(which, layer, 0, n_core).wait_recv()
            spread(which, layer, 2, n_far).wait_recv()
            spread(which, layer, 2, n_side).wait_send()
            if layer == 0:
                spread_sent(which, layer)

    def bias_grad(layer, which, values):
        at = 4 * layer + which
        r.bias_grad[at : at + 1, : values.shape[1]] = jnp.sum(
            values.astype(F32), 0, keepdims=True
        )

    def back_mlp_block(layer, block):
        rows = block_rows(block)
        grad_down = r.grad_down[rows, :]
        for at in range(0, width, 3 * LANES):
            tile = slice(at, at + 3 * LANES)
            grad_act = dot(grad_down, r.down_v[tile, :], ((1,), (1,)))
            up = r.up[layer, rows, tile].astype(F32)
            r.grad_up[rows, tile] = (grad_act * gelu_slope(up)).astype(BF16)
        r.part[block] = dot(r.grad_up[rows, :], r.up_v[...], ((1,), (1,)))

    def back_attn_block(layer, block):
        rows = block_rows(block)
        out = dot(r.grad_branch[rows, :], r.out_v[...], ((1,), (1,))).astype(BF16)
        for j in range(own_heads):
            r.grad_heads[j, rows, :HEAD] = out[:, HEAD * j : HEAD * (j + 1)]

    def back_attend(layer, head):
        @pl.loop(0, narrow)
        def _(i):
            rows = span(local * i, local)
            query = r.heads[layer, head, rows, :HEAD]
            key = r.heads[layer, own_heads + head, :, :HEAD]
            value = r.heads[layer, 2 * own_heads + head, :, :HEAD]
            grad = r.grad_heads[head, rows, :HEAD]
            scores = dot(query, key, ((1,), (1,))) * scale_inv
            probs = jnp.exp(scores - r.log_sum[layer, rows, head : head + 1])
            probs = jnp.where(r.seg_col[rows, :] == r.seg_row[...], probs, 0.0)
            grad_probs = dot(grad, value, ((1,), (1,)))
            inner = jnp.sum(probs * grad_probs, -1, keepdims=True)
            grad_scores = (probs * (grad_probs - inner)).astype(BF16)
            grad_query = dot(grad_scores, key, ((1,), (0,))) * scale_inv
            r.grad_qkv[rows, HEAD * head : HEAD * (head + 1)] = grad_query.astype(BF16)
            grad_key = dot(grad_scores, query, ((0,), (0,)))
            grad_value = dot(probs.astype(BF16), grad, ((0,), (0,)))

            def tile(k):
                return slice(LANES * k, LANES * k + HEAD)

            @pl.when(i == 0)
            def _():
                for k in range(narrow):
                    at = slice(local * k, local * (k + 1))
                    r.grad_hid[:, tile(k)] = grad_key[at]
                    r.grad_hid[:, tile(narrow + k)] = grad_value[at]

            @pl.when(i > 0)
            def _():
                for k in range(narrow):
                    at = slice(local * k, local * (k + 1))
                    r.grad_hid[:, tile(k)] += grad_key[at]
                    r.grad_hid[:, tile(narrow + k)] += grad_value[at]

        at = cols + HEAD * head
        for k in range(narrow):
            rows = slice(local * k, local * (k + 1))
            key_sum = r.grad_hid[:, LANES * k : LANES * k + HEAD]
            value_sum = r.grad_hid[:, LANES * (narrow + k) : LANES * (narrow + k) + HEAD]
            r.grad_qkv[rows, at : at + HEAD] = (key_sum * scale_inv).astype(BF16)
            r.grad_qkv[rows, cols + at : cols + at + HEAD] = value_sum.astype(BF16)

    def both(body):
        for part in range(2):
            each_step(part, body)

    def sums_attn(layer):
        def body(start):
            rows = span(start, STEP)
            seg = seg_of(start)
            unit, _ = norm(state_of(layer, start))
            grad_hidden = r.grad_hid[rows, :]
            mod_sum(layer, 0, seg, grad_hidden)
            mod_sum(layer, 1, seg, grad_hidden * unit)

        both(body)

    def sums_mlp(layer):
        def body(start):
            rows = span(start, STEP)
            seg = seg_of(start)
            unit, _ = norm(r.middle[layer, rows, :])
            grad_hidden = r.grad_hid[rows, :]
            mod_sum(layer, 3, seg, grad_hidden)
            mod_sum(layer, 4, seg, grad_hidden * unit)
            mod_sum(layer, 2, seg, r.branch[layer, rows, :].astype(F32) * r.token_o[rows, :])

        both(body)

    def sums_gate_mlp(layer, grad):
        def body(start):
            rows = span(start, STEP)
            mod_sum(
                layer, 5, seg_of(start), r.down[layer, rows, :].astype(F32) * grad[rows, :].astype(F32)
            )

        both(body)

    def back_middle(layer):
        for part in range(2):
            sum_wait(part)

            def step(start):
                rows = span(start, STEP)
                seg = seg_of(start)
                grad_hidden = sum_take(start)
                unit, inv = norm(r.middle[layer, rows, :])
                r.grad_hid[rows, :] = grad_hidden
                grad = r.token_o[rows, :] + norm_back(
                    grad_hidden * (1.0 + mod(layer, 4, seg)), unit, inv
                )
                r.token_o[rows, :] = grad
                grad_branch = (mod(layer, 2, seg) * grad).astype(BF16)
                r.grad_branch[span(local * n + start, STEP), :] = grad_branch

            each_step(part, step)
            tok_send(r.grad_branch, part)

    def back_state(layer, start):
        rows = span(start, STEP)
        grad_hidden = sum_take(start)
        unit, inv = norm(state_of(layer, start))
        r.grad_hid[rows, :] = grad_hidden
        r.token_o[rows, :] += norm_back(
            grad_hidden * (1.0 + mod(layer, 1, seg_of(start))), unit, inv
        )

    def back_qkv(layer, checked=False):
        for block in range(2):
            rows = block_rows(block)
            r.part[block] = dot(r.grad_qkv[rows, :], r.qkv_v[...], ((1,), (1,)))
            if checked and block == 0:
                pl.semaphore_wait(r.credit_sum.at[0], 1)
            sum_block(block)
            if block == 0:
                if checked:
                    pl.semaphore_wait(r.credit_sum.at[1], 1)
                sum_cross()

    hid = r.hid_mlp.at[1]
    tok_own(hid)
    up_block(1, 1)
    pump(1)
    tok_other(hid)
    up_block(1, 0)
    pump(1)
    grad_product(DOWN, 1)
    bias_grad(1, DOWN, r.grad_down[span(local * n, local), :])
    tok_drain(hid)
    tok_drain(r.grad_down, True)
    pump_through(DOWN, 1)
    grad_send(DOWN, 1)
    weights_ready(DOWN, 1)
    for block in range(2):
        back_mlp_block(1, block)
        sum_block(block)
        if block == 0:
            sum_cross()
    load(UP, 0).start()
    grad_product(UP, 1)
    grad_send(UP, 1)
    bias_grad(1, UP, r.grad_up[...])
    back_middle(1)
    for block in range(2):
        down_block(1, block)
    load(DOWN, 0).start()
    sums_mlp(1)
    bias_grad(1, OUT, r.grad_branch[span(local * n, local), :])
    tok_own(r.grad_branch)
    back_attn_block(1, 1)
    tok_other(r.grad_branch)
    back_attn_block(1, 0)
    load(OUT, 0).start()
    for block in range(2):
        sum_block(block)
        if block == 0:
            sum_cross()
    grad_product(OUT, 1)
    grad_send(OUT, 1)
    for head in range(own_heads):
        back_attend(1, head)
        if head == 1:
            grad_beside(DOWN, 1)
    tok_drain(r.grad_branch)
    for part in range(2):
        sum_wait(part)
        finish_state = after_mlp(1)

        def last(start):
            finish_state(start, seg_of(start))

        each_step(part, last)
    credit(r.credit_sum.at[0], core)
    credit(r.credit_sum.at[1], side)
    back_qkv(1, True)
    load(QKV, 0).start()
    grad_product(QKV, 1)
    grad_send(QKV, 1)
    sums_gate_mlp(1, r.cot)
    grad_beside(UP, 1)
    bias_grad(1, QKV, r.grad_qkv[...])
    for part in range(2):
        sum_wait(part)

        def start_down(start):
            back_state(1, start)
            grad_down = (mod(0, 5, seg_of(start)) * r.token_o[span(start, STEP), :]).astype(BF16)
            r.grad_down[span(local * n + start, STEP), :] = grad_down

        each_step(part, start_down)
        tok_send(r.grad_down, part)
    sums_attn(1)
    sums_gate_mlp(0, r.token_o)
    bias_grad(0, DOWN, r.grad_down[span(local * n, local), :])
    load(DOWN, 0).wait()
    load(UP, 0).wait()
    grad_beside(OUT, 1)
    grad_join(DOWN, 1)
    tok_own(r.grad_down)
    back_mlp_block(0, 1)
    sum_block(1)
    tok_other(r.grad_down)
    back_mlp_block(0, 0)
    sum_block(0)
    sum_cross()
    grad_product(DOWN, 0)
    bias_grad(0, UP, r.grad_up[...])
    tok_drain(r.grad_down)
    back_middle(0)
    grad_product(UP, 0)
    grad_planes(DOWN, 1)
    grad_send(DOWN, 0)
    grad_join(UP, 1)
    grad_join(OUT, 1)
    sums_mlp(0)
    bias_grad(0, OUT, r.grad_branch[span(local * n, local), :])
    grad_beside(QKV, 1)
    load(OUT, 0).wait()
    load(QKV, 0).wait()
    tok_own(r.grad_branch)
    back_attn_block(0, 1)
    tok_other(r.grad_branch)
    back_attn_block(0, 0)
    grad_spread(DOWN, 1)
    grad_product(OUT, 0)
    for head in range(own_heads):
        back_attend(0, head)
        if head == 1:
            grad_planes(UP, 1)
            grad_send(UP, 0)
    back_qkv(0)
    grad_join(QKV, 1)
    grad_product(QKV, 0)
    tok_drain(r.grad_branch)
    bias_grad(0, QKV, r.grad_qkv[...])
    for part in range(2):
        sum_wait(part)
        each_step(part, partial(back_state, 0))
    sums_attn(0)

    def quarter_back(k, incoming=False):
        device, idx = narrow_peers[k]
        at = span(LANES * mod_start(tiles, narrow, idx), mod_cols, LANES)
        return remote(
            r.mod_grad.at[:, at], r.quarter_rx.at[k], (r.back_s.at[k], r.back_r.at[k]), device
        )

    def wide_back(j, incoming=False):
        return remote(
            r.quarter_sum, r.quarter_all.at[(w - j + wide) % wide if incoming else w],
            (r.wide_s.at[j - 1], r.wide_r.at[j - 1]), wide_peer(j),
        )

    def bias_wide(j, incoming=False):
        return remote(
            r.bias_half, r.bias_all.at[(w - j + wide) % wide if incoming else w],
            (r.bias_wide_s.at[j - 1], r.bias_wide_r.at[j - 1]), wide_peer(j),
        )

    def bias_narrow(k, incoming=False):
        device, idx = narrow_peers[k]
        return remote(
            r.bias_row, r.bias_o.at[idx if incoming else n],
            (r.bias_narrow_s.at[k], r.bias_narrow_r.at[k]), device,
        )

    def mod_narrow(k, incoming=False):
        device, idx = narrow_peers[k]
        return remote(
            r.mod_all, r.mod_o.at[idx if incoming else n],
            (r.mod_narrow_s.at[k], r.mod_narrow_r.at[k]), device,
        )

    def lead_back(j, incoming=False):
        return remote(
            r.lead_tx.at[(w + j) % wide], r.lead_back.at[(w - j + wide) % wide if incoming else w],
            (r.lead_back_s.at[j - 1], r.lead_back_r.at[j - 1]), wide_peer(j),
        )

    def lead_narrow(k, incoming=False):
        device, idx = narrow_peers[k]
        return remote(
            r.lead_back, r.lead_g.at[idx if incoming else n],
            (r.lead_narrow_s.at[k], r.lead_narrow_r.at[k]), device,
        )

    for k in range(3):
        quarter_back(k).start()
    own_at = span(LANES * mod_start(tiles, narrow, n), mod_cols, LANES)
    total = r.mod_grad[:, own_at]
    for k in range(3):
        quarter_back(k, True).wait_recv()
        total = total + r.quarter_rx[k]
    r.quarter_sum[...] = folded(total, mod_cols // 2)
    for j in range(1, wide):
        wide_back(j).start()
    r.bias_half[...] = folded(r.bias_grad[...], 5 * LANES)
    for j in range(1, wide):
        bias_wide(j).start()
    r.quarter_all[pl.ds(w, 1)] = r.quarter_sum[...][None]
    r.bias_all[pl.ds(w, 1)] = r.bias_half[...][None]
    grad_planes(OUT, 1)
    grad_send(OUT, 0)
    grad_beside(DOWN, 0)
    grad_planes(QKV, 1)
    grad_send(QKV, 0)
    grad_spread(UP, 1)
    grad_spread(OUT, 1)
    grad_spread(QKV, 1)
    for which in (DOWN, UP, OUT, QKV):
        grad_pass(which, 1)
    grad_join(DOWN, 0)
    grad_beside(UP, 0)
    wait_all(wide_back)
    for j in range(1, wide):
        mod_copy(j).wait_send()
    for row in range(wide):
        r.mod_part[row] = unfolded(r.quarter_all[row], mod_cols)
    r.mod_all[...] = r.mod_part[...].reshape(wide * LAYERS * SEGS, mod_cols).astype(BF16)
    mod_own = pltpu.make_async_copy(r.mod_all, r.mod_o.at[n], r.mod_own_sem)
    mod_own.start()
    for k in range(3):
        mod_narrow(k).start()
    owned = LANES * (mod_start(tiles, narrow, n + 1) - mod_start(tiles, narrow, n))
    lane = lax.broadcasted_iota(jnp.int32, r.mod_all.shape, 1)
    own_grads = jnp.where(lane < owned, r.mod_all[...].astype(F32), 0.0).astype(BF16)
    lead_parts = [dot(own_grads, r.ada_v[layer], ((1,), (1,))) for layer in range(LAYERS)]
    for row in range(wide):
        at = row * LAYERS * SEGS
        r.lead_tx[row] = lead_parts[0][at : at + SEGS] + lead_parts[1][at + SEGS : at + 2 * SEGS]
    for j in range(1, wide):
        lead_back(j).start()
    r.lead_back[pl.ds(w, 1)] = r.lead_tx[pl.ds(w, 1)]
    grad_planes(DOWN, 0)
    grad_spread(DOWN, 0)
    grad_beside(OUT, 0)
    wait_all(bias_wide)
    r.bias_row[...] = unfolded(jnp.sum(r.bias_all[...].astype(F32), 0), width)
    bias_own = pltpu.make_async_copy(r.bias_row, r.bias_o.at[n], r.bias_own_sem)
    bias_own.start()
    for k in range(3):
        bias_narrow(k).start()
    grad_join(UP, 0)
    grad_join(OUT, 0)
    grad_beside(QKV, 0)
    wait_all(lead_back)
    lead_own = pltpu.make_async_copy(r.lead_back, r.lead_g.at[n], r.lead_own_sem)
    lead_own.start()
    for k in range(3):
        lead_narrow(k).start()
    grad_pass(DOWN, 0)
    grad_join(QKV, 0)
    grad_planes(UP, 0)
    grad_spread(UP, 0)
    grad_planes(OUT, 0)
    grad_spread(OUT, 0)
    grad_planes(QKV, 0)
    grad_spread(QKV, 0)
    for which in (UP, OUT, QKV):
        grad_pass(which, 0)

    for layer in range(LAYERS):
        for which in range(4):
            weights_drain(which, layer)
            grad_end(which, layer)
    for j in range(1, wide):
        for copy in (lead_copy, bias_copy, wide_back, bias_wide, lead_back):
            copy(j).wait_send()
    for k in range(3):
        for copy in (quarter_copy, quarter_back, mod_narrow, bias_narrow, lead_narrow):
            copy(k).wait_send()
        mod_narrow(k, True).wait_recv()
        bias_narrow(k, True).wait_recv()
        lead_narrow(k, True).wait_recv()
    mod_own.wait()
    lead_own.wait()
    bias_own.wait()


def gelu_slope(values):
    rate = math.sqrt(2.0 / math.pi)
    bent = jnp.tanh(rate * (values + 0.044715 * values * values * values))
    inner = rate * (1.0 + 3.0 * 0.044715 * values * values)
    return 0.5 * (1.0 + bent) + 0.5 * values * (1.0 - bent * bent) * inner


def chosen_of(cond, index):
    values = cond[...].astype(F32)
    rows = index[...]
    chosen = jnp.zeros(values.shape, F32)
    for k in range(SEGS):
        chosen = jnp.where(rows == k, values[k : k + 1], chosen)
    return chosen


def finish_kernel(cfg, *refs):
    r = SimpleNamespace(**dict(zip(cfg.names, refs)))
    wide, narrow, width, depth, cols = cfg.wide, cfg.narrow, cfg.width, cfg.depth, cfg.cols
    tiles, hidden_own = cfg.tiles, cfg.hidden_own
    w = lax.axis_index("wide")

    for part in range(narrow):
        values = r.qkv_i[0, part].astype(F32)
        for j in range(3):
            at = width * j + cols * part
            r.qkv_g[0, :, at : at + cols] = values[:, cols * j : cols * (j + 1)]
        values = r.up_i[0, part].astype(F32)
        for j in range(wide):
            at = (j * narrow + part) * hidden_own
            r.up_g[0, :, at : at + hidden_own] = values[:, hidden_own * j : hidden_own * (j + 1)]
        at, end = [LANES * mod_start(tiles, narrow, part + k) for k in range(2)]
        r.ada_g[0, :, at:end] = dot(r.lead_i[0], r.mod_i[part, :, : end - at], ((1,), (0,)))
    r.out_g[...] = r.out_i[...].astype(F32)
    r.down_g[...] = r.down_i[...].astype(F32)

    def pick(ref, size):
        start = size * w
        window = LANES * (-(-size // LANES) + 1)
        tile, rest = start // LANES, start % LANES
        values = ref[:, pl.ds(pl.multiple_of(LANES * tile, LANES), window)]
        return pltpu.roll(values, (window - rest) % window, 1)[:, :size]

    @pl.when(pl.program_id(0) + pl.program_id(1) == 0)
    def _():
        for part in range(narrow):
            values = r.bias_i[part]
            for j in range(3):
                at = width * j + cols * part
                r.qkv_t[:, at : at + cols] = values[:, cols * j : cols * (j + 1)]
            for j in range(wide):
                at = (j * narrow + part) * hidden_own
                r.up_t[:, at : at + hidden_own] = values[:, hidden_own * j : hidden_own * (j + 1)]
            at, end = [LANES * mod_start(tiles, narrow, part + k) for k in range(2)]
            values = r.mod_i[part, :, : end - at].astype(F32)
            layer_of = lax.broadcasted_iota(jnp.int32, values.shape, 0) // SEGS % LAYERS
            for layer in range(LAYERS):
                sums = jnp.sum(jnp.where(layer_of == layer, values, 0.0), 0, keepdims=True)
                r.ada_t[layer : layer + 1, at:end] = sums
        r.row_t[:, :width] = jnp.sum(r.bias_i[...], 0)
        for dst, ref, line, step in (
            (r.ada_bg, r.ada_t, 0, 1), (r.qkv_bg, r.qkv_t, QKV, 4), (r.out_bg, r.row_t, OUT, 4),
            (r.up_bg, r.up_t, UP, 4), (r.down_bg, r.row_t, DOWN, 4),
        ):
            values = pick(ref, dst.shape[1])
            for layer in range(LAYERS):
                at = step * layer + line
                dst[layer : layer + 1, :] = values[at : at + 1]
        chosen = chosen_of(r.cond, r.cond_index)
        gate = jax.nn.sigmoid(chosen)
        slope = gate * (1.0 + chosen * (1.0 - gate))
        lead_grad = jnp.sum(r.lead_i2[...], 0)
        for row in range(wide):
            at = slice(depth * row, depth * (row + 1))
            grad = lead_grad[row] * slope[:, at]
            for k in range(SEGS):
                r.cond_g[k : k + 1, at] = jnp.sum(
                    jnp.where(r.cond_index[...] == k, grad, 0.0), 0, keepdims=True
                )


def finish(wide, narrow, got, cond, cond_index, tiles, mod_cols, w):
    width = cond.shape[1]
    depth, cols = width // wide, width // narrow
    hidden_own = got["up_o"].shape[-1] // wide
    hidden_all = got["up_o"].shape[-1] * narrow
    down_rows = narrow * hidden_own
    bands = depth // 16
    shape, vmem = jax.ShapeDtypeStruct, pltpu.VMEM

    def whole(values):
        return pl.BlockSpec(values.shape, lambda i, j: (0,) * values.ndim)

    def band(*dims):
        return pl.BlockSpec(
            (1, *dims), lambda i, j: (i, 0, j, 0) if len(dims) == 3 else (i, j, 0)
        )

    down_i = got["down_o"].reshape(LAYERS, down_rows, width)
    inputs = dict(
        qkv_i=got["qkv_o"], up_i=got["up_o"], out_i=got["out_o"], down_i=down_i,
        lead_i=got["lead_o"], mod_i=got["mod_o"], bias_i=got["bias_o"], lead_i2=got["lead_g"],
        cond=cond, cond_index=cond_index,
    )
    in_specs = [
        band(narrow, 16, 3 * cols), band(narrow, 16, wide * hidden_own), band(16, width),
        band(down_rows // bands, width), band(16, got["lead_o"].shape[-1]),
        *[whole(inputs[name]) for name in ("mod_i", "bias_i", "lead_i2", "cond", "cond_index")],
    ]
    outputs = dict(
        ada_g=shape((LAYERS, depth, tiles * LANES), F32), qkv_g=shape((LAYERS, depth, 3 * width), F32),
        out_g=shape((LAYERS, depth, width), F32), up_g=shape((LAYERS, depth, hidden_all), F32),
        down_g=shape((LAYERS, down_rows, width), F32),
        ada_bg=shape((LAYERS, tiles * LANES // wide), F32), qkv_bg=shape((LAYERS, 3 * width // wide), F32),
        out_bg=shape((LAYERS, depth), F32), up_bg=shape((LAYERS, hidden_all // wide), F32),
        down_bg=shape((LAYERS, depth), F32), cond_g=shape((SEGS, width), F32),
    )
    out_specs = [
        band(16, tiles * LANES), band(16, 3 * width), band(16, width), band(16, hidden_all),
        band(down_rows // bands, width),
        *[whole(outputs[name]) for name in ("ada_bg", "qkv_bg", "out_bg", "up_bg", "down_bg", "cond_g")],
    ]
    scratch = dict(
        ada_t=vmem((8, (tiles + 2) * LANES), F32), qkv_t=vmem((8, 3 * width + 2 * LANES), F32),
        up_t=vmem((8, hidden_all + 2 * LANES), F32), row_t=vmem((8, width + 2 * LANES), F32),
    )
    cfg = SimpleNamespace(
        names=[*inputs, *outputs, *scratch], wide=wide, narrow=narrow, width=width, depth=depth,
        cols=cols, tiles=tiles, hidden_own=hidden_own,
    )
    results = pl.pallas_call(
        partial(finish_kernel, cfg),
        grid=(LAYERS, bands),
        out_shape=list(outputs.values()), in_specs=in_specs, out_specs=out_specs,
        scratch_shapes=list(scratch.values()),
        compiler_params=pltpu.CompilerParams(vmem_limit_bytes=62 * 2**20),
    )(*inputs.values())
    done = dict(zip(outputs, results))
    out = [got["mixed_o"][None], got["token_o"][None], done["cond_g"][None]]
    for name in ("ada", "qkv", "out", "up", "down"):
        out += [done[name + "_g"], done[name + "_bg"]]
    return tuple(out)


def fused_device(
    wide, narrow,
    tokens, cond, seg_ids, cond_index, cotangent,
    ada_weight, ada_bias, qkv_weight, qkv_bias, out_weight, out_bias,
    up_weight, up_bias, down_weight, down_bias,
):
    w = lax.axis_index("wide")
    n = lax.axis_index("narrow")
    local, width = tokens.shape[1:]
    row_len = seg_ids.shape[1]
    depth, cols = width // wide, width // narrow
    hidden_own = up_weight.shape[-1] // wide // narrow
    hidden = wide * hidden_own
    tiles = ada_weight.shape[-1] // LANES
    mod_cols = LANES * -(-tiles // narrow)

    inputs = dict(
        tok=tokens[0], cond=cond[0], cond_index=cond_index.reshape(SEGS, 1), seg_row=seg_ids,
        cot=cotangent[0], ada_b=ada_bias, qkv_b=qkv_bias, out_b=out_bias, up_b=up_bias, down_b=down_bias,
        ada=ada_weight, qkv_w=qkv_weight, out_w=out_weight, up_w=up_weight, down_w=down_weight,
    )
    in_hbm = ("ada", "qkv_w", "out_w", "up_w", "down_w")
    shape = jax.ShapeDtypeStruct
    outputs = dict(
        mixed_o=shape((local, width), BF16), token_o=shape((local, width), F32),
        qkv_o=shape((LAYERS, narrow, depth, 3 * cols), BF16),
        out_o=shape((LAYERS, depth, width), BF16),
        up_o=shape((LAYERS, narrow, depth, hidden), BF16),
        down_o=shape((LAYERS, narrow, hidden_own, width), BF16),
        bias_o=shape((narrow, 4 * LAYERS, width), F32),
        mod_o=shape((narrow, wide * LAYERS * SEGS, mod_cols), BF16),
        lead_o=shape((LAYERS, depth, wide * LAYERS * SEGS), BF16),
        lead_g=shape((narrow, wide, SEGS, depth), F32),
        qkv_h=shape((LAYERS, width, 3 * cols), BF16), out_h=shape((LAYERS, cols, width), BF16),
        up_h=shape((LAYERS, width, hidden), BF16), down_h=shape((LAYERS, hidden, width), BF16),
    )
    out_vmem = ("mixed_o", "token_o", "lead_o")
    vmem, dma = pltpu.VMEM, pltpu.SemaphoreType.DMA
    heads = cols // HEAD
    scratch = dict(
        qkv_v=vmem((width, 3 * cols), BF16), out_v=vmem((cols, width), BF16),
        up_v=vmem((width, hidden), BF16), down_v=vmem((hidden, width), BF16),
        hid_attn=vmem((LAYERS, row_len, width), BF16), hid_mlp=vmem((LAYERS, row_len, width), BF16),
        heads=vmem((LAYERS, 3 * heads, row_len, LANES), BF16),
        mixed=vmem((LAYERS, row_len, cols), BF16), log_sum=vmem((LAYERS, row_len, heads), F32),
        up=vmem((LAYERS, row_len, hidden), BF16), act=vmem((LAYERS, row_len, hidden), BF16),
        state=vmem((local, width), F32), middle=vmem((LAYERS, local, width), F32),
        branch=vmem((LAYERS, local, width), BF16), down=vmem((LAYERS, local, width), BF16),
        grad_hid=vmem((local, width), F32),
        grad_down=vmem((row_len, width), BF16), grad_branch=vmem((row_len, width), BF16),
        grad_up=vmem((row_len, hidden), BF16), grad_qkv=vmem((row_len, 3 * cols), BF16),
        grad_heads=vmem((heads, row_len, LANES), BF16),
        part=vmem((2, 2 * local, width), F32),
        core_tx=vmem((2, local, width), BF16), core_rx=vmem((2, local, width), BF16),
        side_tx=vmem((local, width), BF16), side_rx=vmem((local, width), BF16),
        ada_v=vmem((LAYERS, depth, mod_cols), BF16),
        lead=vmem((wide, 16, depth), BF16), lead_rx=vmem((wide, 16, depth), BF16),
        bias_rows=vmem((32, 3 * LANES), F32), bias_tx=vmem((32, 3 * LANES), BF16),
        bias_rx=vmem((wide, 32, 3 * LANES), BF16),
        ada_full=vmem((1, LAYERS, tiles * LANES), F32), qkv_full=vmem((1, LAYERS, 3 * width), F32),
        out_full=vmem((1, LAYERS, width), F32), up_full=vmem((1, LAYERS, narrow * hidden), F32),
        down_full=vmem((1, LAYERS, width), F32), seg_col=vmem((row_len, 1), jnp.int32),
        qkv_raw=vmem((LAYERS, 3, depth, 3 * LANES), BF16), up_raw=vmem((LAYERS, wide, depth, 2 * LANES), BF16),
        qkv_s=vmem((LAYERS, depth, 3 * cols), BF16), up_s=vmem((LAYERS, depth, hidden), BF16),
        lead_t=vmem((LAYERS, wide * LAYERS * SEGS, depth), F32),
        lead_tx=vmem((wide, SEGS, depth), F32), lead_back=vmem((wide, SEGS, depth), F32),
        bias_sum=vmem((4 * LAYERS, width), F32),
        mod_part=vmem((wide, LAYERS * SEGS, mod_cols), F32),
        mod_rx=vmem((wide, LAYERS * SEGS, mod_cols), F32),
        mod_q=vmem((narrow, LAYERS * SEGS, mod_cols), F32),
        mods=vmem((LAYERS * SEGS, tiles * LANES), F32),
        mod_grad=vmem((LAYERS * SEGS, tiles * LANES), F32),
        quarter_rx=vmem((3, LAYERS * SEGS, mod_cols), F32),
        quarter_sum=vmem((16, mod_cols // 2), BF16),
        quarter_all=vmem((wide, 16, mod_cols // 2), BF16),
        mod_all=vmem((wide * LAYERS * SEGS, mod_cols), BF16),
        bias_grad=vmem((4 * LAYERS, width), F32), bias_all=vmem((wide, 16, 5 * LANES), BF16),
        bias_half=vmem((16, 5 * LANES), BF16),
        bias_row=vmem((4 * LAYERS, width), F32),
        qkv_d=vmem((width, 3 * cols), BF16), out_d=vmem((cols, width), BF16),
        up_d=vmem((width, hidden), BF16), down_d=vmem((hidden, width), BF16),
        qkv_xr=vmem((PLANES, depth, 3 * cols), BF16), out_xr=vmem((1, depth, width), BF16),
        up_xr=vmem((PLANES, depth, hidden), BF16), down_xr=vmem((PLANES, hidden_own, width), BF16),
        qkv_zr=vmem((PLANES, depth, 3 * cols), BF16), out_zr=vmem((PLANES, depth, width), BF16),
        up_zr=vmem((PLANES, depth, hidden), BF16), down_zr=vmem((PLANES, hidden_own, width), BF16),
        qkv_f=vmem((depth, 3 * cols), BF16), out_f=vmem((depth, width), BF16),
        up_f=vmem((depth, hidden), BF16), down_f=vmem((hidden_own, width), BF16),
        wz_s=dma((8, 4)), wz_r=dma((8, 4)), wx_s=dma((8, 4)), wx_r=dma((8, 4)), w_own=dma((8,)),
        load_sem=dma((4,)), tok_s=dma((12,)), tok_r=dma((12,)), sum_s=dma((4,)), sum_r=dma((4,)),
        lead_sem_s=dma((wide - 1,)), lead_sem_r=dma((wide - 1,)),
        bias_sem_s=dma((wide - 1,)), bias_sem_r=dma((wide - 1,)),
        mod_sem_s=dma((wide - 1,)), mod_sem_r=dma((wide - 1,)),
        quarter_s=dma((3,)), quarter_r=dma((3,)), ada_sem=dma, raw_sem=dma((LAYERS, 3 + wide)), lead_own_sem=dma,
        lead_back_s=dma((wide - 1,)), lead_back_r=dma((wide - 1,)),
        lead_narrow_s=dma((3,)), lead_narrow_r=dma((3,)),
        dx_s=dma((4, 4)), dx_r=dma((4, 4)), dz_s=dma((4, 3)), dz_r=dma((4, 4)),
        spread_s=dma((8, 3)), spread_r=dma((8, 3)), spread_l=dma((8,)),
        back_s=dma((3,)), back_r=dma((3,)),
        wide_s=dma((wide - 1,)), wide_r=dma((wide - 1,)),
        bias_wide_s=dma((wide - 1,)), bias_wide_r=dma((wide - 1,)),
        bias_narrow_s=dma((3,)), bias_narrow_r=dma((3,)),
        mod_narrow_s=dma((3,)), mod_narrow_r=dma((3,)), mod_own_sem=dma, bias_own_sem=dma,
        credit_x=pltpu.SemaphoreType.REGULAR((4,)), credit_z=pltpu.SemaphoreType.REGULAR((4, 2)),
        credit_sum=pltpu.SemaphoreType.REGULAR((2,)),
    )
    cfg = SimpleNamespace(
        names=[*inputs, *outputs, *scratch], wide=wide, narrow=narrow, width=width, depth=depth,
        local=local, cols=cols, mod_cols=mod_cols, tiles=tiles,
    )

    def place(name, vmem_ok):
        return pl.BlockSpec(memory_space=pltpu.VMEM if vmem_ok else pl.ANY)

    results = pl.pallas_call(
        partial(block_kernel, cfg),
        out_shape=list(outputs.values()),
        in_specs=[place(name, name not in in_hbm) for name in inputs],
        out_specs=[place(name, name in out_vmem) for name in outputs],
        scratch_shapes=list(scratch.values()),
        compiler_params=pltpu.CompilerParams(
            collective_id=0, has_side_effects=True, vmem_limit_bytes=63 * 2**20
        ),
    )(*inputs.values())
    got = dict(zip(outputs, results))

    return finish(wide, narrow, got, cond[0], inputs["cond_index"], tiles, mod_cols, w)


def solution(mesh):
    matrix, vector = P(None, "wide", None), P(None, "wide")
    rows, cond_rows = P("wide", "narrow", None), P("wide", None, None)
    wide, narrow = mesh.shape["wide"], mesh.shape["narrow"]
    fused = wide == PLANES * PAIR and narrow == PLANES
    return jax.shard_map(
        partial(fused_device if fused else plain_device, wide, narrow),
        mesh=mesh,
        in_specs=(rows, cond_rows, P("wide", None), P("wide", None), rows) + (matrix, vector) * 5,
        out_specs=(rows, rows, cond_rows) + (matrix, vector) * 5,
        check_vma=False,
    )
```

```python
from functools import partial
import math
from types import SimpleNamespace

import jax
import jax.numpy as jnp
from jax import lax
from jax.experimental import pallas as pl
from jax.experimental.pallas import tpu as pltpu
from jax.sharding import PartitionSpec as P

HEADS = 16
HEAD = 72
LAYERS = 2
SEGS = 4
EPS = 1e-06
EXACT = lax.Precision.HIGHEST
F32 = jnp.float32
BF16 = jnp.bfloat16


def dot(left, right, dims):
    return lax.dot_general(left, right, (dims, ((), ())), preferred_element_type=F32)


def norm(values):
    centred = values - jnp.mean(values, -1, keepdims=True)
    inv = lax.rsqrt(jnp.mean(centred * centred, -1, keepdims=True) + EPS)
    return centred * inv, inv


def norm_back(grad, unit, inv):
    return inv * (
        grad
        - jnp.mean(grad, -1, keepdims=True)
        - unit * jnp.mean(grad * unit, -1, keepdims=True)
    )


def gather_tokens(values):
    return lax.all_gather(values, "narrow", axis=0, tiled=True)


def scatter_tokens(values):
    return lax.psum_scatter(
        values.astype(BF16), "narrow", scatter_dimension=0, tiled=True
    ).astype(F32)


def gelu(values):
    return jax.nn.gelu(values, approximate=True)


def layer_forward(state, mods, same_seg, weights):
    qkv_w, qkv_b, out_w, out_b, up_w, up_b, down_w, down_b = weights
    shift_attn, scale_attn, gate_attn, shift_mlp, scale_mlp, gate_mlp = mods
    own_heads = out_w.shape[0] // HEAD
    unit_attn, inv_attn = norm(state)
    hidden_attn = gather_tokens((unit_attn * (1.0 + scale_attn) + shift_attn).astype(BF16))
    full_len = hidden_attn.shape[0]
    qkv = (dot(hidden_attn, qkv_w, ((1,), (0,))) + qkv_b).astype(BF16)
    queries, keys, values = [
        part.reshape(full_len, own_heads, HEAD) for part in jnp.split(qkv, 3, axis=-1)
    ]
    scores = jnp.einsum("qhe,khe->hqk", queries, keys, preferred_element_type=F32) * (
        1.0 / math.sqrt(HEAD)
    )
    probs = jax.nn.softmax(jnp.where(same_seg[None], scores, -1e30), axis=-1)
    mixed = jnp.einsum("hqk,khe->qhe", probs.astype(BF16), values, preferred_element_type=F32)
    mixed = mixed.reshape(full_len, own_heads * HEAD).astype(BF16)
    branch = scatter_tokens(dot(mixed, out_w, ((1,), (0,)))) + out_b
    middle = state + gate_attn * branch
    unit_mlp, inv_mlp = norm(middle)
    hidden_mlp = gather_tokens((unit_mlp * (1.0 + scale_mlp) + shift_mlp).astype(BF16))
    up_proj = dot(hidden_mlp, up_w, ((1,), (0,))) + up_b
    activated = gelu(up_proj).astype(BF16)
    down_proj = scatter_tokens(dot(activated, down_w, ((1,), (0,)))) + down_b
    result = middle + gate_mlp * down_proj
    kept = (
        unit_attn, inv_attn, hidden_attn, queries, keys, values, probs, mixed, branch,
        unit_mlp, inv_mlp, hidden_mlp, up_proj, activated, down_proj,
    )
    return result, kept


def layer_backward(grad_out, kept, mods, weights):
    qkv_w, qkv_b, out_w, out_b, up_w, up_b, down_w, down_b = weights
    shift_attn, scale_attn, gate_attn, shift_mlp, scale_mlp, gate_mlp = mods
    (
        unit_attn, inv_attn, hidden_attn, queries, keys, values, probs, mixed, branch,
        unit_mlp, inv_mlp, hidden_mlp, up_proj, activated, down_proj,
    ) = kept
    scale_inv = 1.0 / math.sqrt(HEAD)
    full_len = hidden_attn.shape[0]
    own_down = (gate_mlp * grad_out).astype(BF16)
    grad_gate_mlp = down_proj * grad_out
    grad_down = gather_tokens(own_down)
    grad_act = dot(grad_down, down_w, ((1,), (1,)))
    grad_up = jax.vjp(gelu, up_proj)[1](grad_act)[0].astype(BF16)
    grad_hidden_mlp = scatter_tokens(dot(grad_up, up_w, ((1,), (1,))))
    grad_down_w = dot(activated, grad_down, ((0,), (0,)))
    grad_up_w = dot(hidden_mlp, grad_up, ((0,), (0,)))
    grad_middle = grad_out + norm_back(grad_hidden_mlp * (1.0 + scale_mlp), unit_mlp, inv_mlp)
    own_branch = (gate_attn * grad_middle).astype(BF16)
    grad_gate_attn = branch * grad_middle
    grad_branch = gather_tokens(own_branch)
    grad_attn = dot(grad_branch, out_w, ((1,), (1,))).astype(BF16).reshape(queries.shape)
    grad_probs = jnp.einsum("qhe,khe->hqk", grad_attn, values, preferred_element_type=F32)
    grad_scores = probs * (grad_probs - jnp.sum(probs * grad_probs, -1, keepdims=True))
    grad_scores = grad_scores.astype(BF16)
    grad_q = jnp.einsum("hqk,khe->qhe", grad_scores, keys, preferred_element_type=F32) * scale_inv
    grad_k = jnp.einsum("hqk,qhe->khe", grad_scores, queries, preferred_element_type=F32) * scale_inv
    grad_v = jnp.einsum("hqk,qhe->khe", probs.astype(BF16), grad_attn, preferred_element_type=F32)
    grad_qkv = jnp.concatenate(
        [part.astype(BF16).reshape(full_len, -1) for part in (grad_q, grad_k, grad_v)], axis=-1
    )
    grad_hidden_attn = scatter_tokens(dot(grad_qkv, qkv_w, ((1,), (1,))))
    grad_out_w = dot(mixed, grad_branch, ((0,), (0,)))
    grad_qkv_w = dot(hidden_attn, grad_qkv, ((0,), (0,)))
    grad_state = grad_middle + norm_back(grad_hidden_attn * (1.0 + scale_attn), unit_attn, inv_attn)
    token_mod = jnp.concatenate(
        [
            grad_hidden_attn, grad_hidden_attn * unit_attn, grad_gate_attn,
            grad_hidden_mlp, grad_hidden_mlp * unit_mlp, grad_gate_mlp,
        ],
        axis=-1,
    )
    bias_grads = (
        jnp.sum(grad_qkv.astype(F32), 0),
        jnp.sum(own_branch.astype(F32), 0),
        jnp.sum(grad_up.astype(F32), 0),
        jnp.sum(own_down.astype(F32), 0),
    )
    return grad_state, token_mod, (grad_qkv_w, grad_out_w, grad_up_w, grad_down_w), bias_grads


def plain_device(
    wide, narrow,
    tokens, cond, seg_ids, cond_index, cotangent,
    ada_weight, ada_bias, qkv_weight, qkv_bias, out_weight, out_bias,
    up_weight, up_bias, down_weight, down_bias,
):
    w = lax.axis_index("wide")
    n = lax.axis_index("narrow")
    local_len, width = tokens.shape[1:]
    depth = width // wide
    cols = width // narrow
    hidden_own = up_weight.shape[-1] // wide // narrow
    mod_cols = ada_weight.shape[-1] // narrow

    def own(values, axis):
        return lax.dynamic_index_in_dim(values, n, axis, keepdims=False)

    bias_parts = (ada_bias, qkv_bias, out_bias, up_bias, down_bias)
    sizes = [part.shape[1] for part in bias_parts]
    packed = lax.all_gather(jnp.concatenate(bias_parts, axis=1), "wide", axis=1, tiled=False)
    biases = []
    at = 0
    for size in sizes:
        biases.append(packed[:, :, at : at + size].reshape(LAYERS, -1).astype(F32))
        at += size
    ada_b, qkv_b, out_b, up_b, down_b = biases
    qkv_b = own(qkv_b.reshape(LAYERS, 3, narrow, cols), 2).reshape(LAYERS, 3 * cols)
    up_b = own(up_b.reshape(LAYERS, wide, narrow, hidden_own), 2).reshape(LAYERS, -1)

    cond_hot = (cond_index[0, :, None] == jnp.arange(SEGS, dtype=jnp.int32)[None, :]).astype(F32)
    chosen = jnp.dot(cond_hot, cond[0].astype(F32), precision=EXACT)
    lead = (chosen * jax.nn.sigmoid(chosen)).astype(BF16)
    lead_all = lax.all_gather(lead, "wide", axis=0, tiled=True)
    lead_own = lax.dynamic_slice_in_dim(lead_all, w * depth, depth, 1)
    ada_quarter = lax.dynamic_slice_in_dim(ada_weight, n * mod_cols, mod_cols, 2)
    mod_part = jnp.einsum("nd,lde->nle", lead_own, ada_quarter, preferred_element_type=F32)
    mod_part = lax.psum_scatter(mod_part, "wide", scatter_dimension=0, tiled=True)
    modulation = lax.all_gather(mod_part, "narrow", axis=2, tiled=True)
    modulation = modulation.transpose(1, 0, 2) + ada_b[:, None, :]

    seg_row = seg_ids[0]
    seg_query = lax.dynamic_slice_in_dim(seg_row, n * local_len, local_len, 0)
    token_hot = (seg_query[:, None] == jnp.arange(SEGS, dtype=jnp.int32)[None, :]).astype(F32)
    same_seg = seg_row[:, None] == seg_row[None, :]

    qkv_own = own(qkv_weight.reshape(LAYERS, depth, 3, narrow, cols), 3).reshape(LAYERS, depth, 3 * cols)
    up_own = own(up_weight.reshape(LAYERS, depth, wide, narrow, hidden_own), 3).reshape(LAYERS, depth, -1)
    down_own = own(down_weight.reshape(LAYERS, narrow, hidden_own, width), 1)

    def fetch(idx):
        out_full = lax.all_gather(out_weight[idx], "wide", axis=0, tiled=True)
        return (
            lax.all_gather(qkv_own[idx], "wide", axis=0, tiled=True),
            qkv_b[idx],
            lax.dynamic_slice_in_dim(out_full, n * cols, cols, 0),
            out_b[idx],
            lax.all_gather(up_own[idx], "wide", axis=0, tiled=True),
            up_b[idx],
            lax.all_gather(down_own[idx], "wide", axis=0, tiled=True),
            down_b[idx],
        )

    state = tokens[0].astype(F32)
    weights, mods, kept = [], [], []
    for idx in range(LAYERS):
        weights.append(fetch(idx))
        per_token = jnp.dot(token_hot, modulation[idx], precision=EXACT)
        mods.append(jnp.split(per_token, 6, axis=-1))
        state, saved = layer_forward(state, mods[idx], same_seg, weights[idx])
        kept.append(saved)
    result = state.astype(BF16)

    grad_state = cotangent[0].astype(F32)
    token_hot_t = token_hot.T
    reduced, bias_sums, mod_grads = [None] * LAYERS, [None] * LAYERS, [None] * LAYERS
    for idx in reversed(range(LAYERS)):
        grad_state, token_mod, grads, bias_grads = layer_backward(
            grad_state, kept[idx], mods[idx], weights[idx]
        )
        mod_grads[idx] = jnp.dot(token_hot_t, token_mod, precision=EXACT)
        qkv_g, out_g, up_g, down_g = [item.astype(BF16) for item in grads]
        qkv_g, up_g, down_g = [
            lax.psum_scatter(item, "wide", scatter_dimension=0, tiled=True)
            for item in (qkv_g, up_g, down_g)
        ]
        out_g = lax.psum(out_g, "wide")
        qkv_g = lax.all_gather(qkv_g.reshape(depth, 3, 1, cols), "narrow", axis=2, tiled=True)
        up_g = lax.all_gather(up_g.reshape(depth, wide, 1, hidden_own), "narrow", axis=2, tiled=True)
        down_g = lax.all_gather(down_g, "narrow", axis=0, tiled=True)
        out_g = lax.all_gather(out_g, "narrow", axis=0, tiled=True)
        out_g = lax.dynamic_slice_in_dim(out_g, w * depth, depth, 0)
        reduced[idx] = (
            qkv_g.reshape(depth, 3 * width),
            out_g,
            up_g.reshape(depth, -1),
            down_g,
        )
        spot = lax.broadcasted_iota(jnp.int32, (1, narrow, 1), 1) == n
        qkv_s = jnp.where(spot, bias_grads[0].reshape(3, 1, cols), 0.0).reshape(-1)
        up_s = jnp.where(spot, bias_grads[2].reshape(wide, 1, hidden_own), 0.0).reshape(-1)
        bias_sums[idx] = [
            item.reshape(wide, -1) for item in (qkv_s, bias_grads[1], up_s, bias_grads[3])
        ]
    sizes = [item.shape[1] for item in bias_sums[0]]
    bias_sum = jnp.stack([jnp.concatenate(item, axis=1) for item in bias_sums], axis=1)
    bias_sum = lax.psum_scatter(lax.psum(bias_sum, "narrow"), "wide", scatter_dimension=0, tiled=True)[0]
    bias_out = []
    at = 0
    for size in sizes:
        bias_out.append(bias_sum[:, at : at + size])
        at += size

    mod_grad = lax.psum(jnp.stack(mod_grads), "narrow").astype(BF16)
    mod_all = lax.all_gather(mod_grad, "wide", axis=1, tiled=True)
    ada_grad = jnp.einsum("nd,lne->lde", lead_own, mod_all, preferred_element_type=F32)
    ada_size = ada_bias.shape[1]
    ada_bias_grad = jnp.sum(
        lax.dynamic_slice_in_dim(mod_all, w * ada_size, ada_size, 2).astype(F32), axis=1
    )
    lead_grad = jnp.einsum("lne,lde->nd", mod_all, ada_weight, preferred_element_type=F32)
    lead_grad = lax.all_to_all(lead_grad.reshape(wide, SEGS, depth), "wide", 0, 0, tiled=False)
    lead_grad = lead_grad.transpose(1, 0, 2).reshape(SEGS, width)
    gate = jax.nn.sigmoid(chosen)
    chosen_grad = lead_grad * (gate * (1.0 + chosen * (1.0 - gate)))
    cond_grad = jnp.dot(cond_hot.T, chosen_grad, precision=EXACT)

    stacked = [
        jnp.stack([reduced[idx][pos].astype(F32) for idx in range(LAYERS)]) for pos in range(4)
    ]
    return (
        result[None], grad_state[None], cond_grad[None],
        ada_grad, ada_bias_grad,
        stacked[0], bias_out[0], stacked[1], bias_out[1],
        stacked[2], bias_out[2], stacked[3], bias_out[3],
    )


QKV, OUT, UP, DOWN = range(4)
PLANES = 4
PAIR = 2
LANES = 128
STEP = 32
MESH = pl.DeviceIdType.MESH


def mod_start(tiles, parts, part):
    return tiles * part // parts


def block_kernel(cfg, *refs):
    r = SimpleNamespace(**dict(zip(cfg.names, refs)))
    wide, narrow, width, depth = cfg.wide, cfg.narrow, cfg.width, cfg.depth
    local, cols, mod_cols, tiles = cfg.local, cfg.cols, cfg.mod_cols, cfg.tiles
    half = local // 2
    own_heads = cols // HEAD
    scale_inv = 1.0 / math.sqrt(HEAD)
    w = lax.axis_index("wide")
    n = lax.axis_index("narrow")
    z, x = w // PAIR, w % PAIR
    y, c = n // 2, n % 2
    n_core = n + 1 - 2 * c
    n_side = n + 2 - 4 * y
    n_far = 3 - n
    core, side, far = (w, n_core), (w, n_side), (w, n_far)
    beside = (w + 1 - 2 * x, n)

    z_half = z // 2
    z_partner, z_inner, z_outer = z + 1 - 2 * (z % 2), 2 - z_half, 3 - 3 * z_half
    is_inner = jnp.logical_or(z == 1, z == 2)

    def at_plane(idx):
        return (idx * PAIR + x, n)

    def wide_peer(j):
        return ((w + j) % wide, n)

    def remote(src, dst, sems, device):
        return pltpu.make_async_remote_copy(
            src_ref=src, dst_ref=dst, send_sem=sems[0], recv_sem=sems[1],
            device_id=device, device_id_type=MESH,
        )

    def span(start, size, step=16):
        return pl.ds(pl.multiple_of(start, step), size)

    ada_load = pltpu.make_async_copy(
        r.ada.at[:, :, span(LANES * mod_start(tiles, narrow, n), mod_cols, LANES)], r.ada_v, r.ada_sem
    )
    hidden_own = r.up_w.shape[-1] // wide // narrow

    def windows(which):
        if which == QKV:
            return [(width * j + cols * n, cols, 3 * LANES) for j in range(3)]
        return [((j * narrow + n) * hidden_own, hidden_own, 2 * LANES) for j in range(wide)]

    def raw(which, layer, k):
        src, dst = ((r.qkv_w, r.qkv_raw), (r.up_w, r.up_raw))[which == UP]
        start, _, window = windows(which)[k]
        at = span(LANES * (start // LANES), window, LANES)
        return pltpu.make_async_copy(
            src.at[layer, :, at], dst.at[layer, k], r.raw_sem.at[layer, k + 3 * (which == UP)]
        )

    for layer in range(LAYERS):
        for which in (QKV, UP):
            for k in range(len(windows(which))):
                raw(which, layer, k).start()
        if layer == 0:
            ada_load.start()
    chosen = chosen_of(r.cond, r.cond_index)
    lead = (chosen * jax.nn.sigmoid(chosen)).astype(BF16).astype(F32)
    r.lead[...] = jnp.zeros_like(r.lead)
    for row in range(wide):
        tile = jnp.concatenate(
            [lead[:, depth * row : depth * (row + 1)], jnp.zeros((16 - SEGS, depth), F32)], 0
        )
        r.lead[row] = tile.astype(BF16)
    bias_refs = (r.ada_b, r.qkv_b, r.out_b, r.up_b, r.down_b)
    bias_places, row = [], 0
    for k, ref in enumerate(bias_refs):
        for start in range(0, ref.shape[1], 3 * LANES):
            size = min(3 * LANES, ref.shape[1] - start)
            bias_places.append((k, row, start, size))
            row += 1
    r.bias_rows[...] = jnp.zeros_like(r.bias_rows)
    for layer in range(LAYERS):
        for k, row, start, size in bias_places:
            line = r.bias_rows.shape[0] // LAYERS * layer + row
            values = bias_refs[k][...].astype(F32)[layer : layer + 1, start : start + size]
            r.bias_rows[line : line + 1, :size] = values
    r.bias_tx[...] = r.bias_rows[...].astype(BF16)

    barrier = pltpu.get_barrier_semaphore()
    partners = [core, side, far] + [wide_peer(j) for j in range(1, wide)]
    for partner in partners:
        pl.semaphore_signal(barrier, inc=1, device_id=partner, device_id_type=MESH)
    pl.semaphore_wait(barrier, len(partners))

    full = (r.qkv_h, r.out_h, r.up_h, r.down_h)
    loaded = (r.qkv_v, r.out_v, r.up_v, r.down_v)

    def shard(which, layer):
        if which == DOWN:
            return r.down_w.at[layer, span(depth * n, depth)]
        return (r.qkv_s, r.out_w, r.up_s)[which].at[layer]

    def w_rows(which, plane_idx, col):
        if which == OUT:
            return span(col * depth, depth)
        return span((plane_idx * PAIR + col) * depth, depth)

    def w_block(which, layer, plane_idx, col):
        return full[which].at[layer, w_rows(which, plane_idx, col)]

    def w_z(which, layer, kind, plane_idx, own=False, other=False):
        slot = 4 * LAYERS if other else layer * 4 + which
        block = w_block(which, layer, plane_idx, 1 - x if other else x)
        return remote(
            shard(which, layer) if own else block, block,
            (r.wz_s.at[slot, kind], r.wz_r.at[slot, plane_idx]),
            at_plane(z_inner if kind == 1 else z_partner),
        )

    x_first = None

    def w_x(which, layer, plane_idx, col, own=False):
        slot = layer * 4 + which
        block = w_block(which, layer, plane_idx, col)
        return remote(
            shard(which, layer) if own else block, block,
            (r.wx_s.at[slot, plane_idx], r.wx_r.at[slot, plane_idx]), beside,
        )

    def w_own(which, layer):
        return pltpu.make_async_copy(
            shard(which, layer), w_block(which, layer, z, x), r.w_own.at[layer * 4 + which]
        )

    def weights_start(which, layer):
        def go():
            w_z(which, layer, 1, z, True).start()
            w_z(which, layer, 0, z, True).start()
            w_x(which, layer, z, x, True).start()
            w_own(which, layer).start()

        if which == OUT:
            pl.when(z == n)(go)
        else:
            go()

    passes_out = jnp.logical_and(is_inner, z_half != n // 2)

    def weights_steps(which, layer):
        def passed(plane_idx, kind):
            w_z(which, layer, 0, plane_idx).wait_recv()
            if kind:
                onward = passes_out if which == OUT else is_inner
                pl.when(onward)(lambda: w_z(which, layer, kind, plane_idx).start())
            w_x(which, layer, plane_idx, x).start()

        def ahead():
            slot = layer * 4 + which + 2
            if 2 < slot < 4 * LAYERS:
                weights_start(slot % 4, slot // 4)

        def step(plane_idx, kind):
            if kind == 0:
                ahead()
            passed(plane_idx, kind)

        def only():
            ahead()
            pl.when(z != n)(lambda: passed(n, 2))

        def beside_first():
            w_x(which, layer, z, 1 - x).wait_recv()
            for kind in (1, 0):
                w_z(which, layer, kind, z, other=True).start()

        def step_both(plane_idx, kind):
            for other in (False, True):
                w_z(which, layer, 0, plane_idx, other=other).wait_recv()
                if kind:
                    pl.when(is_inner)(
                        lambda: w_z(which, layer, kind, plane_idx, other=other).start()
                    )
            if kind == 0:
                ahead()

        if which == OUT:
            return [only]
        if (which, layer) == x_first:
            return [beside_first] + [
                partial(step_both, idx, kind)
                for idx, kind in ((z_partner, 0), (z_inner, 2), (z_outer, 3))
            ]
        return [
            partial(step, idx, kind) for idx, kind in ((z_partner, 0), (z_inner, 2), (z_outer, 3))
        ]

    steps = [
        (layer * 4 + which, step)
        for layer in range(LAYERS)
        for which in (QKV, OUT, UP, DOWN)
        for step in weights_steps(which, layer)
    ]

    def pump(count):
        for _ in range(min(count, len(steps))):
            steps.pop(0)[1]()

    def pump_through(which, layer):
        while steps and steps[0][0] <= layer * 4 + which:
            pump(1)

    def weights_finish(which, layer):
        if which == OUT:
            w_x(which, layer, n, 1 - x).wait_recv()
            pl.when(z == n)(lambda: w_own(which, layer).wait())
        else:
            if (which, layer) != x_first:
                for idx in range(PLANES):
                    w_x(which, layer, idx, 1 - x).wait_recv()
            w_own(which, layer).wait()

    def weights_drain(which, layer):
        both = (False, True) if (which, layer) == x_first else (False,)
        if which == OUT:
            w_x(which, layer, n, x).wait_send()

            @pl.when(z == n)
            def _():
                for kind in range(2):
                    w_z(which, layer, kind, z).wait_send()

            pl.when(passes_out)(lambda: w_z(which, layer, 2, n).wait_send())
        else:
            for other in both:
                for kind in range(2):
                    w_z(which, layer, kind, z, other=other).wait_send()

            if (which, layer) == x_first:
                w_x(which, layer, z, x).wait_send()
            else:
                for idx in range(PLANES):
                    w_x(which, layer, idx, x).wait_send()

            @pl.when(is_inner)
            def _():
                for other in both:
                    w_z(which, layer, 2, z_inner, other=other).wait_send()
                    w_z(which, layer, 3, z_outer, other=other).wait_send()

    def load(which, layer):
        return pltpu.make_async_copy(full[which].at[layer], loaded[which], r.load_sem.at[which])

    def weights_ready(which, layer):
        pump_through(which, layer)
        weights_finish(which, layer)
        load(which, layer).start()
        load(which, layer).wait()

    def tok_rows(chunk, part):
        return span(local * chunk + half * part, half)

    def tok_copy(ref, kind, part, incoming=False, early=False):
        chunk = ((n_core, n_side, n_far) if incoming else (n, n, n_side))[kind]
        rows = ref.at[tok_rows(chunk, part)]
        k = 2 * kind + part + 6 * early
        return remote(rows, rows, (r.tok_s.at[k], r.tok_r.at[k]), side if kind == 1 else core)

    def tok_send(ref, part, early=False):
        tok_copy(ref, 1, part, early=early).start()
        tok_copy(ref, 0, part, early=early).start()

    def tok_own(ref, early=False):
        for part in range(2):
            tok_copy(ref, 0, part, True, early).wait_recv()

    def tok_other(ref, early=False):
        for part in range(2):
            tok_copy(ref, 1, part, True, early).wait_recv()
            tok_copy(ref, 2, part, early=early).start()
        for part in range(2):
            tok_copy(ref, 2, part, True, early).wait_recv()

    def tok_drain(ref, early=False):
        for kind in range(3):
            for part in range(2):
                tok_copy(ref, kind, part, early=early).wait_send()

    def block_rows(block):
        return span(2 * local * (y if block else 1 - y), 2 * local)

    def sum_core(block):
        return remote(
            r.core_tx.at[block], r.core_rx.at[block], (r.sum_s.at[block], r.sum_r.at[block]), core
        )

    def sum_side(part):
        rows = span(half * part, half)
        return remote(
            r.side_tx.at[rows], r.side_rx.at[rows], (r.sum_s.at[2 + part], r.sum_r.at[2 + part]), side
        )

    def sum_block(block):
        r.core_tx[block] = r.part[block, span(local * (1 - c), local), :].astype(BF16)
        sum_core(block).start()

    def sum_cross():
        sum_core(0).wait_recv()
        for part in range(2):
            rows = span(half * part, half)
            mine = r.part[0, span(local * c + half * part, half), :]
            r.side_tx[rows, :] = (mine + r.core_rx[0, rows, :].astype(F32)).astype(BF16)
            sum_side(part).start()

    def sum_wait(part):
        if part == 0:
            sum_core(1).wait_recv()
        sum_side(part).wait_recv()
        if part == 1:
            for block in range(2):
                sum_core(block).wait_send()
                sum_side(block).wait_send()

    def sum_take(start):
        rows = span(start, STEP)
        return (
            r.part[1, span(local * c + start, STEP), :]
            + r.core_rx[1, rows, :].astype(F32)
            + r.side_rx[rows, :].astype(F32)
        )

    def each_step(part, body):
        @pl.loop(0, half // STEP)
        def _(i):
            body(half * part + STEP * i)

    def seg_of(start):
        return r.seg_col[span(local * n + start, STEP), :]

    def mod(layer, block, seg):
        rows = r.mods[SEGS * layer : SEGS * layer + SEGS, width * block : width * (block + 1)]
        out = rows[SEGS - 1 : SEGS]
        for s in range(SEGS - 1):
            out = jnp.where(seg == s, rows[s : s + 1], out)
        return out

    def mod_sum(layer, block, seg, values):
        sums = [jnp.sum(jnp.where(seg == s, values, 0.0), 0, keepdims=True) for s in range(SEGS)]
        at = (slice(SEGS * layer, SEGS * layer + SEGS), slice(width * block, width * (block + 1)))
        r.mod_grad[at] += jnp.concatenate(sums, 0)

    seg_cols = jnp.transpose(jnp.broadcast_to(r.seg_row[...].astype(F32), (8, narrow * local)))
    r.seg_col[...] = seg_cols[:, :1].astype(jnp.int32)

    def shifted(values, rest, size):
        window = values.shape[1]
        return pltpu.roll(values.astype(F32), (window - rest) % window, 1)[:, :size]

    def pick(ref, start, size, window):
        return shifted(ref[0, :, span(LANES * (start // LANES), window, LANES)], start % LANES, size)

    def pack(dst, pieces):
        at = 0
        for piece in pieces:
            size = piece.shape[1]
            dst[..., at : at + size] = piece.astype(dst.dtype)
            at += size

    def pack_shard(which, layer):
        dst, pieces = (r.qkv_s if which == QKV else r.up_s).at[layer], []
        for k, (start, size, _) in enumerate(windows(which)):
            raw(which, layer, k).wait()
            buffer = r.qkv_raw if which == QKV else r.up_raw
            pieces.append(shifted(buffer[layer, k], start % LANES, size))
        pack(dst, pieces)

    def folded(values, size):
        rest = values[:, size:]
        if rest.shape[1] < size:
            rest = jnp.concatenate([rest, jnp.zeros((8, size - rest.shape[1]), F32)], 1)
        return jnp.concatenate([values[:, :size], rest], 0).astype(BF16)

    def unfolded(values, size):
        values = values.astype(F32)
        return jnp.concatenate([values[:8], values[8:]], 1)[:, :size]

    def lead_copy(j, incoming=False):
        return remote(
            r.lead.at[(w + j) % wide], r.lead_rx.at[(w - j + wide) % wide if incoming else w],
            (r.lead_sem_s.at[j - 1], r.lead_sem_r.at[j - 1]), wide_peer(j),
        )

    def bias_copy(j, incoming=False):
        return remote(
            r.bias_tx, r.bias_rx.at[(w - j + wide) % wide if incoming else w],
            (r.bias_sem_s.at[j - 1], r.bias_sem_r.at[j - 1]), wide_peer(j),
        )

    def mod_copy(j, incoming=False):
        return remote(
            r.mod_part.at[(w + j) % wide], r.mod_rx.at[(w - j + wide) % wide if incoming else w],
            (r.mod_sem_s.at[j - 1], r.mod_sem_r.at[j - 1]), wide_peer(j),
        )

    def wait_all(copy, count=wide):
        for j in range(1, count):
            copy(j, True).wait_recv()

    narrow_peers = ((core, n_core), (side, n_side), (far, n_far))

    def quarter_copy(k, incoming=False):
        device, idx = narrow_peers[k]
        return remote(
            r.mod_q.at[n], r.mod_q.at[idx if incoming else n],
            (r.quarter_s.at[k], r.quarter_r.at[k]), device,
        )

    for j in range(1, wide):
        lead_copy(j).start()
    for j in range(1, wide):
        bias_copy(j).start()
    r.bias_rx[pl.ds(w, 1)] = r.bias_tx[...][None]
    pack_shard(QKV, 0)
    weights_start(QKV, 0)
    r.lead_rx[pl.ds(w, 1)] = r.lead[pl.ds(w, 1)]
    ada_load.wait()
    wait_all(lead_copy)
    lead_all = r.lead_rx[...].reshape(wide * 16, depth)
    for layer in range(LAYERS):
        product = dot(lead_all, r.ada_v[layer], ((1,), (0,)))
        for row in range(wide):
            at = slice(SEGS * layer, SEGS * layer + SEGS)
            r.mod_part[row, at, :] = product[16 * row : 16 * row + SEGS]
    for j in range(1, wide):
        mod_copy(j).start()
    weights_start(OUT, 0)
    r.mod_rx[pl.ds(w, 1)] = r.mod_part[pl.ds(w, 1)]
    for which, layer in ((UP, 0), (QKV, 1), (UP, 1)):
        pack_shard(which, layer)
    pump_through(QKV, 0)
    weights_start(UP, 0)
    r.mod_grad[...] = jnp.zeros_like(r.mod_grad)
    r.lead_t[...] = jnp.zeros_like(r.lead_t)
    for layer in range(LAYERS):
        for row in range(wide):
            at = (row * LAYERS + layer) * SEGS
            r.lead_t[layer, at : at + SEGS, :] = r.lead_rx[row].astype(F32)[:SEGS]
        r.lead_o[layer] = jnp.transpose(r.lead_t[layer]).astype(BF16)

    wait_all(bias_copy)
    bias_full = (r.ada_full, r.qkv_full, r.out_full, r.up_full, r.down_full)
    for peer in range(wide):
        values = r.bias_rx[peer].astype(F32)
        for layer in range(LAYERS):
            for k, row, start, size in bias_places:
                line = values.shape[0] // LAYERS * layer + row
                at = bias_refs[k].shape[1] * peer + start
                bias_full[k][0, layer : layer + 1, at : at + size] = values[line : line + 1, :size]
    for which, ref in ((QKV, r.qkv_full), (UP, r.up_full)):
        pieces = [pick(ref, *window) for window in windows(which)]
        for layer in range(LAYERS):
            at = 4 * layer + which
            pack(r.bias_sum.at[at : at + 1], [piece[layer : layer + 1] for piece in pieces])
    for layer in range(LAYERS):
        at = 4 * layer
        r.bias_sum[at + OUT : at + OUT + 1] = r.out_full[0, layer : layer + 1]
        r.bias_sum[at + DOWN : at + DOWN + 1] = r.down_full[0, layer : layer + 1]

    wait_all(mod_copy)
    ada_own = r.ada_full[0, :, span(LANES * mod_start(tiles, narrow, n), mod_cols, LANES)]
    total = jnp.sum(r.mod_rx[...], 0)
    for layer in range(LAYERS):
        at = slice(SEGS * layer, SEGS * layer + SEGS)
        r.mod_q[pl.ds(n, 1), at, :] = (total[at] + ada_own[layer : layer + 1])[None]
    for k in range(3):
        quarter_copy(k).start()
    for k in range(3):
        quarter_copy(k, True).wait_recv()
    for part in range(narrow):
        at = LANES * mod_start(tiles, narrow, part)
        r.mods[:, at : at + mod_cols] = r.mod_q[part]

    def bias_row(layer, which, size):
        return r.bias_sum[4 * layer + which : 4 * layer + which + 1, :size]

    def gather_norm(layer, hid, shift, scale, take, before):
        for part in range(2):
            before(part)

            def step(start):
                seg = seg_of(start)
                unit, _ = norm(take(start, seg))
                hidden = unit * (1.0 + mod(layer, scale, seg)) + mod(layer, shift, seg)
                hid[span(local * n + start, STEP), :] = hidden.astype(BF16)

            each_step(part, step)
            tok_send(hid, part)

    def qkv_block(layer, block):
        rows = block_rows(block)
        out = dot(r.hid_attn[layer, rows, :], r.qkv_v[...], ((1,), (0,)))
        out = (out + bias_row(layer, QKV, 3 * cols)).astype(BF16)
        for j in range(3 * own_heads):
            r.heads[layer, j, rows, :HEAD] = out[:, HEAD * j : HEAD * (j + 1)]

    def attend(layer):
        for head in range(own_heads):

            @pl.loop(0, narrow)
            def _(i):
                rows = span(local * i, local)
                query = r.heads[layer, head, rows, :HEAD]
                key = r.heads[layer, own_heads + head, :, :HEAD]
                value = r.heads[layer, 2 * own_heads + head, :, :HEAD]
                scores = dot(query, key, ((1,), (1,))) * scale_inv
                scores = jnp.where(r.seg_col[rows, :] == r.seg_row[...], scores, -1e30)
                top = jnp.max(scores, -1, keepdims=True)
                power = jnp.exp(scores - top)
                total = jnp.sum(power, -1, keepdims=True)
                probs = (power / total).astype(BF16)
                mixed = dot(probs, value, ((1,), (0,)))
                r.mixed[layer, rows, HEAD * head : HEAD * (head + 1)] = mixed.astype(BF16)
                r.log_sum[layer, rows, head : head + 1] = top + jnp.log(total)

            if head % 2:
                pump(1)

    def up_block(layer, block):
        rows = block_rows(block)
        hidden = r.hid_mlp[layer, rows, :]
        for at in range(0, width, 3 * LANES):
            tile = slice(at, at + 3 * LANES)
            up = dot(hidden, r.up_v[:, tile], ((1,), (0,)))
            up = up + r.bias_sum[4 * layer + UP : 4 * layer + UP + 1, tile]
            r.up[layer, rows, tile] = up.astype(BF16)
            r.act[layer, rows, tile] = gelu(up).astype(BF16)

    def down_block(layer, block):
        r.part[block] = dot(r.act[layer, block_rows(block), :], r.down_v[...], ((1,), (0,)))

    def state_of(layer, start):
        rows = span(start, STEP)
        return r.tok[rows, :].astype(F32) if layer == 0 else r.state[rows, :]

    def after_attn(layer):
        def take(start, seg):
            rows = span(start, STEP)
            branch = sum_take(start) + bias_row(layer, OUT, width)
            r.branch[layer, rows, :] = branch.astype(BF16)
            middle = state_of(layer, start) + mod(layer, 2, seg) * branch
            r.middle[layer, rows, :] = middle
            return middle

        return take

    def after_mlp(layer):
        def take(start, seg):
            rows = span(start, STEP)
            down = sum_take(start) + bias_row(layer, DOWN, width)
            r.down[layer, rows, :] = down.astype(BF16)
            result = r.middle[layer, rows, :] + mod(layer, 5, seg) * down
            if layer == 0:
                r.state[rows, :] = result
            else:
                r.mixed_o[rows, :] = result.astype(BF16)
            return result

        return take

    def attn_forward(layer, take, before):
        hid = r.hid_attn.at[layer]
        gather_norm(layer, hid, 0, 1, take, before)
        if layer == 0:
            early_grad()
        pump(1)
        weights_ready(QKV, layer)
        tok_own(hid)
        qkv_block(layer, 1)
        pump(1)
        tok_other(hid)
        qkv_block(layer, 0)
        pump(1)
        if layer == 0:
            tok_own(r.grad_down, True)
            tok_other(r.grad_down, True)
        attend(layer)
        weights_ready(OUT, layer)
        tok_drain(hid)
        for block in range(2):
            r.part[block] = dot(r.mixed[layer, block_rows(block), :], r.out_v[...], ((1,), (0,)))
            sum_block(block)
            if block == 0:
                sum_cross()
        pump(1)
        gather_norm(layer, r.hid_mlp.at[layer], 3, 4, after_attn(layer), sum_wait)
        pump(1)
        weights_ready(UP, layer)

    def early_grad():
        for part in range(2):

            def step(start):
                rows = span(start, STEP)
                grad = r.cot[rows, :].astype(F32)
                r.token_o[rows, :] = grad
                grad_down = (mod(LAYERS - 1, 5, seg_of(start)) * grad).astype(BF16)
                r.grad_down[span(local * n + start, STEP), :] = grad_down

            each_step(part, step)
            tok_send(r.grad_down, part, True)

    attn_forward(0, lambda start, seg: state_of(0, start), lambda part: None)
    weights_ready(DOWN, 0)
    hid = r.hid_mlp.at[0]
    tok_own(hid)
    up_block(0, 1)
    down_block(0, 1)
    sum_block(1)
    pump(1)
    tok_other(hid)
    up_block(0, 0)
    down_block(0, 0)
    sum_block(0)
    sum_cross()
    tok_drain(hid)
    pump(2)
    attn_forward(1, after_mlp(0), sum_wait)

    sums = (r.qkv_d, r.out_d, r.up_d, r.down_d)
    from_x = (r.qkv_xr, r.out_xr, r.up_xr, r.down_xr)
    from_z = (r.qkv_zr, r.out_zr, r.up_zr, r.down_zr)
    final = (r.qkv_f, r.out_f, r.up_f, r.down_f)
    grads_o = (r.qkv_o, r.out_o, r.up_o, r.down_o)
    same_y, same_c = y == z // 2, c == z % 2

    def d_rows(which, plane_idx, col):
        return w_rows(which, plane_idx, col)

    def d_x(which, plane_idx, incoming=False):
        k = 0 if which == OUT else plane_idx
        src = sums[which].at[d_rows(which, plane_idx, 1 - x)]
        return remote(
            src, from_x[which].at[k], (r.dx_s.at[which, k], r.dx_r.at[which, k]), beside
        )

    def d_z(which, kind):
        idx = 0 if which == OUT else (z_partner, z_inner, z_outer)[kind]
        src = from_x[which].at[idx]

        def send(slot, plane_idx):
            return remote(
                src, from_z[which].at[slot], (r.dz_s.at[which, kind], r.dz_r.at[which, slot]),
                at_plane(plane_idx),
            )

        return send

    def d_z_in(which, slot):
        ref = from_z[which].at[slot]
        return remote(ref, ref, (r.dz_s.at[which, 0], r.dz_r.at[which, slot]), at_plane(z_partner))

    def grad_product(which, layer):
        left, right = (
            (r.hid_attn, r.grad_qkv), (r.mixed, r.grad_branch),
            (r.hid_mlp, r.grad_up), (r.act, r.grad_down),
        )[which]
        if which == OUT:
            product = dot(left[layer], right[...], ((0,), (0,)))
            sums[which][...] = product.astype(BF16)
        else:

            @pl.loop(0, width // (3 * LANES))
            def _(i):
                tile = span(3 * LANES * i, 3 * LANES, LANES)
                product = dot(left[layer, :, tile], right[...], ((0,), (0,)))
                sums[which][tile, :] = product.astype(BF16)

    def grad_send(which, layer):
        if layer == 0:
            pl.semaphore_wait(r.credit_x.at[which], 1)
        if which == OUT:
            d_x(which, 0).start()
        else:
            for idx in (z_outer, z_inner, z_partner, z):
                d_x(which, idx).start()

    out_home = z == n
    out_near = z_partner == n
    out_far = z_half != n // 2

    def credit(sem, device):
        pl.semaphore_signal(sem, inc=1, device_id=device, device_id_type=MESH)

    def grad_beside(which, layer):
        def add(slot, rows):
            total = sums[which][rows, :].astype(F32) + from_x[which][slot].astype(F32)
            from_x[which][slot] = total.astype(BF16)

        if which == OUT:
            d_x(which, 0).wait_recv()
            add(0, d_rows(which, n, x))
            outer_far = jnp.logical_and(out_far, jnp.logical_not(is_inner))

            @pl.when(jnp.logical_or(out_near, outer_far))
            def _():
                if layer == 0:
                    pl.semaphore_wait(r.credit_z.at[which, 0], 1)

            pl.when(out_near)(lambda: d_z(which, 0)(0, z_partner).start())
            pl.when(outer_far)(lambda: d_z(which, 0)(2, z_partner).start())
            d_x(which, 0).wait_send()
        else:
            for k, idx in ((2, z_outer), (1, z_inner), (0, z_partner), (None, z)):
                d_x(which, idx).wait_recv()
                add(idx, d_rows(which, idx, x))
                if k == 0:
                    if layer == 0:
                        pl.semaphore_wait(r.credit_z.at[which, 0], 1)

                    @pl.when(jnp.logical_not(is_inner))
                    def _():
                        d_z(which, 2)(3, z_partner).start()
                        d_z(which, 1)(2, z_partner).start()

                    d_z(which, 0)(0, z_partner).start()
            for idx in range(PLANES):
                d_x(which, idx).wait_send()

    def grad_join(which, layer):
        def add(slot, idx):
            d_z_in(which, slot).wait_recv()
            total = from_x[which][idx].astype(F32) + from_z[which][slot].astype(F32)
            from_x[which][idx] = total.astype(BF16)

        if which == OUT:

            @pl.when(jnp.logical_and(out_far, is_inner))
            def _():
                add(2, 0)
                if layer == 0:
                    pl.semaphore_wait(r.credit_z.at[which, 1], 1)
                else:
                    credit(r.credit_z.at[which, 0], at_plane(z_partner))
                d_z(which, 0)(1, n).start()
        else:

            @pl.when(is_inner)
            def _():
                if layer == 0:
                    pl.semaphore_wait(r.credit_z.at[which, 1], 2)
                add(3, z_outer)
                d_z(which, 2)(1, z_outer).start()
                add(2, z_inner)
                d_z(which, 1)(1, z_inner).start()

    def grad_planes(which, layer):
        def add():
            d_z_in(which, 0).wait_recv()
            d_z_in(which, 1).wait_recv()
            total = from_x[which][0 if which == OUT else z].astype(F32)
            total = total + from_z[which][0].astype(F32) + from_z[which][1].astype(F32)
            if layer == 0:
                spread_sent(which, 1)
            final[which][...] = total.astype(BF16)
            if layer == 1:
                credit(r.credit_z.at[which, 0], at_plane(z_partner))
                credit(r.credit_z.at[which, 1], at_plane(z_inner))

        if which == OUT:
            pl.when(out_home)(add)
            pl.when(jnp.logical_not(out_home))(lambda: d_z(which, 0)(0, z_partner).wait_send())
        else:
            add()
            for kind in range(3):
                d_z(which, kind)(0, z_partner).wait_send()
        if layer == 1:
            credit(r.credit_x.at[which], beside)

    def e_z(kind, other):
        idx = (z_partner, z_inner, z_outer)[kind]
        src = sums[DOWN].at[d_rows(DOWN, idx, 1 - x if other else x)]
        slots = from_x[DOWN] if other else from_z[DOWN]

        def send(slot, plane_idx):
            return remote(
                src, slots.at[slot], (r.e_s.at[int(other), kind], r.e_r.at[int(other), slot]),
                at_plane(plane_idx),
            )

        return send

    def e_in(slot, other):
        ref = (from_x[DOWN] if other else from_z[DOWN]).at[slot]
        remote(
            ref, ref, (r.e_s.at[int(other), 0], r.e_r.at[int(other), slot]), at_plane(z_partner)
        ).wait_recv()
        return ref[...].astype(F32)

    def e_x():
        return remote(from_x[DOWN].at[0], r.down_e, (r.ex_s, r.ex_r), beside)

    def first_send():
        @pl.when(jnp.logical_not(is_inner))
        def _():
            for kind in (2, 1):
                for other in (True, False):
                    e_z(kind, other)(kind + 1, z_partner).start()

        for other in (True, False):
            e_z(0, other)(0, z_partner).start()

    def first_join():
        @pl.when(is_inner)
        def _():
            for kind, idx in ((2, z_outer), (1, z_inner)):
                for other in (True, False):
                    rows = d_rows(DOWN, idx, 1 - x if other else x)
                    total = sums[DOWN][rows, :].astype(F32) + e_in(kind + 1, other)
                    sums[DOWN][rows, :] = total.astype(BF16)
                    e_z(kind, other)(1, idx).start()

    def first_planes():
        for other in (True, False):
            rows = d_rows(DOWN, z, 1 - x if other else x)
            total = sums[DOWN][rows, :].astype(F32) + e_in(0, other) + e_in(1, other)
            if other:
                from_x[DOWN][0] = total.astype(BF16)
                e_x().start()
            else:
                final[DOWN][...] = total.astype(BF16)
        for kind in range(3):
            for other in (True, False):
                e_z(kind, other)(0, z_partner).wait_send()
        credit(r.credit_z.at[DOWN, 0], at_plane(z_partner))
        credit(r.credit_z.at[DOWN, 1], at_plane(z_inner))

    def first_beside():
        e_x().wait_recv()
        total = final[DOWN][...].astype(F32) + r.down_e[...].astype(F32)
        final[DOWN][...] = total.astype(BF16)
        e_x().wait_send()
        credit(r.credit_x.at[DOWN], beside)

    def spread(which, layer, kind, source=None):
        slot = layer * 4 + which
        if which == OUT:
            dst = grads_o[which].at[layer]
        else:
            dst = grads_o[which].at[layer, n if source is None else source]
        src = final[which] if kind < 2 else dst
        return remote(
            src, dst, (r.spread_s.at[slot, kind], r.spread_r.at[slot, kind]), side if kind == 1 else core
        )

    def spread_own(which, layer):
        dst = grads_o[which].at[layer] if which == OUT else grads_o[which].at[layer, n]
        return pltpu.make_async_copy(final[which], dst, r.spread_l.at[layer * 4 + which])

    def spread_sent(which, layer):
        spread(which, layer, 1).wait_send()
        spread(which, layer, 0).wait_send()
        spread_own(which, layer).wait()

    def grad_spread(which, layer):
        def go():
            spread(which, layer, 1).start()
            spread(which, layer, 0).start()
            spread_own(which, layer).start()

        if which == OUT:
            pl.when(jnp.logical_and(same_y, same_c))(go)
        else:
            go()

    def grad_pass(which, layer):
        def go():
            spread(which, layer, 1, n_side).wait_recv()
            spread(which, layer, 2, n_side).start()

        if which == OUT:
            pl.when(jnp.logical_and(jnp.logical_not(same_y), same_c))(go)
        else:
            go()

    def grad_end(which, layer):
        if which == OUT:
            if layer == 0:
                pl.when(jnp.logical_and(same_y, same_c))(lambda: spread_sent(which, layer))

            @pl.when(jnp.logical_and(jnp.logical_not(same_y), same_c))
            def _():
                spread(which, layer, 2).wait_send()

            @pl.when(jnp.logical_and(same_y, jnp.logical_not(same_c)))
            def _():
                spread(which, layer, 0).wait_recv()

            @pl.when(jnp.logical_and(jnp.logical_not(same_y), jnp.logical_not(same_c)))
            def _():
                spread(which, layer, 2).wait_recv()
        else:
            spread(which, layer, 0, n_core).wait_recv()
            spread(which, layer, 2, n_far).wait_recv()
            spread(which, layer, 2, n_side).wait_send()
            if layer == 0:
                spread_sent(which, layer)

    def bias_grad(layer, which, values):
        at = 4 * layer + which
        r.bias_grad[at : at + 1, : values.shape[1]] = jnp.sum(
            values.astype(F32), 0, keepdims=True
        )

    def back_mlp_block(layer, block):
        rows = block_rows(block)
        grad_down = r.grad_down[rows, :]
        for at in range(0, width, 3 * LANES):
            tile = slice(at, at + 3 * LANES)
            grad_act = dot(grad_down, r.down_v[tile, :], ((1,), (1,)))
            up = r.up[layer, rows, tile].astype(F32)
            r.grad_up[rows, tile] = (grad_act * gelu_slope(up)).astype(BF16)
        r.part[block] = dot(r.grad_up[rows, :], r.up_v[...], ((1,), (1,)))

    def back_attn_block(layer, block):
        rows = block_rows(block)
        out = dot(r.grad_branch[rows, :], r.out_v[...], ((1,), (1,))).astype(BF16)
        for j in range(own_heads):
            r.grad_heads[j, rows, :HEAD] = out[:, HEAD * j : HEAD * (j + 1)]

    def back_attend(layer, head):
        @pl.loop(0, narrow)
        def _(i):
            rows = span(local * i, local)
            query = r.heads[layer, head, rows, :HEAD]
            key = r.heads[layer, own_heads + head, :, :HEAD]
            value = r.heads[layer, 2 * own_heads + head, :, :HEAD]
            grad = r.grad_heads[head, rows, :HEAD]
            scores = dot(query, key, ((1,), (1,))) * scale_inv
            probs = jnp.exp(scores - r.log_sum[layer, rows, head : head + 1])
            probs = jnp.where(r.seg_col[rows, :] == r.seg_row[...], probs, 0.0)
            grad_probs = dot(grad, value, ((1,), (1,)))
            inner = jnp.sum(probs * grad_probs, -1, keepdims=True)
            grad_scores = (probs * (grad_probs - inner)).astype(BF16)
            grad_query = dot(grad_scores, key, ((1,), (0,))) * scale_inv
            r.grad_qkv[rows, HEAD * head : HEAD * (head + 1)] = grad_query.astype(BF16)
            grad_key = dot(grad_scores, query, ((0,), (0,)))
            grad_value = dot(probs.astype(BF16), grad, ((0,), (0,)))

            def tile(k):
                return slice(LANES * k, LANES * k + HEAD)

            @pl.when(i == 0)
            def _():
                for k in range(narrow):
                    at = slice(local * k, local * (k + 1))
                    r.grad_hid[:, tile(k)] = grad_key[at]
                    r.grad_hid[:, tile(narrow + k)] = grad_value[at]

            @pl.when(i > 0)
            def _():
                for k in range(narrow):
                    at = slice(local * k, local * (k + 1))
                    r.grad_hid[:, tile(k)] += grad_key[at]
                    r.grad_hid[:, tile(narrow + k)] += grad_value[at]

        at = cols + HEAD * head
        for k in range(narrow):
            rows = slice(local * k, local * (k + 1))
            key_sum = r.grad_hid[:, LANES * k : LANES * k + HEAD]
            value_sum = r.grad_hid[:, LANES * (narrow + k) : LANES * (narrow + k) + HEAD]
            r.grad_qkv[rows, at : at + HEAD] = (key_sum * scale_inv).astype(BF16)
            r.grad_qkv[rows, cols + at : cols + at + HEAD] = value_sum.astype(BF16)

    def both(body):
        for part in range(2):
            each_step(part, body)

    def sums_attn(layer):
        def body(start):
            rows = span(start, STEP)
            seg = seg_of(start)
            unit, _ = norm(state_of(layer, start))
            grad_hidden = r.grad_hid[rows, :]
            mod_sum(layer, 0, seg, grad_hidden)
            mod_sum(layer, 1, seg, grad_hidden * unit)

        both(body)

    def sums_mlp(layer):
        def body(start):
            rows = span(start, STEP)
            seg = seg_of(start)
            unit, _ = norm(r.middle[layer, rows, :])
            grad_hidden = r.grad_hid[rows, :]
            mod_sum(layer, 3, seg, grad_hidden)
            mod_sum(layer, 4, seg, grad_hidden * unit)
            mod_sum(layer, 2, seg, r.branch[layer, rows, :].astype(F32) * r.token_o[rows, :])

        both(body)

    def sums_gate_mlp(layer, grad):
        def body(start):
            rows = span(start, STEP)
            mod_sum(
                layer, 5, seg_of(start), r.down[layer, rows, :].astype(F32) * grad[rows, :].astype(F32)
            )

        both(body)

    def back_middle(layer):
        for part in range(2):
            sum_wait(part)

            def step(start):
                rows = span(start, STEP)
                seg = seg_of(start)
                grad_hidden = sum_take(start)
                unit, inv = norm(r.middle[layer, rows, :])
                r.grad_hid[rows, :] = grad_hidden
                grad = r.token_o[rows, :] + norm_back(
                    grad_hidden * (1.0 + mod(layer, 4, seg)), unit, inv
                )
                r.token_o[rows, :] = grad
                grad_branch = (mod(layer, 2, seg) * grad).astype(BF16)
                r.grad_branch[span(local * n + start, STEP), :] = grad_branch

            each_step(part, step)
            tok_send(r.grad_branch, part)

    def back_state(layer, start):
        rows = span(start, STEP)
        grad_hidden = sum_take(start)
        unit, inv = norm(state_of(layer, start))
        r.grad_hid[rows, :] = grad_hidden
        r.token_o[rows, :] += norm_back(
            grad_hidden * (1.0 + mod(layer, 1, seg_of(start))), unit, inv
        )

    def back_qkv(layer, checked=False):
        for block in range(2):
            rows = block_rows(block)
            r.part[block] = dot(r.grad_qkv[rows, :], r.qkv_v[...], ((1,), (1,)))
            if checked and block == 0:
                pl.semaphore_wait(r.credit_sum.at[0], 1)
            sum_block(block)
            if block == 0:
                if checked:
                    pl.semaphore_wait(r.credit_sum.at[1], 1)
                sum_cross()

    hid = r.hid_mlp.at[1]
    tok_own(hid)
    up_block(1, 1)
    pump(1)
    tok_other(hid)
    up_block(1, 0)
    pump(1)
    grad_product(DOWN, 1)
    bias_grad(1, DOWN, r.grad_down[span(local * n, local), :])
    tok_drain(hid)
    tok_drain(r.grad_down, True)
    pump_through(DOWN, 1)
    first_send()
    weights_ready(DOWN, 1)
    for block in range(2):
        back_mlp_block(1, block)
        sum_block(block)
        if block == 0:
            sum_cross()
    load(UP, 0).start()
    grad_product(UP, 1)
    grad_send(UP, 1)
    bias_grad(1, UP, r.grad_up[...])
    back_middle(1)
    for block in range(2):
        down_block(1, block)
    load(DOWN, 0).start()
    sums_mlp(1)
    bias_grad(1, OUT, r.grad_branch[span(local * n, local), :])
    tok_own(r.grad_branch)
    back_attn_block(1, 1)
    tok_other(r.grad_branch)
    back_attn_block(1, 0)
    load(OUT, 0).start()
    for block in range(2):
        sum_block(block)
        if block == 0:
            sum_cross()
    grad_product(OUT, 1)
    grad_send(OUT, 1)
    for head in range(own_heads):
        back_attend(1, head)
        if head == 2:
            first_join()
    tok_drain(r.grad_branch)
    for part in range(2):
        sum_wait(part)
        finish_state = after_mlp(1)

        def last(start):
            finish_state(start, seg_of(start))

        each_step(part, last)
    credit(r.credit_sum.at[0], core)
    credit(r.credit_sum.at[1], side)
    back_qkv(1, True)
    load(QKV, 0).start()
    grad_product(QKV, 1)
    grad_send(QKV, 1)
    sums_gate_mlp(1, r.cot)
    grad_beside(UP, 1)
    bias_grad(1, QKV, r.grad_qkv[...])
    for part in range(2):
        sum_wait(part)

        def start_down(start):
            back_state(1, start)
            grad_down = (mod(0, 5, seg_of(start)) * r.token_o[span(start, STEP), :]).astype(BF16)
            r.grad_down[span(local * n + start, STEP), :] = grad_down

        each_step(part, start_down)
        tok_send(r.grad_down, part)
    sums_attn(1)
    sums_gate_mlp(0, r.token_o)
    bias_grad(0, DOWN, r.grad_down[span(local * n, local), :])
    load(DOWN, 0).wait()
    load(UP, 0).wait()
    grad_beside(OUT, 1)
    first_planes()
    tok_own(r.grad_down)
    back_mlp_block(0, 1)
    sum_block(1)
    tok_other(r.grad_down)
    back_mlp_block(0, 0)
    sum_block(0)
    sum_cross()
    grad_product(DOWN, 0)
    bias_grad(0, UP, r.grad_up[...])
    tok_drain(r.grad_down)
    back_middle(0)
    grad_product(UP, 0)
    first_beside()
    grad_send(DOWN, 0)
    grad_join(UP, 1)
    grad_join(OUT, 1)
    sums_mlp(0)
    bias_grad(0, OUT, r.grad_branch[span(local * n, local), :])
    grad_beside(QKV, 1)
    load(OUT, 0).wait()
    load(QKV, 0).wait()
    tok_own(r.grad_branch)
    back_attn_block(0, 1)
    tok_other(r.grad_branch)
    back_attn_block(0, 0)
    grad_spread(DOWN, 1)
    grad_product(OUT, 0)
    for head in range(own_heads):
        back_attend(0, head)
        if head == 1:
            grad_planes(UP, 1)
            grad_send(UP, 0)
    back_qkv(0)
    grad_join(QKV, 1)
    grad_product(QKV, 0)
    tok_drain(r.grad_branch)
    bias_grad(0, QKV, r.grad_qkv[...])
    for part in range(2):
        sum_wait(part)
        each_step(part, partial(back_state, 0))
    sums_attn(0)

    def quarter_back(k, incoming=False):
        device, idx = narrow_peers[k]
        at = span(LANES * mod_start(tiles, narrow, idx), mod_cols, LANES)
        return remote(
            r.mod_grad.at[:, at], r.quarter_rx.at[k], (r.back_s.at[k], r.back_r.at[k]), device
        )

    def wide_back(j, incoming=False):
        return remote(
            r.quarter_sum, r.quarter_all.at[(w - j + wide) % wide if incoming else w],
            (r.wide_s.at[j - 1], r.wide_r.at[j - 1]), wide_peer(j),
        )

    def bias_wide(j, incoming=False):
        return remote(
            r.bias_half, r.bias_all.at[(w - j + wide) % wide if incoming else w],
            (r.bias_wide_s.at[j - 1], r.bias_wide_r.at[j - 1]), wide_peer(j),
        )

    def bias_narrow(k, incoming=False):
        device, idx = narrow_peers[k]
        return remote(
            r.bias_row, r.bias_o.at[idx if incoming else n],
            (r.bias_narrow_s.at[k], r.bias_narrow_r.at[k]), device,
        )

    def mod_narrow(k, incoming=False):
        device, idx = narrow_peers[k]
        return remote(
            r.mod_all, r.mod_o.at[idx if incoming else n],
            (r.mod_narrow_s.at[k], r.mod_narrow_r.at[k]), device,
        )

    def lead_back(j, incoming=False):
        return remote(
            r.lead_tx.at[(w + j) % wide], r.lead_back.at[(w - j + wide) % wide if incoming else w],
            (r.lead_back_s.at[j - 1], r.lead_back_r.at[j - 1]), wide_peer(j),
        )

    def lead_narrow(k, incoming=False):
        device, idx = narrow_peers[k]
        return remote(
            r.lead_back, r.lead_g.at[idx if incoming else n],
            (r.lead_narrow_s.at[k], r.lead_narrow_r.at[k]), device,
        )

    for k in range(3):
        quarter_back(k).start()
    own_at = span(LANES * mod_start(tiles, narrow, n), mod_cols, LANES)
    total = r.mod_grad[:, own_at]
    for k in range(3):
        quarter_back(k, True).wait_recv()
        total = total + r.quarter_rx[k]
    r.quarter_sum[...] = folded(total, mod_cols // 2)
    for j in range(1, wide):
        wide_back(j).start()
    r.bias_half[...] = folded(r.bias_grad[...], 5 * LANES)
    for j in range(1, wide):
        bias_wide(j).start()
    r.quarter_all[pl.ds(w, 1)] = r.quarter_sum[...][None]
    r.bias_all[pl.ds(w, 1)] = r.bias_half[...][None]
    grad_planes(OUT, 1)
    grad_send(OUT, 0)
    grad_beside(DOWN, 0)
    grad_planes(QKV, 1)
    grad_send(QKV, 0)
    grad_spread(UP, 1)
    grad_spread(OUT, 1)
    grad_spread(QKV, 1)
    for which in (DOWN, UP, OUT, QKV):
        grad_pass(which, 1)
    grad_join(DOWN, 0)
    grad_beside(UP, 0)
    wait_all(wide_back)
    for j in range(1, wide):
        mod_copy(j).wait_send()
    for row in range(wide):
        r.mod_part[row] = unfolded(r.quarter_all[row], mod_cols)
    r.mod_all[...] = r.mod_part[...].reshape(wide * LAYERS * SEGS, mod_cols).astype(BF16)
    mod_own = pltpu.make_async_copy(r.mod_all, r.mod_o.at[n], r.mod_own_sem)
    mod_own.start()
    for k in range(3):
        mod_narrow(k).start()
    owned = LANES * (mod_start(tiles, narrow, n + 1) - mod_start(tiles, narrow, n))
    lane = lax.broadcasted_iota(jnp.int32, r.mod_all.shape, 1)
    own_grads = jnp.where(lane < owned, r.mod_all[...].astype(F32), 0.0).astype(BF16)
    lead_parts = [dot(own_grads, r.ada_v[layer], ((1,), (1,))) for layer in range(LAYERS)]
    for row in range(wide):
        at = row * LAYERS * SEGS
        r.lead_tx[row] = lead_parts[0][at : at + SEGS] + lead_parts[1][at + SEGS : at + 2 * SEGS]
    for j in range(1, wide):
        lead_back(j).start()
    r.lead_back[pl.ds(w, 1)] = r.lead_tx[pl.ds(w, 1)]
    grad_planes(DOWN, 0)
    grad_spread(DOWN, 0)
    grad_beside(OUT, 0)
    wait_all(bias_wide)
    r.bias_row[...] = unfolded(jnp.sum(r.bias_all[...].astype(F32), 0), width)
    bias_own = pltpu.make_async_copy(r.bias_row, r.bias_o.at[n], r.bias_own_sem)
    bias_own.start()
    for k in range(3):
        bias_narrow(k).start()
    grad_join(UP, 0)
    grad_join(OUT, 0)
    grad_beside(QKV, 0)
    wait_all(lead_back)
    lead_own = pltpu.make_async_copy(r.lead_back, r.lead_g.at[n], r.lead_own_sem)
    lead_own.start()
    for k in range(3):
        lead_narrow(k).start()
    grad_pass(DOWN, 0)
    grad_join(QKV, 0)
    grad_planes(UP, 0)
    grad_spread(UP, 0)
    grad_planes(OUT, 0)
    grad_spread(OUT, 0)
    grad_planes(QKV, 0)
    grad_spread(QKV, 0)
    for which in (UP, OUT, QKV):
        grad_pass(which, 0)

    for layer in range(LAYERS):
        for which in range(4):
            weights_drain(which, layer)
            grad_end(which, layer)
    for j in range(1, wide):
        for copy in (lead_copy, bias_copy, wide_back, bias_wide, lead_back):
            copy(j).wait_send()
    for k in range(3):
        for copy in (quarter_copy, quarter_back, mod_narrow, bias_narrow, lead_narrow):
            copy(k).wait_send()
        mod_narrow(k, True).wait_recv()
        bias_narrow(k, True).wait_recv()
        lead_narrow(k, True).wait_recv()
    mod_own.wait()
    lead_own.wait()
    bias_own.wait()


def gelu_slope(values):
    rate = math.sqrt(2.0 / math.pi)
    bent = jnp.tanh(rate * (values + 0.044715 * values * values * values))
    inner = rate * (1.0 + 3.0 * 0.044715 * values * values)
    return 0.5 * (1.0 + bent) + 0.5 * values * (1.0 - bent * bent) * inner


def chosen_of(cond, index):
    values = cond[...].astype(F32)
    rows = index[...]
    chosen = jnp.zeros(values.shape, F32)
    for k in range(SEGS):
        chosen = jnp.where(rows == k, values[k : k + 1], chosen)
    return chosen


def finish_kernel(cfg, *refs):
    r = SimpleNamespace(**dict(zip(cfg.names, refs)))
    wide, narrow, width, depth, cols = cfg.wide, cfg.narrow, cfg.width, cfg.depth, cfg.cols
    tiles, hidden_own = cfg.tiles, cfg.hidden_own
    w = lax.axis_index("wide")

    for part in range(narrow):
        values = r.qkv_i[0, part].astype(F32)
        for j in range(3):
            at = width * j + cols * part
            r.qkv_g[0, :, at : at + cols] = values[:, cols * j : cols * (j + 1)]
        values = r.up_i[0, part].astype(F32)
        for j in range(wide):
            at = (j * narrow + part) * hidden_own
            r.up_g[0, :, at : at + hidden_own] = values[:, hidden_own * j : hidden_own * (j + 1)]
        at, end = [LANES * mod_start(tiles, narrow, part + k) for k in range(2)]
        r.ada_g[0, :, at:end] = dot(r.lead_i[0], r.mod_i[part, :, : end - at], ((1,), (0,)))
    r.out_g[...] = r.out_i[...].astype(F32)
    r.down_g[...] = r.down_i[...].astype(F32)

    def pick(ref, size):
        start = size * w
        window = LANES * (-(-size // LANES) + 1)
        tile, rest = start // LANES, start % LANES
        values = ref[:, pl.ds(pl.multiple_of(LANES * tile, LANES), window)]
        return pltpu.roll(values, (window - rest) % window, 1)[:, :size]

    @pl.when(pl.program_id(0) + pl.program_id(1) == 0)
    def _():
        for part in range(narrow):
            values = r.bias_i[part]
            for j in range(3):
                at = width * j + cols * part
                r.qkv_t[:, at : at + cols] = values[:, cols * j : cols * (j + 1)]
            for j in range(wide):
                at = (j * narrow + part) * hidden_own
                r.up_t[:, at : at + hidden_own] = values[:, hidden_own * j : hidden_own * (j + 1)]
            at, end = [LANES * mod_start(tiles, narrow, part + k) for k in range(2)]
            values = r.mod_i[part, :, : end - at].astype(F32)
            layer_of = lax.broadcasted_iota(jnp.int32, values.shape, 0) // SEGS % LAYERS
            for layer in range(LAYERS):
                sums = jnp.sum(jnp.where(layer_of == layer, values, 0.0), 0, keepdims=True)
                r.ada_t[layer : layer + 1, at:end] = sums
        r.row_t[:, :width] = jnp.sum(r.bias_i[...], 0)
        for dst, ref, line, step in (
            (r.ada_bg, r.ada_t, 0, 1), (r.qkv_bg, r.qkv_t, QKV, 4), (r.out_bg, r.row_t, OUT, 4),
            (r.up_bg, r.up_t, UP, 4), (r.down_bg, r.row_t, DOWN, 4),
        ):
            values = pick(ref, dst.shape[1])
            for layer in range(LAYERS):
                at = step * layer + line
                dst[layer : layer + 1, :] = values[at : at + 1]
        chosen = chosen_of(r.cond, r.cond_index)
        gate = jax.nn.sigmoid(chosen)
        slope = gate * (1.0 + chosen * (1.0 - gate))
        lead_grad = jnp.sum(r.lead_i2[...], 0)
        for row in range(wide):
            at = slice(depth * row, depth * (row + 1))
            grad = lead_grad[row] * slope[:, at]
            for k in range(SEGS):
                r.cond_g[k : k + 1, at] = jnp.sum(
                    jnp.where(r.cond_index[...] == k, grad, 0.0), 0, keepdims=True
                )


def finish(wide, narrow, got, cond, cond_index, tiles, mod_cols, w):
    width = cond.shape[1]
    depth, cols = width // wide, width // narrow
    hidden_own = got["up_o"].shape[-1] // wide
    hidden_all = got["up_o"].shape[-1] * narrow
    down_rows = narrow * hidden_own
    bands = depth // 48
    rows = depth // bands
    shape, vmem = jax.ShapeDtypeStruct, pltpu.VMEM

    def whole(values):
        return pl.BlockSpec(values.shape, lambda i, j: (0,) * values.ndim)

    def band(*dims):
        return pl.BlockSpec(
            (1, *dims), lambda i, j: (i, 0, j, 0) if len(dims) == 3 else (i, j, 0)
        )

    down_i = got["down_o"].reshape(LAYERS, down_rows, width)
    inputs = dict(
        qkv_i=got["qkv_o"], up_i=got["up_o"], out_i=got["out_o"], down_i=down_i,
        lead_i=got["lead_o"], mod_i=got["mod_o"], bias_i=got["bias_o"], lead_i2=got["lead_g"],
        cond=cond, cond_index=cond_index,
    )
    in_specs = [
        band(narrow, rows, 3 * cols), band(narrow, rows, wide * hidden_own), band(rows, width),
        band(down_rows // bands, width), band(rows, got["lead_o"].shape[-1]),
        *[whole(inputs[name]) for name in ("mod_i", "bias_i", "lead_i2", "cond", "cond_index")],
    ]
    outputs = dict(
        ada_g=shape((LAYERS, depth, tiles * LANES), F32), qkv_g=shape((LAYERS, depth, 3 * width), F32),
        out_g=shape((LAYERS, depth, width), F32), up_g=shape((LAYERS, depth, hidden_all), F32),
        down_g=shape((LAYERS, down_rows, width), F32),
        ada_bg=shape((LAYERS, tiles * LANES // wide), F32), qkv_bg=shape((LAYERS, 3 * width // wide), F32),
        out_bg=shape((LAYERS, depth), F32), up_bg=shape((LAYERS, hidden_all // wide), F32),
        down_bg=shape((LAYERS, depth), F32), cond_g=shape((SEGS, width), F32),
    )
    out_specs = [
        band(rows, tiles * LANES), band(rows, 3 * width), band(rows, width), band(rows, hidden_all),
        band(down_rows // bands, width),
        *[whole(outputs[name]) for name in ("ada_bg", "qkv_bg", "out_bg", "up_bg", "down_bg", "cond_g")],
    ]
    scratch = dict(
        ada_t=vmem((8, (tiles + 2) * LANES), F32), qkv_t=vmem((8, 3 * width + 2 * LANES), F32),
        up_t=vmem((8, hidden_all + 2 * LANES), F32), row_t=vmem((8, width + 2 * LANES), F32),
    )
    cfg = SimpleNamespace(
        names=[*inputs, *outputs, *scratch], wide=wide, narrow=narrow, width=width, depth=depth,
        cols=cols, tiles=tiles, hidden_own=hidden_own,
    )
    results = pl.pallas_call(
        partial(finish_kernel, cfg),
        grid=(LAYERS, bands),
        out_shape=list(outputs.values()), in_specs=in_specs, out_specs=out_specs,
        scratch_shapes=list(scratch.values()),
        compiler_params=pltpu.CompilerParams(vmem_limit_bytes=62 * 2**20),
    )(*inputs.values())
    done = dict(zip(outputs, results))
    out = [got["mixed_o"][None], got["token_o"][None], done["cond_g"][None]]
    for name in ("ada", "qkv", "out", "up", "down"):
        out += [done[name + "_g"], done[name + "_bg"]]
    return tuple(out)


def fused_device(
    wide, narrow,
    tokens, cond, seg_ids, cond_index, cotangent,
    ada_weight, ada_bias, qkv_weight, qkv_bias, out_weight, out_bias,
    up_weight, up_bias, down_weight, down_bias,
):
    w = lax.axis_index("wide")
    n = lax.axis_index("narrow")
    local, width = tokens.shape[1:]
    row_len = seg_ids.shape[1]
    depth, cols = width // wide, width // narrow
    hidden_own = up_weight.shape[-1] // wide // narrow
    hidden = wide * hidden_own
    tiles = ada_weight.shape[-1] // LANES
    mod_cols = LANES * -(-tiles // narrow)

    inputs = dict(
        tok=tokens[0], cond=cond[0], cond_index=cond_index.reshape(SEGS, 1), seg_row=seg_ids,
        cot=cotangent[0], ada_b=ada_bias, qkv_b=qkv_bias, out_b=out_bias, up_b=up_bias, down_b=down_bias,
        ada=ada_weight, qkv_w=qkv_weight, out_w=out_weight, up_w=up_weight, down_w=down_weight,
    )
    in_hbm = ("ada", "qkv_w", "out_w", "up_w", "down_w")
    shape = jax.ShapeDtypeStruct
    outputs = dict(
        mixed_o=shape((local, width), BF16), token_o=shape((local, width), F32),
        qkv_o=shape((LAYERS, narrow, depth, 3 * cols), BF16),
        out_o=shape((LAYERS, depth, width), BF16),
        up_o=shape((LAYERS, narrow, depth, hidden), BF16),
        down_o=shape((LAYERS, narrow, hidden_own, width), BF16),
        bias_o=shape((narrow, 4 * LAYERS, width), F32),
        mod_o=shape((narrow, wide * LAYERS * SEGS, mod_cols), BF16),
        lead_o=shape((LAYERS, depth, wide * LAYERS * SEGS), BF16),
        lead_g=shape((narrow, wide, SEGS, depth), F32),
        qkv_h=shape((LAYERS, width, 3 * cols), BF16), out_h=shape((LAYERS, cols, width), BF16),
        up_h=shape((LAYERS, width, hidden), BF16), down_h=shape((LAYERS, hidden, width), BF16),
    )
    out_vmem = ("mixed_o", "token_o", "lead_o")
    vmem, dma = pltpu.VMEM, pltpu.SemaphoreType.DMA
    heads = cols // HEAD
    scratch = dict(
        qkv_v=vmem((width, 3 * cols), BF16), out_v=vmem((cols, width), BF16),
        up_v=vmem((width, hidden), BF16), down_v=vmem((hidden, width), BF16),
        hid_attn=vmem((LAYERS, row_len, width), BF16), hid_mlp=vmem((LAYERS, row_len, width), BF16),
        heads=vmem((LAYERS, 3 * heads, row_len, LANES), BF16),
        mixed=vmem((LAYERS, row_len, cols), BF16), log_sum=vmem((LAYERS, row_len, heads), F32),
        up=vmem((LAYERS, row_len, hidden), BF16), act=vmem((LAYERS, row_len, hidden), BF16),
        state=vmem((local, width), F32), middle=vmem((LAYERS, local, width), F32),
        branch=vmem((LAYERS, local, width), BF16), down=vmem((LAYERS, local, width), BF16),
        grad_hid=vmem((local, width), F32),
        grad_down=vmem((row_len, width), BF16), grad_branch=vmem((row_len, width), BF16),
        grad_up=vmem((row_len, hidden), BF16), grad_qkv=vmem((row_len, 3 * cols), BF16),
        grad_heads=vmem((heads, row_len, LANES), BF16),
        part=vmem((2, 2 * local, width), F32),
        core_tx=vmem((2, local, width), BF16), core_rx=vmem((2, local, width), BF16),
        side_tx=vmem((local, width), BF16), side_rx=vmem((local, width), BF16),
        ada_v=vmem((LAYERS, depth, mod_cols), BF16),
        lead=vmem((wide, 16, depth), BF16), lead_rx=vmem((wide, 16, depth), BF16),
        bias_rows=vmem((32, 3 * LANES), F32), bias_tx=vmem((32, 3 * LANES), BF16),
        bias_rx=vmem((wide, 32, 3 * LANES), BF16),
        ada_full=vmem((1, LAYERS, tiles * LANES), F32), qkv_full=vmem((1, LAYERS, 3 * width), F32),
        out_full=vmem((1, LAYERS, width), F32), up_full=vmem((1, LAYERS, narrow * hidden), F32),
        down_full=vmem((1, LAYERS, width), F32), seg_col=vmem((row_len, 1), jnp.int32),
        qkv_raw=vmem((LAYERS, 3, depth, 3 * LANES), BF16), up_raw=vmem((LAYERS, wide, depth, 2 * LANES), BF16),
        qkv_s=vmem((LAYERS, depth, 3 * cols), BF16), up_s=vmem((LAYERS, depth, hidden), BF16),
        lead_t=vmem((LAYERS, wide * LAYERS * SEGS, depth), F32),
        lead_tx=vmem((wide, SEGS, depth), F32), lead_back=vmem((wide, SEGS, depth), F32),
        bias_sum=vmem((4 * LAYERS, width), F32),
        mod_part=vmem((wide, LAYERS * SEGS, mod_cols), F32),
        mod_rx=vmem((wide, LAYERS * SEGS, mod_cols), F32),
        mod_q=vmem((narrow, LAYERS * SEGS, mod_cols), F32),
        mods=vmem((LAYERS * SEGS, tiles * LANES), F32),
        mod_grad=vmem((LAYERS * SEGS, tiles * LANES), F32),
        quarter_rx=vmem((3, LAYERS * SEGS, mod_cols), F32),
        quarter_sum=vmem((16, mod_cols // 2), BF16),
        quarter_all=vmem((wide, 16, mod_cols // 2), BF16),
        mod_all=vmem((wide * LAYERS * SEGS, mod_cols), BF16),
        bias_grad=vmem((4 * LAYERS, width), F32), bias_all=vmem((wide, 16, 5 * LANES), BF16),
        bias_half=vmem((16, 5 * LANES), BF16),
        bias_row=vmem((4 * LAYERS, width), F32),
        qkv_d=vmem((width, 3 * cols), BF16), out_d=vmem((cols, width), BF16),
        up_d=vmem((width, hidden), BF16), down_d=vmem((hidden, width), BF16),
        qkv_xr=vmem((PLANES, depth, 3 * cols), BF16), out_xr=vmem((1, depth, width), BF16),
        up_xr=vmem((PLANES, depth, hidden), BF16), down_xr=vmem((PLANES, hidden_own, width), BF16),
        qkv_zr=vmem((PLANES, depth, 3 * cols), BF16), out_zr=vmem((PLANES, depth, width), BF16),
        up_zr=vmem((PLANES, depth, hidden), BF16), down_zr=vmem((PLANES, hidden_own, width), BF16),
        qkv_f=vmem((depth, 3 * cols), BF16), out_f=vmem((depth, width), BF16),
        up_f=vmem((depth, hidden), BF16), down_f=vmem((hidden_own, width), BF16),
        wz_s=dma((9, 4)), wz_r=dma((9, 4)), wx_s=dma((8, 4)), wx_r=dma((8, 4)), w_own=dma((8,)),
        load_sem=dma((4,)), tok_s=dma((12,)), tok_r=dma((12,)), sum_s=dma((4,)), sum_r=dma((4,)),
        lead_sem_s=dma((wide - 1,)), lead_sem_r=dma((wide - 1,)),
        bias_sem_s=dma((wide - 1,)), bias_sem_r=dma((wide - 1,)),
        mod_sem_s=dma((wide - 1,)), mod_sem_r=dma((wide - 1,)),
        quarter_s=dma((3,)), quarter_r=dma((3,)), ada_sem=dma, raw_sem=dma((LAYERS, 3 + wide)), lead_own_sem=dma,
        lead_back_s=dma((wide - 1,)), lead_back_r=dma((wide - 1,)),
        lead_narrow_s=dma((3,)), lead_narrow_r=dma((3,)),
        dx_s=dma((4, 4)), dx_r=dma((4, 4)), dz_s=dma((4, 3)), dz_r=dma((4, 4)),
        e_s=dma((2, 3)), e_r=dma((2, 4)), ex_s=dma, ex_r=dma,
        down_e=vmem((hidden_own, width), BF16),
        spread_s=dma((8, 3)), spread_r=dma((8, 3)), spread_l=dma((8,)),
        back_s=dma((3,)), back_r=dma((3,)),
        wide_s=dma((wide - 1,)), wide_r=dma((wide - 1,)),
        bias_wide_s=dma((wide - 1,)), bias_wide_r=dma((wide - 1,)),
        bias_narrow_s=dma((3,)), bias_narrow_r=dma((3,)),
        mod_narrow_s=dma((3,)), mod_narrow_r=dma((3,)), mod_own_sem=dma, bias_own_sem=dma,
        credit_x=pltpu.SemaphoreType.REGULAR((4,)), credit_z=pltpu.SemaphoreType.REGULAR((4, 2)),
        credit_sum=pltpu.SemaphoreType.REGULAR((2,)),
    )
    cfg = SimpleNamespace(
        names=[*inputs, *outputs, *scratch], wide=wide, narrow=narrow, width=width, depth=depth,
        local=local, cols=cols, mod_cols=mod_cols, tiles=tiles,
    )

    def place(name, vmem_ok):
        return pl.BlockSpec(memory_space=pltpu.VMEM if vmem_ok else pl.ANY)

    results = pl.pallas_call(
        partial(block_kernel, cfg),
        out_shape=list(outputs.values()),
        in_specs=[place(name, name not in in_hbm) for name in inputs],
        out_specs=[place(name, name in out_vmem) for name in outputs],
        scratch_shapes=list(scratch.values()),
        compiler_params=pltpu.CompilerParams(
            collective_id=0, has_side_effects=True, vmem_limit_bytes=63 * 2**20
        ),
    )(*inputs.values())
    got = dict(zip(outputs, results))

    return finish(wide, narrow, got, cond[0], inputs["cond_index"], tiles, mod_cols, w)


def solution(mesh):
    matrix, vector = P(None, "wide", None), P(None, "wide")
    rows, cond_rows = P("wide", "narrow", None), P("wide", None, None)
    wide, narrow = mesh.shape["wide"], mesh.shape["narrow"]
    fused = wide == PLANES * PAIR and narrow == PLANES
    return jax.shard_map(
        partial(fused_device if fused else plain_device, wide, narrow),
        mesh=mesh,
        in_specs=(rows, cond_rows, P("wide", None), P("wide", None), rows) + (matrix, vector) * 5,
        out_specs=(rows, rows, cond_rows) + (matrix, vector) * 5,
        check_vma=False,
    )
```

```python
from functools import partial
import math
from types import SimpleNamespace

import jax
import jax.numpy as jnp
from jax import lax
from jax.experimental import pallas as pl
from jax.experimental.pallas import tpu as pltpu
from jax.sharding import PartitionSpec as P

HEADS = 16
HEAD = 72
LAYERS = 2
SEGS = 4
EPS = 1e-06
EXACT = lax.Precision.HIGHEST
F32 = jnp.float32
BF16 = jnp.bfloat16


def dot(left, right, dims):
    return lax.dot_general(left, right, (dims, ((), ())), preferred_element_type=F32)


def norm(values):
    centred = values - jnp.mean(values, -1, keepdims=True)
    inv = lax.rsqrt(jnp.mean(centred * centred, -1, keepdims=True) + EPS)
    return centred * inv, inv


def norm_back(grad, unit, inv):
    return inv * (
        grad
        - jnp.mean(grad, -1, keepdims=True)
        - unit * jnp.mean(grad * unit, -1, keepdims=True)
    )


def gather_tokens(values):
    return lax.all_gather(values, "narrow", axis=0, tiled=True)


def scatter_tokens(values):
    return lax.psum_scatter(
        values.astype(BF16), "narrow", scatter_dimension=0, tiled=True
    ).astype(F32)


def gelu(values):
    return jax.nn.gelu(values, approximate=True)


def layer_forward(state, mods, same_seg, weights):
    qkv_w, qkv_b, out_w, out_b, up_w, up_b, down_w, down_b = weights
    shift_attn, scale_attn, gate_attn, shift_mlp, scale_mlp, gate_mlp = mods
    own_heads = out_w.shape[0] // HEAD
    unit_attn, inv_attn = norm(state)
    hidden_attn = gather_tokens((unit_attn * (1.0 + scale_attn) + shift_attn).astype(BF16))
    full_len = hidden_attn.shape[0]
    qkv = (dot(hidden_attn, qkv_w, ((1,), (0,))) + qkv_b).astype(BF16)
    queries, keys, values = [
        part.reshape(full_len, own_heads, HEAD) for part in jnp.split(qkv, 3, axis=-1)
    ]
    scores = jnp.einsum("qhe,khe->hqk", queries, keys, preferred_element_type=F32) * (
        1.0 / math.sqrt(HEAD)
    )
    probs = jax.nn.softmax(jnp.where(same_seg[None], scores, -1e30), axis=-1)
    mixed = jnp.einsum("hqk,khe->qhe", probs.astype(BF16), values, preferred_element_type=F32)
    mixed = mixed.reshape(full_len, own_heads * HEAD).astype(BF16)
    branch = scatter_tokens(dot(mixed, out_w, ((1,), (0,)))) + out_b
    middle = state + gate_attn * branch
    unit_mlp, inv_mlp = norm(middle)
    hidden_mlp = gather_tokens((unit_mlp * (1.0 + scale_mlp) + shift_mlp).astype(BF16))
    up_proj = dot(hidden_mlp, up_w, ((1,), (0,))) + up_b
    activated = gelu(up_proj).astype(BF16)
    down_proj = scatter_tokens(dot(activated, down_w, ((1,), (0,)))) + down_b
    result = middle + gate_mlp * down_proj
    kept = (
        unit_attn, inv_attn, hidden_attn, queries, keys, values, probs, mixed, branch,
        unit_mlp, inv_mlp, hidden_mlp, up_proj, activated, down_proj,
    )
    return result, kept


def layer_backward(grad_out, kept, mods, weights):
    qkv_w, qkv_b, out_w, out_b, up_w, up_b, down_w, down_b = weights
    shift_attn, scale_attn, gate_attn, shift_mlp, scale_mlp, gate_mlp = mods
    (
        unit_attn, inv_attn, hidden_attn, queries, keys, values, probs, mixed, branch,
        unit_mlp, inv_mlp, hidden_mlp, up_proj, activated, down_proj,
    ) = kept
    scale_inv = 1.0 / math.sqrt(HEAD)
    full_len = hidden_attn.shape[0]
    own_down = (gate_mlp * grad_out).astype(BF16)
    grad_gate_mlp = down_proj * grad_out
    grad_down = gather_tokens(own_down)
    grad_act = dot(grad_down, down_w, ((1,), (1,)))
    grad_up = jax.vjp(gelu, up_proj)[1](grad_act)[0].astype(BF16)
    grad_hidden_mlp = scatter_tokens(dot(grad_up, up_w, ((1,), (1,))))
    grad_down_w = dot(activated, grad_down, ((0,), (0,)))
    grad_up_w = dot(hidden_mlp, grad_up, ((0,), (0,)))
    grad_middle = grad_out + norm_back(grad_hidden_mlp * (1.0 + scale_mlp), unit_mlp, inv_mlp)
    own_branch = (gate_attn * grad_middle).astype(BF16)
    grad_gate_attn = branch * grad_middle
    grad_branch = gather_tokens(own_branch)
    grad_attn = dot(grad_branch, out_w, ((1,), (1,))).astype(BF16).reshape(queries.shape)
    grad_probs = jnp.einsum("qhe,khe->hqk", grad_attn, values, preferred_element_type=F32)
    grad_scores = probs * (grad_probs - jnp.sum(probs * grad_probs, -1, keepdims=True))
    grad_scores = grad_scores.astype(BF16)
    grad_q = jnp.einsum("hqk,khe->qhe", grad_scores, keys, preferred_element_type=F32) * scale_inv
    grad_k = jnp.einsum("hqk,qhe->khe", grad_scores, queries, preferred_element_type=F32) * scale_inv
    grad_v = jnp.einsum("hqk,qhe->khe", probs.astype(BF16), grad_attn, preferred_element_type=F32)
    grad_qkv = jnp.concatenate(
        [part.astype(BF16).reshape(full_len, -1) for part in (grad_q, grad_k, grad_v)], axis=-1
    )
    grad_hidden_attn = scatter_tokens(dot(grad_qkv, qkv_w, ((1,), (1,))))
    grad_out_w = dot(mixed, grad_branch, ((0,), (0,)))
    grad_qkv_w = dot(hidden_attn, grad_qkv, ((0,), (0,)))
    grad_state = grad_middle + norm_back(grad_hidden_attn * (1.0 + scale_attn), unit_attn, inv_attn)
    token_mod = jnp.concatenate(
        [
            grad_hidden_attn, grad_hidden_attn * unit_attn, grad_gate_attn,
            grad_hidden_mlp, grad_hidden_mlp * unit_mlp, grad_gate_mlp,
        ],
        axis=-1,
    )
    bias_grads = (
        jnp.sum(grad_qkv.astype(F32), 0),
        jnp.sum(own_branch.astype(F32), 0),
        jnp.sum(grad_up.astype(F32), 0),
        jnp.sum(own_down.astype(F32), 0),
    )
    return grad_state, token_mod, (grad_qkv_w, grad_out_w, grad_up_w, grad_down_w), bias_grads


def plain_device(
    wide, narrow,
    tokens, cond, seg_ids, cond_index, cotangent,
    ada_weight, ada_bias, qkv_weight, qkv_bias, out_weight, out_bias,
    up_weight, up_bias, down_weight, down_bias,
):
    w = lax.axis_index("wide")
    n = lax.axis_index("narrow")
    local_len, width = tokens.shape[1:]
    depth = width // wide
    cols = width // narrow
    hidden_own = up_weight.shape[-1] // wide // narrow
    mod_cols = ada_weight.shape[-1] // narrow

    def own(values, axis):
        return lax.dynamic_index_in_dim(values, n, axis, keepdims=False)

    bias_parts = (ada_bias, qkv_bias, out_bias, up_bias, down_bias)
    sizes = [part.shape[1] for part in bias_parts]
    packed = lax.all_gather(jnp.concatenate(bias_parts, axis=1), "wide", axis=1, tiled=False)
    biases = []
    at = 0
    for size in sizes:
        biases.append(packed[:, :, at : at + size].reshape(LAYERS, -1).astype(F32))
        at += size
    ada_b, qkv_b, out_b, up_b, down_b = biases
    qkv_b = own(qkv_b.reshape(LAYERS, 3, narrow, cols), 2).reshape(LAYERS, 3 * cols)
    up_b = own(up_b.reshape(LAYERS, wide, narrow, hidden_own), 2).reshape(LAYERS, -1)

    cond_hot = (cond_index[0, :, None] == jnp.arange(SEGS, dtype=jnp.int32)[None, :]).astype(F32)
    chosen = jnp.dot(cond_hot, cond[0].astype(F32), precision=EXACT)
    lead = (chosen * jax.nn.sigmoid(chosen)).astype(BF16)
    lead_all = lax.all_gather(lead, "wide", axis=0, tiled=True)
    lead_own = lax.dynamic_slice_in_dim(lead_all, w * depth, depth, 1)
    ada_quarter = lax.dynamic_slice_in_dim(ada_weight, n * mod_cols, mod_cols, 2)
    mod_part = jnp.einsum("nd,lde->nle", lead_own, ada_quarter, preferred_element_type=F32)
    mod_part = lax.psum_scatter(mod_part, "wide", scatter_dimension=0, tiled=True)
    modulation = lax.all_gather(mod_part, "narrow", axis=2, tiled=True)
    modulation = modulation.transpose(1, 0, 2) + ada_b[:, None, :]

    seg_row = seg_ids[0]
    seg_query = lax.dynamic_slice_in_dim(seg_row, n * local_len, local_len, 0)
    token_hot = (seg_query[:, None] == jnp.arange(SEGS, dtype=jnp.int32)[None, :]).astype(F32)
    same_seg = seg_row[:, None] == seg_row[None, :]

    qkv_own = own(qkv_weight.reshape(LAYERS, depth, 3, narrow, cols), 3).reshape(LAYERS, depth, 3 * cols)
    up_own = own(up_weight.reshape(LAYERS, depth, wide, narrow, hidden_own), 3).reshape(LAYERS, depth, -1)
    down_own = own(down_weight.reshape(LAYERS, narrow, hidden_own, width), 1)

    def fetch(idx):
        out_full = lax.all_gather(out_weight[idx], "wide", axis=0, tiled=True)
        return (
            lax.all_gather(qkv_own[idx], "wide", axis=0, tiled=True),
            qkv_b[idx],
            lax.dynamic_slice_in_dim(out_full, n * cols, cols, 0),
            out_b[idx],
            lax.all_gather(up_own[idx], "wide", axis=0, tiled=True),
            up_b[idx],
            lax.all_gather(down_own[idx], "wide", axis=0, tiled=True),
            down_b[idx],
        )

    state = tokens[0].astype(F32)
    weights, mods, kept = [], [], []
    for idx in range(LAYERS):
        weights.append(fetch(idx))
        per_token = jnp.dot(token_hot, modulation[idx], precision=EXACT)
        mods.append(jnp.split(per_token, 6, axis=-1))
        state, saved = layer_forward(state, mods[idx], same_seg, weights[idx])
        kept.append(saved)
    result = state.astype(BF16)

    grad_state = cotangent[0].astype(F32)
    token_hot_t = token_hot.T
    reduced, bias_sums, mod_grads = [None] * LAYERS, [None] * LAYERS, [None] * LAYERS
    for idx in reversed(range(LAYERS)):
        grad_state, token_mod, grads, bias_grads = layer_backward(
            grad_state, kept[idx], mods[idx], weights[idx]
        )
        mod_grads[idx] = jnp.dot(token_hot_t, token_mod, precision=EXACT)
        qkv_g, out_g, up_g, down_g = [item.astype(BF16) for item in grads]
        qkv_g, up_g, down_g = [
            lax.psum_scatter(item, "wide", scatter_dimension=0, tiled=True)
            for item in (qkv_g, up_g, down_g)
        ]
        out_g = lax.psum(out_g, "wide")
        qkv_g = lax.all_gather(qkv_g.reshape(depth, 3, 1, cols), "narrow", axis=2, tiled=True)
        up_g = lax.all_gather(up_g.reshape(depth, wide, 1, hidden_own), "narrow", axis=2, tiled=True)
        down_g = lax.all_gather(down_g, "narrow", axis=0, tiled=True)
        out_g = lax.all_gather(out_g, "narrow", axis=0, tiled=True)
        out_g = lax.dynamic_slice_in_dim(out_g, w * depth, depth, 0)
        reduced[idx] = (
            qkv_g.reshape(depth, 3 * width),
            out_g,
            up_g.reshape(depth, -1),
            down_g,
        )
        spot = lax.broadcasted_iota(jnp.int32, (1, narrow, 1), 1) == n
        qkv_s = jnp.where(spot, bias_grads[0].reshape(3, 1, cols), 0.0).reshape(-1)
        up_s = jnp.where(spot, bias_grads[2].reshape(wide, 1, hidden_own), 0.0).reshape(-1)
        bias_sums[idx] = [
            item.reshape(wide, -1) for item in (qkv_s, bias_grads[1], up_s, bias_grads[3])
        ]
    sizes = [item.shape[1] for item in bias_sums[0]]
    bias_sum = jnp.stack([jnp.concatenate(item, axis=1) for item in bias_sums], axis=1)
    bias_sum = lax.psum_scatter(lax.psum(bias_sum, "narrow"), "wide", scatter_dimension=0, tiled=True)[0]
    bias_out = []
    at = 0
    for size in sizes:
        bias_out.append(bias_sum[:, at : at + size])
        at += size

    mod_grad = lax.psum(jnp.stack(mod_grads), "narrow").astype(BF16)
    mod_all = lax.all_gather(mod_grad, "wide", axis=1, tiled=True)
    ada_grad = jnp.einsum("nd,lne->lde", lead_own, mod_all, preferred_element_type=F32)
    ada_size = ada_bias.shape[1]
    ada_bias_grad = jnp.sum(
        lax.dynamic_slice_in_dim(mod_all, w * ada_size, ada_size, 2).astype(F32), axis=1
    )
    lead_grad = jnp.einsum("lne,lde->nd", mod_all, ada_weight, preferred_element_type=F32)
    lead_grad = lax.all_to_all(lead_grad.reshape(wide, SEGS, depth), "wide", 0, 0, tiled=False)
    lead_grad = lead_grad.transpose(1, 0, 2).reshape(SEGS, width)
    gate = jax.nn.sigmoid(chosen)
    chosen_grad = lead_grad * (gate * (1.0 + chosen * (1.0 - gate)))
    cond_grad = jnp.dot(cond_hot.T, chosen_grad, precision=EXACT)

    stacked = [
        jnp.stack([reduced[idx][pos].astype(F32) for idx in range(LAYERS)]) for pos in range(4)
    ]
    return (
        result[None], grad_state[None], cond_grad[None],
        ada_grad, ada_bias_grad,
        stacked[0], bias_out[0], stacked[1], bias_out[1],
        stacked[2], bias_out[2], stacked[3], bias_out[3],
    )


QKV, OUT, UP, DOWN = range(4)
PLANES = 4
PAIR = 2
LANES = 128
STEP = 32
MESH = pl.DeviceIdType.MESH


def mod_start(tiles, parts, part):
    return tiles * part // parts


def block_kernel(cfg, *refs):
    r = SimpleNamespace(**dict(zip(cfg.names, refs)))
    wide, narrow, width, depth = cfg.wide, cfg.narrow, cfg.width, cfg.depth
    local, cols, mod_cols, tiles = cfg.local, cfg.cols, cfg.mod_cols, cfg.tiles
    half = local // 2
    own_heads = cols // HEAD
    scale_inv = 1.0 / math.sqrt(HEAD)
    w = lax.axis_index("wide")
    n = lax.axis_index("narrow")
    z, x = w // PAIR, w % PAIR
    y, c = n // 2, n % 2
    n_core = n + 1 - 2 * c
    n_side = n + 2 - 4 * y
    n_far = 3 - n
    core, side, far = (w, n_core), (w, n_side), (w, n_far)
    beside = (w + 1 - 2 * x, n)

    z_half = z // 2
    z_partner, z_inner, z_outer = z + 1 - 2 * (z % 2), 2 - z_half, 3 - 3 * z_half
    is_inner = jnp.logical_or(z == 1, z == 2)

    def at_plane(idx):
        return (idx * PAIR + x, n)

    def wide_peer(j):
        return ((w + j) % wide, n)

    def remote(src, dst, sems, device):
        return pltpu.make_async_remote_copy(
            src_ref=src, dst_ref=dst, send_sem=sems[0], recv_sem=sems[1],
            device_id=device, device_id_type=MESH,
        )

    def span(start, size, step=16):
        return pl.ds(pl.multiple_of(start, step), size)

    ada_load = pltpu.make_async_copy(
        r.ada.at[:, :, span(LANES * mod_start(tiles, narrow, n), mod_cols, LANES)], r.ada_v, r.ada_sem
    )
    hidden_own = r.up_w.shape[-1] // wide // narrow

    def windows(which):
        if which == QKV:
            return [(width * j + cols * n, cols, 3 * LANES) for j in range(3)]
        return [((j * narrow + n) * hidden_own, hidden_own, 2 * LANES) for j in range(wide)]

    def raw(which, layer, k):
        src, dst = ((r.qkv_w, r.qkv_raw), (r.up_w, r.up_raw))[which == UP]
        start, _, window = windows(which)[k]
        at = span(LANES * (start // LANES), window, LANES)
        return pltpu.make_async_copy(
            src.at[layer, :, at], dst.at[layer, k], r.raw_sem.at[layer, k + 3 * (which == UP)]
        )

    for layer in range(LAYERS):
        for which in (QKV, UP):
            for k in range(len(windows(which))):
                raw(which, layer, k).start()
        if layer == 0:
            ada_load.start()
    chosen = chosen_of(r.cond, r.cond_index)
    lead = (chosen * jax.nn.sigmoid(chosen)).astype(BF16).astype(F32)
    r.lead[...] = jnp.zeros_like(r.lead)
    for row in range(wide):
        tile = jnp.concatenate(
            [lead[:, depth * row : depth * (row + 1)], jnp.zeros((16 - SEGS, depth), F32)], 0
        )
        r.lead[row] = tile.astype(BF16)
    bias_refs = (r.ada_b, r.qkv_b, r.out_b, r.up_b, r.down_b)
    bias_places, row = [], 0
    for k, ref in enumerate(bias_refs):
        for start in range(0, ref.shape[1], 3 * LANES):
            size = min(3 * LANES, ref.shape[1] - start)
            bias_places.append((k, row, start, size))
            row += 1
    r.bias_rows[...] = jnp.zeros_like(r.bias_rows)
    for layer in range(LAYERS):
        for k, row, start, size in bias_places:
            line = r.bias_rows.shape[0] // LAYERS * layer + row
            values = bias_refs[k][...].astype(F32)[layer : layer + 1, start : start + size]
            r.bias_rows[line : line + 1, :size] = values
    r.bias_tx[...] = r.bias_rows[...].astype(BF16)

    barrier = pltpu.get_barrier_semaphore()
    partners = [core, side, far] + [wide_peer(j) for j in range(1, wide)]
    for partner in partners:
        pl.semaphore_signal(barrier, inc=1, device_id=partner, device_id_type=MESH)
    pl.semaphore_wait(barrier, len(partners))

    full = (r.qkv_h, r.out_h, r.up_h, r.down_h)
    loaded = (r.qkv_v, r.out_v, r.up_v, r.down_v)

    def shard(which, layer):
        if which == DOWN:
            return r.down_w.at[layer, span(depth * n, depth)]
        return (r.qkv_s, r.out_w, r.up_s)[which].at[layer]

    def w_rows(which, plane_idx, col):
        if which == OUT:
            return span(col * depth, depth)
        return span((plane_idx * PAIR + col) * depth, depth)

    def w_block(which, layer, plane_idx, col):
        return full[which].at[layer, w_rows(which, plane_idx, col)]

    def w_z(which, layer, kind, plane_idx, own=False):
        slot = layer * 4 + which
        block = w_block(which, layer, plane_idx, x)
        return remote(
            shard(which, layer) if own else block, block,
            (r.wz_s.at[slot, kind], r.wz_r.at[slot, plane_idx]),
            at_plane(z_inner if kind == 1 else z_partner),
        )

    def w_x(which, layer, plane_idx, col, own=False):
        slot = layer * 4 + which
        block = w_block(which, layer, plane_idx, col)
        return remote(
            shard(which, layer) if own else block, block,
            (r.wx_s.at[slot, plane_idx], r.wx_r.at[slot, plane_idx]), beside,
        )

    def w_own(which, layer):
        return pltpu.make_async_copy(
            shard(which, layer), w_block(which, layer, z, x), r.w_own.at[layer * 4 + which]
        )

    def weights_beside(which, layer):
        w_x(which, layer, z, x, True).start()
        w_own(which, layer).start()

    def weights_along(which, layer):
        w_z(which, layer, 1, z, True).start()
        w_z(which, layer, 0, z, True).start()

    early, early_outer = ((UP, 0), (DOWN, 0)), ((QKV, 1), (UP, 1))

    def weights_start(which, layer):
        def go():
            weights_along(which, layer)
            if (which, layer) in early_outer:
                pl.when(is_inner)(lambda: weights_beside(which, layer))
            elif (which, layer) not in early:
                weights_beside(which, layer)

        if which == OUT:
            pl.when(z == n)(go)
        else:
            go()

    passes_out = jnp.logical_and(is_inner, z_half != n // 2)

    def weights_steps(which, layer):
        def passed(plane_idx, kind):
            w_z(which, layer, 0, plane_idx).wait_recv()
            if kind:
                onward = passes_out if which == OUT else is_inner
                pl.when(onward)(lambda: w_z(which, layer, kind, plane_idx).start())
            w_x(which, layer, plane_idx, x).start()

        def ahead():
            slot = layer * 4 + which + 2
            if 2 < slot < 4 * LAYERS:
                weights_start(slot % 4, slot // 4)

        def step(plane_idx, kind):
            if kind == 0:
                ahead()
            passed(plane_idx, kind)

        def only():
            ahead()
            pl.when(z != n)(lambda: passed(n, 2))

        if which == OUT:
            return [only]
        return [
            partial(step, idx, kind) for idx, kind in ((z_partner, 0), (z_inner, 2), (z_outer, 3))
        ]

    steps = [
        (layer * 4 + which, step)
        for layer in range(LAYERS)
        for which in (QKV, OUT, UP, DOWN)
        for step in weights_steps(which, layer)
    ]

    def pump(count):
        for _ in range(min(count, len(steps))):
            steps.pop(0)[1]()

    def pump_through(which, layer):
        while steps and steps[0][0] <= layer * 4 + which:
            pump(1)

    def weights_finish(which, layer):
        if which == OUT:
            w_x(which, layer, n, 1 - x).wait_recv()
            pl.when(z == n)(lambda: w_own(which, layer).wait())
        else:
            for idx in range(PLANES):
                w_x(which, layer, idx, 1 - x).wait_recv()
            w_own(which, layer).wait()

    def weights_drain(which, layer):
        if which == OUT:
            w_x(which, layer, n, x).wait_send()

            @pl.when(z == n)
            def _():
                for kind in range(2):
                    w_z(which, layer, kind, z).wait_send()

            pl.when(passes_out)(lambda: w_z(which, layer, 2, n).wait_send())
        else:
            for kind in range(2):
                w_z(which, layer, kind, z).wait_send()
            for idx in range(PLANES):
                w_x(which, layer, idx, x).wait_send()

            @pl.when(is_inner)
            def _():
                w_z(which, layer, 2, z_inner).wait_send()
                w_z(which, layer, 3, z_outer).wait_send()

    def load(which, layer):
        return pltpu.make_async_copy(full[which].at[layer], loaded[which], r.load_sem.at[which])

    def weights_ready(which, layer):
        pump_through(which, layer)
        weights_finish(which, layer)
        load(which, layer).start()
        load(which, layer).wait()

    def tok_rows(chunk, part):
        return span(local * chunk + half * part, half)

    def tok_copy(ref, kind, part, incoming=False, early=False):
        chunk = ((n_core, n_side, n_far) if incoming else (n, n, n_side))[kind]
        rows = ref.at[tok_rows(chunk, part)]
        k = 2 * kind + part + 6 * early
        return remote(rows, rows, (r.tok_s.at[k], r.tok_r.at[k]), side if kind == 1 else core)

    def tok_send(ref, part, early=False):
        tok_copy(ref, 1, part, early=early).start()
        tok_copy(ref, 0, part, early=early).start()

    def tok_own(ref, early=False):
        for part in range(2):
            tok_copy(ref, 0, part, True, early).wait_recv()

    def tok_other(ref, early=False):
        for part in range(2):
            tok_copy(ref, 1, part, True, early).wait_recv()
            tok_copy(ref, 2, part, early=early).start()
        for part in range(2):
            tok_copy(ref, 2, part, True, early).wait_recv()

    def tok_drain(ref, early=False):
        for kind in range(3):
            for part in range(2):
                tok_copy(ref, kind, part, early=early).wait_send()

    def block_rows(block):
        return span(2 * local * (y if block else 1 - y), 2 * local)

    def sum_core(block):
        return remote(
            r.core_tx.at[block], r.core_rx.at[block], (r.sum_s.at[block], r.sum_r.at[block]), core
        )

    def sum_side(part):
        rows = span(half * part, half)
        return remote(
            r.side_tx.at[rows], r.side_rx.at[rows], (r.sum_s.at[2 + part], r.sum_r.at[2 + part]), side
        )

    def sum_block(block):
        r.core_tx[block] = r.part[block, span(local * (1 - c), local), :].astype(BF16)
        sum_core(block).start()

    def sum_cross():
        sum_core(0).wait_recv()
        for part in range(2):
            rows = span(half * part, half)
            mine = r.part[0, span(local * c + half * part, half), :]
            r.side_tx[rows, :] = (mine + r.core_rx[0, rows, :].astype(F32)).astype(BF16)
            sum_side(part).start()

    def sum_wait(part):
        if part == 0:
            sum_core(1).wait_recv()
        sum_side(part).wait_recv()
        if part == 1:
            for block in range(2):
                sum_core(block).wait_send()
                sum_side(block).wait_send()

    def sum_take(start):
        rows = span(start, STEP)
        return (
            r.part[1, span(local * c + start, STEP), :]
            + r.core_rx[1, rows, :].astype(F32)
            + r.side_rx[rows, :].astype(F32)
        )

    def each_step(part, body):
        @pl.loop(0, half // STEP)
        def _(i):
            body(half * part + STEP * i)

    def seg_of(start):
        return r.seg_col[span(local * n + start, STEP), :]

    def mod(layer, block, seg):
        rows = r.mods[SEGS * layer : SEGS * layer + SEGS, width * block : width * (block + 1)]
        out = rows[SEGS - 1 : SEGS]
        for s in range(SEGS - 1):
            out = jnp.where(seg == s, rows[s : s + 1], out)
        return out

    def mod_sum(layer, block, seg, values):
        sums = [jnp.sum(jnp.where(seg == s, values, 0.0), 0, keepdims=True) for s in range(SEGS)]
        at = (slice(SEGS * layer, SEGS * layer + SEGS), slice(width * block, width * (block + 1)))
        r.mod_grad[at] += jnp.concatenate(sums, 0)

    seg_cols = jnp.transpose(jnp.broadcast_to(r.seg_row[...].astype(F32), (8, narrow * local)))
    r.seg_col[...] = seg_cols[:, :1].astype(jnp.int32)

    def shifted(values, rest, size):
        window = values.shape[1]
        return pltpu.roll(values.astype(F32), (window - rest) % window, 1)[:, :size]

    def pick(ref, start, size, window):
        return shifted(ref[0, :, span(LANES * (start // LANES), window, LANES)], start % LANES, size)

    def pack(dst, pieces):
        at = 0
        for piece in pieces:
            size = piece.shape[1]
            dst[..., at : at + size] = piece.astype(dst.dtype)
            at += size

    def pack_shard(which, layer):
        dst, pieces = (r.qkv_s if which == QKV else r.up_s).at[layer], []
        for k, (start, size, _) in enumerate(windows(which)):
            raw(which, layer, k).wait()
            buffer = r.qkv_raw if which == QKV else r.up_raw
            pieces.append(shifted(buffer[layer, k], start % LANES, size))
        pack(dst, pieces)

    def folded(values, size):
        rest = values[:, size:]
        if rest.shape[1] < size:
            rest = jnp.concatenate([rest, jnp.zeros((8, size - rest.shape[1]), F32)], 1)
        return jnp.concatenate([values[:, :size], rest], 0).astype(BF16)

    def unfolded(values, size):
        values = values.astype(F32)
        return jnp.concatenate([values[:8], values[8:]], 1)[:, :size]

    def lead_copy(j, incoming=False):
        return remote(
            r.lead.at[(w + j) % wide], r.lead_rx.at[(w - j + wide) % wide if incoming else w],
            (r.lead_sem_s.at[j - 1], r.lead_sem_r.at[j - 1]), wide_peer(j),
        )

    def bias_copy(j, incoming=False):
        return remote(
            r.bias_tx, r.bias_rx.at[(w - j + wide) % wide if incoming else w],
            (r.bias_sem_s.at[j - 1], r.bias_sem_r.at[j - 1]), wide_peer(j),
        )

    def mod_copy(j, incoming=False):
        return remote(
            r.mod_part.at[(w + j) % wide], r.mod_rx.at[(w - j + wide) % wide if incoming else w],
            (r.mod_sem_s.at[j - 1], r.mod_sem_r.at[j - 1]), wide_peer(j),
        )

    def wait_all(copy, count=wide):
        for j in range(1, count):
            copy(j, True).wait_recv()

    narrow_peers = ((core, n_core), (side, n_side), (far, n_far))

    def quarter_copy(k, incoming=False):
        device, idx = narrow_peers[k]
        return remote(
            r.mod_q.at[n], r.mod_q.at[idx if incoming else n],
            (r.quarter_s.at[k], r.quarter_r.at[k]), device,
        )

    for j in range(1, wide):
        lead_copy(j).start()
    for j in range(1, wide):
        bias_copy(j).start()
    r.bias_rx[pl.ds(w, 1)] = r.bias_tx[...][None]
    pack_shard(QKV, 0)
    weights_start(QKV, 0)
    r.lead_rx[pl.ds(w, 1)] = r.lead[pl.ds(w, 1)]
    ada_load.wait()
    wait_all(lead_copy)
    lead_all = r.lead_rx[...].reshape(wide * 16, depth)
    for layer in range(LAYERS):
        product = dot(lead_all, r.ada_v[layer], ((1,), (0,)))
        for row in range(wide):
            at = slice(SEGS * layer, SEGS * layer + SEGS)
            r.mod_part[row, at, :] = product[16 * row : 16 * row + SEGS]
    for j in range(1, wide):
        mod_copy(j).start()
    r.mod_rx[pl.ds(w, 1)] = r.mod_part[pl.ds(w, 1)]
    for which, layer in ((UP, 0), (QKV, 1), (UP, 1)):
        pack_shard(which, layer)
    for item in early:
        weights_beside(*item)

    def after_first():
        weights_start(OUT, 0)
        weights_along(UP, 0)

    @pl.when(jnp.logical_not(is_inner))
    def _():
        for item in early_outer:
            weights_beside(*item)
        after_first()

    pump_through(QKV, 0)
    pl.when(is_inner)(after_first)
    r.mod_grad[...] = jnp.zeros_like(r.mod_grad)
    r.lead_t[...] = jnp.zeros_like(r.lead_t)
    for layer in range(LAYERS):
        for row in range(wide):
            at = (row * LAYERS + layer) * SEGS
            r.lead_t[layer, at : at + SEGS, :] = r.lead_rx[row].astype(F32)[:SEGS]
        r.lead_o[layer] = jnp.transpose(r.lead_t[layer]).astype(BF16)

    wait_all(bias_copy)
    bias_full = (r.ada_full, r.qkv_full, r.out_full, r.up_full, r.down_full)
    for peer in range(wide):
        values = r.bias_rx[peer].astype(F32)
        for layer in range(LAYERS):
            for k, row, start, size in bias_places:
                line = values.shape[0] // LAYERS * layer + row
                at = bias_refs[k].shape[1] * peer + start
                bias_full[k][0, layer : layer + 1, at : at + size] = values[line : line + 1, :size]
    for which, ref in ((QKV, r.qkv_full), (UP, r.up_full)):
        pieces = [pick(ref, *window) for window in windows(which)]
        for layer in range(LAYERS):
            at = 4 * layer + which
            pack(r.bias_sum.at[at : at + 1], [piece[layer : layer + 1] for piece in pieces])
    for layer in range(LAYERS):
        at = 4 * layer
        r.bias_sum[at + OUT : at + OUT + 1] = r.out_full[0, layer : layer + 1]
        r.bias_sum[at + DOWN : at + DOWN + 1] = r.down_full[0, layer : layer + 1]

    wait_all(mod_copy)
    ada_own = r.ada_full[0, :, span(LANES * mod_start(tiles, narrow, n), mod_cols, LANES)]
    total = jnp.sum(r.mod_rx[...], 0)
    for layer in range(LAYERS):
        at = slice(SEGS * layer, SEGS * layer + SEGS)
        r.mod_q[pl.ds(n, 1), at, :] = (total[at] + ada_own[layer : layer + 1])[None]
    for k in range(3):
        quarter_copy(k).start()
    for k in range(3):
        quarter_copy(k, True).wait_recv()
    for part in range(narrow):
        at = LANES * mod_start(tiles, narrow, part)
        r.mods[:, at : at + mod_cols] = r.mod_q[part]

    def bias_row(layer, which, size):
        return r.bias_sum[4 * layer + which : 4 * layer + which + 1, :size]

    def gather_norm(layer, hid, shift, scale, take, before):
        for part in range(2):
            before(part)

            def step(start):
                seg = seg_of(start)
                unit, _ = norm(take(start, seg))
                hidden = unit * (1.0 + mod(layer, scale, seg)) + mod(layer, shift, seg)
                hid[span(local * n + start, STEP), :] = hidden.astype(BF16)

            each_step(part, step)
            tok_send(hid, part)

    def qkv_block(layer, block):
        rows = block_rows(block)
        out = dot(r.hid_attn[layer, rows, :], r.qkv_v[...], ((1,), (0,)))
        out = (out + bias_row(layer, QKV, 3 * cols)).astype(BF16)
        for j in range(3 * own_heads):
            r.heads[layer, j, rows, :HEAD] = out[:, HEAD * j : HEAD * (j + 1)]

    def attend(layer):
        for head in range(own_heads):

            @pl.loop(0, narrow)
            def _(i):
                rows = span(local * i, local)
                query = r.heads[layer, head, rows, :HEAD]
                key = r.heads[layer, own_heads + head, :, :HEAD]
                value = r.heads[layer, 2 * own_heads + head, :, :HEAD]
                scores = dot(query, key, ((1,), (1,))) * scale_inv
                scores = jnp.where(r.seg_col[rows, :] == r.seg_row[...], scores, -1e30)
                top = jnp.max(scores, -1, keepdims=True)
                power = jnp.exp(scores - top)
                total = jnp.sum(power, -1, keepdims=True)
                probs = (power / total).astype(BF16)
                mixed = dot(probs, value, ((1,), (0,)))
                r.mixed[layer, rows, HEAD * head : HEAD * (head + 1)] = mixed.astype(BF16)
                r.log_sum[layer, rows, head : head + 1] = top + jnp.log(total)

            if head % 2:
                pump(1)

    def up_block(layer, block):
        rows = block_rows(block)
        hidden = r.hid_mlp[layer, rows, :]
        for at in range(0, width, 3 * LANES):
            tile = slice(at, at + 3 * LANES)
            up = dot(hidden, r.up_v[:, tile], ((1,), (0,)))
            up = up + r.bias_sum[4 * layer + UP : 4 * layer + UP + 1, tile]
            r.up[layer, rows, tile] = up.astype(BF16)
            r.act[layer, rows, tile] = gelu(up).astype(BF16)

    def down_block(layer, block):
        r.part[block] = dot(r.act[layer, block_rows(block), :], r.down_v[...], ((1,), (0,)))

    def state_of(layer, start):
        rows = span(start, STEP)
        return r.tok[rows, :].astype(F32) if layer == 0 else r.state[rows, :]

    def after_attn(layer):
        def take(start, seg):
            rows = span(start, STEP)
            branch = sum_take(start) + bias_row(layer, OUT, width)
            r.branch[layer, rows, :] = branch.astype(BF16)
            middle = state_of(layer, start) + mod(layer, 2, seg) * branch
            r.middle[layer, rows, :] = middle
            return middle

        return take

    def after_mlp(layer):
        def take(start, seg):
            rows = span(start, STEP)
            down = sum_take(start) + bias_row(layer, DOWN, width)
            r.down[layer, rows, :] = down.astype(BF16)
            result = r.middle[layer, rows, :] + mod(layer, 5, seg) * down
            if layer == 0:
                r.state[rows, :] = result
            else:
                r.mixed_o[rows, :] = result.astype(BF16)
            return result

        return take

    def attn_forward(layer, take, before):
        hid = r.hid_attn.at[layer]
        gather_norm(layer, hid, 0, 1, take, before)
        if layer == 0:
            early_grad()
        pump(1)
        weights_ready(QKV, layer)
        tok_own(hid)
        qkv_block(layer, 1)
        pump(1)
        tok_other(hid)
        qkv_block(layer, 0)
        pump(1)
        if layer == 0:
            tok_own(r.grad_down, True)
            tok_other(r.grad_down, True)
        attend(layer)
        weights_ready(OUT, layer)
        tok_drain(hid)
        for block in range(2):
            r.part[block] = dot(r.mixed[layer, block_rows(block), :], r.out_v[...], ((1,), (0,)))
            sum_block(block)
            if block == 0:
                sum_cross()
        pump(1)
        gather_norm(layer, r.hid_mlp.at[layer], 3, 4, after_attn(layer), sum_wait)
        pump(1)
        weights_ready(UP, layer)

    def early_grad():
        for part in range(2):

            def step(start):
                rows = span(start, STEP)
                grad = r.cot[rows, :].astype(F32)
                r.token_o[rows, :] = grad
                grad_down = (mod(LAYERS - 1, 5, seg_of(start)) * grad).astype(BF16)
                r.grad_down[span(local * n + start, STEP), :] = grad_down

            each_step(part, step)
            tok_send(r.grad_down, part, True)

    attn_forward(0, lambda start, seg: state_of(0, start), lambda part: None)
    weights_ready(DOWN, 0)
    hid = r.hid_mlp.at[0]
    tok_own(hid)
    up_block(0, 1)
    down_block(0, 1)
    sum_block(1)
    pump(1)
    tok_other(hid)
    up_block(0, 0)
    down_block(0, 0)
    sum_block(0)
    sum_cross()
    tok_drain(hid)
    pump(2)
    attn_forward(1, after_mlp(0), sum_wait)

    sums = (r.qkv_d, r.out_d, r.up_d, r.down_d)
    from_x = (r.qkv_xr, r.out_xr, r.up_xr, r.down_xr)
    from_z = (r.qkv_zr, r.out_zr, r.up_zr, r.down_zr)
    final = (r.qkv_f, r.out_f, r.up_f, r.down_f)
    grads_o = (r.qkv_o, r.out_o, r.up_o, r.down_o)
    same_y, same_c = y == z // 2, c == z % 2

    def d_rows(which, plane_idx, col):
        return w_rows(which, plane_idx, col)

    def d_x(which, plane_idx, incoming=False):
        k = 0 if which == OUT else plane_idx
        src = sums[which].at[d_rows(which, plane_idx, 1 - x)]
        return remote(
            src, from_x[which].at[k], (r.dx_s.at[which, k], r.dx_r.at[which, k]), beside
        )

    def d_z(which, kind):
        idx = 0 if which == OUT else (z_partner, z_inner, z_outer)[kind]
        src = from_x[which].at[idx]

        def send(slot, plane_idx):
            return remote(
                src, from_z[which].at[slot], (r.dz_s.at[which, kind], r.dz_r.at[which, slot]),
                at_plane(plane_idx),
            )

        return send

    def d_z_in(which, slot):
        ref = from_z[which].at[slot]
        return remote(ref, ref, (r.dz_s.at[which, 0], r.dz_r.at[which, slot]), at_plane(z_partner))

    def grad_product(which, layer):
        left, right = (
            (r.hid_attn, r.grad_qkv), (r.mixed, r.grad_branch),
            (r.hid_mlp, r.grad_up), (r.act, r.grad_down),
        )[which]
        if which == OUT:
            product = dot(left[layer], right[...], ((0,), (0,)))
            sums[which][...] = product.astype(BF16)
        else:

            @pl.loop(0, width // (3 * LANES))
            def _(i):
                tile = span(3 * LANES * i, 3 * LANES, LANES)
                product = dot(left[layer, :, tile], right[...], ((0,), (0,)))
                sums[which][tile, :] = product.astype(BF16)

    def grad_send(which, layer):
        if layer == 0:
            pl.semaphore_wait(r.credit_x.at[which], 1)
        if which == OUT:
            d_x(which, 0).start()
        else:
            for idx in (z_outer, z_inner, z_partner, z):
                d_x(which, idx).start()

    out_home = z == n
    out_near = z_partner == n
    out_far = z_half != n // 2

    def credit(sem, device):
        pl.semaphore_signal(sem, inc=1, device_id=device, device_id_type=MESH)

    def grad_beside(which, layer):
        def add(slot, rows):
            total = sums[which][rows, :].astype(F32) + from_x[which][slot].astype(F32)
            from_x[which][slot] = total.astype(BF16)

        if which == OUT:
            d_x(which, 0).wait_recv()
            add(0, d_rows(which, n, x))
            outer_far = jnp.logical_and(out_far, jnp.logical_not(is_inner))

            @pl.when(jnp.logical_or(out_near, outer_far))
            def _():
                if layer == 0:
                    pl.semaphore_wait(r.credit_z.at[which, 0], 1)

            pl.when(out_near)(lambda: d_z(which, 0)(0, z_partner).start())
            pl.when(outer_far)(lambda: d_z(which, 0)(2, z_partner).start())
            d_x(which, 0).wait_send()
        else:
            for k, idx in ((2, z_outer), (1, z_inner), (0, z_partner), (None, z)):
                d_x(which, idx).wait_recv()
                add(idx, d_rows(which, idx, x))
                if k == 2 and layer == 0:
                    pl.semaphore_wait(r.credit_z.at[which, 0], 1)
                if k == 0:
                    d_z(which, 0)(0, z_partner).start()
                elif k:
                    pl.when(jnp.logical_not(is_inner))(
                        lambda: d_z(which, k)(k + 1, z_partner).start()
                    )
            for idx in range(PLANES):
                d_x(which, idx).wait_send()

    def grad_join(which, layer):
        def add(slot, idx):
            d_z_in(which, slot).wait_recv()
            total = from_x[which][idx].astype(F32) + from_z[which][slot].astype(F32)
            from_x[which][idx] = total.astype(BF16)

        if which == OUT:

            @pl.when(jnp.logical_and(out_far, is_inner))
            def _():
                add(2, 0)
                if layer == 0:
                    pl.semaphore_wait(r.credit_z.at[which, 1], 1)
                else:
                    credit(r.credit_z.at[which, 0], at_plane(z_partner))
                d_z(which, 0)(1, n).start()
        else:

            @pl.when(is_inner)
            def _():
                if layer == 0:
                    pl.semaphore_wait(r.credit_z.at[which, 1], 2)
                add(3, z_outer)
                d_z(which, 2)(1, z_outer).start()
                add(2, z_inner)
                d_z(which, 1)(1, z_inner).start()

    def grad_planes(which, layer):
        def add():
            d_z_in(which, 0).wait_recv()
            d_z_in(which, 1).wait_recv()
            total = from_x[which][0 if which == OUT else z].astype(F32)
            total = total + from_z[which][0].astype(F32) + from_z[which][1].astype(F32)
            if layer == 0:
                spread_sent(which, 1)
            final[which][...] = total.astype(BF16)
            if layer == 1:
                credit(r.credit_z.at[which, 0], at_plane(z_partner))
                credit(r.credit_z.at[which, 1], at_plane(z_inner))

        if which == OUT:
            pl.when(out_home)(add)
            pl.when(jnp.logical_not(out_home))(lambda: d_z(which, 0)(0, z_partner).wait_send())
        else:
            add()
            for kind in range(3):
                d_z(which, kind)(0, z_partner).wait_send()
        if layer == 1:
            credit(r.credit_x.at[which], beside)

    def e_z(kind, other):
        idx = (z_partner, z_inner, z_outer)[kind]
        src = sums[DOWN].at[d_rows(DOWN, idx, 1 - x if other else x)]
        slots = from_x[DOWN] if other else from_z[DOWN]

        def send(slot, plane_idx):
            return remote(
                src, slots.at[slot], (r.e_s.at[int(other), kind], r.e_r.at[int(other), slot]),
                at_plane(plane_idx),
            )

        return send

    def e_in(slot, other):
        ref = (from_x[DOWN] if other else from_z[DOWN]).at[slot]
        remote(
            ref, ref, (r.e_s.at[int(other), 0], r.e_r.at[int(other), slot]), at_plane(z_partner)
        ).wait_recv()
        return ref[...].astype(F32)

    def e_x():
        return remote(from_x[DOWN].at[0], r.down_e, (r.ex_s, r.ex_r), beside)

    def first_send():
        @pl.when(jnp.logical_not(is_inner))
        def _():
            for kind in (2, 1):
                for other in (True, False):
                    e_z(kind, other)(kind + 1, z_partner).start()

        for other in (True, False):
            e_z(0, other)(0, z_partner).start()

    def first_join():
        @pl.when(is_inner)
        def _():
            for kind, idx in ((2, z_outer), (1, z_inner)):
                for other in (True, False):
                    rows = d_rows(DOWN, idx, 1 - x if other else x)
                    total = sums[DOWN][rows, :].astype(F32) + e_in(kind + 1, other)
                    sums[DOWN][rows, :] = total.astype(BF16)
                    e_z(kind, other)(1, idx).start()

    def first_planes():
        for other in (True, False):
            rows = d_rows(DOWN, z, 1 - x if other else x)
            total = sums[DOWN][rows, :].astype(F32) + e_in(0, other) + e_in(1, other)
            if other:
                from_x[DOWN][0] = total.astype(BF16)
                e_x().start()
            else:
                final[DOWN][...] = total.astype(BF16)
        for kind in range(3):
            for other in (True, False):
                e_z(kind, other)(0, z_partner).wait_send()
        credit(r.credit_z.at[DOWN, 0], at_plane(z_partner))
        credit(r.credit_z.at[DOWN, 1], at_plane(z_inner))

    def first_beside():
        e_x().wait_recv()
        total = final[DOWN][...].astype(F32) + r.down_e[...].astype(F32)
        final[DOWN][...] = total.astype(BF16)
        e_x().wait_send()
        credit(r.credit_x.at[DOWN], beside)

    def spread(which, layer, kind, source=None):
        slot = layer * 4 + which
        if which == OUT:
            dst = grads_o[which].at[layer]
        else:
            dst = grads_o[which].at[layer, n if source is None else source]
        src = final[which] if kind < 2 else dst
        return remote(
            src, dst, (r.spread_s.at[slot, kind], r.spread_r.at[slot, kind]), side if kind == 1 else core
        )

    def spread_own(which, layer):
        dst = grads_o[which].at[layer] if which == OUT else grads_o[which].at[layer, n]
        return pltpu.make_async_copy(final[which], dst, r.spread_l.at[layer * 4 + which])

    def spread_sent(which, layer):
        spread(which, layer, 1).wait_send()
        spread(which, layer, 0).wait_send()
        spread_own(which, layer).wait()

    def grad_spread(which, layer):
        def go():
            spread(which, layer, 1).start()
            spread(which, layer, 0).start()
            spread_own(which, layer).start()

        if which == OUT:
            pl.when(jnp.logical_and(same_y, same_c))(go)
        else:
            go()

    def grad_pass(which, layer):
        def go():
            spread(which, layer, 1, n_side).wait_recv()
            spread(which, layer, 2, n_side).start()

        if which == OUT:
            pl.when(jnp.logical_and(jnp.logical_not(same_y), same_c))(go)
        else:
            go()

    def grad_end(which, layer):
        if which == OUT:
            if layer == 0:
                pl.when(jnp.logical_and(same_y, same_c))(lambda: spread_sent(which, layer))

            @pl.when(jnp.logical_and(jnp.logical_not(same_y), same_c))
            def _():
                spread(which, layer, 2).wait_send()

            @pl.when(jnp.logical_and(same_y, jnp.logical_not(same_c)))
            def _():
                spread(which, layer, 0).wait_recv()

            @pl.when(jnp.logical_and(jnp.logical_not(same_y), jnp.logical_not(same_c)))
            def _():
                spread(which, layer, 2).wait_recv()
        else:
            spread(which, layer, 0, n_core).wait_recv()
            spread(which, layer, 2, n_far).wait_recv()
            spread(which, layer, 2, n_side).wait_send()
            if layer == 0:
                spread_sent(which, layer)

    def bias_grad(layer, which, values):
        at = 4 * layer + which
        r.bias_grad[at : at + 1, : values.shape[1]] = jnp.sum(
            values.astype(F32), 0, keepdims=True
        )

    def back_mlp_block(layer, block):
        rows = block_rows(block)
        grad_down = r.grad_down[rows, :]
        for at in range(0, width, 3 * LANES):
            tile = slice(at, at + 3 * LANES)
            grad_act = dot(grad_down, r.down_v[tile, :], ((1,), (1,)))
            up = r.up[layer, rows, tile].astype(F32)
            r.grad_up[rows, tile] = (grad_act * gelu_slope(up)).astype(BF16)
        r.part[block] = dot(r.grad_up[rows, :], r.up_v[...], ((1,), (1,)))

    def back_attn_block(layer, block):
        rows = block_rows(block)
        out = dot(r.grad_branch[rows, :], r.out_v[...], ((1,), (1,))).astype(BF16)
        for j in range(own_heads):
            r.grad_heads[j, rows, :HEAD] = out[:, HEAD * j : HEAD * (j + 1)]

    def back_attend(layer, head):
        @pl.loop(0, narrow)
        def _(i):
            rows = span(local * i, local)
            query = r.heads[layer, head, rows, :HEAD]
            key = r.heads[layer, own_heads + head, :, :HEAD]
            value = r.heads[layer, 2 * own_heads + head, :, :HEAD]
            grad = r.grad_heads[head, rows, :HEAD]
            scores = dot(query, key, ((1,), (1,))) * scale_inv
            probs = jnp.exp(scores - r.log_sum[layer, rows, head : head + 1])
            probs = jnp.where(r.seg_col[rows, :] == r.seg_row[...], probs, 0.0)
            grad_probs = dot(grad, value, ((1,), (1,)))
            inner = jnp.sum(probs * grad_probs, -1, keepdims=True)
            grad_scores = (probs * (grad_probs - inner)).astype(BF16)
            grad_query = dot(grad_scores, key, ((1,), (0,))) * scale_inv
            r.grad_qkv[rows, HEAD * head : HEAD * (head + 1)] = grad_query.astype(BF16)
            grad_key = dot(grad_scores, query, ((0,), (0,)))
            grad_value = dot(probs.astype(BF16), grad, ((0,), (0,)))

            def tile(k):
                return slice(LANES * k, LANES * k + HEAD)

            @pl.when(i == 0)
            def _():
                for k in range(narrow):
                    at = slice(local * k, local * (k + 1))
                    r.grad_hid[:, tile(k)] = grad_key[at]
                    r.grad_hid[:, tile(narrow + k)] = grad_value[at]

            @pl.when(i > 0)
            def _():
                for k in range(narrow):
                    at = slice(local * k, local * (k + 1))
                    r.grad_hid[:, tile(k)] += grad_key[at]
                    r.grad_hid[:, tile(narrow + k)] += grad_value[at]

        at = cols + HEAD * head
        for k in range(narrow):
            rows = slice(local * k, local * (k + 1))
            key_sum = r.grad_hid[:, LANES * k : LANES * k + HEAD]
            value_sum = r.grad_hid[:, LANES * (narrow + k) : LANES * (narrow + k) + HEAD]
            r.grad_qkv[rows, at : at + HEAD] = (key_sum * scale_inv).astype(BF16)
            r.grad_qkv[rows, cols + at : cols + at + HEAD] = value_sum.astype(BF16)

    def both(body):
        for part in range(2):
            each_step(part, body)

    def sums_attn(layer):
        def body(start):
            rows = span(start, STEP)
            seg = seg_of(start)
            unit, _ = norm(state_of(layer, start))
            grad_hidden = r.grad_hid[rows, :]
            mod_sum(layer, 0, seg, grad_hidden)
            mod_sum(layer, 1, seg, grad_hidden * unit)

        both(body)

    def sums_mlp(layer):
        def body(start):
            rows = span(start, STEP)
            seg = seg_of(start)
            unit, _ = norm(r.middle[layer, rows, :])
            grad_hidden = r.grad_hid[rows, :]
            mod_sum(layer, 3, seg, grad_hidden)
            mod_sum(layer, 4, seg, grad_hidden * unit)
            mod_sum(layer, 2, seg, r.branch[layer, rows, :].astype(F32) * r.token_o[rows, :])

        both(body)

    def sums_gate_mlp(layer, grad):
        def body(start):
            rows = span(start, STEP)
            mod_sum(
                layer, 5, seg_of(start), r.down[layer, rows, :].astype(F32) * grad[rows, :].astype(F32)
            )

        both(body)

    def back_middle(layer):
        for part in range(2):
            sum_wait(part)

            def step(start):
                rows = span(start, STEP)
                seg = seg_of(start)
                grad_hidden = sum_take(start)
                unit, inv = norm(r.middle[layer, rows, :])
                r.grad_hid[rows, :] = grad_hidden
                grad = r.token_o[rows, :] + norm_back(
                    grad_hidden * (1.0 + mod(layer, 4, seg)), unit, inv
                )
                r.token_o[rows, :] = grad
                grad_branch = (mod(layer, 2, seg) * grad).astype(BF16)
                r.grad_branch[span(local * n + start, STEP), :] = grad_branch

            each_step(part, step)
            tok_send(r.grad_branch, part)

    def back_state(layer, start):
        rows = span(start, STEP)
        grad_hidden = sum_take(start)
        unit, inv = norm(state_of(layer, start))
        r.grad_hid[rows, :] = grad_hidden
        r.token_o[rows, :] += norm_back(
            grad_hidden * (1.0 + mod(layer, 1, seg_of(start))), unit, inv
        )

    def back_qkv(layer, checked=False):
        for block in range(2):
            rows = block_rows(block)
            r.part[block] = dot(r.grad_qkv[rows, :], r.qkv_v[...], ((1,), (1,)))
            if checked and block == 0:
                pl.semaphore_wait(r.credit_sum.at[0], 1)
            sum_block(block)
            if block == 0:
                if checked:
                    pl.semaphore_wait(r.credit_sum.at[1], 1)
                sum_cross()

    hid = r.hid_mlp.at[1]
    tok_own(hid)
    up_block(1, 1)
    pump(1)
    tok_other(hid)
    up_block(1, 0)
    pump(1)
    grad_product(DOWN, 1)
    bias_grad(1, DOWN, r.grad_down[span(local * n, local), :])
    tok_drain(hid)
    tok_drain(r.grad_down, True)
    pump_through(DOWN, 1)
    first_send()
    weights_ready(DOWN, 1)
    for block in range(2):
        back_mlp_block(1, block)
        sum_block(block)
        if block == 0:
            sum_cross()
    load(UP, 0).start()
    grad_product(UP, 1)
    grad_send(UP, 1)
    bias_grad(1, UP, r.grad_up[...])
    back_middle(1)
    for block in range(2):
        down_block(1, block)
    load(DOWN, 0).start()
    sums_mlp(1)
    bias_grad(1, OUT, r.grad_branch[span(local * n, local), :])
    tok_own(r.grad_branch)
    back_attn_block(1, 1)
    tok_other(r.grad_branch)
    back_attn_block(1, 0)
    load(OUT, 0).start()
    for block in range(2):
        sum_block(block)
        if block == 0:
            sum_cross()
    grad_product(OUT, 1)
    grad_send(OUT, 1)
    for head in range(own_heads):
        back_attend(1, head)
        if head == 2:
            first_join()
    tok_drain(r.grad_branch)
    for part in range(2):
        sum_wait(part)
        finish_state = after_mlp(1)

        def last(start):
            finish_state(start, seg_of(start))

        each_step(part, last)
    credit(r.credit_sum.at[0], core)
    credit(r.credit_sum.at[1], side)
    back_qkv(1, True)
    load(QKV, 0).start()
    grad_product(QKV, 1)
    grad_send(QKV, 1)
    sums_gate_mlp(1, r.cot)
    grad_beside(UP, 1)
    bias_grad(1, QKV, r.grad_qkv[...])
    for part in range(2):
        sum_wait(part)

        def start_down(start):
            back_state(1, start)
            grad_down = (mod(0, 5, seg_of(start)) * r.token_o[span(start, STEP), :]).astype(BF16)
            r.grad_down[span(local * n + start, STEP), :] = grad_down

        each_step(part, start_down)
        tok_send(r.grad_down, part)
    sums_attn(1)
    sums_gate_mlp(0, r.token_o)
    bias_grad(0, DOWN, r.grad_down[span(local * n, local), :])
    load(DOWN, 0).wait()
    load(UP, 0).wait()
    grad_beside(OUT, 1)
    first_planes()
    tok_own(r.grad_down)
    back_mlp_block(0, 1)
    sum_block(1)
    tok_other(r.grad_down)
    back_mlp_block(0, 0)
    sum_block(0)
    sum_cross()
    grad_product(DOWN, 0)
    bias_grad(0, UP, r.grad_up[...])
    tok_drain(r.grad_down)
    back_middle(0)
    grad_product(UP, 0)
    first_beside()
    grad_send(DOWN, 0)
    grad_join(UP, 1)
    grad_join(OUT, 1)
    sums_mlp(0)
    bias_grad(0, OUT, r.grad_branch[span(local * n, local), :])
    grad_beside(QKV, 1)
    load(OUT, 0).wait()
    load(QKV, 0).wait()
    tok_own(r.grad_branch)
    back_attn_block(0, 1)
    tok_other(r.grad_branch)
    back_attn_block(0, 0)
    grad_spread(DOWN, 1)
    grad_product(OUT, 0)
    for head in range(own_heads):
        back_attend(0, head)
        if head == 1:
            grad_planes(UP, 1)
            grad_send(UP, 0)
    back_qkv(0)
    grad_join(QKV, 1)
    grad_product(QKV, 0)
    tok_drain(r.grad_branch)
    grad_beside(DOWN, 0)
    bias_grad(0, QKV, r.grad_qkv[...])
    for part in range(2):
        sum_wait(part)
        each_step(part, partial(back_state, 0))
    sums_attn(0)

    def quarter_back(k, incoming=False):
        device, idx = narrow_peers[k]
        at = span(LANES * mod_start(tiles, narrow, idx), mod_cols, LANES)
        return remote(
            r.mod_grad.at[:, at], r.quarter_rx.at[k], (r.back_s.at[k], r.back_r.at[k]), device
        )

    def wide_back(j, incoming=False):
        return remote(
            r.quarter_sum, r.quarter_all.at[(w - j + wide) % wide if incoming else w],
            (r.wide_s.at[j - 1], r.wide_r.at[j - 1]), wide_peer(j),
        )

    def bias_wide(j, incoming=False):
        return remote(
            r.bias_half, r.bias_all.at[(w - j + wide) % wide if incoming else w],
            (r.bias_wide_s.at[j - 1], r.bias_wide_r.at[j - 1]), wide_peer(j),
        )

    def bias_narrow(k, incoming=False):
        device, idx = narrow_peers[k]
        return remote(
            r.bias_row, r.bias_o.at[idx if incoming else n],
            (r.bias_narrow_s.at[k], r.bias_narrow_r.at[k]), device,
        )

    def mod_narrow(k, incoming=False):
        device, idx = narrow_peers[k]
        return remote(
            r.mod_all, r.mod_o.at[idx if incoming else n],
            (r.mod_narrow_s.at[k], r.mod_narrow_r.at[k]), device,
        )

    def lead_back(j, incoming=False):
        return remote(
            r.lead_tx.at[(w + j) % wide], r.lead_back.at[(w - j + wide) % wide if incoming else w],
            (r.lead_back_s.at[j - 1], r.lead_back_r.at[j - 1]), wide_peer(j),
        )

    def lead_narrow(k, incoming=False):
        device, idx = narrow_peers[k]
        return remote(
            r.lead_back, r.lead_g.at[idx if incoming else n],
            (r.lead_narrow_s.at[k], r.lead_narrow_r.at[k]), device,
        )

    for k in range(3):
        quarter_back(k).start()
    own_at = span(LANES * mod_start(tiles, narrow, n), mod_cols, LANES)
    total = r.mod_grad[:, own_at]
    for k in range(3):
        quarter_back(k, True).wait_recv()
        total = total + r.quarter_rx[k]
    r.quarter_sum[...] = folded(total, mod_cols // 2)
    for j in range(1, wide):
        wide_back(j).start()
    r.bias_half[...] = folded(r.bias_grad[...], 5 * LANES)
    for j in range(1, wide):
        bias_wide(j).start()
    r.quarter_all[pl.ds(w, 1)] = r.quarter_sum[...][None]
    r.bias_all[pl.ds(w, 1)] = r.bias_half[...][None]
    grad_planes(OUT, 1)
    grad_send(OUT, 0)
    grad_planes(QKV, 1)
    grad_send(QKV, 0)
    grad_spread(UP, 1)
    grad_spread(OUT, 1)
    grad_spread(QKV, 1)
    for which in (DOWN, UP, OUT, QKV):
        grad_pass(which, 1)
    grad_join(DOWN, 0)
    grad_beside(UP, 0)
    wait_all(wide_back)
    for j in range(1, wide):
        mod_copy(j).wait_send()
    for row in range(wide):
        r.mod_part[row] = unfolded(r.quarter_all[row], mod_cols)
    r.mod_all[...] = r.mod_part[...].reshape(wide * LAYERS * SEGS, mod_cols).astype(BF16)
    mod_own = pltpu.make_async_copy(r.mod_all, r.mod_o.at[n], r.mod_own_sem)
    mod_own.start()
    for k in range(3):
        mod_narrow(k).start()
    owned = LANES * (mod_start(tiles, narrow, n + 1) - mod_start(tiles, narrow, n))
    lane = lax.broadcasted_iota(jnp.int32, r.mod_all.shape, 1)
    own_grads = jnp.where(lane < owned, r.mod_all[...].astype(F32), 0.0).astype(BF16)
    lead_parts = [dot(own_grads, r.ada_v[layer], ((1,), (1,))) for layer in range(LAYERS)]
    for row in range(wide):
        at = row * LAYERS * SEGS
        r.lead_tx[row] = lead_parts[0][at : at + SEGS] + lead_parts[1][at + SEGS : at + 2 * SEGS]
    for j in range(1, wide):
        lead_back(j).start()
    r.lead_back[pl.ds(w, 1)] = r.lead_tx[pl.ds(w, 1)]
    grad_planes(DOWN, 0)
    grad_spread(DOWN, 0)
    grad_beside(OUT, 0)
    wait_all(bias_wide)
    r.bias_row[...] = unfolded(jnp.sum(r.bias_all[...].astype(F32), 0), width)
    bias_own = pltpu.make_async_copy(r.bias_row, r.bias_o.at[n], r.bias_own_sem)
    bias_own.start()
    for k in range(3):
        bias_narrow(k).start()
    grad_join(UP, 0)
    grad_join(OUT, 0)
    grad_beside(QKV, 0)
    wait_all(lead_back)
    lead_own = pltpu.make_async_copy(r.lead_back, r.lead_g.at[n], r.lead_own_sem)
    lead_own.start()
    for k in range(3):
        lead_narrow(k).start()
    grad_pass(DOWN, 0)
    grad_join(QKV, 0)
    grad_planes(UP, 0)
    grad_spread(UP, 0)
    grad_planes(OUT, 0)
    grad_spread(OUT, 0)
    grad_planes(QKV, 0)
    grad_spread(QKV, 0)
    for which in (UP, OUT, QKV):
        grad_pass(which, 0)

    for layer in range(LAYERS):
        for which in range(4):
            weights_drain(which, layer)
            grad_end(which, layer)
    for j in range(1, wide):
        for copy in (lead_copy, bias_copy, wide_back, bias_wide, lead_back):
            copy(j).wait_send()
    for k in range(3):
        for copy in (quarter_copy, quarter_back, mod_narrow, bias_narrow, lead_narrow):
            copy(k).wait_send()
        mod_narrow(k, True).wait_recv()
        bias_narrow(k, True).wait_recv()
        lead_narrow(k, True).wait_recv()
    mod_own.wait()
    lead_own.wait()
    bias_own.wait()


def gelu_slope(values):
    rate = math.sqrt(2.0 / math.pi)
    bent = jnp.tanh(rate * (values + 0.044715 * values * values * values))
    inner = rate * (1.0 + 3.0 * 0.044715 * values * values)
    return 0.5 * (1.0 + bent) + 0.5 * values * (1.0 - bent * bent) * inner


def chosen_of(cond, index):
    values = cond[...].astype(F32)
    rows = index[...]
    chosen = jnp.zeros(values.shape, F32)
    for k in range(SEGS):
        chosen = jnp.where(rows == k, values[k : k + 1], chosen)
    return chosen


def finish_kernel(cfg, *refs):
    r = SimpleNamespace(**dict(zip(cfg.names, refs)))
    wide, narrow, width, depth, cols = cfg.wide, cfg.narrow, cfg.width, cfg.depth, cfg.cols
    tiles, hidden_own = cfg.tiles, cfg.hidden_own
    w = lax.axis_index("wide")

    for part in range(narrow):
        values = r.qkv_i[0, part].astype(F32)
        for j in range(3):
            at = width * j + cols * part
            r.qkv_g[0, :, at : at + cols] = values[:, cols * j : cols * (j + 1)]
        values = r.up_i[0, part].astype(F32)
        for j in range(wide):
            at = (j * narrow + part) * hidden_own
            r.up_g[0, :, at : at + hidden_own] = values[:, hidden_own * j : hidden_own * (j + 1)]
        at, end = [LANES * mod_start(tiles, narrow, part + k) for k in range(2)]
        r.ada_g[0, :, at:end] = dot(r.lead_i[0], r.mod_i[part, :, : end - at], ((1,), (0,)))
    r.out_g[...] = r.out_i[...].astype(F32)
    r.down_g[...] = r.down_i[...].astype(F32)

    def pick(ref, size):
        start = size * w
        window = LANES * (-(-size // LANES) + 1)
        tile, rest = start // LANES, start % LANES
        values = ref[:, pl.ds(pl.multiple_of(LANES * tile, LANES), window)]
        return pltpu.roll(values, (window - rest) % window, 1)[:, :size]

    @pl.when(pl.program_id(0) + pl.program_id(1) == 0)
    def _():
        for part in range(narrow):
            values = r.bias_i[part]
            for j in range(3):
                at = width * j + cols * part
                r.qkv_t[:, at : at + cols] = values[:, cols * j : cols * (j + 1)]
            for j in range(wide):
                at = (j * narrow + part) * hidden_own
                r.up_t[:, at : at + hidden_own] = values[:, hidden_own * j : hidden_own * (j + 1)]
            at, end = [LANES * mod_start(tiles, narrow, part + k) for k in range(2)]
            values = r.mod_i[part, :, : end - at].astype(F32)
            layer_of = lax.broadcasted_iota(jnp.int32, values.shape, 0) // SEGS % LAYERS
            for layer in range(LAYERS):
                sums = jnp.sum(jnp.where(layer_of == layer, values, 0.0), 0, keepdims=True)
                r.ada_t[layer : layer + 1, at:end] = sums
        r.row_t[:, :width] = jnp.sum(r.bias_i[...], 0)
        for dst, ref, line, step in (
            (r.ada_bg, r.ada_t, 0, 1), (r.qkv_bg, r.qkv_t, QKV, 4), (r.out_bg, r.row_t, OUT, 4),
            (r.up_bg, r.up_t, UP, 4), (r.down_bg, r.row_t, DOWN, 4),
        ):
            values = pick(ref, dst.shape[1])
            for layer in range(LAYERS):
                at = step * layer + line
                dst[layer : layer + 1, :] = values[at : at + 1]
        chosen = chosen_of(r.cond, r.cond_index)
        gate = jax.nn.sigmoid(chosen)
        slope = gate * (1.0 + chosen * (1.0 - gate))
        lead_grad = jnp.sum(r.lead_i2[...], 0)
        for row in range(wide):
            at = slice(depth * row, depth * (row + 1))
            grad = lead_grad[row] * slope[:, at]
            for k in range(SEGS):
                r.cond_g[k : k + 1, at] = jnp.sum(
                    jnp.where(r.cond_index[...] == k, grad, 0.0), 0, keepdims=True
                )


def finish(wide, narrow, got, cond, cond_index, tiles, mod_cols, w):
    width = cond.shape[1]
    depth, cols = width // wide, width // narrow
    hidden_own = got["up_o"].shape[-1] // wide
    hidden_all = got["up_o"].shape[-1] * narrow
    down_rows = narrow * hidden_own
    bands = depth // 48
    rows = depth // bands
    shape, vmem = jax.ShapeDtypeStruct, pltpu.VMEM

    def whole(values):
        return pl.BlockSpec(values.shape, lambda i, j: (0,) * values.ndim)

    def band(*dims):
        return pl.BlockSpec(
            (1, *dims), lambda i, j: (i, 0, j, 0) if len(dims) == 3 else (i, j, 0)
        )

    down_i = got["down_o"].reshape(LAYERS, down_rows, width)
    inputs = dict(
        qkv_i=got["qkv_o"], up_i=got["up_o"], out_i=got["out_o"], down_i=down_i,
        lead_i=got["lead_o"], mod_i=got["mod_o"], bias_i=got["bias_o"], lead_i2=got["lead_g"],
        cond=cond, cond_index=cond_index,
    )
    in_specs = [
        band(narrow, rows, 3 * cols), band(narrow, rows, wide * hidden_own), band(rows, width),
        band(down_rows // bands, width), band(rows, got["lead_o"].shape[-1]),
        *[whole(inputs[name]) for name in ("mod_i", "bias_i", "lead_i2", "cond", "cond_index")],
    ]
    outputs = dict(
        ada_g=shape((LAYERS, depth, tiles * LANES), F32), qkv_g=shape((LAYERS, depth, 3 * width), F32),
        out_g=shape((LAYERS, depth, width), F32), up_g=shape((LAYERS, depth, hidden_all), F32),
        down_g=shape((LAYERS, down_rows, width), F32),
        ada_bg=shape((LAYERS, tiles * LANES // wide), F32), qkv_bg=shape((LAYERS, 3 * width // wide), F32),
        out_bg=shape((LAYERS, depth), F32), up_bg=shape((LAYERS, hidden_all // wide), F32),
        down_bg=shape((LAYERS, depth), F32), cond_g=shape((SEGS, width), F32),
    )
    out_specs = [
        band(rows, tiles * LANES), band(rows, 3 * width), band(rows, width), band(rows, hidden_all),
        band(down_rows // bands, width),
        *[whole(outputs[name]) for name in ("ada_bg", "qkv_bg", "out_bg", "up_bg", "down_bg", "cond_g")],
    ]
    scratch = dict(
        ada_t=vmem((8, (tiles + 2) * LANES), F32), qkv_t=vmem((8, 3 * width + 2 * LANES), F32),
        up_t=vmem((8, hidden_all + 2 * LANES), F32), row_t=vmem((8, width + 2 * LANES), F32),
    )
    cfg = SimpleNamespace(
        names=[*inputs, *outputs, *scratch], wide=wide, narrow=narrow, width=width, depth=depth,
        cols=cols, tiles=tiles, hidden_own=hidden_own,
    )
    results = pl.pallas_call(
        partial(finish_kernel, cfg),
        grid=(LAYERS, bands),
        out_shape=list(outputs.values()), in_specs=in_specs, out_specs=out_specs,
        scratch_shapes=list(scratch.values()),
        compiler_params=pltpu.CompilerParams(vmem_limit_bytes=62 * 2**20),
    )(*inputs.values())
    done = dict(zip(outputs, results))
    out = [got["mixed_o"][None], got["token_o"][None], done["cond_g"][None]]
    for name in ("ada", "qkv", "out", "up", "down"):
        out += [done[name + "_g"], done[name + "_bg"]]
    return tuple(out)


def fused_device(
    wide, narrow,
    tokens, cond, seg_ids, cond_index, cotangent,
    ada_weight, ada_bias, qkv_weight, qkv_bias, out_weight, out_bias,
    up_weight, up_bias, down_weight, down_bias,
):
    w = lax.axis_index("wide")
    n = lax.axis_index("narrow")
    local, width = tokens.shape[1:]
    row_len = seg_ids.shape[1]
    depth, cols = width // wide, width // narrow
    hidden_own = up_weight.shape[-1] // wide // narrow
    hidden = wide * hidden_own
    tiles = ada_weight.shape[-1] // LANES
    mod_cols = LANES * -(-tiles // narrow)

    inputs = dict(
        tok=tokens[0], cond=cond[0], cond_index=cond_index.reshape(SEGS, 1), seg_row=seg_ids,
        cot=cotangent[0], ada_b=ada_bias, qkv_b=qkv_bias, out_b=out_bias, up_b=up_bias, down_b=down_bias,
        ada=ada_weight, qkv_w=qkv_weight, out_w=out_weight, up_w=up_weight, down_w=down_weight,
    )
    in_hbm = ("ada", "qkv_w", "out_w", "up_w", "down_w")
    shape = jax.ShapeDtypeStruct
    outputs = dict(
        mixed_o=shape((local, width), BF16), token_o=shape((local, width), F32),
        qkv_o=shape((LAYERS, narrow, depth, 3 * cols), BF16),
        out_o=shape((LAYERS, depth, width), BF16),
        up_o=shape((LAYERS, narrow, depth, hidden), BF16),
        down_o=shape((LAYERS, narrow, hidden_own, width), BF16),
        bias_o=shape((narrow, 4 * LAYERS, width), F32),
        mod_o=shape((narrow, wide * LAYERS * SEGS, mod_cols), BF16),
        lead_o=shape((LAYERS, depth, wide * LAYERS * SEGS), BF16),
        lead_g=shape((narrow, wide, SEGS, depth), F32),
        qkv_h=shape((LAYERS, width, 3 * cols), BF16), out_h=shape((LAYERS, cols, width), BF16),
        up_h=shape((LAYERS, width, hidden), BF16), down_h=shape((LAYERS, hidden, width), BF16),
    )
    out_vmem = ("mixed_o", "token_o", "lead_o")
    vmem, dma = pltpu.VMEM, pltpu.SemaphoreType.DMA
    heads = cols // HEAD
    scratch = dict(
        qkv_v=vmem((width, 3 * cols), BF16), out_v=vmem((cols, width), BF16),
        up_v=vmem((width, hidden), BF16), down_v=vmem((hidden, width), BF16),
        hid_attn=vmem((LAYERS, row_len, width), BF16), hid_mlp=vmem((LAYERS, row_len, width), BF16),
        heads=vmem((LAYERS, 3 * heads, row_len, LANES), BF16),
        mixed=vmem((LAYERS, row_len, cols), BF16), log_sum=vmem((LAYERS, row_len, heads), F32),
        up=vmem((LAYERS, row_len, hidden), BF16), act=vmem((LAYERS, row_len, hidden), BF16),
        state=vmem((local, width), F32), middle=vmem((LAYERS, local, width), F32),
        branch=vmem((LAYERS, local, width), BF16), down=vmem((LAYERS, local, width), BF16),
        grad_hid=vmem((local, width), F32),
        grad_down=vmem((row_len, width), BF16), grad_branch=vmem((row_len, width), BF16),
        grad_up=vmem((row_len, hidden), BF16), grad_qkv=vmem((row_len, 3 * cols), BF16),
        grad_heads=vmem((heads, row_len, LANES), BF16),
        part=vmem((2, 2 * local, width), F32),
        core_tx=vmem((2, local, width), BF16), core_rx=vmem((2, local, width), BF16),
        side_tx=vmem((local, width), BF16), side_rx=vmem((local, width), BF16),
        ada_v=vmem((LAYERS, depth, mod_cols), BF16),
        lead=vmem((wide, 16, depth), BF16), lead_rx=vmem((wide, 16, depth), BF16),
        bias_rows=vmem((32, 3 * LANES), F32), bias_tx=vmem((32, 3 * LANES), BF16),
        bias_rx=vmem((wide, 32, 3 * LANES), BF16),
        ada_full=vmem((1, LAYERS, tiles * LANES), F32), qkv_full=vmem((1, LAYERS, 3 * width), F32),
        out_full=vmem((1, LAYERS, width), F32), up_full=vmem((1, LAYERS, narrow * hidden), F32),
        down_full=vmem((1, LAYERS, width), F32), seg_col=vmem((row_len, 1), jnp.int32),
        qkv_raw=vmem((LAYERS, 3, depth, 3 * LANES), BF16), up_raw=vmem((LAYERS, wide, depth, 2 * LANES), BF16),
        qkv_s=vmem((LAYERS, depth, 3 * cols), BF16), up_s=vmem((LAYERS, depth, hidden), BF16),
        lead_t=vmem((LAYERS, wide * LAYERS * SEGS, depth), F32),
        lead_tx=vmem((wide, SEGS, depth), F32), lead_back=vmem((wide, SEGS, depth), F32),
        bias_sum=vmem((4 * LAYERS, width), F32),
        mod_part=vmem((wide, LAYERS * SEGS, mod_cols), F32),
        mod_rx=vmem((wide, LAYERS * SEGS, mod_cols), F32),
        mod_q=vmem((narrow, LAYERS * SEGS, mod_cols), F32),
        mods=vmem((LAYERS * SEGS, tiles * LANES), F32),
        mod_grad=vmem((LAYERS * SEGS, tiles * LANES), F32),
        quarter_rx=vmem((3, LAYERS * SEGS, mod_cols), F32),
        quarter_sum=vmem((16, mod_cols // 2), BF16),
        quarter_all=vmem((wide, 16, mod_cols // 2), BF16),
        mod_all=vmem((wide * LAYERS * SEGS, mod_cols), BF16),
        bias_grad=vmem((4 * LAYERS, width), F32), bias_all=vmem((wide, 16, 5 * LANES), BF16),
        bias_half=vmem((16, 5 * LANES), BF16),
        bias_row=vmem((4 * LAYERS, width), F32),
        qkv_d=vmem((width, 3 * cols), BF16), out_d=vmem((cols, width), BF16),
        up_d=vmem((width, hidden), BF16), down_d=vmem((hidden, width), BF16),
        qkv_xr=vmem((PLANES, depth, 3 * cols), BF16), out_xr=vmem((1, depth, width), BF16),
        up_xr=vmem((PLANES, depth, hidden), BF16), down_xr=vmem((PLANES, hidden_own, width), BF16),
        qkv_zr=vmem((PLANES, depth, 3 * cols), BF16), out_zr=vmem((PLANES, depth, width), BF16),
        up_zr=vmem((PLANES, depth, hidden), BF16), down_zr=vmem((PLANES, hidden_own, width), BF16),
        qkv_f=vmem((depth, 3 * cols), BF16), out_f=vmem((depth, width), BF16),
        up_f=vmem((depth, hidden), BF16), down_f=vmem((hidden_own, width), BF16),
        wz_s=dma((8, 4)), wz_r=dma((8, 4)), wx_s=dma((8, 4)), wx_r=dma((8, 4)), w_own=dma((8,)),
        load_sem=dma((4,)), tok_s=dma((12,)), tok_r=dma((12,)), sum_s=dma((4,)), sum_r=dma((4,)),
        lead_sem_s=dma((wide - 1,)), lead_sem_r=dma((wide - 1,)),
        bias_sem_s=dma((wide - 1,)), bias_sem_r=dma((wide - 1,)),
        mod_sem_s=dma((wide - 1,)), mod_sem_r=dma((wide - 1,)),
        quarter_s=dma((3,)), quarter_r=dma((3,)), ada_sem=dma, raw_sem=dma((LAYERS, 3 + wide)), lead_own_sem=dma,
        lead_back_s=dma((wide - 1,)), lead_back_r=dma((wide - 1,)),
        lead_narrow_s=dma((3,)), lead_narrow_r=dma((3,)),
        dx_s=dma((4, 4)), dx_r=dma((4, 4)), dz_s=dma((4, 3)), dz_r=dma((4, 4)),
        e_s=dma((2, 3)), e_r=dma((2, 4)), ex_s=dma, ex_r=dma,
        down_e=vmem((hidden_own, width), BF16),
        spread_s=dma((8, 3)), spread_r=dma((8, 3)), spread_l=dma((8,)),
        back_s=dma((3,)), back_r=dma((3,)),
        wide_s=dma((wide - 1,)), wide_r=dma((wide - 1,)),
        bias_wide_s=dma((wide - 1,)), bias_wide_r=dma((wide - 1,)),
        bias_narrow_s=dma((3,)), bias_narrow_r=dma((3,)),
        mod_narrow_s=dma((3,)), mod_narrow_r=dma((3,)), mod_own_sem=dma, bias_own_sem=dma,
        credit_x=pltpu.SemaphoreType.REGULAR((4,)), credit_z=pltpu.SemaphoreType.REGULAR((4, 2)),
        credit_sum=pltpu.SemaphoreType.REGULAR((2,)),
    )
    cfg = SimpleNamespace(
        names=[*inputs, *outputs, *scratch], wide=wide, narrow=narrow, width=width, depth=depth,
        local=local, cols=cols, mod_cols=mod_cols, tiles=tiles,
    )

    def place(name, vmem_ok):
        return pl.BlockSpec(memory_space=pltpu.VMEM if vmem_ok else pl.ANY)

    results = pl.pallas_call(
        partial(block_kernel, cfg),
        out_shape=list(outputs.values()),
        in_specs=[place(name, name not in in_hbm) for name in inputs],
        out_specs=[place(name, name in out_vmem) for name in outputs],
        scratch_shapes=list(scratch.values()),
        compiler_params=pltpu.CompilerParams(
            collective_id=0, has_side_effects=True, vmem_limit_bytes=63 * 2**20
        ),
    )(*inputs.values())
    got = dict(zip(outputs, results))

    return finish(wide, narrow, got, cond[0], inputs["cond_index"], tiles, mod_cols, w)


def solution(mesh):
    matrix, vector = P(None, "wide", None), P(None, "wide")
    rows, cond_rows = P("wide", "narrow", None), P("wide", None, None)
    wide, narrow = mesh.shape["wide"], mesh.shape["narrow"]
    fused = wide == PLANES * PAIR and narrow == PLANES
    return jax.shard_map(
        partial(fused_device if fused else plain_device, wide, narrow),
        mesh=mesh,
        in_specs=(rows, cond_rows, P("wide", None), P("wide", None), rows) + (matrix, vector) * 5,
        out_specs=(rows, rows, cond_rows) + (matrix, vector) * 5,
        check_vma=False,
    )
```

```python
from functools import partial
import math
from types import SimpleNamespace

import jax
import jax.numpy as jnp
from jax import lax
from jax.experimental import pallas as pl
from jax.experimental.pallas import tpu as pltpu
from jax.sharding import PartitionSpec as P

HEADS = 16
HEAD = 72
LAYERS = 2
SEGS = 4
EPS = 1e-06
EXACT = lax.Precision.HIGHEST
F32 = jnp.float32
BF16 = jnp.bfloat16


def dot(left, right, dims):
    return lax.dot_general(left, right, (dims, ((), ())), preferred_element_type=F32)


def norm(values):
    centred = values - jnp.mean(values, -1, keepdims=True)
    inv = lax.rsqrt(jnp.mean(centred * centred, -1, keepdims=True) + EPS)
    return centred * inv, inv


def norm_back(grad, unit, inv):
    return inv * (
        grad
        - jnp.mean(grad, -1, keepdims=True)
        - unit * jnp.mean(grad * unit, -1, keepdims=True)
    )


def gather_tokens(values):
    return lax.all_gather(values, "narrow", axis=0, tiled=True)


def scatter_tokens(values):
    return lax.psum_scatter(
        values.astype(BF16), "narrow", scatter_dimension=0, tiled=True
    ).astype(F32)


def gelu(values):
    return jax.nn.gelu(values, approximate=True)


def layer_forward(state, mods, same_seg, weights):
    qkv_w, qkv_b, out_w, out_b, up_w, up_b, down_w, down_b = weights
    shift_attn, scale_attn, gate_attn, shift_mlp, scale_mlp, gate_mlp = mods
    own_heads = out_w.shape[0] // HEAD
    unit_attn, inv_attn = norm(state)
    hidden_attn = gather_tokens((unit_attn * (1.0 + scale_attn) + shift_attn).astype(BF16))
    full_len = hidden_attn.shape[0]
    qkv = (dot(hidden_attn, qkv_w, ((1,), (0,))) + qkv_b).astype(BF16)
    queries, keys, values = [
        part.reshape(full_len, own_heads, HEAD) for part in jnp.split(qkv, 3, axis=-1)
    ]
    scores = jnp.einsum("qhe,khe->hqk", queries, keys, preferred_element_type=F32) * (
        1.0 / math.sqrt(HEAD)
    )
    probs = jax.nn.softmax(jnp.where(same_seg[None], scores, -1e30), axis=-1)
    mixed = jnp.einsum("hqk,khe->qhe", probs.astype(BF16), values, preferred_element_type=F32)
    mixed = mixed.reshape(full_len, own_heads * HEAD).astype(BF16)
    branch = scatter_tokens(dot(mixed, out_w, ((1,), (0,)))) + out_b
    middle = state + gate_attn * branch
    unit_mlp, inv_mlp = norm(middle)
    hidden_mlp = gather_tokens((unit_mlp * (1.0 + scale_mlp) + shift_mlp).astype(BF16))
    up_proj = dot(hidden_mlp, up_w, ((1,), (0,))) + up_b
    activated = gelu(up_proj).astype(BF16)
    down_proj = scatter_tokens(dot(activated, down_w, ((1,), (0,)))) + down_b
    result = middle + gate_mlp * down_proj
    kept = (
        unit_attn, inv_attn, hidden_attn, queries, keys, values, probs, mixed, branch,
        unit_mlp, inv_mlp, hidden_mlp, up_proj, activated, down_proj,
    )
    return result, kept


def layer_backward(grad_out, kept, mods, weights):
    qkv_w, qkv_b, out_w, out_b, up_w, up_b, down_w, down_b = weights
    shift_attn, scale_attn, gate_attn, shift_mlp, scale_mlp, gate_mlp = mods
    (
        unit_attn, inv_attn, hidden_attn, queries, keys, values, probs, mixed, branch,
        unit_mlp, inv_mlp, hidden_mlp, up_proj, activated, down_proj,
    ) = kept
    scale_inv = 1.0 / math.sqrt(HEAD)
    full_len = hidden_attn.shape[0]
    own_down = (gate_mlp * grad_out).astype(BF16)
    grad_gate_mlp = down_proj * grad_out
    grad_down = gather_tokens(own_down)
    grad_act = dot(grad_down, down_w, ((1,), (1,)))
    grad_up = jax.vjp(gelu, up_proj)[1](grad_act)[0].astype(BF16)
    grad_hidden_mlp = scatter_tokens(dot(grad_up, up_w, ((1,), (1,))))
    grad_down_w = dot(activated, grad_down, ((0,), (0,)))
    grad_up_w = dot(hidden_mlp, grad_up, ((0,), (0,)))
    grad_middle = grad_out + norm_back(grad_hidden_mlp * (1.0 + scale_mlp), unit_mlp, inv_mlp)
    own_branch = (gate_attn * grad_middle).astype(BF16)
    grad_gate_attn = branch * grad_middle
    grad_branch = gather_tokens(own_branch)
    grad_attn = dot(grad_branch, out_w, ((1,), (1,))).astype(BF16).reshape(queries.shape)
    grad_probs = jnp.einsum("qhe,khe->hqk", grad_attn, values, preferred_element_type=F32)
    grad_scores = probs * (grad_probs - jnp.sum(probs * grad_probs, -1, keepdims=True))
    grad_scores = grad_scores.astype(BF16)
    grad_q = jnp.einsum("hqk,khe->qhe", grad_scores, keys, preferred_element_type=F32) * scale_inv
    grad_k = jnp.einsum("hqk,qhe->khe", grad_scores, queries, preferred_element_type=F32) * scale_inv
    grad_v = jnp.einsum("hqk,qhe->khe", probs.astype(BF16), grad_attn, preferred_element_type=F32)
    grad_qkv = jnp.concatenate(
        [part.astype(BF16).reshape(full_len, -1) for part in (grad_q, grad_k, grad_v)], axis=-1
    )
    grad_hidden_attn = scatter_tokens(dot(grad_qkv, qkv_w, ((1,), (1,))))
    grad_out_w = dot(mixed, grad_branch, ((0,), (0,)))
    grad_qkv_w = dot(hidden_attn, grad_qkv, ((0,), (0,)))
    grad_state = grad_middle + norm_back(grad_hidden_attn * (1.0 + scale_attn), unit_attn, inv_attn)
    token_mod = jnp.concatenate(
        [
            grad_hidden_attn, grad_hidden_attn * unit_attn, grad_gate_attn,
            grad_hidden_mlp, grad_hidden_mlp * unit_mlp, grad_gate_mlp,
        ],
        axis=-1,
    )
    bias_grads = (
        jnp.sum(grad_qkv.astype(F32), 0),
        jnp.sum(own_branch.astype(F32), 0),
        jnp.sum(grad_up.astype(F32), 0),
        jnp.sum(own_down.astype(F32), 0),
    )
    return grad_state, token_mod, (grad_qkv_w, grad_out_w, grad_up_w, grad_down_w), bias_grads


def plain_device(
    wide, narrow,
    tokens, cond, seg_ids, cond_index, cotangent,
    ada_weight, ada_bias, qkv_weight, qkv_bias, out_weight, out_bias,
    up_weight, up_bias, down_weight, down_bias,
):
    w = lax.axis_index("wide")
    n = lax.axis_index("narrow")
    local_len, width = tokens.shape[1:]
    depth = width // wide
    cols = width // narrow
    hidden_own = up_weight.shape[-1] // wide // narrow
    mod_cols = ada_weight.shape[-1] // narrow

    def own(values, axis):
        return lax.dynamic_index_in_dim(values, n, axis, keepdims=False)

    bias_parts = (ada_bias, qkv_bias, out_bias, up_bias, down_bias)
    sizes = [part.shape[1] for part in bias_parts]
    packed = lax.all_gather(jnp.concatenate(bias_parts, axis=1), "wide", axis=1, tiled=False)
    biases = []
    at = 0
    for size in sizes:
        biases.append(packed[:, :, at : at + size].reshape(LAYERS, -1).astype(F32))
        at += size
    ada_b, qkv_b, out_b, up_b, down_b = biases
    qkv_b = own(qkv_b.reshape(LAYERS, 3, narrow, cols), 2).reshape(LAYERS, 3 * cols)
    up_b = own(up_b.reshape(LAYERS, wide, narrow, hidden_own), 2).reshape(LAYERS, -1)

    cond_hot = (cond_index[0, :, None] == jnp.arange(SEGS, dtype=jnp.int32)[None, :]).astype(F32)
    chosen = jnp.dot(cond_hot, cond[0].astype(F32), precision=EXACT)
    lead = (chosen * jax.nn.sigmoid(chosen)).astype(BF16)
    lead_all = lax.all_gather(lead, "wide", axis=0, tiled=True)
    lead_own = lax.dynamic_slice_in_dim(lead_all, w * depth, depth, 1)
    ada_quarter = lax.dynamic_slice_in_dim(ada_weight, n * mod_cols, mod_cols, 2)
    mod_part = jnp.einsum("nd,lde->nle", lead_own, ada_quarter, preferred_element_type=F32)
    mod_part = lax.psum_scatter(mod_part, "wide", scatter_dimension=0, tiled=True)
    modulation = lax.all_gather(mod_part, "narrow", axis=2, tiled=True)
    modulation = modulation.transpose(1, 0, 2) + ada_b[:, None, :]

    seg_row = seg_ids[0]
    seg_query = lax.dynamic_slice_in_dim(seg_row, n * local_len, local_len, 0)
    token_hot = (seg_query[:, None] == jnp.arange(SEGS, dtype=jnp.int32)[None, :]).astype(F32)
    same_seg = seg_row[:, None] == seg_row[None, :]

    qkv_own = own(qkv_weight.reshape(LAYERS, depth, 3, narrow, cols), 3).reshape(LAYERS, depth, 3 * cols)
    up_own = own(up_weight.reshape(LAYERS, depth, wide, narrow, hidden_own), 3).reshape(LAYERS, depth, -1)
    down_own = own(down_weight.reshape(LAYERS, narrow, hidden_own, width), 1)

    def fetch(idx):
        out_full = lax.all_gather(out_weight[idx], "wide", axis=0, tiled=True)
        return (
            lax.all_gather(qkv_own[idx], "wide", axis=0, tiled=True),
            qkv_b[idx],
            lax.dynamic_slice_in_dim(out_full, n * cols, cols, 0),
            out_b[idx],
            lax.all_gather(up_own[idx], "wide", axis=0, tiled=True),
            up_b[idx],
            lax.all_gather(down_own[idx], "wide", axis=0, tiled=True),
            down_b[idx],
        )

    state = tokens[0].astype(F32)
    weights, mods, kept = [], [], []
    for idx in range(LAYERS):
        weights.append(fetch(idx))
        per_token = jnp.dot(token_hot, modulation[idx], precision=EXACT)
        mods.append(jnp.split(per_token, 6, axis=-1))
        state, saved = layer_forward(state, mods[idx], same_seg, weights[idx])
        kept.append(saved)
    result = state.astype(BF16)

    grad_state = cotangent[0].astype(F32)
    token_hot_t = token_hot.T
    reduced, bias_sums, mod_grads = [None] * LAYERS, [None] * LAYERS, [None] * LAYERS
    for idx in reversed(range(LAYERS)):
        grad_state, token_mod, grads, bias_grads = layer_backward(
            grad_state, kept[idx], mods[idx], weights[idx]
        )
        mod_grads[idx] = jnp.dot(token_hot_t, token_mod, precision=EXACT)
        qkv_g, out_g, up_g, down_g = [item.astype(BF16) for item in grads]
        qkv_g, up_g, down_g = [
            lax.psum_scatter(item, "wide", scatter_dimension=0, tiled=True)
            for item in (qkv_g, up_g, down_g)
        ]
        out_g = lax.psum(out_g, "wide")
        qkv_g = lax.all_gather(qkv_g.reshape(depth, 3, 1, cols), "narrow", axis=2, tiled=True)
        up_g = lax.all_gather(up_g.reshape(depth, wide, 1, hidden_own), "narrow", axis=2, tiled=True)
        down_g = lax.all_gather(down_g, "narrow", axis=0, tiled=True)
        out_g = lax.all_gather(out_g, "narrow", axis=0, tiled=True)
        out_g = lax.dynamic_slice_in_dim(out_g, w * depth, depth, 0)
        reduced[idx] = (
            qkv_g.reshape(depth, 3 * width),
            out_g,
            up_g.reshape(depth, -1),
            down_g,
        )
        spot = lax.broadcasted_iota(jnp.int32, (1, narrow, 1), 1) == n
        qkv_s = jnp.where(spot, bias_grads[0].reshape(3, 1, cols), 0.0).reshape(-1)
        up_s = jnp.where(spot, bias_grads[2].reshape(wide, 1, hidden_own), 0.0).reshape(-1)
        bias_sums[idx] = [
            item.reshape(wide, -1) for item in (qkv_s, bias_grads[1], up_s, bias_grads[3])
        ]
    sizes = [item.shape[1] for item in bias_sums[0]]
    bias_sum = jnp.stack([jnp.concatenate(item, axis=1) for item in bias_sums], axis=1)
    bias_sum = lax.psum_scatter(lax.psum(bias_sum, "narrow"), "wide", scatter_dimension=0, tiled=True)[0]
    bias_out = []
    at = 0
    for size in sizes:
        bias_out.append(bias_sum[:, at : at + size])
        at += size

    mod_grad = lax.psum(jnp.stack(mod_grads), "narrow").astype(BF16)
    mod_all = lax.all_gather(mod_grad, "wide", axis=1, tiled=True)
    ada_grad = jnp.einsum("nd,lne->lde", lead_own, mod_all, preferred_element_type=F32)
    ada_size = ada_bias.shape[1]
    ada_bias_grad = jnp.sum(
        lax.dynamic_slice_in_dim(mod_all, w * ada_size, ada_size, 2).astype(F32), axis=1
    )
    lead_grad = jnp.einsum("lne,lde->nd", mod_all, ada_weight, preferred_element_type=F32)
    lead_grad = lax.all_to_all(lead_grad.reshape(wide, SEGS, depth), "wide", 0, 0, tiled=False)
    lead_grad = lead_grad.transpose(1, 0, 2).reshape(SEGS, width)
    gate = jax.nn.sigmoid(chosen)
    chosen_grad = lead_grad * (gate * (1.0 + chosen * (1.0 - gate)))
    cond_grad = jnp.dot(cond_hot.T, chosen_grad, precision=EXACT)

    stacked = [
        jnp.stack([reduced[idx][pos].astype(F32) for idx in range(LAYERS)]) for pos in range(4)
    ]
    return (
        result[None], grad_state[None], cond_grad[None],
        ada_grad, ada_bias_grad,
        stacked[0], bias_out[0], stacked[1], bias_out[1],
        stacked[2], bias_out[2], stacked[3], bias_out[3],
    )


QKV, OUT, UP, DOWN = range(4)
PLANES = 4
PAIR = 2
LANES = 128
STEP = 32
MESH = pl.DeviceIdType.MESH


def mod_start(tiles, parts, part):
    return tiles * part // parts


def block_kernel(cfg, *refs):
    r = SimpleNamespace(**dict(zip(cfg.names, refs)))
    wide, narrow, width, depth = cfg.wide, cfg.narrow, cfg.width, cfg.depth
    local, cols, mod_cols, tiles = cfg.local, cfg.cols, cfg.mod_cols, cfg.tiles
    half = local // 2
    own_heads = cols // HEAD
    scale_inv = 1.0 / math.sqrt(HEAD)
    w = lax.axis_index("wide")
    n = lax.axis_index("narrow")
    z, x = w // PAIR, w % PAIR
    y, c = n // 2, n % 2
    n_core = n + 1 - 2 * c
    n_side = n + 2 - 4 * y
    n_far = 3 - n
    core, side, far = (w, n_core), (w, n_side), (w, n_far)
    beside = (w + 1 - 2 * x, n)

    z_half = z // 2
    z_partner, z_inner, z_outer = z + 1 - 2 * (z % 2), 2 - z_half, 3 - 3 * z_half
    is_inner = jnp.logical_or(z == 1, z == 2)

    def at_plane(idx):
        return (idx * PAIR + x, n)

    def wide_peer(j):
        return ((w + j) % wide, n)

    def remote(src, dst, sems, device):
        return pltpu.make_async_remote_copy(
            src_ref=src, dst_ref=dst, send_sem=sems[0], recv_sem=sems[1],
            device_id=device, device_id_type=MESH,
        )

    def span(start, size, step=16):
        return pl.ds(pl.multiple_of(start, step), size)

    ada_load = pltpu.make_async_copy(
        r.ada.at[:, :, span(LANES * mod_start(tiles, narrow, n), mod_cols, LANES)], r.ada_v, r.ada_sem
    )
    hidden_own = r.up_w.shape[-1] // wide // narrow

    def windows(which):
        if which == QKV:
            return [(width * j + cols * n, cols, 3 * LANES) for j in range(3)]
        return [((j * narrow + n) * hidden_own, hidden_own, 2 * LANES) for j in range(wide)]

    def raw(which, layer, k):
        src, dst = ((r.qkv_w, r.qkv_raw), (r.up_w, r.up_raw))[which == UP]
        start, _, window = windows(which)[k]
        at = span(LANES * (start // LANES), window, LANES)
        return pltpu.make_async_copy(
            src.at[layer, :, at], dst.at[layer, k], r.raw_sem.at[layer, k + 3 * (which == UP)]
        )

    for layer in range(LAYERS):
        for which in (QKV, UP):
            for k in range(len(windows(which))):
                raw(which, layer, k).start()
        if layer == 0:
            ada_load.start()
    chosen = chosen_of(r.cond, r.cond_index)
    lead = (chosen * jax.nn.sigmoid(chosen)).astype(BF16).astype(F32)
    r.lead[...] = jnp.zeros_like(r.lead)
    for row in range(wide):
        tile = jnp.concatenate(
            [lead[:, depth * row : depth * (row + 1)], jnp.zeros((16 - SEGS, depth), F32)], 0
        )
        r.lead[row] = tile.astype(BF16)
    bias_refs = (r.ada_b, r.qkv_b, r.out_b, r.up_b, r.down_b)
    bias_places, row = [], 0
    for k, ref in enumerate(bias_refs):
        for start in range(0, ref.shape[1], 3 * LANES):
            size = min(3 * LANES, ref.shape[1] - start)
            bias_places.append((k, row, start, size))
            row += 1
    r.bias_rows[...] = jnp.zeros_like(r.bias_rows)
    for layer in range(LAYERS):
        for k, row, start, size in bias_places:
            line = r.bias_rows.shape[0] // LAYERS * layer + row
            values = bias_refs[k][...].astype(F32)[layer : layer + 1, start : start + size]
            r.bias_rows[line : line + 1, :size] = values
    r.bias_tx[...] = r.bias_rows[...].astype(BF16)

    barrier = pltpu.get_barrier_semaphore()
    partners = [core, side, far] + [wide_peer(j) for j in range(1, wide)]
    for partner in partners:
        pl.semaphore_signal(barrier, inc=1, device_id=partner, device_id_type=MESH)
    pl.semaphore_wait(barrier, len(partners))

    full = (r.qkv_h, r.out_h, r.up_h, r.down_h)
    loaded = (r.qkv_v, r.out_v, r.up_v, r.down_v)

    def shard(which, layer):
        if which == DOWN:
            return r.down_w.at[layer, span(depth * n, depth)]
        return (r.qkv_s, r.out_w, r.up_s)[which].at[layer]

    def w_rows(which, plane_idx, col):
        if which == OUT:
            return span(col * depth, depth)
        return span((plane_idx * PAIR + col) * depth, depth)

    def w_block(which, layer, plane_idx, col):
        return full[which].at[layer, w_rows(which, plane_idx, col)]

    def w_z(which, layer, kind, plane_idx, own=False):
        slot = layer * 4 + which
        block = w_block(which, layer, plane_idx, x)
        return remote(
            shard(which, layer) if own else block, block,
            (r.wz_s.at[slot, kind], r.wz_r.at[slot, plane_idx]),
            at_plane(z_inner if kind == 1 else z_partner),
        )

    def w_x(which, layer, plane_idx, col, own=False):
        slot = layer * 4 + which
        block = w_block(which, layer, plane_idx, col)
        return remote(
            shard(which, layer) if own else block, block,
            (r.wx_s.at[slot, plane_idx], r.wx_r.at[slot, plane_idx]), beside,
        )

    def w_own(which, layer):
        return pltpu.make_async_copy(
            shard(which, layer), w_block(which, layer, z, x), r.w_own.at[layer * 4 + which]
        )

    def weights_beside(which, layer):
        w_x(which, layer, z, x, True).start()
        w_own(which, layer).start()

    def weights_along(which, layer):
        w_z(which, layer, 1, z, True).start()
        w_z(which, layer, 0, z, True).start()

    early, early_outer = ((UP, 0), (DOWN, 0)), ((QKV, 1), (UP, 1))

    def weights_start(which, layer):
        def go():
            weights_along(which, layer)
            if (which, layer) in early_outer:
                pl.when(is_inner)(lambda: weights_beside(which, layer))
            elif (which, layer) not in early:
                weights_beside(which, layer)

        if which == OUT:
            pl.when(z == n)(go)
        else:
            go()

    passes_out = jnp.logical_and(is_inner, z_half != n // 2)

    def weights_steps(which, layer):
        def passed(plane_idx, kind):
            w_z(which, layer, 0, plane_idx).wait_recv()
            if kind:
                onward = passes_out if which == OUT else is_inner
                pl.when(onward)(lambda: w_z(which, layer, kind, plane_idx).start())
            w_x(which, layer, plane_idx, x).start()

        def ahead():
            slot = layer * 4 + which + 2
            if 2 < slot < 4 * LAYERS:
                weights_start(slot % 4, slot // 4)

        def step(plane_idx, kind):
            if kind == 0:
                ahead()
            passed(plane_idx, kind)

        def only():
            ahead()
            pl.when(z != n)(lambda: passed(n, 2))

        if which == OUT:
            return [only]
        return [
            partial(step, idx, kind) for idx, kind in ((z_partner, 0), (z_inner, 2), (z_outer, 3))
        ]

    steps = [
        (layer * 4 + which, step)
        for layer in range(LAYERS)
        for which in (QKV, OUT, UP, DOWN)
        for step in weights_steps(which, layer)
    ]

    def pump(count):
        for _ in range(min(count, len(steps))):
            steps.pop(0)[1]()

    def pump_through(which, layer):
        while steps and steps[0][0] <= layer * 4 + which:
            pump(1)

    def weights_finish(which, layer):
        if which == OUT:
            w_x(which, layer, n, 1 - x).wait_recv()
            pl.when(z == n)(lambda: w_own(which, layer).wait())
        else:
            for idx in range(PLANES):
                w_x(which, layer, idx, 1 - x).wait_recv()
            w_own(which, layer).wait()

    def weights_drain(which, layer):
        if which == OUT:
            w_x(which, layer, n, x).wait_send()

            @pl.when(z == n)
            def _():
                for kind in range(2):
                    w_z(which, layer, kind, z).wait_send()

            pl.when(passes_out)(lambda: w_z(which, layer, 2, n).wait_send())
        else:
            for kind in range(2):
                w_z(which, layer, kind, z).wait_send()
            for idx in range(PLANES):
                w_x(which, layer, idx, x).wait_send()

            @pl.when(is_inner)
            def _():
                w_z(which, layer, 2, z_inner).wait_send()
                w_z(which, layer, 3, z_outer).wait_send()

    def load(which, layer):
        return pltpu.make_async_copy(full[which].at[layer], loaded[which], r.load_sem.at[which])

    def weights_ready(which, layer):
        pump_through(which, layer)
        weights_finish(which, layer)
        load(which, layer).start()
        load(which, layer).wait()

    def tok_rows(chunk, part):
        return span(local * chunk + half * part, half)

    def tok_copy(ref, kind, part, incoming=False, early=False):
        chunk = ((n_core, n_side, n_far) if incoming else (n, n, n_side))[kind]
        rows = ref.at[tok_rows(chunk, part)]
        k = 2 * kind + part + 6 * early
        return remote(rows, rows, (r.tok_s.at[k], r.tok_r.at[k]), side if kind == 1 else core)

    def tok_send(ref, part, early=False):
        tok_copy(ref, 1, part, early=early).start()
        tok_copy(ref, 0, part, early=early).start()

    def tok_own(ref, early=False):
        for part in range(2):
            tok_copy(ref, 0, part, True, early).wait_recv()

    def tok_other(ref, early=False):
        for part in range(2):
            tok_copy(ref, 1, part, True, early).wait_recv()
            tok_copy(ref, 2, part, early=early).start()
        for part in range(2):
            tok_copy(ref, 2, part, True, early).wait_recv()

    def tok_drain(ref, early=False):
        for kind in range(3):
            for part in range(2):
                tok_copy(ref, kind, part, early=early).wait_send()

    def block_rows(block):
        return span(2 * local * (y if block else 1 - y), 2 * local)

    def sum_core(block):
        return remote(
            r.core_tx.at[block], r.core_rx.at[block], (r.sum_s.at[block], r.sum_r.at[block]), core
        )

    def sum_side(part):
        rows = span(half * part, half)
        return remote(
            r.side_tx.at[rows], r.side_rx.at[rows], (r.sum_s.at[2 + part], r.sum_r.at[2 + part]), side
        )

    def sum_block(block):
        r.core_tx[block] = r.part[block, span(local * (1 - c), local), :].astype(BF16)
        sum_core(block).start()

    def sum_cross():
        sum_core(0).wait_recv()
        for part in range(2):
            rows = span(half * part, half)
            mine = r.part[0, span(local * c + half * part, half), :]
            r.side_tx[rows, :] = (mine + r.core_rx[0, rows, :].astype(F32)).astype(BF16)
            sum_side(part).start()

    def sum_wait(part):
        if part == 0:
            sum_core(1).wait_recv()
        sum_side(part).wait_recv()
        if part == 1:
            for block in range(2):
                sum_core(block).wait_send()
                sum_side(block).wait_send()

    def sum_take(start):
        rows = span(start, STEP)
        return (
            r.part[1, span(local * c + start, STEP), :]
            + r.core_rx[1, rows, :].astype(F32)
            + r.side_rx[rows, :].astype(F32)
        )

    def each_step(part, body):
        @pl.loop(0, half // STEP)
        def _(i):
            body(half * part + STEP * i)

    def seg_of(start):
        return r.seg_col[span(local * n + start, STEP), :]

    def mod(layer, block, seg):
        rows = r.mods[SEGS * layer : SEGS * layer + SEGS, width * block : width * (block + 1)]
        out = rows[SEGS - 1 : SEGS]
        for s in range(SEGS - 1):
            out = jnp.where(seg == s, rows[s : s + 1], out)
        return out

    def mod_sum(layer, block, seg, values):
        sums = [jnp.sum(jnp.where(seg == s, values, 0.0), 0, keepdims=True) for s in range(SEGS)]
        at = (slice(SEGS * layer, SEGS * layer + SEGS), slice(width * block, width * (block + 1)))
        r.mod_grad[at] += jnp.concatenate(sums, 0)

    seg_cols = jnp.transpose(jnp.broadcast_to(r.seg_row[...].astype(F32), (8, narrow * local)))
    r.seg_col[...] = seg_cols[:, :1].astype(jnp.int32)

    def shifted(values, rest, size):
        window = values.shape[1]
        return pltpu.roll(values.astype(F32), (window - rest) % window, 1)[:, :size]

    def pick(ref, start, size, window):
        return shifted(ref[0, :, span(LANES * (start // LANES), window, LANES)], start % LANES, size)

    def pack(dst, pieces):
        at = 0
        for piece in pieces:
            size = piece.shape[1]
            dst[..., at : at + size] = piece.astype(dst.dtype)
            at += size

    def pack_shard(which, layer):
        dst, pieces = (r.qkv_s if which == QKV else r.up_s).at[layer], []
        for k, (start, size, _) in enumerate(windows(which)):
            raw(which, layer, k).wait()
            buffer = r.qkv_raw if which == QKV else r.up_raw
            pieces.append(shifted(buffer[layer, k], start % LANES, size))
        pack(dst, pieces)

    def folded(values, size):
        rest = values[:, size:]
        if rest.shape[1] < size:
            rest = jnp.concatenate([rest, jnp.zeros((8, size - rest.shape[1]), F32)], 1)
        return jnp.concatenate([values[:, :size], rest], 0).astype(BF16)

    def unfolded(values, size):
        values = values.astype(F32)
        return jnp.concatenate([values[:8], values[8:]], 1)[:, :size]

    def lead_copy(j, incoming=False):
        return remote(
            r.lead.at[(w + j) % wide], r.lead_rx.at[(w - j + wide) % wide if incoming else w],
            (r.lead_sem_s.at[j - 1], r.lead_sem_r.at[j - 1]), wide_peer(j),
        )

    def bias_copy(j, incoming=False):
        return remote(
            r.bias_tx, r.bias_rx.at[(w - j + wide) % wide if incoming else w],
            (r.bias_sem_s.at[j - 1], r.bias_sem_r.at[j - 1]), wide_peer(j),
        )

    def mod_copy(j, incoming=False):
        return remote(
            r.mod_part.at[(w + j) % wide], r.mod_rx.at[(w - j + wide) % wide if incoming else w],
            (r.mod_sem_s.at[j - 1], r.mod_sem_r.at[j - 1]), wide_peer(j),
        )

    def wait_all(copy, count=wide):
        for j in range(1, count):
            copy(j, True).wait_recv()

    narrow_peers = ((core, n_core), (side, n_side), (far, n_far))

    def quarter_copy(k, incoming=False):
        device, idx = narrow_peers[k]
        return remote(
            r.mod_q.at[n], r.mod_q.at[idx if incoming else n],
            (r.quarter_s.at[k], r.quarter_r.at[k]), device,
        )

    for j in range(1, wide):
        lead_copy(j).start()
    for j in range(1, wide):
        bias_copy(j).start()
    r.bias_rx[pl.ds(w, 1)] = r.bias_tx[...][None]
    pack_shard(QKV, 0)
    weights_start(QKV, 0)
    r.lead_rx[pl.ds(w, 1)] = r.lead[pl.ds(w, 1)]
    ada_load.wait()
    wait_all(lead_copy)
    lead_all = r.lead_rx[...].reshape(wide * 16, depth)
    for layer in range(LAYERS):
        product = dot(lead_all, r.ada_v[layer], ((1,), (0,)))
        for row in range(wide):
            at = slice(SEGS * layer, SEGS * layer + SEGS)
            r.mod_part[row, at, :] = product[16 * row : 16 * row + SEGS]
    for j in range(1, wide):
        mod_copy(j).start()
    r.mod_rx[pl.ds(w, 1)] = r.mod_part[pl.ds(w, 1)]
    for which, layer in ((UP, 0), (QKV, 1), (UP, 1)):
        pack_shard(which, layer)
    for item in early:
        weights_beside(*item)

    def after_first():
        weights_start(OUT, 0)
        weights_along(UP, 0)

    @pl.when(jnp.logical_not(is_inner))
    def _():
        for item in early_outer:
            weights_beside(*item)
        after_first()

    pump_through(QKV, 0)
    pl.when(is_inner)(after_first)
    r.mod_grad[...] = jnp.zeros_like(r.mod_grad)
    r.lead_t[...] = jnp.zeros_like(r.lead_t)
    for layer in range(LAYERS):
        for row in range(wide):
            at = (row * LAYERS + layer) * SEGS
            r.lead_t[layer, at : at + SEGS, :] = r.lead_rx[row].astype(F32)[:SEGS]
        r.lead_o[layer] = jnp.transpose(r.lead_t[layer]).astype(BF16)

    wait_all(bias_copy)
    bias_full = (r.ada_full, r.qkv_full, r.out_full, r.up_full, r.down_full)
    for peer in range(wide):
        values = r.bias_rx[peer].astype(F32)
        for layer in range(LAYERS):
            for k, row, start, size in bias_places:
                line = values.shape[0] // LAYERS * layer + row
                at = bias_refs[k].shape[1] * peer + start
                bias_full[k][0, layer : layer + 1, at : at + size] = values[line : line + 1, :size]
    for which, ref in ((QKV, r.qkv_full), (UP, r.up_full)):
        pieces = [pick(ref, *window) for window in windows(which)]
        for layer in range(LAYERS):
            at = 4 * layer + which
            pack(r.bias_sum.at[at : at + 1], [piece[layer : layer + 1] for piece in pieces])
    for layer in range(LAYERS):
        at = 4 * layer
        r.bias_sum[at + OUT : at + OUT + 1] = r.out_full[0, layer : layer + 1]
        r.bias_sum[at + DOWN : at + DOWN + 1] = r.down_full[0, layer : layer + 1]

    wait_all(mod_copy)
    ada_own = r.ada_full[0, :, span(LANES * mod_start(tiles, narrow, n), mod_cols, LANES)]
    total = jnp.sum(r.mod_rx[...], 0)
    for layer in range(LAYERS):
        at = slice(SEGS * layer, SEGS * layer + SEGS)
        r.mod_q[pl.ds(n, 1), at, :] = (total[at] + ada_own[layer : layer + 1])[None]
    for k in range(3):
        quarter_copy(k).start()
    for k in range(3):
        quarter_copy(k, True).wait_recv()
    for part in range(narrow):
        at = LANES * mod_start(tiles, narrow, part)
        r.mods[:, at : at + mod_cols] = r.mod_q[part]

    def bias_row(layer, which, size):
        return r.bias_sum[4 * layer + which : 4 * layer + which + 1, :size]

    def gather_norm(layer, hid, shift, scale, take, before):
        for part in range(2):
            before(part)

            def step(start):
                seg = seg_of(start)
                unit, _ = norm(take(start, seg))
                hidden = unit * (1.0 + mod(layer, scale, seg)) + mod(layer, shift, seg)
                hid[span(local * n + start, STEP), :] = hidden.astype(BF16)

            each_step(part, step)
            tok_send(hid, part)

    def qkv_block(layer, block):
        rows = block_rows(block)
        out = dot(r.hid_attn[layer, rows, :], r.qkv_v[...], ((1,), (0,)))
        out = (out + bias_row(layer, QKV, 3 * cols)).astype(BF16)
        for j in range(3 * own_heads):
            r.heads[layer, j, rows, :HEAD] = out[:, HEAD * j : HEAD * (j + 1)]

    def attend(layer):
        for head in range(own_heads):

            @pl.loop(0, narrow)
            def _(i):
                rows = span(local * i, local)
                query = r.heads[layer, head, rows, :HEAD]
                key = r.heads[layer, own_heads + head, :, :HEAD]
                value = r.heads[layer, 2 * own_heads + head, :, :HEAD]
                scores = dot(query, key, ((1,), (1,))) * scale_inv
                scores = jnp.where(r.seg_col[rows, :] == r.seg_row[...], scores, -1e30)
                top = jnp.max(scores, -1, keepdims=True)
                power = jnp.exp(scores - top)
                total = jnp.sum(power, -1, keepdims=True)
                probs = (power / total).astype(BF16)
                mixed = dot(probs, value, ((1,), (0,)))
                r.mixed[layer, rows, HEAD * head : HEAD * (head + 1)] = mixed.astype(BF16)
                r.log_sum[layer, rows, head : head + 1] = top + jnp.log(total)

            if head % 2:
                pump(1)

    def up_block(layer, block):
        rows = block_rows(block)
        hidden = r.hid_mlp[layer, rows, :]
        for at in range(0, width, 3 * LANES):
            tile = slice(at, at + 3 * LANES)
            up = dot(hidden, r.up_v[:, tile], ((1,), (0,)))
            up = up + r.bias_sum[4 * layer + UP : 4 * layer + UP + 1, tile]
            r.up[layer, rows, tile] = up.astype(BF16)
            r.act[layer, rows, tile] = gelu(up).astype(BF16)

    def down_block(layer, block):
        r.part[block] = dot(r.act[layer, block_rows(block), :], r.down_v[...], ((1,), (0,)))

    def state_of(layer, start):
        rows = span(start, STEP)
        return r.tok[rows, :].astype(F32) if layer == 0 else r.state[rows, :]

    def after_attn(layer):
        def take(start, seg):
            rows = span(start, STEP)
            branch = sum_take(start) + bias_row(layer, OUT, width)
            r.branch[layer, rows, :] = branch.astype(BF16)
            middle = state_of(layer, start) + mod(layer, 2, seg) * branch
            r.middle[layer, rows, :] = middle
            return middle

        return take

    def after_mlp(layer):
        def take(start, seg):
            rows = span(start, STEP)
            down = sum_take(start) + bias_row(layer, DOWN, width)
            r.down[layer, rows, :] = down.astype(BF16)
            result = r.middle[layer, rows, :] + mod(layer, 5, seg) * down
            if layer == 0:
                r.state[rows, :] = result
            else:
                r.mixed_o[rows, :] = result.astype(BF16)
            return result

        return take

    def attn_forward(layer, take, before):
        hid = r.hid_attn.at[layer]
        gather_norm(layer, hid, 0, 1, take, before)
        if layer == 0:
            early_grad()
        pump(1)
        weights_ready(QKV, layer)
        tok_own(hid)
        qkv_block(layer, 1)
        pump(1)
        tok_other(hid)
        qkv_block(layer, 0)
        pump(1)
        if layer == 0:
            tok_own(r.grad_down, True)
            tok_other(r.grad_down, True)
        attend(layer)
        weights_ready(OUT, layer)
        tok_drain(hid)
        for block in range(2):
            r.part[block] = dot(r.mixed[layer, block_rows(block), :], r.out_v[...], ((1,), (0,)))
            sum_block(block)
            if block == 0:
                sum_cross()
        pump(1)
        gather_norm(layer, r.hid_mlp.at[layer], 3, 4, after_attn(layer), sum_wait)
        pump(1)
        weights_ready(UP, layer)

    def early_grad():
        for part in range(2):

            def step(start):
                rows = span(start, STEP)
                grad = r.cot[rows, :].astype(F32)
                r.token_o[rows, :] = grad
                grad_down = (mod(LAYERS - 1, 5, seg_of(start)) * grad).astype(BF16)
                r.grad_down[span(local * n + start, STEP), :] = grad_down

            each_step(part, step)
            tok_send(r.grad_down, part, True)

    attn_forward(0, lambda start, seg: state_of(0, start), lambda part: None)
    weights_ready(DOWN, 0)
    hid = r.hid_mlp.at[0]
    tok_own(hid)
    up_block(0, 1)
    down_block(0, 1)
    sum_block(1)
    pump(1)
    tok_other(hid)
    up_block(0, 0)
    down_block(0, 0)
    sum_block(0)
    sum_cross()
    tok_drain(hid)
    pump(2)
    attn_forward(1, after_mlp(0), sum_wait)

    sums = (r.qkv_d, r.out_d, r.up_d, r.down_d)
    from_x = (r.qkv_xr, r.out_xr, r.up_xr, r.down_xr)
    from_z = (r.qkv_zr, r.out_zr, r.up_zr, r.down_zr)
    final = (r.qkv_f, r.out_f, r.up_f, r.down_f)
    grads_o = (r.qkv_o, r.out_o, r.up_o, r.down_o)
    same_y, same_c = y == z // 2, c == z % 2

    def d_rows(which, plane_idx, col):
        return w_rows(which, plane_idx, col)

    def d_x(which, plane_idx, incoming=False):
        k = 0 if which == OUT else plane_idx
        src = sums[which].at[d_rows(which, plane_idx, 1 - x)]
        return remote(
            src, from_x[which].at[k], (r.dx_s.at[which, k], r.dx_r.at[which, k]), beside
        )

    def d_z(which, kind):
        idx = 0 if which == OUT else (z_partner, z_inner, z_outer)[kind]
        src = from_x[which].at[idx]

        def send(slot, plane_idx):
            return remote(
                src, from_z[which].at[slot], (r.dz_s.at[which, kind], r.dz_r.at[which, slot]),
                at_plane(plane_idx),
            )

        return send

    def d_z_in(which, slot):
        ref = from_z[which].at[slot]
        return remote(ref, ref, (r.dz_s.at[which, 0], r.dz_r.at[which, slot]), at_plane(z_partner))

    def grad_product(which, layer):
        left, right = (
            (r.hid_attn, r.grad_qkv), (r.mixed, r.grad_branch),
            (r.hid_mlp, r.grad_up), (r.act, r.grad_down),
        )[which]
        if which == OUT:
            product = dot(left[layer], right[...], ((0,), (0,)))
            sums[which][...] = product.astype(BF16)
        else:

            @pl.loop(0, width // (3 * LANES))
            def _(i):
                tile = span(3 * LANES * i, 3 * LANES, LANES)
                product = dot(left[layer, :, tile], right[...], ((0,), (0,)))
                sums[which][tile, :] = product.astype(BF16)

    def grad_send(which, layer):
        if layer == 0:
            pl.semaphore_wait(r.credit_x.at[which], 1)
        if which == OUT:
            d_x(which, 0).start()
        else:
            for idx in (z_outer, z_inner, z_partner, z):
                d_x(which, idx).start()

    out_home = z == n
    out_near = z_partner == n
    out_far = z_half != n // 2

    def credit(sem, device):
        pl.semaphore_signal(sem, inc=1, device_id=device, device_id_type=MESH)

    def grad_beside(which, layer):
        def add(slot, rows):
            total = sums[which][rows, :].astype(F32) + from_x[which][slot].astype(F32)
            from_x[which][slot] = total.astype(BF16)

        if which == OUT:
            d_x(which, 0).wait_recv()
            add(0, d_rows(which, n, x))
            outer_far = jnp.logical_and(out_far, jnp.logical_not(is_inner))

            @pl.when(jnp.logical_or(out_near, outer_far))
            def _():
                if layer == 0:
                    pl.semaphore_wait(r.credit_z.at[which, 0], 1)

            pl.when(out_near)(lambda: d_z(which, 0)(0, z_partner).start())
            pl.when(outer_far)(lambda: d_z(which, 0)(2, z_partner).start())
            d_x(which, 0).wait_send()
        else:
            for k, idx in ((2, z_outer), (1, z_inner), (0, z_partner), (None, z)):
                d_x(which, idx).wait_recv()
                add(idx, d_rows(which, idx, x))
                if k == 2 and layer == 0:
                    pl.semaphore_wait(r.credit_z.at[which, 0], 1)
                if k == 0:
                    d_z(which, 0)(0, z_partner).start()
                elif k:
                    pl.when(jnp.logical_not(is_inner))(
                        lambda: d_z(which, k)(k + 1, z_partner).start()
                    )
            for idx in range(PLANES):
                d_x(which, idx).wait_send()

    def grad_join(which, layer):
        def add(slot, idx):
            d_z_in(which, slot).wait_recv()
            total = from_x[which][idx].astype(F32) + from_z[which][slot].astype(F32)
            from_x[which][idx] = total.astype(BF16)

        if which == OUT:

            @pl.when(jnp.logical_and(out_far, is_inner))
            def _():
                add(2, 0)
                if layer == 0:
                    pl.semaphore_wait(r.credit_z.at[which, 1], 1)
                else:
                    credit(r.credit_z.at[which, 0], at_plane(z_partner))
                d_z(which, 0)(1, n).start()
        else:

            @pl.when(is_inner)
            def _():
                if layer == 0:
                    pl.semaphore_wait(r.credit_z.at[which, 1], 2)
                add(3, z_outer)
                d_z(which, 2)(1, z_outer).start()
                add(2, z_inner)
                d_z(which, 1)(1, z_inner).start()

    def grad_planes(which, layer):
        def add():
            d_z_in(which, 0).wait_recv()
            d_z_in(which, 1).wait_recv()
            total = from_x[which][0 if which == OUT else z].astype(F32)
            total = total + from_z[which][0].astype(F32) + from_z[which][1].astype(F32)
            if layer == 0:
                spread_sent(which, 1)
            final[which][...] = total.astype(BF16)
            if layer == 1:
                credit(r.credit_z.at[which, 0], at_plane(z_partner))
                credit(r.credit_z.at[which, 1], at_plane(z_inner))

        if which == OUT:
            pl.when(out_home)(add)
            pl.when(jnp.logical_not(out_home))(lambda: d_z(which, 0)(0, z_partner).wait_send())
        else:
            add()
            for kind in range(3):
                d_z(which, kind)(0, z_partner).wait_send()
        if layer == 1:
            credit(r.credit_x.at[which], beside)

    def e_z(kind, other):
        idx = (z_partner, z_inner, z_outer)[kind]
        src = sums[DOWN].at[d_rows(DOWN, idx, 1 - x if other else x)]
        slots = from_x[DOWN] if other else from_z[DOWN]

        def send(slot, plane_idx):
            return remote(
                src, slots.at[slot], (r.e_s.at[int(other), kind], r.e_r.at[int(other), slot]),
                at_plane(plane_idx),
            )

        return send

    def e_in(slot, other):
        ref = (from_x[DOWN] if other else from_z[DOWN]).at[slot]
        remote(
            ref, ref, (r.e_s.at[int(other), 0], r.e_r.at[int(other), slot]), at_plane(z_partner)
        ).wait_recv()
        return ref[...].astype(F32)

    def e_x():
        return remote(from_x[DOWN].at[0], r.down_e, (r.ex_s, r.ex_r), beside)

    def first_send():
        @pl.when(jnp.logical_not(is_inner))
        def _():
            for kind in (2, 1):
                for other in (True, False):
                    e_z(kind, other)(kind + 1, z_partner).start()

        for other in (True, False):
            e_z(0, other)(0, z_partner).start()

    def first_join():
        @pl.when(is_inner)
        def _():
            for kind, idx in ((2, z_outer), (1, z_inner)):
                for other in (True, False):
                    rows = d_rows(DOWN, idx, 1 - x if other else x)
                    total = sums[DOWN][rows, :].astype(F32) + e_in(kind + 1, other)
                    sums[DOWN][rows, :] = total.astype(BF16)
                    e_z(kind, other)(1, idx).start()

    def first_planes():
        for other in (True, False):
            rows = d_rows(DOWN, z, 1 - x if other else x)
            total = sums[DOWN][rows, :].astype(F32) + e_in(0, other) + e_in(1, other)
            if other:
                from_x[DOWN][0] = total.astype(BF16)
                e_x().start()
            else:
                final[DOWN][...] = total.astype(BF16)
        for kind in range(3):
            for other in (True, False):
                e_z(kind, other)(0, z_partner).wait_send()
        credit(r.credit_z.at[DOWN, 0], at_plane(z_partner))
        credit(r.credit_z.at[DOWN, 1], at_plane(z_inner))

    def first_beside():
        e_x().wait_recv()
        total = final[DOWN][...].astype(F32) + r.down_e[...].astype(F32)
        final[DOWN][...] = total.astype(BF16)
        e_x().wait_send()
        credit(r.credit_x.at[DOWN], beside)

    def spread(which, layer, kind, source=None):
        slot = layer * 4 + which
        if which == OUT:
            dst = grads_o[which].at[layer]
        else:
            dst = grads_o[which].at[layer, n if source is None else source]
        src = final[which] if kind < 2 else dst
        return remote(
            src, dst, (r.spread_s.at[slot, kind], r.spread_r.at[slot, kind]), side if kind == 1 else core
        )

    def spread_own(which, layer):
        dst = grads_o[which].at[layer] if which == OUT else grads_o[which].at[layer, n]
        return pltpu.make_async_copy(final[which], dst, r.spread_l.at[layer * 4 + which])

    def spread_sent(which, layer):
        spread(which, layer, 1).wait_send()
        spread(which, layer, 0).wait_send()
        spread_own(which, layer).wait()

    def grad_spread(which, layer):
        def go():
            spread(which, layer, 1).start()
            spread(which, layer, 0).start()
            spread_own(which, layer).start()

        if which == OUT:
            pl.when(jnp.logical_and(same_y, same_c))(go)
        else:
            go()

    def grad_pass(which, layer):
        def go():
            spread(which, layer, 1, n_side).wait_recv()
            spread(which, layer, 2, n_side).start()

        if which == OUT:
            pl.when(jnp.logical_and(jnp.logical_not(same_y), same_c))(go)
        else:
            go()

    def grad_end(which, layer):
        if which == OUT:
            if layer == 0:
                pl.when(jnp.logical_and(same_y, same_c))(lambda: spread_sent(which, layer))

            @pl.when(jnp.logical_and(jnp.logical_not(same_y), same_c))
            def _():
                spread(which, layer, 2).wait_send()

            @pl.when(jnp.logical_and(same_y, jnp.logical_not(same_c)))
            def _():
                spread(which, layer, 0).wait_recv()

            @pl.when(jnp.logical_and(jnp.logical_not(same_y), jnp.logical_not(same_c)))
            def _():
                spread(which, layer, 2).wait_recv()
        else:
            spread(which, layer, 0, n_core).wait_recv()
            spread(which, layer, 2, n_far).wait_recv()
            spread(which, layer, 2, n_side).wait_send()
            if layer == 0:
                spread_sent(which, layer)

    def bias_grad(layer, which, values):
        at = 4 * layer + which
        r.bias_grad[at : at + 1, : values.shape[1]] = jnp.sum(
            values.astype(F32), 0, keepdims=True
        )

    def back_mlp_block(layer, block):
        rows = block_rows(block)
        grad_down = r.grad_down[rows, :]
        for at in range(0, width, 3 * LANES):
            tile = slice(at, at + 3 * LANES)
            grad_act = dot(grad_down, r.down_v[tile, :], ((1,), (1,)))
            up = r.up[layer, rows, tile].astype(F32)
            r.grad_up[rows, tile] = (grad_act * gelu_slope(up)).astype(BF16)
        r.part[block] = dot(r.grad_up[rows, :], r.up_v[...], ((1,), (1,)))

    def back_attn_block(layer, block):
        rows = block_rows(block)
        out = dot(r.grad_branch[rows, :], r.out_v[...], ((1,), (1,))).astype(BF16)
        for j in range(own_heads):
            r.grad_heads[j, rows, :HEAD] = out[:, HEAD * j : HEAD * (j + 1)]

    def back_attend(layer, head):
        @pl.loop(0, narrow)
        def _(i):
            rows = span(local * i, local)
            query = r.heads[layer, head, rows, :HEAD]
            key = r.heads[layer, own_heads + head, :, :HEAD]
            value = r.heads[layer, 2 * own_heads + head, :, :HEAD]
            grad = r.grad_heads[head, rows, :HEAD]
            scores = dot(query, key, ((1,), (1,))) * scale_inv
            probs = jnp.exp(scores - r.log_sum[layer, rows, head : head + 1])
            probs = jnp.where(r.seg_col[rows, :] == r.seg_row[...], probs, 0.0)
            grad_probs = dot(grad, value, ((1,), (1,)))
            inner = jnp.sum(probs * grad_probs, -1, keepdims=True)
            grad_scores = (probs * (grad_probs - inner)).astype(BF16)
            grad_query = dot(grad_scores, key, ((1,), (0,))) * scale_inv
            r.grad_qkv[rows, HEAD * head : HEAD * (head + 1)] = grad_query.astype(BF16)
            grad_key = dot(grad_scores, query, ((0,), (0,)))
            grad_value = dot(probs.astype(BF16), grad, ((0,), (0,)))

            def tile(k):
                return slice(LANES * k, LANES * k + HEAD)

            @pl.when(i == 0)
            def _():
                for k in range(narrow):
                    at = slice(local * k, local * (k + 1))
                    r.grad_hid[:, tile(k)] = grad_key[at]
                    r.grad_hid[:, tile(narrow + k)] = grad_value[at]

            @pl.when(i > 0)
            def _():
                for k in range(narrow):
                    at = slice(local * k, local * (k + 1))
                    r.grad_hid[:, tile(k)] += grad_key[at]
                    r.grad_hid[:, tile(narrow + k)] += grad_value[at]

        at = cols + HEAD * head
        for k in range(narrow):
            rows = slice(local * k, local * (k + 1))
            key_sum = r.grad_hid[:, LANES * k : LANES * k + HEAD]
            value_sum = r.grad_hid[:, LANES * (narrow + k) : LANES * (narrow + k) + HEAD]
            r.grad_qkv[rows, at : at + HEAD] = (key_sum * scale_inv).astype(BF16)
            r.grad_qkv[rows, cols + at : cols + at + HEAD] = value_sum.astype(BF16)

    def both(body):
        for part in range(2):
            each_step(part, body)

    def sums_attn(layer):
        def body(start):
            rows = span(start, STEP)
            seg = seg_of(start)
            unit, _ = norm(state_of(layer, start))
            grad_hidden = r.grad_hid[rows, :]
            mod_sum(layer, 0, seg, grad_hidden)
            mod_sum(layer, 1, seg, grad_hidden * unit)

        both(body)

    def sums_mlp(layer):
        def body(start):
            rows = span(start, STEP)
            seg = seg_of(start)
            unit, _ = norm(r.middle[layer, rows, :])
            grad_hidden = r.grad_hid[rows, :]
            mod_sum(layer, 3, seg, grad_hidden)
            mod_sum(layer, 4, seg, grad_hidden * unit)
            mod_sum(layer, 2, seg, r.branch[layer, rows, :].astype(F32) * r.token_o[rows, :])

        both(body)

    def sums_gate_mlp(layer, grad):
        def body(start):
            rows = span(start, STEP)
            mod_sum(
                layer, 5, seg_of(start), r.down[layer, rows, :].astype(F32) * grad[rows, :].astype(F32)
            )

        both(body)

    def back_middle(layer):
        for part in range(2):
            sum_wait(part)

            def step(start):
                rows = span(start, STEP)
                seg = seg_of(start)
                grad_hidden = sum_take(start)
                unit, inv = norm(r.middle[layer, rows, :])
                r.grad_hid[rows, :] = grad_hidden
                grad = r.token_o[rows, :] + norm_back(
                    grad_hidden * (1.0 + mod(layer, 4, seg)), unit, inv
                )
                r.token_o[rows, :] = grad
                grad_branch = (mod(layer, 2, seg) * grad).astype(BF16)
                r.grad_branch[span(local * n + start, STEP), :] = grad_branch

            each_step(part, step)
            tok_send(r.grad_branch, part)

    def back_state(layer, start):
        rows = span(start, STEP)
        grad_hidden = sum_take(start)
        unit, inv = norm(state_of(layer, start))
        r.grad_hid[rows, :] = grad_hidden
        r.token_o[rows, :] += norm_back(
            grad_hidden * (1.0 + mod(layer, 1, seg_of(start))), unit, inv
        )

    def back_qkv(layer, checked=False):
        for block in range(2):
            rows = block_rows(block)
            r.part[block] = dot(r.grad_qkv[rows, :], r.qkv_v[...], ((1,), (1,)))
            if checked and block == 0:
                pl.semaphore_wait(r.credit_sum.at[0], 1)
            sum_block(block)
            if block == 0:
                if checked:
                    pl.semaphore_wait(r.credit_sum.at[1], 1)
                sum_cross()

    hid = r.hid_mlp.at[1]
    tok_own(hid)
    up_block(1, 1)
    pump(1)
    tok_other(hid)
    up_block(1, 0)
    pump(1)
    grad_product(DOWN, 1)
    bias_grad(1, DOWN, r.grad_down[span(local * n, local), :])
    tok_drain(hid)
    tok_drain(r.grad_down, True)
    pump_through(DOWN, 1)
    first_send()
    weights_ready(DOWN, 1)
    for block in range(2):
        back_mlp_block(1, block)
        sum_block(block)
        if block == 0:
            sum_cross()
    load(UP, 0).start()
    grad_product(UP, 1)
    grad_send(UP, 1)
    bias_grad(1, UP, r.grad_up[...])
    back_middle(1)
    for block in range(2):
        down_block(1, block)
    load(DOWN, 0).start()
    sums_mlp(1)
    bias_grad(1, OUT, r.grad_branch[span(local * n, local), :])
    tok_own(r.grad_branch)
    back_attn_block(1, 1)
    tok_other(r.grad_branch)
    back_attn_block(1, 0)
    load(OUT, 0).start()
    for block in range(2):
        sum_block(block)
        if block == 0:
            sum_cross()
    grad_product(OUT, 1)
    grad_send(OUT, 1)
    for head in range(own_heads):
        back_attend(1, head)
        if head == 2:
            first_join()
    tok_drain(r.grad_branch)
    for part in range(2):
        sum_wait(part)
        finish_state = after_mlp(1)

        def last(start):
            finish_state(start, seg_of(start))

        each_step(part, last)
    credit(r.credit_sum.at[0], core)
    credit(r.credit_sum.at[1], side)
    back_qkv(1, True)
    load(QKV, 0).start()
    grad_product(QKV, 1)
    grad_send(QKV, 1)
    sums_gate_mlp(1, r.cot)
    grad_beside(UP, 1)
    bias_grad(1, QKV, r.grad_qkv[...])
    for part in range(2):
        sum_wait(part)

        def start_down(start):
            back_state(1, start)
            grad_down = (mod(0, 5, seg_of(start)) * r.token_o[span(start, STEP), :]).astype(BF16)
            r.grad_down[span(local * n + start, STEP), :] = grad_down

        each_step(part, start_down)
        tok_send(r.grad_down, part)
    sums_attn(1)
    sums_gate_mlp(0, r.token_o)
    bias_grad(0, DOWN, r.grad_down[span(local * n, local), :])
    load(DOWN, 0).wait()
    load(UP, 0).wait()
    grad_beside(OUT, 1)
    tok_own(r.grad_down)
    back_mlp_block(0, 1)
    sum_block(1)
    tok_other(r.grad_down)
    back_mlp_block(0, 0)
    sum_block(0)
    sum_cross()
    first_planes()
    grad_product(DOWN, 0)
    bias_grad(0, UP, r.grad_up[...])
    tok_drain(r.grad_down)
    back_middle(0)
    grad_product(UP, 0)
    first_beside()
    grad_send(DOWN, 0)
    grad_join(UP, 1)
    grad_join(OUT, 1)
    sums_mlp(0)
    bias_grad(0, OUT, r.grad_branch[span(local * n, local), :])
    grad_beside(QKV, 1)
    load(OUT, 0).wait()
    load(QKV, 0).wait()
    tok_own(r.grad_branch)
    back_attn_block(0, 1)
    tok_other(r.grad_branch)
    back_attn_block(0, 0)
    grad_spread(DOWN, 1)
    grad_product(OUT, 0)
    for head in range(own_heads):
        back_attend(0, head)
        if head == 1:
            grad_planes(UP, 1)
            grad_send(UP, 0)
    back_qkv(0)
    grad_join(QKV, 1)
    grad_product(QKV, 0)
    tok_drain(r.grad_branch)
    grad_beside(DOWN, 0)
    bias_grad(0, QKV, r.grad_qkv[...])
    for part in range(2):
        sum_wait(part)
        each_step(part, partial(back_state, 0))
    sums_attn(0)

    def quarter_back(k, incoming=False):
        device, idx = narrow_peers[k]
        at = span(LANES * mod_start(tiles, narrow, idx), mod_cols, LANES)
        return remote(
            r.mod_grad.at[:, at], r.quarter_rx.at[k], (r.back_s.at[k], r.back_r.at[k]), device
        )

    def wide_back(j, incoming=False):
        return remote(
            r.quarter_sum, r.quarter_all.at[(w - j + wide) % wide if incoming else w],
            (r.wide_s.at[j - 1], r.wide_r.at[j - 1]), wide_peer(j),
        )

    def bias_wide(j, incoming=False):
        return remote(
            r.bias_half, r.bias_all.at[(w - j + wide) % wide if incoming else w],
            (r.bias_wide_s.at[j - 1], r.bias_wide_r.at[j - 1]), wide_peer(j),
        )

    def bias_narrow(k, incoming=False):
        device, idx = narrow_peers[k]
        return remote(
            r.bias_row, r.bias_o.at[idx if incoming else n],
            (r.bias_narrow_s.at[k], r.bias_narrow_r.at[k]), device,
        )

    def mod_narrow(k, incoming=False):
        device, idx = narrow_peers[k]
        return remote(
            r.mod_all, r.mod_o.at[idx if incoming else n],
            (r.mod_narrow_s.at[k], r.mod_narrow_r.at[k]), device,
        )

    def lead_back(j, incoming=False):
        return remote(
            r.lead_tx.at[(w + j) % wide], r.lead_back.at[(w - j + wide) % wide if incoming else w],
            (r.lead_back_s.at[j - 1], r.lead_back_r.at[j - 1]), wide_peer(j),
        )

    def lead_narrow(k, incoming=False):
        device, idx = narrow_peers[k]
        return remote(
            r.lead_back, r.lead_g.at[idx if incoming else n],
            (r.lead_narrow_s.at[k], r.lead_narrow_r.at[k]), device,
        )

    for k in range(3):
        quarter_back(k).start()
    own_at = span(LANES * mod_start(tiles, narrow, n), mod_cols, LANES)
    total = r.mod_grad[:, own_at]
    for k in range(3):
        quarter_back(k, True).wait_recv()
        total = total + r.quarter_rx[k]
    r.quarter_sum[...] = folded(total, mod_cols // 2)
    for j in range(1, wide):
        wide_back(j).start()
    r.bias_half[...] = folded(r.bias_grad[...], 5 * LANES)
    for j in range(1, wide):
        bias_wide(j).start()
    r.quarter_all[pl.ds(w, 1)] = r.quarter_sum[...][None]
    r.bias_all[pl.ds(w, 1)] = r.bias_half[...][None]
    grad_planes(OUT, 1)
    grad_send(OUT, 0)
    grad_planes(QKV, 1)
    grad_send(QKV, 0)
    grad_spread(UP, 1)
    grad_spread(OUT, 1)
    grad_spread(QKV, 1)
    for which in (DOWN, UP, OUT, QKV):
        grad_pass(which, 1)
    grad_join(DOWN, 0)
    grad_beside(UP, 0)
    wait_all(wide_back)
    for j in range(1, wide):
        mod_copy(j).wait_send()
    for row in range(wide):
        r.mod_part[row] = unfolded(r.quarter_all[row], mod_cols)
    r.mod_all[...] = r.mod_part[...].reshape(wide * LAYERS * SEGS, mod_cols).astype(BF16)
    mod_own = pltpu.make_async_copy(r.mod_all, r.mod_o.at[n], r.mod_own_sem)
    mod_own.start()
    for k in range(3):
        mod_narrow(k).start()
    owned = LANES * (mod_start(tiles, narrow, n + 1) - mod_start(tiles, narrow, n))
    lane = lax.broadcasted_iota(jnp.int32, r.mod_all.shape, 1)
    own_grads = jnp.where(lane < owned, r.mod_all[...].astype(F32), 0.0).astype(BF16)
    lead_parts = [dot(own_grads, r.ada_v[layer], ((1,), (1,))) for layer in range(LAYERS)]
    for row in range(wide):
        at = row * LAYERS * SEGS
        r.lead_tx[row] = lead_parts[0][at : at + SEGS] + lead_parts[1][at + SEGS : at + 2 * SEGS]
    for j in range(1, wide):
        lead_back(j).start()
    r.lead_back[pl.ds(w, 1)] = r.lead_tx[pl.ds(w, 1)]
    grad_planes(DOWN, 0)
    grad_spread(DOWN, 0)
    grad_beside(OUT, 0)
    wait_all(bias_wide)
    r.bias_row[...] = unfolded(jnp.sum(r.bias_all[...].astype(F32), 0), width)
    bias_own = pltpu.make_async_copy(r.bias_row, r.bias_o.at[n], r.bias_own_sem)
    bias_own.start()
    for k in range(3):
        bias_narrow(k).start()
    grad_join(UP, 0)
    grad_join(OUT, 0)
    grad_beside(QKV, 0)
    wait_all(lead_back)
    lead_own = pltpu.make_async_copy(r.lead_back, r.lead_g.at[n], r.lead_own_sem)
    lead_own.start()
    for k in range(3):
        lead_narrow(k).start()
    grad_pass(DOWN, 0)
    grad_join(QKV, 0)
    grad_planes(UP, 0)
    grad_spread(UP, 0)
    grad_planes(OUT, 0)
    grad_spread(OUT, 0)
    grad_planes(QKV, 0)
    grad_spread(QKV, 0)
    for which in (UP, OUT, QKV):
        grad_pass(which, 0)

    for layer in range(LAYERS):
        for which in range(4):
            weights_drain(which, layer)
            grad_end(which, layer)
    for j in range(1, wide):
        for copy in (lead_copy, bias_copy, wide_back, bias_wide, lead_back):
            copy(j).wait_send()
    for k in range(3):
        for copy in (quarter_copy, quarter_back, mod_narrow, bias_narrow, lead_narrow):
            copy(k).wait_send()
        mod_narrow(k, True).wait_recv()
        bias_narrow(k, True).wait_recv()
        lead_narrow(k, True).wait_recv()
    mod_own.wait()
    lead_own.wait()
    bias_own.wait()


def gelu_slope(values):
    rate = math.sqrt(2.0 / math.pi)
    bent = jnp.tanh(rate * (values + 0.044715 * values * values * values))
    inner = rate * (1.0 + 3.0 * 0.044715 * values * values)
    return 0.5 * (1.0 + bent) + 0.5 * values * (1.0 - bent * bent) * inner


def chosen_of(cond, index):
    values = cond[...].astype(F32)
    rows = []
    for s in range(SEGS):
        row = values[SEGS - 1 : SEGS]
        for k in range(SEGS - 1):
            row = jnp.where(index[:, s : s + 1] == k, values[k : k + 1], row)
        rows.append(row)
    return jnp.concatenate(rows, 0)


def finish_kernel(cfg, *refs):
    r = SimpleNamespace(**dict(zip(cfg.names, refs)))
    wide, narrow, width, depth, cols = cfg.wide, cfg.narrow, cfg.width, cfg.depth, cfg.cols
    tiles, hidden_own = cfg.tiles, cfg.hidden_own
    w = lax.axis_index("wide")

    for part in range(narrow):
        values = r.qkv_i[0, part].astype(F32)
        for j in range(3):
            at = width * j + cols * part
            r.qkv_g[0, :, at : at + cols] = values[:, cols * j : cols * (j + 1)]
        values = r.up_i[0, part].astype(F32)
        for j in range(wide):
            at = (j * narrow + part) * hidden_own
            r.up_g[0, :, at : at + hidden_own] = values[:, hidden_own * j : hidden_own * (j + 1)]
        at, end = [LANES * mod_start(tiles, narrow, part + k) for k in range(2)]
        r.ada_g[0, :, at:end] = dot(r.lead_i[0], r.mod_i[part, :, : end - at], ((1,), (0,)))
    r.out_g[...] = r.out_i[...].astype(F32)
    r.down_g[...] = r.down_i[...].astype(F32)

    def pick(ref, size):
        start = size * w
        window = LANES * (-(-size // LANES) + 1)
        tile, rest = start // LANES, start % LANES
        values = ref[:, pl.ds(pl.multiple_of(LANES * tile, LANES), window)]
        return pltpu.roll(values, (window - rest) % window, 1)[:, :size]

    @pl.when(pl.program_id(0) + pl.program_id(1) == 0)
    def _():
        for part in range(narrow):
            values = r.bias_i[part]
            for j in range(3):
                at = width * j + cols * part
                r.qkv_t[:, at : at + cols] = values[:, cols * j : cols * (j + 1)]
            for j in range(wide):
                at = (j * narrow + part) * hidden_own
                r.up_t[:, at : at + hidden_own] = values[:, hidden_own * j : hidden_own * (j + 1)]
            at, end = [LANES * mod_start(tiles, narrow, part + k) for k in range(2)]
            values = r.mod_i[part, :, : end - at].astype(F32)
            layer_of = lax.broadcasted_iota(jnp.int32, values.shape, 0) // SEGS % LAYERS
            for layer in range(LAYERS):
                sums = jnp.sum(jnp.where(layer_of == layer, values, 0.0), 0, keepdims=True)
                r.ada_t[layer : layer + 1, at:end] = sums
        r.row_t[:, :width] = jnp.sum(r.bias_i[...], 0)
        for dst, ref, line, step in (
            (r.ada_bg, r.ada_t, 0, 1), (r.qkv_bg, r.qkv_t, QKV, 4), (r.out_bg, r.row_t, OUT, 4),
            (r.up_bg, r.up_t, UP, 4), (r.down_bg, r.row_t, DOWN, 4),
        ):
            values = pick(ref, dst.shape[1])
            for layer in range(LAYERS):
                at = step * layer + line
                dst[layer : layer + 1, :] = values[at : at + 1]
        chosen = chosen_of(r.cond, r.cond_index)
        gate = jax.nn.sigmoid(chosen)
        slope = gate * (1.0 + chosen * (1.0 - gate))
        lead_grad = jnp.sum(r.lead_i2[...], 0)
        for row in range(wide):
            at = slice(depth * row, depth * (row + 1))
            grad = lead_grad[row] * slope[:, at]
            for k in range(SEGS):
                total = jnp.zeros((1, depth), F32)
                for s in range(SEGS):
                    own = r.cond_index[:, s : s + 1] == k
                    total = total + jnp.where(own, grad[s : s + 1], 0.0)
                r.cond_g[k : k + 1, at] = total


def finish(wide, narrow, got, cond, cond_index, tiles, mod_cols, w):
    width = cond.shape[1]
    depth, cols = width // wide, width // narrow
    hidden_own = got["up_o"].shape[-1] // wide
    hidden_all = got["up_o"].shape[-1] * narrow
    down_rows = narrow * hidden_own
    bands = depth // 48
    rows = depth // bands
    shape, vmem = jax.ShapeDtypeStruct, pltpu.VMEM

    def whole(values):
        return pl.BlockSpec(values.shape, lambda i, j: (0,) * values.ndim)

    def band(*dims):
        return pl.BlockSpec(
            (1, *dims), lambda i, j: (i, 0, j, 0) if len(dims) == 3 else (i, j, 0)
        )

    down_i = got["down_o"].reshape(LAYERS, down_rows, width)
    inputs = dict(
        qkv_i=got["qkv_o"], up_i=got["up_o"], out_i=got["out_o"], down_i=down_i,
        lead_i=got["lead_o"], mod_i=got["mod_o"], bias_i=got["bias_o"], lead_i2=got["lead_g"],
        cond=cond, cond_index=cond_index,
    )
    in_specs = [
        band(narrow, rows, 3 * cols), band(narrow, rows, wide * hidden_own), band(rows, width),
        band(down_rows // bands, width), band(rows, got["lead_o"].shape[-1]),
        *[whole(inputs[name]) for name in ("mod_i", "bias_i", "lead_i2", "cond", "cond_index")],
    ]
    outputs = dict(
        ada_g=shape((LAYERS, depth, tiles * LANES), F32), qkv_g=shape((LAYERS, depth, 3 * width), F32),
        out_g=shape((LAYERS, depth, width), F32), up_g=shape((LAYERS, depth, hidden_all), F32),
        down_g=shape((LAYERS, down_rows, width), F32),
        ada_bg=shape((LAYERS, tiles * LANES // wide), F32), qkv_bg=shape((LAYERS, 3 * width // wide), F32),
        out_bg=shape((LAYERS, depth), F32), up_bg=shape((LAYERS, hidden_all // wide), F32),
        down_bg=shape((LAYERS, depth), F32), cond_g=shape((SEGS, width), F32),
    )
    out_specs = [
        band(rows, tiles * LANES), band(rows, 3 * width), band(rows, width), band(rows, hidden_all),
        band(down_rows // bands, width),
        *[whole(outputs[name]) for name in ("ada_bg", "qkv_bg", "out_bg", "up_bg", "down_bg", "cond_g")],
    ]
    scratch = dict(
        ada_t=vmem((8, (tiles + 2) * LANES), F32), qkv_t=vmem((8, 3 * width + 2 * LANES), F32),
        up_t=vmem((8, hidden_all + 2 * LANES), F32), row_t=vmem((8, width + 2 * LANES), F32),
    )
    cfg = SimpleNamespace(
        names=[*inputs, *outputs, *scratch], wide=wide, narrow=narrow, width=width, depth=depth,
        cols=cols, tiles=tiles, hidden_own=hidden_own,
    )
    results = pl.pallas_call(
        partial(finish_kernel, cfg),
        grid=(LAYERS, bands),
        out_shape=list(outputs.values()), in_specs=in_specs, out_specs=out_specs,
        scratch_shapes=list(scratch.values()),
        compiler_params=pltpu.CompilerParams(vmem_limit_bytes=62 * 2**20),
    )(*inputs.values())
    done = dict(zip(outputs, results))
    out = [got["mixed_o"][None], got["token_o"][None], done["cond_g"][None]]
    for name in ("ada", "qkv", "out", "up", "down"):
        out += [done[name + "_g"], done[name + "_bg"]]
    return tuple(out)


def fused_device(
    wide, narrow,
    tokens, cond, seg_ids, cond_index, cotangent,
    ada_weight, ada_bias, qkv_weight, qkv_bias, out_weight, out_bias,
    up_weight, up_bias, down_weight, down_bias,
):
    w = lax.axis_index("wide")
    n = lax.axis_index("narrow")
    local, width = tokens.shape[1:]
    row_len = seg_ids.shape[1]
    depth, cols = width // wide, width // narrow
    hidden_own = up_weight.shape[-1] // wide // narrow
    hidden = wide * hidden_own
    tiles = ada_weight.shape[-1] // LANES
    mod_cols = LANES * -(-tiles // narrow)

    inputs = dict(
        tok=tokens[0], cond=cond[0], cond_index=cond_index, seg_row=seg_ids,
        cot=cotangent[0], ada_b=ada_bias, qkv_b=qkv_bias, out_b=out_bias, up_b=up_bias, down_b=down_bias,
        ada=ada_weight, qkv_w=qkv_weight, out_w=out_weight, up_w=up_weight, down_w=down_weight,
    )
    in_hbm = ("ada", "qkv_w", "out_w", "up_w", "down_w")
    shape = jax.ShapeDtypeStruct
    outputs = dict(
        mixed_o=shape((local, width), BF16), token_o=shape((local, width), F32),
        qkv_o=shape((LAYERS, narrow, depth, 3 * cols), BF16),
        out_o=shape((LAYERS, depth, width), BF16),
        up_o=shape((LAYERS, narrow, depth, hidden), BF16),
        down_o=shape((LAYERS, narrow, hidden_own, width), BF16),
        bias_o=shape((narrow, 4 * LAYERS, width), F32),
        mod_o=shape((narrow, wide * LAYERS * SEGS, mod_cols), BF16),
        lead_o=shape((LAYERS, depth, wide * LAYERS * SEGS), BF16),
        lead_g=shape((narrow, wide, SEGS, depth), F32),
        qkv_h=shape((LAYERS, width, 3 * cols), BF16), out_h=shape((LAYERS, cols, width), BF16),
        up_h=shape((LAYERS, width, hidden), BF16), down_h=shape((LAYERS, hidden, width), BF16),
    )
    out_vmem = ("mixed_o", "token_o", "lead_o")
    vmem, dma = pltpu.VMEM, pltpu.SemaphoreType.DMA
    heads = cols // HEAD
    scratch = dict(
        qkv_v=vmem((width, 3 * cols), BF16), out_v=vmem((cols, width), BF16),
        up_v=vmem((width, hidden), BF16), down_v=vmem((hidden, width), BF16),
        hid_attn=vmem((LAYERS, row_len, width), BF16), hid_mlp=vmem((LAYERS, row_len, width), BF16),
        heads=vmem((LAYERS, 3 * heads, row_len, LANES), BF16),
        mixed=vmem((LAYERS, row_len, cols), BF16), log_sum=vmem((LAYERS, row_len, heads), F32),
        up=vmem((LAYERS, row_len, hidden), BF16), act=vmem((LAYERS, row_len, hidden), BF16),
        state=vmem((local, width), F32), middle=vmem((LAYERS, local, width), F32),
        branch=vmem((LAYERS, local, width), BF16), down=vmem((LAYERS, local, width), BF16),
        grad_hid=vmem((local, width), F32),
        grad_down=vmem((row_len, width), BF16), grad_branch=vmem((row_len, width), BF16),
        grad_up=vmem((row_len, hidden), BF16), grad_qkv=vmem((row_len, 3 * cols), BF16),
        grad_heads=vmem((heads, row_len, LANES), BF16),
        part=vmem((2, 2 * local, width), F32),
        core_tx=vmem((2, local, width), BF16), core_rx=vmem((2, local, width), BF16),
        side_tx=vmem((local, width), BF16), side_rx=vmem((local, width), BF16),
        ada_v=vmem((LAYERS, depth, mod_cols), BF16),
        lead=vmem((wide, 16, depth), BF16), lead_rx=vmem((wide, 16, depth), BF16),
        bias_rows=vmem((32, 3 * LANES), F32), bias_tx=vmem((32, 3 * LANES), BF16),
        bias_rx=vmem((wide, 32, 3 * LANES), BF16),
        ada_full=vmem((1, LAYERS, tiles * LANES), F32), qkv_full=vmem((1, LAYERS, 3 * width), F32),
        out_full=vmem((1, LAYERS, width), F32), up_full=vmem((1, LAYERS, narrow * hidden), F32),
        down_full=vmem((1, LAYERS, width), F32), seg_col=vmem((row_len, 1), jnp.int32),
        qkv_raw=vmem((LAYERS, 3, depth, 3 * LANES), BF16), up_raw=vmem((LAYERS, wide, depth, 2 * LANES), BF16),
        qkv_s=vmem((LAYERS, depth, 3 * cols), BF16), up_s=vmem((LAYERS, depth, hidden), BF16),
        lead_t=vmem((LAYERS, wide * LAYERS * SEGS, depth), F32),
        lead_tx=vmem((wide, SEGS, depth), F32), lead_back=vmem((wide, SEGS, depth), F32),
        bias_sum=vmem((4 * LAYERS, width), F32),
        mod_part=vmem((wide, LAYERS * SEGS, mod_cols), F32),
        mod_rx=vmem((wide, LAYERS * SEGS, mod_cols), F32),
        mod_q=vmem((narrow, LAYERS * SEGS, mod_cols), F32),
        mods=vmem((LAYERS * SEGS, tiles * LANES), F32),
        mod_grad=vmem((LAYERS * SEGS, tiles * LANES), F32),
        quarter_rx=vmem((3, LAYERS * SEGS, mod_cols), F32),
        quarter_sum=vmem((16, mod_cols // 2), BF16),
        quarter_all=vmem((wide, 16, mod_cols // 2), BF16),
        mod_all=vmem((wide * LAYERS * SEGS, mod_cols), BF16),
        bias_grad=vmem((4 * LAYERS, width), F32), bias_all=vmem((wide, 16, 5 * LANES), BF16),
        bias_half=vmem((16, 5 * LANES), BF16),
        bias_row=vmem((4 * LAYERS, width), F32),
        qkv_d=vmem((width, 3 * cols), BF16), out_d=vmem((cols, width), BF16),
        up_d=vmem((width, hidden), BF16), down_d=vmem((hidden, width), BF16),
        qkv_xr=vmem((PLANES, depth, 3 * cols), BF16), out_xr=vmem((1, depth, width), BF16),
        up_xr=vmem((PLANES, depth, hidden), BF16), down_xr=vmem((PLANES, hidden_own, width), BF16),
        qkv_zr=vmem((PLANES, depth, 3 * cols), BF16), out_zr=vmem((PLANES, depth, width), BF16),
        up_zr=vmem((PLANES, depth, hidden), BF16), down_zr=vmem((PLANES, hidden_own, width), BF16),
        qkv_f=vmem((depth, 3 * cols), BF16), out_f=vmem((depth, width), BF16),
        up_f=vmem((depth, hidden), BF16), down_f=vmem((hidden_own, width), BF16),
        wz_s=dma((8, 4)), wz_r=dma((8, 4)), wx_s=dma((8, 4)), wx_r=dma((8, 4)), w_own=dma((8,)),
        load_sem=dma((4,)), tok_s=dma((12,)), tok_r=dma((12,)), sum_s=dma((4,)), sum_r=dma((4,)),
        lead_sem_s=dma((wide - 1,)), lead_sem_r=dma((wide - 1,)),
        bias_sem_s=dma((wide - 1,)), bias_sem_r=dma((wide - 1,)),
        mod_sem_s=dma((wide - 1,)), mod_sem_r=dma((wide - 1,)),
        quarter_s=dma((3,)), quarter_r=dma((3,)), ada_sem=dma, raw_sem=dma((LAYERS, 3 + wide)), lead_own_sem=dma,
        lead_back_s=dma((wide - 1,)), lead_back_r=dma((wide - 1,)),
        lead_narrow_s=dma((3,)), lead_narrow_r=dma((3,)),
        dx_s=dma((4, 4)), dx_r=dma((4, 4)), dz_s=dma((4, 3)), dz_r=dma((4, 4)),
        e_s=dma((2, 3)), e_r=dma((2, 4)), ex_s=dma, ex_r=dma,
        down_e=vmem((hidden_own, width), BF16),
        spread_s=dma((8, 3)), spread_r=dma((8, 3)), spread_l=dma((8,)),
        back_s=dma((3,)), back_r=dma((3,)),
        wide_s=dma((wide - 1,)), wide_r=dma((wide - 1,)),
        bias_wide_s=dma((wide - 1,)), bias_wide_r=dma((wide - 1,)),
        bias_narrow_s=dma((3,)), bias_narrow_r=dma((3,)),
        mod_narrow_s=dma((3,)), mod_narrow_r=dma((3,)), mod_own_sem=dma, bias_own_sem=dma,
        credit_x=pltpu.SemaphoreType.REGULAR((4,)), credit_z=pltpu.SemaphoreType.REGULAR((4, 2)),
        credit_sum=pltpu.SemaphoreType.REGULAR((2,)),
    )
    cfg = SimpleNamespace(
        names=[*inputs, *outputs, *scratch], wide=wide, narrow=narrow, width=width, depth=depth,
        local=local, cols=cols, mod_cols=mod_cols, tiles=tiles,
    )

    def place(name, vmem_ok):
        return pl.BlockSpec(memory_space=pltpu.VMEM if vmem_ok else pl.ANY)

    results = pl.pallas_call(
        partial(block_kernel, cfg),
        out_shape=list(outputs.values()),
        in_specs=[place(name, name not in in_hbm) for name in inputs],
        out_specs=[place(name, name in out_vmem) for name in outputs],
        scratch_shapes=list(scratch.values()),
        compiler_params=pltpu.CompilerParams(
            collective_id=0, has_side_effects=True, vmem_limit_bytes=63 * 2**20
        ),
    )(*inputs.values())
    got = dict(zip(outputs, results))

    return finish(wide, narrow, got, cond[0], inputs["cond_index"], tiles, mod_cols, w)


def solution(mesh):
    matrix, vector = P(None, "wide", None), P(None, "wide")
    rows, cond_rows = P("wide", "narrow", None), P("wide", None, None)
    wide, narrow = mesh.shape["wide"], mesh.shape["narrow"]
    fused = wide == PLANES * PAIR and narrow == PLANES
    return jax.shard_map(
        partial(fused_device if fused else plain_device, wide, narrow),
        mesh=mesh,
        in_specs=(rows, cond_rows, P("wide", None), P("wide", None), rows) + (matrix, vector) * 5,
        out_specs=(rows, rows, cond_rows) + (matrix, vector) * 5,
        check_vma=False,
    )
```

```python
from functools import partial
import math
from types import SimpleNamespace

import jax
import jax.numpy as jnp
from jax import lax
from jax.experimental import pallas as pl
from jax.experimental.pallas import tpu as pltpu
from jax.sharding import PartitionSpec as P

HEADS = 16
HEAD = 72
LAYERS = 2
SEGS = 4
EPS = 1e-06
EXACT = lax.Precision.HIGHEST
F32 = jnp.float32
BF16 = jnp.bfloat16


def dot(left, right, dims):
    return lax.dot_general(left, right, (dims, ((), ())), preferred_element_type=F32)


def norm(values):
    centred = values - jnp.mean(values, -1, keepdims=True)
    inv = lax.rsqrt(jnp.mean(centred * centred, -1, keepdims=True) + EPS)
    return centred * inv, inv


def norm_back(grad, unit, inv):
    return inv * (
        grad
        - jnp.mean(grad, -1, keepdims=True)
        - unit * jnp.mean(grad * unit, -1, keepdims=True)
    )


def gather_tokens(values):
    return lax.all_gather(values, "narrow", axis=0, tiled=True)


def scatter_tokens(values):
    return lax.psum_scatter(
        values.astype(BF16), "narrow", scatter_dimension=0, tiled=True
    ).astype(F32)


def gelu(values):
    return jax.nn.gelu(values, approximate=True)


def layer_forward(state, mods, same_seg, weights):
    qkv_w, qkv_b, out_w, out_b, up_w, up_b, down_w, down_b = weights
    shift_attn, scale_attn, gate_attn, shift_mlp, scale_mlp, gate_mlp = mods
    own_heads = out_w.shape[0] // HEAD
    unit_attn, inv_attn = norm(state)
    hidden_attn = gather_tokens((unit_attn * (1.0 + scale_attn) + shift_attn).astype(BF16))
    full_len = hidden_attn.shape[0]
    qkv = (dot(hidden_attn, qkv_w, ((1,), (0,))) + qkv_b).astype(BF16)
    queries, keys, values = [
        part.reshape(full_len, own_heads, HEAD) for part in jnp.split(qkv, 3, axis=-1)
    ]
    scores = jnp.einsum("qhe,khe->hqk", queries, keys, preferred_element_type=F32) * (
        1.0 / math.sqrt(HEAD)
    )
    probs = jax.nn.softmax(jnp.where(same_seg[None], scores, -1e30), axis=-1)
    mixed = jnp.einsum("hqk,khe->qhe", probs.astype(BF16), values, preferred_element_type=F32)
    mixed = mixed.reshape(full_len, own_heads * HEAD).astype(BF16)
    branch = scatter_tokens(dot(mixed, out_w, ((1,), (0,)))) + out_b
    middle = state + gate_attn * branch
    unit_mlp, inv_mlp = norm(middle)
    hidden_mlp = gather_tokens((unit_mlp * (1.0 + scale_mlp) + shift_mlp).astype(BF16))
    up_proj = dot(hidden_mlp, up_w, ((1,), (0,))) + up_b
    activated = gelu(up_proj).astype(BF16)
    down_proj = scatter_tokens(dot(activated, down_w, ((1,), (0,)))) + down_b
    result = middle + gate_mlp * down_proj
    kept = (
        unit_attn, inv_attn, hidden_attn, queries, keys, values, probs, mixed, branch,
        unit_mlp, inv_mlp, hidden_mlp, up_proj, activated, down_proj,
    )
    return result, kept


def layer_backward(grad_out, kept, mods, weights):
    qkv_w, qkv_b, out_w, out_b, up_w, up_b, down_w, down_b = weights
    shift_attn, scale_attn, gate_attn, shift_mlp, scale_mlp, gate_mlp = mods
    (
        unit_attn, inv_attn, hidden_attn, queries, keys, values, probs, mixed, branch,
        unit_mlp, inv_mlp, hidden_mlp, up_proj, activated, down_proj,
    ) = kept
    scale_inv = 1.0 / math.sqrt(HEAD)
    full_len = hidden_attn.shape[0]
    own_down = (gate_mlp * grad_out).astype(BF16)
    grad_gate_mlp = down_proj * grad_out
    grad_down = gather_tokens(own_down)
    grad_act = dot(grad_down, down_w, ((1,), (1,)))
    grad_up = jax.vjp(gelu, up_proj)[1](grad_act)[0].astype(BF16)
    grad_hidden_mlp = scatter_tokens(dot(grad_up, up_w, ((1,), (1,))))
    grad_down_w = dot(activated, grad_down, ((0,), (0,)))
    grad_up_w = dot(hidden_mlp, grad_up, ((0,), (0,)))
    grad_middle = grad_out + norm_back(grad_hidden_mlp * (1.0 + scale_mlp), unit_mlp, inv_mlp)
    own_branch = (gate_attn * grad_middle).astype(BF16)
    grad_gate_attn = branch * grad_middle
    grad_branch = gather_tokens(own_branch)
    grad_attn = dot(grad_branch, out_w, ((1,), (1,))).astype(BF16).reshape(queries.shape)
    grad_probs = jnp.einsum("qhe,khe->hqk", grad_attn, values, preferred_element_type=F32)
    grad_scores = probs * (grad_probs - jnp.sum(probs * grad_probs, -1, keepdims=True))
    grad_scores = grad_scores.astype(BF16)
    grad_q = jnp.einsum("hqk,khe->qhe", grad_scores, keys, preferred_element_type=F32) * scale_inv
    grad_k = jnp.einsum("hqk,qhe->khe", grad_scores, queries, preferred_element_type=F32) * scale_inv
    grad_v = jnp.einsum("hqk,qhe->khe", probs.astype(BF16), grad_attn, preferred_element_type=F32)
    grad_qkv = jnp.concatenate(
        [part.astype(BF16).reshape(full_len, -1) for part in (grad_q, grad_k, grad_v)], axis=-1
    )
    grad_hidden_attn = scatter_tokens(dot(grad_qkv, qkv_w, ((1,), (1,))))
    grad_out_w = dot(mixed, grad_branch, ((0,), (0,)))
    grad_qkv_w = dot(hidden_attn, grad_qkv, ((0,), (0,)))
    grad_state = grad_middle + norm_back(grad_hidden_attn * (1.0 + scale_attn), unit_attn, inv_attn)
    token_mod = jnp.concatenate(
        [
            grad_hidden_attn, grad_hidden_attn * unit_attn, grad_gate_attn,
            grad_hidden_mlp, grad_hidden_mlp * unit_mlp, grad_gate_mlp,
        ],
        axis=-1,
    )
    bias_grads = (
        jnp.sum(grad_qkv.astype(F32), 0),
        jnp.sum(own_branch.astype(F32), 0),
        jnp.sum(grad_up.astype(F32), 0),
        jnp.sum(own_down.astype(F32), 0),
    )
    return grad_state, token_mod, (grad_qkv_w, grad_out_w, grad_up_w, grad_down_w), bias_grads


def plain_device(
    wide, narrow,
    tokens, cond, seg_ids, cond_index, cotangent,
    ada_weight, ada_bias, qkv_weight, qkv_bias, out_weight, out_bias,
    up_weight, up_bias, down_weight, down_bias,
):
    w = lax.axis_index("wide")
    n = lax.axis_index("narrow")
    local_len, width = tokens.shape[1:]
    depth = width // wide
    cols = width // narrow
    hidden_own = up_weight.shape[-1] // wide // narrow
    mod_cols = ada_weight.shape[-1] // narrow

    def own(values, axis):
        return lax.dynamic_index_in_dim(values, n, axis, keepdims=False)

    bias_parts = (ada_bias, qkv_bias, out_bias, up_bias, down_bias)
    sizes = [part.shape[1] for part in bias_parts]
    packed = lax.all_gather(jnp.concatenate(bias_parts, axis=1), "wide", axis=1, tiled=False)
    biases = []
    at = 0
    for size in sizes:
        biases.append(packed[:, :, at : at + size].reshape(LAYERS, -1).astype(F32))
        at += size
    ada_b, qkv_b, out_b, up_b, down_b = biases
    qkv_b = own(qkv_b.reshape(LAYERS, 3, narrow, cols), 2).reshape(LAYERS, 3 * cols)
    up_b = own(up_b.reshape(LAYERS, wide, narrow, hidden_own), 2).reshape(LAYERS, -1)

    cond_hot = (cond_index[0, :, None] == jnp.arange(SEGS, dtype=jnp.int32)[None, :]).astype(F32)
    chosen = jnp.dot(cond_hot, cond[0].astype(F32), precision=EXACT)
    lead = (chosen * jax.nn.sigmoid(chosen)).astype(BF16)
    lead_all = lax.all_gather(lead, "wide", axis=0, tiled=True)
    lead_own = lax.dynamic_slice_in_dim(lead_all, w * depth, depth, 1)
    ada_quarter = lax.dynamic_slice_in_dim(ada_weight, n * mod_cols, mod_cols, 2)
    mod_part = jnp.einsum("nd,lde->nle", lead_own, ada_quarter, preferred_element_type=F32)
    mod_part = lax.psum_scatter(mod_part, "wide", scatter_dimension=0, tiled=True)
    modulation = lax.all_gather(mod_part, "narrow", axis=2, tiled=True)
    modulation = modulation.transpose(1, 0, 2) + ada_b[:, None, :]

    seg_row = seg_ids[0]
    seg_query = lax.dynamic_slice_in_dim(seg_row, n * local_len, local_len, 0)
    token_hot = (seg_query[:, None] == jnp.arange(SEGS, dtype=jnp.int32)[None, :]).astype(F32)
    same_seg = seg_row[:, None] == seg_row[None, :]

    qkv_own = own(qkv_weight.reshape(LAYERS, depth, 3, narrow, cols), 3).reshape(LAYERS, depth, 3 * cols)
    up_own = own(up_weight.reshape(LAYERS, depth, wide, narrow, hidden_own), 3).reshape(LAYERS, depth, -1)
    down_own = own(down_weight.reshape(LAYERS, narrow, hidden_own, width), 1)

    def fetch(idx):
        out_full = lax.all_gather(out_weight[idx], "wide", axis=0, tiled=True)
        return (
            lax.all_gather(qkv_own[idx], "wide", axis=0, tiled=True),
            qkv_b[idx],
            lax.dynamic_slice_in_dim(out_full, n * cols, cols, 0),
            out_b[idx],
            lax.all_gather(up_own[idx], "wide", axis=0, tiled=True),
            up_b[idx],
            lax.all_gather(down_own[idx], "wide", axis=0, tiled=True),
            down_b[idx],
        )

    state = tokens[0].astype(F32)
    weights, mods, kept = [], [], []
    for idx in range(LAYERS):
        weights.append(fetch(idx))
        per_token = jnp.dot(token_hot, modulation[idx], precision=EXACT)
        mods.append(jnp.split(per_token, 6, axis=-1))
        state, saved = layer_forward(state, mods[idx], same_seg, weights[idx])
        kept.append(saved)
    result = state.astype(BF16)

    grad_state = cotangent[0].astype(F32)
    token_hot_t = token_hot.T
    reduced, bias_sums, mod_grads = [None] * LAYERS, [None] * LAYERS, [None] * LAYERS
    for idx in reversed(range(LAYERS)):
        grad_state, token_mod, grads, bias_grads = layer_backward(
            grad_state, kept[idx], mods[idx], weights[idx]
        )
        mod_grads[idx] = jnp.dot(token_hot_t, token_mod, precision=EXACT)
        qkv_g, out_g, up_g, down_g = [item.astype(BF16) for item in grads]
        qkv_g, up_g, down_g = [
            lax.psum_scatter(item, "wide", scatter_dimension=0, tiled=True)
            for item in (qkv_g, up_g, down_g)
        ]
        out_g = lax.psum(out_g, "wide")
        qkv_g = lax.all_gather(qkv_g.reshape(depth, 3, 1, cols), "narrow", axis=2, tiled=True)
        up_g = lax.all_gather(up_g.reshape(depth, wide, 1, hidden_own), "narrow", axis=2, tiled=True)
        down_g = lax.all_gather(down_g, "narrow", axis=0, tiled=True)
        out_g = lax.all_gather(out_g, "narrow", axis=0, tiled=True)
        out_g = lax.dynamic_slice_in_dim(out_g, w * depth, depth, 0)
        reduced[idx] = (
            qkv_g.reshape(depth, 3 * width),
            out_g,
            up_g.reshape(depth, -1),
            down_g,
        )
        spot = lax.broadcasted_iota(jnp.int32, (1, narrow, 1), 1) == n
        qkv_s = jnp.where(spot, bias_grads[0].reshape(3, 1, cols), 0.0).reshape(-1)
        up_s = jnp.where(spot, bias_grads[2].reshape(wide, 1, hidden_own), 0.0).reshape(-1)
        bias_sums[idx] = [
            item.reshape(wide, -1) for item in (qkv_s, bias_grads[1], up_s, bias_grads[3])
        ]
    sizes = [item.shape[1] for item in bias_sums[0]]
    bias_sum = jnp.stack([jnp.concatenate(item, axis=1) for item in bias_sums], axis=1)
    bias_sum = lax.psum_scatter(lax.psum(bias_sum, "narrow"), "wide", scatter_dimension=0, tiled=True)[0]
    bias_out = []
    at = 0
    for size in sizes:
        bias_out.append(bias_sum[:, at : at + size])
        at += size

    mod_grad = lax.psum(jnp.stack(mod_grads), "narrow").astype(BF16)
    mod_all = lax.all_gather(mod_grad, "wide", axis=1, tiled=True)
    ada_grad = jnp.einsum("nd,lne->lde", lead_own, mod_all, preferred_element_type=F32)
    ada_size = ada_bias.shape[1]
    ada_bias_grad = jnp.sum(
        lax.dynamic_slice_in_dim(mod_all, w * ada_size, ada_size, 2).astype(F32), axis=1
    )
    lead_grad = jnp.einsum("lne,lde->nd", mod_all, ada_weight, preferred_element_type=F32)
    lead_grad = lax.all_to_all(lead_grad.reshape(wide, SEGS, depth), "wide", 0, 0, tiled=False)
    lead_grad = lead_grad.transpose(1, 0, 2).reshape(SEGS, width)
    gate = jax.nn.sigmoid(chosen)
    chosen_grad = lead_grad * (gate * (1.0 + chosen * (1.0 - gate)))
    cond_grad = jnp.dot(cond_hot.T, chosen_grad, precision=EXACT)

    stacked = [
        jnp.stack([reduced[idx][pos].astype(F32) for idx in range(LAYERS)]) for pos in range(4)
    ]
    return (
        result[None], grad_state[None], cond_grad[None],
        ada_grad, ada_bias_grad,
        stacked[0], bias_out[0], stacked[1], bias_out[1],
        stacked[2], bias_out[2], stacked[3], bias_out[3],
    )


QKV, OUT, UP, DOWN = range(4)
PLANES = 4
PAIR = 2
LANES = 128
STEP = 32
MESH = pl.DeviceIdType.MESH


def mod_start(tiles, parts, part):
    return tiles * part // parts


def block_kernel(cfg, *refs):
    r = SimpleNamespace(**dict(zip(cfg.names, refs)))
    wide, narrow, width, depth = cfg.wide, cfg.narrow, cfg.width, cfg.depth
    local, cols, mod_cols, tiles = cfg.local, cfg.cols, cfg.mod_cols, cfg.tiles
    half = local // 2
    own_heads = cols // HEAD
    scale_inv = 1.0 / math.sqrt(HEAD)
    w = lax.axis_index("wide")
    n = lax.axis_index("narrow")
    z, x = w // PAIR, w % PAIR
    y, c = n // 2, n % 2
    n_core = n + 1 - 2 * c
    n_side = n + 2 - 4 * y
    n_far = 3 - n
    core, side, far = (w, n_core), (w, n_side), (w, n_far)
    beside = (w + 1 - 2 * x, n)

    z_half = z // 2
    z_partner, z_inner, z_outer = z + 1 - 2 * (z % 2), 2 - z_half, 3 - 3 * z_half
    is_inner = jnp.logical_or(z == 1, z == 2)

    def at_plane(idx):
        return (idx * PAIR + x, n)

    def wide_peer(j):
        return ((w + j) % wide, n)

    def remote(src, dst, sems, device):
        return pltpu.make_async_remote_copy(
            src_ref=src, dst_ref=dst, send_sem=sems[0], recv_sem=sems[1],
            device_id=device, device_id_type=MESH,
        )

    def span(start, size, step=16):
        return pl.ds(pl.multiple_of(start, step), size)

    ada_load = pltpu.make_async_copy(
        r.ada.at[:, :, span(LANES * mod_start(tiles, narrow, n), mod_cols, LANES)], r.ada_v, r.ada_sem
    )
    hidden_own = r.up_w.shape[-1] // wide // narrow

    def windows(which):
        if which == QKV:
            return [(width * j + cols * n, cols, 3 * LANES) for j in range(3)]
        return [((j * narrow + n) * hidden_own, hidden_own, 2 * LANES) for j in range(wide)]

    def raw(which, layer, k):
        src, dst = ((r.qkv_w, r.qkv_raw), (r.up_w, r.up_raw))[which == UP]
        start, _, window = windows(which)[k]
        at = span(LANES * (start // LANES), window, LANES)
        return pltpu.make_async_copy(
            src.at[layer, :, at], dst.at[layer, k], r.raw_sem.at[layer, k + 3 * (which == UP)]
        )

    for layer in range(LAYERS):
        for which in (QKV, UP):
            for k in range(len(windows(which))):
                raw(which, layer, k).start()
        if layer == 0:
            ada_load.start()
    chosen = chosen_of(r.cond, r.cond_index)
    lead = (chosen * jax.nn.sigmoid(chosen)).astype(BF16).astype(F32)
    r.lead[...] = jnp.zeros_like(r.lead)
    for row in range(wide):
        tile = jnp.concatenate(
            [lead[:, depth * row : depth * (row + 1)], jnp.zeros((16 - SEGS, depth), F32)], 0
        )
        r.lead[row] = tile.astype(BF16)
    bias_refs = (r.ada_b, r.qkv_b, r.out_b, r.up_b, r.down_b)
    bias_places, row = [], 0
    for k, ref in enumerate(bias_refs):
        for start in range(0, ref.shape[1], 3 * LANES):
            size = min(3 * LANES, ref.shape[1] - start)
            bias_places.append((k, row, start, size))
            row += 1
    r.bias_rows[...] = jnp.zeros_like(r.bias_rows)
    for layer in range(LAYERS):
        for k, row, start, size in bias_places:
            line = r.bias_rows.shape[0] // LAYERS * layer + row
            values = bias_refs[k][...].astype(F32)[layer : layer + 1, start : start + size]
            r.bias_rows[line : line + 1, :size] = values
    r.bias_tx[...] = r.bias_rows[...].astype(BF16)

    barrier = pltpu.get_barrier_semaphore()
    partners = [core, side, far] + [wide_peer(j) for j in range(1, wide)]
    for partner in partners:
        pl.semaphore_signal(barrier, inc=1, device_id=partner, device_id_type=MESH)
    pl.semaphore_wait(barrier, len(partners))

    full = (r.qkv_h, r.out_h, r.up_h, r.down_h)
    loaded = (r.qkv_v, r.out_v, r.up_v, r.down_v)

    def shard(which, layer):
        if which == DOWN:
            return r.down_w.at[layer, span(depth * n, depth)]
        return (r.qkv_s, r.out_w, r.up_s)[which].at[layer]

    def w_rows(which, plane_idx, col):
        if which == OUT:
            return span(col * depth, depth)
        return span((plane_idx * PAIR + col) * depth, depth)

    def w_block(which, layer, plane_idx, col):
        return full[which].at[layer, w_rows(which, plane_idx, col)]

    def w_z(which, layer, kind, plane_idx, own=False):
        slot = layer * 4 + which
        block = w_block(which, layer, plane_idx, x)
        return remote(
            shard(which, layer) if own else block, block,
            (r.wz_s.at[slot, kind], r.wz_r.at[slot, plane_idx]),
            at_plane(z_inner if kind == 1 else z_partner),
        )

    def w_x(which, layer, plane_idx, col, own=False):
        slot = layer * 4 + which
        block = w_block(which, layer, plane_idx, col)
        return remote(
            shard(which, layer) if own else block, block,
            (r.wx_s.at[slot, plane_idx], r.wx_r.at[slot, plane_idx]), beside,
        )

    def w_own(which, layer):
        return pltpu.make_async_copy(
            shard(which, layer), w_block(which, layer, z, x), r.w_own.at[layer * 4 + which]
        )

    def weights_beside(which, layer):
        w_x(which, layer, z, x, True).start()
        w_own(which, layer).start()

    def weights_along(which, layer):
        w_z(which, layer, 1, z, True).start()
        w_z(which, layer, 0, z, True).start()

    early, early_outer = ((UP, 0), (DOWN, 0)), ((QKV, 1), (UP, 1))

    def weights_start(which, layer):
        def go():
            weights_along(which, layer)
            if (which, layer) in early_outer:
                pl.when(is_inner)(lambda: weights_beside(which, layer))
            elif (which, layer) not in early:
                weights_beside(which, layer)

        if which == OUT:
            pl.when(z == n)(go)
        else:
            go()

    passes_out = jnp.logical_and(is_inner, z_half != n // 2)

    def weights_steps(which, layer):
        def passed(plane_idx, kind):
            w_z(which, layer, 0, plane_idx).wait_recv()
            if kind:
                onward = passes_out if which == OUT else is_inner
                pl.when(onward)(lambda: w_z(which, layer, kind, plane_idx).start())
            w_x(which, layer, plane_idx, x).start()

        def ahead():
            slot = layer * 4 + which + 2
            if 2 < slot < 4 * LAYERS:
                weights_start(slot % 4, slot // 4)

        def step(plane_idx, kind):
            if kind == 0:
                ahead()
            passed(plane_idx, kind)

        def only():
            ahead()
            pl.when(z != n)(lambda: passed(n, 2))

        if which == OUT:
            return [only]
        return [
            partial(step, idx, kind) for idx, kind in ((z_partner, 0), (z_inner, 2), (z_outer, 3))
        ]

    steps = [
        (layer * 4 + which, step)
        for layer in range(LAYERS)
        for which in (QKV, OUT, UP, DOWN)
        for step in weights_steps(which, layer)
    ]

    def pump(count):
        for _ in range(min(count, len(steps))):
            steps.pop(0)[1]()

    def pump_through(which, layer):
        while steps and steps[0][0] <= layer * 4 + which:
            pump(1)

    def weights_finish(which, layer):
        if which == OUT:
            w_x(which, layer, n, 1 - x).wait_recv()
            pl.when(z == n)(lambda: w_own(which, layer).wait())
        else:
            for idx in range(PLANES):
                w_x(which, layer, idx, 1 - x).wait_recv()
            w_own(which, layer).wait()

    def weights_drain(which, layer):
        if which == OUT:
            w_x(which, layer, n, x).wait_send()

            @pl.when(z == n)
            def _():
                for kind in range(2):
                    w_z(which, layer, kind, z).wait_send()

            pl.when(passes_out)(lambda: w_z(which, layer, 2, n).wait_send())
        else:
            for kind in range(2):
                w_z(which, layer, kind, z).wait_send()
            for idx in range(PLANES):
                w_x(which, layer, idx, x).wait_send()

            @pl.when(is_inner)
            def _():
                w_z(which, layer, 2, z_inner).wait_send()
                w_z(which, layer, 3, z_outer).wait_send()

    def load(which, layer):
        return pltpu.make_async_copy(full[which].at[layer], loaded[which], r.load_sem.at[which])

    def weights_ready(which, layer):
        pump_through(which, layer)
        weights_finish(which, layer)
        load(which, layer).start()
        load(which, layer).wait()

    def tok_rows(chunk, part):
        return span(local * chunk + half * part, half)

    def tok_copy(ref, kind, part, incoming=False, early=False):
        chunk = ((n_core, n_side, n_far) if incoming else (n, n, n_side))[kind]
        rows = ref.at[tok_rows(chunk, part)]
        k = 2 * kind + part + 6 * early
        return remote(rows, rows, (r.tok_s.at[k], r.tok_r.at[k]), side if kind == 1 else core)

    def tok_send(ref, part, early=False):
        tok_copy(ref, 1, part, early=early).start()
        tok_copy(ref, 0, part, early=early).start()

    def tok_own(ref, early=False):
        for part in range(2):
            tok_copy(ref, 0, part, True, early).wait_recv()

    def tok_other(ref, early=False):
        for part in range(2):
            tok_copy(ref, 1, part, True, early).wait_recv()
            tok_copy(ref, 2, part, early=early).start()
        for part in range(2):
            tok_copy(ref, 2, part, True, early).wait_recv()

    def tok_drain(ref, early=False):
        for kind in range(3):
            for part in range(2):
                tok_copy(ref, kind, part, early=early).wait_send()

    def block_rows(block):
        return span(2 * local * (y if block else 1 - y), 2 * local)

    def sum_core(block):
        return remote(
            r.core_tx.at[block], r.core_rx.at[block], (r.sum_s.at[block], r.sum_r.at[block]), core
        )

    def sum_side(part):
        rows = span(half * part, half)
        return remote(
            r.side_tx.at[rows], r.side_rx.at[rows], (r.sum_s.at[2 + part], r.sum_r.at[2 + part]), side
        )

    def sum_block(block):
        r.core_tx[block] = r.part[block, span(local * (1 - c), local), :].astype(BF16)
        sum_core(block).start()

    def sum_cross():
        sum_core(0).wait_recv()
        for part in range(2):
            rows = span(half * part, half)
            mine = r.part[0, span(local * c + half * part, half), :]
            r.side_tx[rows, :] = (mine + r.core_rx[0, rows, :].astype(F32)).astype(BF16)
            sum_side(part).start()

    def sum_wait(part):
        if part == 0:
            sum_core(1).wait_recv()
        sum_side(part).wait_recv()
        if part == 1:
            for block in range(2):
                sum_core(block).wait_send()
                sum_side(block).wait_send()

    def sum_take(start):
        rows = span(start, STEP)
        return (
            r.part[1, span(local * c + start, STEP), :]
            + r.core_rx[1, rows, :].astype(F32)
            + r.side_rx[rows, :].astype(F32)
        )

    def each_step(part, body):
        @pl.loop(0, half // STEP)
        def _(i):
            body(half * part + STEP * i)

    def seg_of(start):
        return r.seg_col[span(local * n + start, STEP), :]

    def mod(layer, block, seg):
        rows = r.mods[SEGS * layer : SEGS * layer + SEGS, width * block : width * (block + 1)]
        out = rows[SEGS - 1 : SEGS]
        for s in range(SEGS - 1):
            out = jnp.where(seg == s, rows[s : s + 1], out)
        return out

    def mod_sum(layer, block, seg, values):
        sums = [jnp.sum(jnp.where(seg == s, values, 0.0), 0, keepdims=True) for s in range(SEGS)]
        at = (slice(SEGS * layer, SEGS * layer + SEGS), slice(width * block, width * (block + 1)))
        r.mod_grad[at] += jnp.concatenate(sums, 0)

    seg_cols = jnp.transpose(jnp.broadcast_to(r.seg_row[...].astype(F32), (8, narrow * local)))
    r.seg_col[...] = seg_cols[:, :1].astype(jnp.int32)

    def shifted(values, rest, size):
        window = values.shape[1]
        return pltpu.roll(values.astype(F32), (window - rest) % window, 1)[:, :size]

    def pick(ref, start, size, window):
        return shifted(ref[0, :, span(LANES * (start // LANES), window, LANES)], start % LANES, size)

    def pack(dst, pieces):
        at = 0
        for piece in pieces:
            size = piece.shape[1]
            dst[..., at : at + size] = piece.astype(dst.dtype)
            at += size

    def pack_shard(which, layer):
        dst, pieces = (r.qkv_s if which == QKV else r.up_s).at[layer], []
        for k, (start, size, _) in enumerate(windows(which)):
            raw(which, layer, k).wait()
            buffer = r.qkv_raw if which == QKV else r.up_raw
            pieces.append(shifted(buffer[layer, k], start % LANES, size))
        pack(dst, pieces)

    def folded(values, size):
        rest = values[:, size:]
        if rest.shape[1] < size:
            rest = jnp.concatenate([rest, jnp.zeros((8, size - rest.shape[1]), F32)], 1)
        return jnp.concatenate([values[:, :size], rest], 0).astype(BF16)

    def unfolded(values, size):
        values = values.astype(F32)
        return jnp.concatenate([values[:8], values[8:]], 1)[:, :size]

    def lead_copy(j, incoming=False):
        return remote(
            r.lead.at[(w + j) % wide], r.lead_rx.at[(w - j + wide) % wide if incoming else w],
            (r.lead_sem_s.at[j - 1], r.lead_sem_r.at[j - 1]), wide_peer(j),
        )

    def bias_copy(j, incoming=False):
        return remote(
            r.bias_tx, r.bias_rx.at[(w - j + wide) % wide if incoming else w],
            (r.bias_sem_s.at[j - 1], r.bias_sem_r.at[j - 1]), wide_peer(j),
        )

    def mod_copy(j, incoming=False):
        return remote(
            r.mod_part.at[(w + j) % wide], r.mod_rx.at[(w - j + wide) % wide if incoming else w],
            (r.mod_sem_s.at[j - 1], r.mod_sem_r.at[j - 1]), wide_peer(j),
        )

    def wait_all(copy, count=wide):
        for j in range(1, count):
            copy(j, True).wait_recv()

    narrow_peers = ((core, n_core), (side, n_side), (far, n_far))

    def quarter_copy(k, incoming=False):
        device, idx = narrow_peers[k]
        return remote(
            r.mod_q.at[n], r.mod_q.at[idx if incoming else n],
            (r.quarter_s.at[k], r.quarter_r.at[k]), device,
        )

    for j in range(1, wide):
        lead_copy(j).start()
    for j in range(1, wide):
        bias_copy(j).start()
    r.bias_rx[pl.ds(w, 1)] = r.bias_tx[...][None]
    pack_shard(QKV, 0)
    weights_start(QKV, 0)
    r.lead_rx[pl.ds(w, 1)] = r.lead[pl.ds(w, 1)]
    ada_load.wait()
    wait_all(lead_copy)
    lead_all = r.lead_rx[...].reshape(wide * 16, depth)
    for layer in range(LAYERS):
        product = dot(lead_all, r.ada_v[layer], ((1,), (0,)))
        for row in range(wide):
            at = slice(SEGS * layer, SEGS * layer + SEGS)
            r.mod_part[row, at, :] = product[16 * row : 16 * row + SEGS]
    for j in range(1, wide):
        mod_copy(j).start()
    r.mod_rx[pl.ds(w, 1)] = r.mod_part[pl.ds(w, 1)]
    for which, layer in ((UP, 0), (QKV, 1), (UP, 1)):
        pack_shard(which, layer)
    for item in early:
        weights_beside(*item)

    def after_first():
        weights_start(OUT, 0)
        weights_along(UP, 0)

    @pl.when(jnp.logical_not(is_inner))
    def _():
        for item in early_outer:
            weights_beside(*item)
        after_first()

    pump_through(QKV, 0)
    pl.when(is_inner)(after_first)
    r.mod_grad[...] = jnp.zeros_like(r.mod_grad)
    r.lead_t[...] = jnp.zeros_like(r.lead_t)
    for layer in range(LAYERS):
        for row in range(wide):
            at = (row * LAYERS + layer) * SEGS
            r.lead_t[layer, at : at + SEGS, :] = r.lead_rx[row].astype(F32)[:SEGS]
        r.lead_o[layer] = jnp.transpose(r.lead_t[layer]).astype(BF16)

    wait_all(bias_copy)
    bias_full = (r.ada_full, r.qkv_full, r.out_full, r.up_full, r.down_full)
    for peer in range(wide):
        values = r.bias_rx[peer].astype(F32)
        for layer in range(LAYERS):
            for k, row, start, size in bias_places:
                line = values.shape[0] // LAYERS * layer + row
                at = bias_refs[k].shape[1] * peer + start
                bias_full[k][0, layer : layer + 1, at : at + size] = values[line : line + 1, :size]
    for which, ref in ((QKV, r.qkv_full), (UP, r.up_full)):
        pieces = [pick(ref, *window) for window in windows(which)]
        for layer in range(LAYERS):
            at = 4 * layer + which
            pack(r.bias_sum.at[at : at + 1], [piece[layer : layer + 1] for piece in pieces])
    for layer in range(LAYERS):
        at = 4 * layer
        r.bias_sum[at + OUT : at + OUT + 1] = r.out_full[0, layer : layer + 1]
        r.bias_sum[at + DOWN : at + DOWN + 1] = r.down_full[0, layer : layer + 1]

    wait_all(mod_copy)
    ada_own = r.ada_full[0, :, span(LANES * mod_start(tiles, narrow, n), mod_cols, LANES)]
    total = jnp.sum(r.mod_rx[...], 0)
    for layer in range(LAYERS):
        at = slice(SEGS * layer, SEGS * layer + SEGS)
        r.mod_q[pl.ds(n, 1), at, :] = (total[at] + ada_own[layer : layer + 1])[None]
    for k in range(3):
        quarter_copy(k).start()
    for k in range(3):
        quarter_copy(k, True).wait_recv()
    for part in range(narrow):
        at = LANES * mod_start(tiles, narrow, part)
        r.mods[:, at : at + mod_cols] = r.mod_q[part]

    def bias_row(layer, which, size):
        return r.bias_sum[4 * layer + which : 4 * layer + which + 1, :size]

    def gather_norm(layer, hid, shift, scale, take, before):
        for part in range(2):
            before(part)

            def step(start):
                seg = seg_of(start)
                unit, _ = norm(take(start, seg))
                hidden = unit * (1.0 + mod(layer, scale, seg)) + mod(layer, shift, seg)
                hid[span(local * n + start, STEP), :] = hidden.astype(BF16)

            each_step(part, step)
            tok_send(hid, part)

    def qkv_block(layer, block):
        rows = block_rows(block)
        out = dot(r.hid_attn[layer, rows, :], r.qkv_v[...], ((1,), (0,)))
        out = (out + bias_row(layer, QKV, 3 * cols)).astype(BF16)
        for j in range(3 * own_heads):
            r.heads[layer, j, rows, :HEAD] = out[:, HEAD * j : HEAD * (j + 1)]

    def attend(layer):
        for head in range(own_heads):

            @pl.loop(0, narrow)
            def _(i):
                rows = span(local * i, local)
                query = r.heads[layer, head, rows, :HEAD]
                key = r.heads[layer, own_heads + head, :, :HEAD]
                value = r.heads[layer, 2 * own_heads + head, :, :HEAD]
                scores = dot(query, key, ((1,), (1,))) * scale_inv
                scores = jnp.where(r.seg_col[rows, :] == r.seg_row[...], scores, -1e30)
                top = jnp.max(scores, -1, keepdims=True)
                power = jnp.exp(scores - top)
                total = jnp.sum(power, -1, keepdims=True)
                probs = (power / total).astype(BF16)
                mixed = dot(probs, value, ((1,), (0,)))
                r.mixed[layer, rows, HEAD * head : HEAD * (head + 1)] = mixed.astype(BF16)
                r.log_sum[layer, rows, head : head + 1] = top + jnp.log(total)

            if head % 2:
                pump(1)

    def up_block(layer, block):
        rows = block_rows(block)
        hidden = r.hid_mlp[layer, rows, :]
        for at in range(0, width, 3 * LANES):
            tile = slice(at, at + 3 * LANES)
            up = dot(hidden, r.up_v[:, tile], ((1,), (0,)))
            up = up + r.bias_sum[4 * layer + UP : 4 * layer + UP + 1, tile]
            r.up[layer, rows, tile] = up.astype(BF16)
            r.act[layer, rows, tile] = gelu(up).astype(BF16)

    def down_block(layer, block):
        r.part[block] = dot(r.act[layer, block_rows(block), :], r.down_v[...], ((1,), (0,)))

    def state_of(layer, start):
        rows = span(start, STEP)
        return r.tok[rows, :].astype(F32) if layer == 0 else r.state[rows, :]

    def after_attn(layer):
        def take(start, seg):
            rows = span(start, STEP)
            branch = sum_take(start) + bias_row(layer, OUT, width)
            r.branch[layer, rows, :] = branch.astype(BF16)
            middle = state_of(layer, start) + mod(layer, 2, seg) * branch
            r.middle[layer, rows, :] = middle
            return middle

        return take

    def after_mlp(layer):
        def take(start, seg):
            rows = span(start, STEP)
            down = sum_take(start) + bias_row(layer, DOWN, width)
            r.down[layer, rows, :] = down.astype(BF16)
            result = r.middle[layer, rows, :] + mod(layer, 5, seg) * down
            if layer == 0:
                r.state[rows, :] = result
            else:
                r.mixed_o[rows, :] = result.astype(BF16)
            return result

        return take

    def attn_forward(layer, take, before):
        hid = r.hid_attn.at[layer]
        gather_norm(layer, hid, 0, 1, take, before)
        if layer == 0:
            early_grad()
        pump(1)
        weights_ready(QKV, layer)
        tok_own(hid)
        qkv_block(layer, 1)
        pump(1)
        tok_other(hid)
        qkv_block(layer, 0)
        pump(1)
        if layer == 0:
            tok_own(r.grad_down, True)
            tok_other(r.grad_down, True)
        attend(layer)
        weights_ready(OUT, layer)
        tok_drain(hid)
        for block in range(2):
            r.part[block] = dot(r.mixed[layer, block_rows(block), :], r.out_v[...], ((1,), (0,)))
            sum_block(block)
            if block == 0:
                sum_cross()
        pump(1)
        gather_norm(layer, r.hid_mlp.at[layer], 3, 4, after_attn(layer), sum_wait)
        pump(1)
        weights_ready(UP, layer)

    def early_grad():
        for part in range(2):

            def step(start):
                rows = span(start, STEP)
                grad = r.cot[rows, :].astype(F32)
                r.token_o[rows, :] = grad
                grad_down = (mod(LAYERS - 1, 5, seg_of(start)) * grad).astype(BF16)
                r.grad_down[span(local * n + start, STEP), :] = grad_down

            each_step(part, step)
            tok_send(r.grad_down, part, True)

    attn_forward(0, lambda start, seg: state_of(0, start), lambda part: None)
    weights_ready(DOWN, 0)
    hid = r.hid_mlp.at[0]
    tok_own(hid)
    up_block(0, 1)
    down_block(0, 1)
    sum_block(1)
    pump(1)
    tok_other(hid)
    up_block(0, 0)
    down_block(0, 0)
    sum_block(0)
    sum_cross()
    tok_drain(hid)
    pump(2)
    attn_forward(1, after_mlp(0), sum_wait)

    sums = (r.qkv_d, r.out_d, r.up_d, r.down_d)
    from_x = (r.qkv_xr, r.out_xr, r.up_xr, r.down_xr)
    from_z = (r.qkv_zr, r.out_zr, r.up_zr, r.down_zr)
    final = (r.qkv_f, r.out_f, r.up_f, r.down_f)
    grads_o = (r.qkv_o, r.out_o, r.up_o, r.down_o)
    same_y, same_c = y == z // 2, c == z % 2

    def d_rows(which, plane_idx, col):
        return w_rows(which, plane_idx, col)

    def d_x(which, plane_idx, incoming=False):
        k = 0 if which == OUT else plane_idx
        src = sums[which].at[d_rows(which, plane_idx, 1 - x)]
        return remote(
            src, from_x[which].at[k], (r.dx_s.at[which, k], r.dx_r.at[which, k]), beside
        )

    def d_z(which, kind):
        idx = 0 if which == OUT else (z_partner, z_inner, z_outer)[kind]
        src = from_x[which].at[idx]

        def send(slot, plane_idx):
            return remote(
                src, from_z[which].at[slot], (r.dz_s.at[which, kind], r.dz_r.at[which, slot]),
                at_plane(plane_idx),
            )

        return send

    def d_z_in(which, slot):
        ref = from_z[which].at[slot]
        return remote(ref, ref, (r.dz_s.at[which, 0], r.dz_r.at[which, slot]), at_plane(z_partner))

    def grad_product(which, layer):
        left, right = (
            (r.hid_attn, r.grad_qkv), (r.mixed, r.grad_branch),
            (r.hid_mlp, r.grad_up), (r.act, r.grad_down),
        )[which]
        if which == OUT:
            product = dot(left[layer], right[...], ((0,), (0,)))
            sums[which][...] = product.astype(BF16)
        else:

            @pl.loop(0, width // (3 * LANES))
            def _(i):
                tile = span(3 * LANES * i, 3 * LANES, LANES)
                product = dot(left[layer, :, tile], right[...], ((0,), (0,)))
                sums[which][tile, :] = product.astype(BF16)

    def grad_send(which, layer):
        if layer == 0:
            pl.semaphore_wait(r.credit_x.at[which], 1)
        if which == OUT:
            d_x(which, 0).start()
        else:
            for idx in (z_outer, z_inner, z_partner, z):
                d_x(which, idx).start()

    out_home = z == n
    out_near = z_partner == n
    out_far = z_half != n // 2

    def credit(sem, device):
        pl.semaphore_signal(sem, inc=1, device_id=device, device_id_type=MESH)

    def grad_beside(which, layer):
        def add(slot, rows):
            total = sums[which][rows, :].astype(F32) + from_x[which][slot].astype(F32)
            from_x[which][slot] = total.astype(BF16)

        if which == OUT:
            d_x(which, 0).wait_recv()
            add(0, d_rows(which, n, x))
            outer_far = jnp.logical_and(out_far, jnp.logical_not(is_inner))

            @pl.when(jnp.logical_or(out_near, outer_far))
            def _():
                if layer == 0:
                    pl.semaphore_wait(r.credit_z.at[which, 0], 1)

            pl.when(out_near)(lambda: d_z(which, 0)(0, z_partner).start())
            pl.when(outer_far)(lambda: d_z(which, 0)(2, z_partner).start())
            d_x(which, 0).wait_send()
        else:
            for k, idx in ((2, z_outer), (1, z_inner), (0, z_partner), (None, z)):
                d_x(which, idx).wait_recv()
                add(idx, d_rows(which, idx, x))
                if k == 2 and layer == 0:
                    pl.semaphore_wait(r.credit_z.at[which, 0], 1)
                if k == 0:
                    d_z(which, 0)(0, z_partner).start()
                elif k:
                    pl.when(jnp.logical_not(is_inner))(
                        lambda: d_z(which, k)(k + 1, z_partner).start()
                    )
            for idx in range(PLANES):
                d_x(which, idx).wait_send()

    def grad_join(which, layer):
        def add(slot, idx):
            d_z_in(which, slot).wait_recv()
            total = from_x[which][idx].astype(F32) + from_z[which][slot].astype(F32)
            from_x[which][idx] = total.astype(BF16)

        if which == OUT:

            @pl.when(jnp.logical_and(out_far, is_inner))
            def _():
                add(2, 0)
                if layer == 0:
                    pl.semaphore_wait(r.credit_z.at[which, 1], 1)
                else:
                    credit(r.credit_z.at[which, 0], at_plane(z_partner))
                d_z(which, 0)(1, n).start()
        else:

            @pl.when(is_inner)
            def _():
                if layer == 0:
                    pl.semaphore_wait(r.credit_z.at[which, 1], 2)
                add(3, z_outer)
                d_z(which, 2)(1, z_outer).start()
                add(2, z_inner)
                d_z(which, 1)(1, z_inner).start()

    def grad_planes(which, layer):
        def add():
            d_z_in(which, 0).wait_recv()
            d_z_in(which, 1).wait_recv()
            total = from_x[which][0 if which == OUT else z].astype(F32)
            total = total + from_z[which][0].astype(F32) + from_z[which][1].astype(F32)
            if layer == 0:
                spread_sent(which, 1)
            final[which][...] = total.astype(BF16)
            if layer == 1:
                credit(r.credit_z.at[which, 0], at_plane(z_partner))
                credit(r.credit_z.at[which, 1], at_plane(z_inner))

        if which == OUT:
            pl.when(out_home)(add)
            pl.when(jnp.logical_not(out_home))(lambda: d_z(which, 0)(0, z_partner).wait_send())
        else:
            add()
            for kind in range(3):
                d_z(which, kind)(0, z_partner).wait_send()
        if layer == 1:
            credit(r.credit_x.at[which], beside)

    def e_z(kind, other):
        idx = (z_partner, z_inner, z_outer)[kind]
        src = sums[DOWN].at[d_rows(DOWN, idx, 1 - x if other else x)]
        slots = from_x[DOWN] if other else from_z[DOWN]

        def send(slot, plane_idx):
            return remote(
                src, slots.at[slot], (r.e_s.at[int(other), kind], r.e_r.at[int(other), slot]),
                at_plane(plane_idx),
            )

        return send

    def e_in(slot, other):
        ref = (from_x[DOWN] if other else from_z[DOWN]).at[slot]
        remote(
            ref, ref, (r.e_s.at[int(other), 0], r.e_r.at[int(other), slot]), at_plane(z_partner)
        ).wait_recv()
        return ref[...].astype(F32)

    def e_x():
        return remote(from_x[DOWN].at[0], r.down_e, (r.ex_s, r.ex_r), beside)

    def first_send():
        @pl.when(jnp.logical_not(is_inner))
        def _():
            for kind in (2, 1):
                for other in (True, False):
                    e_z(kind, other)(kind + 1, z_partner).start()

        for other in (True, False):
            e_z(0, other)(0, z_partner).start()

    def first_join():
        @pl.when(is_inner)
        def _():
            for kind, idx in ((2, z_outer), (1, z_inner)):
                for other in (True, False):
                    rows = d_rows(DOWN, idx, 1 - x if other else x)
                    total = sums[DOWN][rows, :].astype(F32) + e_in(kind + 1, other)
                    sums[DOWN][rows, :] = total.astype(BF16)
                    e_z(kind, other)(1, idx).start()

    def first_planes():
        for other in (True, False):
            rows = d_rows(DOWN, z, 1 - x if other else x)
            total = sums[DOWN][rows, :].astype(F32) + e_in(0, other) + e_in(1, other)
            if other:
                from_x[DOWN][0] = total.astype(BF16)
                e_x().start()
            else:
                final[DOWN][...] = total.astype(BF16)
        for kind in range(3):
            for other in (True, False):
                e_z(kind, other)(0, z_partner).wait_send()
        credit(r.credit_z.at[DOWN, 0], at_plane(z_partner))
        credit(r.credit_z.at[DOWN, 1], at_plane(z_inner))

    def first_beside():
        e_x().wait_recv()
        total = final[DOWN][...].astype(F32) + r.down_e[...].astype(F32)
        final[DOWN][...] = total.astype(BF16)
        e_x().wait_send()
        credit(r.credit_x.at[DOWN], beside)

    def spread(which, layer, kind, source=None):
        slot = layer * 4 + which
        if which == OUT:
            dst = grads_o[which].at[layer]
        else:
            dst = grads_o[which].at[layer, n if source is None else source]
        src = final[which] if kind < 2 else dst
        return remote(
            src, dst, (r.spread_s.at[slot, kind], r.spread_r.at[slot, kind]), side if kind == 1 else core
        )

    def spread_own(which, layer):
        dst = grads_o[which].at[layer] if which == OUT else grads_o[which].at[layer, n]
        return pltpu.make_async_copy(final[which], dst, r.spread_l.at[layer * 4 + which])

    def spread_sent(which, layer):
        spread(which, layer, 1).wait_send()
        spread(which, layer, 0).wait_send()
        spread_own(which, layer).wait()

    def grad_spread(which, layer):
        def go():
            spread(which, layer, 1).start()
            spread(which, layer, 0).start()
            spread_own(which, layer).start()

        if which == OUT:
            pl.when(jnp.logical_and(same_y, same_c))(go)
        else:
            go()

    def grad_pass(which, layer):
        def go():
            spread(which, layer, 1, n_side).wait_recv()
            spread(which, layer, 2, n_side).start()

        if which == OUT:
            pl.when(jnp.logical_and(jnp.logical_not(same_y), same_c))(go)
        else:
            go()

    def grad_end(which, layer):
        if which == OUT:
            if layer == 0:
                pl.when(jnp.logical_and(same_y, same_c))(lambda: spread_sent(which, layer))

            @pl.when(jnp.logical_and(jnp.logical_not(same_y), same_c))
            def _():
                spread(which, layer, 2).wait_send()

            @pl.when(jnp.logical_and(same_y, jnp.logical_not(same_c)))
            def _():
                spread(which, layer, 0).wait_recv()

            @pl.when(jnp.logical_and(jnp.logical_not(same_y), jnp.logical_not(same_c)))
            def _():
                spread(which, layer, 2).wait_recv()
        else:
            spread(which, layer, 0, n_core).wait_recv()
            spread(which, layer, 2, n_far).wait_recv()
            spread(which, layer, 2, n_side).wait_send()
            if layer == 0:
                spread_sent(which, layer)

    def bias_grad(layer, which, values):
        at = 4 * layer + which
        r.bias_grad[at : at + 1, : values.shape[1]] = jnp.sum(
            values.astype(F32), 0, keepdims=True
        )

    def back_mlp_block(layer, block):
        rows = block_rows(block)
        grad_down = r.grad_down[rows, :]
        for at in range(0, width, 3 * LANES):
            tile = slice(at, at + 3 * LANES)
            grad_act = dot(grad_down, r.down_v[tile, :], ((1,), (1,)))
            up = r.up[layer, rows, tile].astype(F32)
            r.grad_up[rows, tile] = (grad_act * gelu_slope(up)).astype(BF16)
        r.part[block] = dot(r.grad_up[rows, :], r.up_v[...], ((1,), (1,)))

    def back_attn_block(layer, block):
        rows = block_rows(block)
        out = dot(r.grad_branch[rows, :], r.out_v[...], ((1,), (1,))).astype(BF16)
        for j in range(own_heads):
            r.grad_heads[j, rows, :HEAD] = out[:, HEAD * j : HEAD * (j + 1)]

    def back_attend(layer, head):
        @pl.loop(0, narrow)
        def _(i):
            rows = span(local * i, local)
            query = r.heads[layer, head, rows, :HEAD]
            key = r.heads[layer, own_heads + head, :, :HEAD]
            value = r.heads[layer, 2 * own_heads + head, :, :HEAD]
            grad = r.grad_heads[head, rows, :HEAD]
            scores = dot(query, key, ((1,), (1,))) * scale_inv
            probs = jnp.exp(scores - r.log_sum[layer, rows, head : head + 1])
            probs = jnp.where(r.seg_col[rows, :] == r.seg_row[...], probs, 0.0)
            grad_probs = dot(grad, value, ((1,), (1,)))
            inner = jnp.sum(probs * grad_probs, -1, keepdims=True)
            grad_scores = (probs * (grad_probs - inner)).astype(BF16)
            grad_query = dot(grad_scores, key, ((1,), (0,))) * scale_inv
            r.grad_qkv[rows, HEAD * head : HEAD * (head + 1)] = grad_query.astype(BF16)
            grad_key = dot(grad_scores, query, ((0,), (0,)))
            grad_value = dot(probs.astype(BF16), grad, ((0,), (0,)))

            def tile(k):
                return slice(LANES * k, LANES * k + HEAD)

            @pl.when(i == 0)
            def _():
                for k in range(narrow):
                    at = slice(local * k, local * (k + 1))
                    r.grad_hid[:, tile(k)] = grad_key[at]
                    r.grad_hid[:, tile(narrow + k)] = grad_value[at]

            @pl.when(i > 0)
            def _():
                for k in range(narrow):
                    at = slice(local * k, local * (k + 1))
                    r.grad_hid[:, tile(k)] += grad_key[at]
                    r.grad_hid[:, tile(narrow + k)] += grad_value[at]

        at = cols + HEAD * head
        for k in range(narrow):
            rows = slice(local * k, local * (k + 1))
            key_sum = r.grad_hid[:, LANES * k : LANES * k + HEAD]
            value_sum = r.grad_hid[:, LANES * (narrow + k) : LANES * (narrow + k) + HEAD]
            r.grad_qkv[rows, at : at + HEAD] = (key_sum * scale_inv).astype(BF16)
            r.grad_qkv[rows, cols + at : cols + at + HEAD] = value_sum.astype(BF16)

    def both(body):
        for part in range(2):
            each_step(part, body)

    def sums_attn(layer):
        def body(start):
            rows = span(start, STEP)
            seg = seg_of(start)
            unit, _ = norm(state_of(layer, start))
            grad_hidden = r.grad_hid[rows, :]
            mod_sum(layer, 0, seg, grad_hidden)
            mod_sum(layer, 1, seg, grad_hidden * unit)

        both(body)

    def sums_mlp(layer):
        def body(start):
            rows = span(start, STEP)
            seg = seg_of(start)
            unit, _ = norm(r.middle[layer, rows, :])
            grad_hidden = r.grad_hid[rows, :]
            mod_sum(layer, 3, seg, grad_hidden)
            mod_sum(layer, 4, seg, grad_hidden * unit)
            mod_sum(layer, 2, seg, r.branch[layer, rows, :].astype(F32) * r.token_o[rows, :])

        both(body)

    def sums_gate_mlp(layer, grad):
        def body(start):
            rows = span(start, STEP)
            mod_sum(
                layer, 5, seg_of(start), r.down[layer, rows, :].astype(F32) * grad[rows, :].astype(F32)
            )

        both(body)

    def back_middle(layer):
        for part in range(2):
            sum_wait(part)

            def step(start):
                rows = span(start, STEP)
                seg = seg_of(start)
                grad_hidden = sum_take(start)
                unit, inv = norm(r.middle[layer, rows, :])
                r.grad_hid[rows, :] = grad_hidden
                grad = r.token_o[rows, :] + norm_back(
                    grad_hidden * (1.0 + mod(layer, 4, seg)), unit, inv
                )
                r.token_o[rows, :] = grad
                grad_branch = (mod(layer, 2, seg) * grad).astype(BF16)
                r.grad_branch[span(local * n + start, STEP), :] = grad_branch

            each_step(part, step)
            tok_send(r.grad_branch, part)

    def back_state(layer, start):
        rows = span(start, STEP)
        grad_hidden = sum_take(start)
        unit, inv = norm(state_of(layer, start))
        r.grad_hid[rows, :] = grad_hidden
        r.token_o[rows, :] += norm_back(
            grad_hidden * (1.0 + mod(layer, 1, seg_of(start))), unit, inv
        )

    def back_qkv(layer, checked=False):
        for block in range(2):
            rows = block_rows(block)
            r.part[block] = dot(r.grad_qkv[rows, :], r.qkv_v[...], ((1,), (1,)))
            if checked and block == 0:
                pl.semaphore_wait(r.credit_sum.at[0], 1)
            sum_block(block)
            if block == 0:
                if checked:
                    pl.semaphore_wait(r.credit_sum.at[1], 1)
                sum_cross()

    hid = r.hid_mlp.at[1]
    tok_own(hid)
    up_block(1, 1)
    pump(1)
    tok_other(hid)
    up_block(1, 0)
    pump(1)
    grad_product(DOWN, 1)
    bias_grad(1, DOWN, r.grad_down[span(local * n, local), :])
    tok_drain(hid)
    tok_drain(r.grad_down, True)
    pump_through(DOWN, 1)
    first_send()
    weights_ready(DOWN, 1)
    for block in range(2):
        back_mlp_block(1, block)
        sum_block(block)
        if block == 0:
            sum_cross()
    load(UP, 0).start()
    grad_product(UP, 1)
    grad_send(UP, 1)
    bias_grad(1, UP, r.grad_up[...])
    back_middle(1)
    for block in range(2):
        down_block(1, block)
    load(DOWN, 0).start()
    sums_mlp(1)
    bias_grad(1, OUT, r.grad_branch[span(local * n, local), :])
    tok_own(r.grad_branch)
    back_attn_block(1, 1)
    tok_other(r.grad_branch)
    back_attn_block(1, 0)
    load(OUT, 0).start()
    for block in range(2):
        sum_block(block)
        if block == 0:
            sum_cross()
    grad_product(OUT, 1)
    grad_send(OUT, 1)
    for head in range(own_heads):
        back_attend(1, head)
        if head == 2:
            first_join()
    tok_drain(r.grad_branch)
    for part in range(2):
        sum_wait(part)
        finish_state = after_mlp(1)

        def last(start):
            finish_state(start, seg_of(start))

        each_step(part, last)
    credit(r.credit_sum.at[0], core)
    credit(r.credit_sum.at[1], side)
    back_qkv(1, True)
    load(QKV, 0).start()
    grad_product(QKV, 1)
    grad_send(QKV, 1)
    sums_gate_mlp(1, r.cot)
    grad_beside(UP, 1)
    bias_grad(1, QKV, r.grad_qkv[...])
    for part in range(2):
        sum_wait(part)

        def start_down(start):
            back_state(1, start)
            grad_down = (mod(0, 5, seg_of(start)) * r.token_o[span(start, STEP), :]).astype(BF16)
            r.grad_down[span(local * n + start, STEP), :] = grad_down

        each_step(part, start_down)
        tok_send(r.grad_down, part)
    sums_attn(1)
    sums_gate_mlp(0, r.token_o)
    bias_grad(0, DOWN, r.grad_down[span(local * n, local), :])
    load(DOWN, 0).wait()
    load(UP, 0).wait()
    grad_beside(OUT, 1)
    tok_own(r.grad_down)
    back_mlp_block(0, 1)
    sum_block(1)
    tok_other(r.grad_down)
    back_mlp_block(0, 0)
    sum_block(0)
    sum_cross()
    first_planes()
    grad_product(DOWN, 0)
    bias_grad(0, UP, r.grad_up[...])
    tok_drain(r.grad_down)
    back_middle(0)
    grad_product(UP, 0)
    first_beside()
    grad_send(DOWN, 0)
    grad_join(UP, 1)
    grad_join(OUT, 1)
    sums_mlp(0)
    bias_grad(0, OUT, r.grad_branch[span(local * n, local), :])
    grad_beside(QKV, 1)
    load(OUT, 0).wait()
    load(QKV, 0).wait()
    tok_own(r.grad_branch)
    back_attn_block(0, 1)
    tok_other(r.grad_branch)
    back_attn_block(0, 0)
    grad_spread(DOWN, 1)
    grad_product(OUT, 0)
    for head in range(own_heads):
        back_attend(0, head)
        if head == 1:
            grad_planes(UP, 1)
            grad_send(UP, 0)
    back_qkv(0)
    grad_join(QKV, 1)
    grad_product(QKV, 0)
    tok_drain(r.grad_branch)
    grad_beside(DOWN, 0)
    bias_grad(0, QKV, r.grad_qkv[...])
    for part in range(2):
        sum_wait(part)
        each_step(part, partial(back_state, 0))
    sums_attn(0)

    def quarter_back(k, incoming=False):
        device, idx = narrow_peers[k]
        at = span(LANES * mod_start(tiles, narrow, idx), mod_cols, LANES)
        return remote(
            r.mod_grad.at[:, at], r.quarter_rx.at[k], (r.back_s.at[k], r.back_r.at[k]), device
        )

    def wide_back(j, incoming=False):
        return remote(
            r.quarter_sum, r.quarter_all.at[(w - j + wide) % wide if incoming else w],
            (r.wide_s.at[j - 1], r.wide_r.at[j - 1]), wide_peer(j),
        )

    def bias_wide(j, incoming=False):
        return remote(
            r.bias_half, r.bias_all.at[(w - j + wide) % wide if incoming else w],
            (r.bias_wide_s.at[j - 1], r.bias_wide_r.at[j - 1]), wide_peer(j),
        )

    def bias_narrow(k, incoming=False):
        device, idx = narrow_peers[k]
        return remote(
            r.bias_row, r.bias_o.at[idx if incoming else n],
            (r.bias_narrow_s.at[k], r.bias_narrow_r.at[k]), device,
        )

    def mod_narrow(k, incoming=False):
        device, idx = narrow_peers[k]
        return remote(
            r.mod_all, r.mod_o.at[idx if incoming else n],
            (r.mod_narrow_s.at[k], r.mod_narrow_r.at[k]), device,
        )

    def lead_back(j, incoming=False):
        return remote(
            r.lead_tx.at[(w + j) % wide], r.lead_back.at[(w - j + wide) % wide if incoming else w],
            (r.lead_back_s.at[j - 1], r.lead_back_r.at[j - 1]), wide_peer(j),
        )

    def lead_narrow(k, incoming=False):
        device, idx = narrow_peers[k]
        return remote(
            r.lead_back, r.lead_g.at[idx if incoming else n],
            (r.lead_narrow_s.at[k], r.lead_narrow_r.at[k]), device,
        )

    for k in range(3):
        quarter_back(k).start()
    own_at = span(LANES * mod_start(tiles, narrow, n), mod_cols, LANES)
    total = r.mod_grad[:, own_at]
    for k in range(3):
        quarter_back(k, True).wait_recv()
        total = total + r.quarter_rx[k]
    r.quarter_sum[...] = folded(total, mod_cols // 2)
    for j in range(1, wide):
        wide_back(j).start()
    r.bias_half[...] = folded(r.bias_grad[...], 5 * LANES)
    for j in range(1, wide):
        bias_wide(j).start()
    r.quarter_all[pl.ds(w, 1)] = r.quarter_sum[...][None]
    r.bias_all[pl.ds(w, 1)] = r.bias_half[...][None]
    grad_planes(OUT, 1)
    grad_send(OUT, 0)
    grad_planes(QKV, 1)
    grad_send(QKV, 0)
    grad_spread(UP, 1)
    grad_spread(OUT, 1)
    grad_spread(QKV, 1)
    grad_join(DOWN, 0)
    for which in (DOWN, UP, OUT, QKV):
        grad_pass(which, 1)
    grad_beside(UP, 0)
    wait_all(wide_back)
    for j in range(1, wide):
        mod_copy(j).wait_send()
    for row in range(wide):
        r.mod_part[row] = unfolded(r.quarter_all[row], mod_cols)
    r.mod_all[...] = r.mod_part[...].reshape(wide * LAYERS * SEGS, mod_cols).astype(BF16)
    mod_own = pltpu.make_async_copy(r.mod_all, r.mod_o.at[n], r.mod_own_sem)
    mod_own.start()
    for k in range(3):
        mod_narrow(k).start()
    owned = LANES * (mod_start(tiles, narrow, n + 1) - mod_start(tiles, narrow, n))
    lane = lax.broadcasted_iota(jnp.int32, r.mod_all.shape, 1)
    own_grads = jnp.where(lane < owned, r.mod_all[...].astype(F32), 0.0).astype(BF16)
    lead_parts = [dot(own_grads, r.ada_v[layer], ((1,), (1,))) for layer in range(LAYERS)]
    for row in range(wide):
        at = row * LAYERS * SEGS
        r.lead_tx[row] = lead_parts[0][at : at + SEGS] + lead_parts[1][at + SEGS : at + 2 * SEGS]
    for j in range(1, wide):
        lead_back(j).start()
    r.lead_back[pl.ds(w, 1)] = r.lead_tx[pl.ds(w, 1)]
    grad_planes(DOWN, 0)
    grad_spread(DOWN, 0)
    grad_beside(OUT, 0)
    wait_all(bias_wide)
    r.bias_row[...] = unfolded(jnp.sum(r.bias_all[...].astype(F32), 0), width)
    bias_own = pltpu.make_async_copy(r.bias_row, r.bias_o.at[n], r.bias_own_sem)
    bias_own.start()
    for k in range(3):
        bias_narrow(k).start()
    grad_join(UP, 0)
    grad_join(OUT, 0)
    grad_beside(QKV, 0)
    wait_all(lead_back)
    lead_own = pltpu.make_async_copy(r.lead_back, r.lead_g.at[n], r.lead_own_sem)
    lead_own.start()
    for k in range(3):
        lead_narrow(k).start()
    grad_pass(DOWN, 0)
    grad_join(QKV, 0)
    grad_planes(UP, 0)
    grad_spread(UP, 0)
    grad_planes(OUT, 0)
    grad_spread(OUT, 0)
    grad_planes(QKV, 0)
    grad_spread(QKV, 0)
    for which in (UP, OUT, QKV):
        grad_pass(which, 0)

    for layer in range(LAYERS):
        for which in range(4):
            weights_drain(which, layer)
            grad_end(which, layer)
    for j in range(1, wide):
        for copy in (lead_copy, bias_copy, wide_back, bias_wide, lead_back):
            copy(j).wait_send()
    for k in range(3):
        for copy in (quarter_copy, quarter_back, mod_narrow, bias_narrow, lead_narrow):
            copy(k).wait_send()
        mod_narrow(k, True).wait_recv()
        bias_narrow(k, True).wait_recv()
        lead_narrow(k, True).wait_recv()
    mod_own.wait()
    lead_own.wait()
    bias_own.wait()


def gelu_slope(values):
    rate = math.sqrt(2.0 / math.pi)
    bent = jnp.tanh(rate * (values + 0.044715 * values * values * values))
    inner = rate * (1.0 + 3.0 * 0.044715 * values * values)
    return 0.5 * (1.0 + bent) + 0.5 * values * (1.0 - bent * bent) * inner


def chosen_of(cond, index):
    values = cond[...].astype(F32)
    rows = []
    for s in range(SEGS):
        row = values[SEGS - 1 : SEGS]
        for k in range(SEGS - 1):
            row = jnp.where(index[:, s : s + 1] == k, values[k : k + 1], row)
        rows.append(row)
    return jnp.concatenate(rows, 0)


def finish_kernel(cfg, *refs):
    r = SimpleNamespace(**dict(zip(cfg.names, refs)))
    wide, narrow, width, depth, cols = cfg.wide, cfg.narrow, cfg.width, cfg.depth, cfg.cols
    tiles, hidden_own = cfg.tiles, cfg.hidden_own
    w = lax.axis_index("wide")

    for part in range(narrow):
        values = r.qkv_i[0, part].astype(F32)
        for j in range(3):
            at = width * j + cols * part
            r.qkv_g[0, :, at : at + cols] = values[:, cols * j : cols * (j + 1)]
        values = r.up_i[0, part].astype(F32)
        for j in range(wide):
            at = (j * narrow + part) * hidden_own
            r.up_g[0, :, at : at + hidden_own] = values[:, hidden_own * j : hidden_own * (j + 1)]
        at, end = [LANES * mod_start(tiles, narrow, part + k) for k in range(2)]
        r.ada_g[0, :, at:end] = dot(r.lead_i[0], r.mod_i[part, :, : end - at], ((1,), (0,)))
    r.out_g[...] = r.out_i[...].astype(F32)
    r.down_g[...] = r.down_i[...].astype(F32)

    def pick(ref, size):
        start = size * w
        window = LANES * (-(-size // LANES) + 1)
        tile, rest = start // LANES, start % LANES
        values = ref[:, pl.ds(pl.multiple_of(LANES * tile, LANES), window)]
        return pltpu.roll(values, (window - rest) % window, 1)[:, :size]

    @pl.when(pl.program_id(0) + pl.program_id(1) == 0)
    def _():
        for part in range(narrow):
            values = r.bias_i[part]
            for j in range(3):
                at = width * j + cols * part
                r.qkv_t[:, at : at + cols] = values[:, cols * j : cols * (j + 1)]
            for j in range(wide):
                at = (j * narrow + part) * hidden_own
                r.up_t[:, at : at + hidden_own] = values[:, hidden_own * j : hidden_own * (j + 1)]
            at, end = [LANES * mod_start(tiles, narrow, part + k) for k in range(2)]
            values = r.mod_i[part, :, : end - at].astype(F32)
            layer_of = lax.broadcasted_iota(jnp.int32, values.shape, 0) // SEGS % LAYERS
            for layer in range(LAYERS):
                sums = jnp.sum(jnp.where(layer_of == layer, values, 0.0), 0, keepdims=True)
                r.ada_t[layer : layer + 1, at:end] = sums
        r.row_t[:, :width] = jnp.sum(r.bias_i[...], 0)
        for dst, ref, line, step in (
            (r.ada_bg, r.ada_t, 0, 1), (r.qkv_bg, r.qkv_t, QKV, 4), (r.out_bg, r.row_t, OUT, 4),
            (r.up_bg, r.up_t, UP, 4), (r.down_bg, r.row_t, DOWN, 4),
        ):
            values = pick(ref, dst.shape[1])
            for layer in range(LAYERS):
                at = step * layer + line
                dst[layer : layer + 1, :] = values[at : at + 1]
        chosen = chosen_of(r.cond, r.cond_index)
        gate = jax.nn.sigmoid(chosen)
        slope = gate * (1.0 + chosen * (1.0 - gate))
        lead_grad = jnp.sum(r.lead_i2[...], 0)
        for row in range(wide):
            at = slice(depth * row, depth * (row + 1))
            grad = lead_grad[row] * slope[:, at]
            for k in range(SEGS):
                total = jnp.zeros((1, depth), F32)
                for s in range(SEGS):
                    own = r.cond_index[:, s : s + 1] == k
                    total = total + jnp.where(own, grad[s : s + 1], 0.0)
                r.cond_g[k : k + 1, at] = total


def finish(wide, narrow, got, cond, cond_index, tiles, mod_cols, w):
    width = cond.shape[1]
    depth, cols = width // wide, width // narrow
    hidden_own = got["up_o"].shape[-1] // wide
    hidden_all = got["up_o"].shape[-1] * narrow
    down_rows = narrow * hidden_own
    bands = depth // 48
    rows = depth // bands
    shape, vmem = jax.ShapeDtypeStruct, pltpu.VMEM

    def whole(values):
        return pl.BlockSpec(values.shape, lambda i, j: (0,) * values.ndim)

    def band(*dims):
        return pl.BlockSpec(
            (1, *dims), lambda i, j: (i, 0, j, 0) if len(dims) == 3 else (i, j, 0)
        )

    down_i = got["down_o"].reshape(LAYERS, down_rows, width)
    inputs = dict(
        qkv_i=got["qkv_o"], up_i=got["up_o"], out_i=got["out_o"], down_i=down_i,
        lead_i=got["lead_o"], mod_i=got["mod_o"], bias_i=got["bias_o"], lead_i2=got["lead_g"],
        cond=cond, cond_index=cond_index,
    )
    in_specs = [
        band(narrow, rows, 3 * cols), band(narrow, rows, wide * hidden_own), band(rows, width),
        band(down_rows // bands, width), band(rows, got["lead_o"].shape[-1]),
        *[whole(inputs[name]) for name in ("mod_i", "bias_i", "lead_i2", "cond", "cond_index")],
    ]
    outputs = dict(
        ada_g=shape((LAYERS, depth, tiles * LANES), F32), qkv_g=shape((LAYERS, depth, 3 * width), F32),
        out_g=shape((LAYERS, depth, width), F32), up_g=shape((LAYERS, depth, hidden_all), F32),
        down_g=shape((LAYERS, down_rows, width), F32),
        ada_bg=shape((LAYERS, tiles * LANES // wide), F32), qkv_bg=shape((LAYERS, 3 * width // wide), F32),
        out_bg=shape((LAYERS, depth), F32), up_bg=shape((LAYERS, hidden_all // wide), F32),
        down_bg=shape((LAYERS, depth), F32), cond_g=shape((SEGS, width), F32),
    )
    out_specs = [
        band(rows, tiles * LANES), band(rows, 3 * width), band(rows, width), band(rows, hidden_all),
        band(down_rows // bands, width),
        *[whole(outputs[name]) for name in ("ada_bg", "qkv_bg", "out_bg", "up_bg", "down_bg", "cond_g")],
    ]
    scratch = dict(
        ada_t=vmem((8, (tiles + 2) * LANES), F32), qkv_t=vmem((8, 3 * width + 2 * LANES), F32),
        up_t=vmem((8, hidden_all + 2 * LANES), F32), row_t=vmem((8, width + 2 * LANES), F32),
    )
    cfg = SimpleNamespace(
        names=[*inputs, *outputs, *scratch], wide=wide, narrow=narrow, width=width, depth=depth,
        cols=cols, tiles=tiles, hidden_own=hidden_own,
    )
    results = pl.pallas_call(
        partial(finish_kernel, cfg),
        grid=(LAYERS, bands),
        out_shape=list(outputs.values()), in_specs=in_specs, out_specs=out_specs,
        scratch_shapes=list(scratch.values()),
        compiler_params=pltpu.CompilerParams(vmem_limit_bytes=62 * 2**20),
    )(*inputs.values())
    done = dict(zip(outputs, results))
    out = [got["mixed_o"][None], got["token_o"][None], done["cond_g"][None]]
    for name in ("ada", "qkv", "out", "up", "down"):
        out += [done[name + "_g"], done[name + "_bg"]]
    return tuple(out)


def fused_device(
    wide, narrow,
    tokens, cond, seg_ids, cond_index, cotangent,
    ada_weight, ada_bias, qkv_weight, qkv_bias, out_weight, out_bias,
    up_weight, up_bias, down_weight, down_bias,
):
    w = lax.axis_index("wide")
    n = lax.axis_index("narrow")
    local, width = tokens.shape[1:]
    row_len = seg_ids.shape[1]
    depth, cols = width // wide, width // narrow
    hidden_own = up_weight.shape[-1] // wide // narrow
    hidden = wide * hidden_own
    tiles = ada_weight.shape[-1] // LANES
    mod_cols = LANES * -(-tiles // narrow)

    inputs = dict(
        tok=tokens[0], cond=cond[0], cond_index=cond_index, seg_row=seg_ids,
        cot=cotangent[0], ada_b=ada_bias, qkv_b=qkv_bias, out_b=out_bias, up_b=up_bias, down_b=down_bias,
        ada=ada_weight, qkv_w=qkv_weight, out_w=out_weight, up_w=up_weight, down_w=down_weight,
    )
    in_hbm = ("ada", "qkv_w", "out_w", "up_w", "down_w")
    shape = jax.ShapeDtypeStruct
    outputs = dict(
        mixed_o=shape((local, width), BF16), token_o=shape((local, width), F32),
        qkv_o=shape((LAYERS, narrow, depth, 3 * cols), BF16),
        out_o=shape((LAYERS, depth, width), BF16),
        up_o=shape((LAYERS, narrow, depth, hidden), BF16),
        down_o=shape((LAYERS, narrow, hidden_own, width), BF16),
        bias_o=shape((narrow, 4 * LAYERS, width), F32),
        mod_o=shape((narrow, wide * LAYERS * SEGS, mod_cols), BF16),
        lead_o=shape((LAYERS, depth, wide * LAYERS * SEGS), BF16),
        lead_g=shape((narrow, wide, SEGS, depth), F32),
        qkv_h=shape((LAYERS, width, 3 * cols), BF16), out_h=shape((LAYERS, cols, width), BF16),
        up_h=shape((LAYERS, width, hidden), BF16), down_h=shape((LAYERS, hidden, width), BF16),
    )
    out_vmem = ("mixed_o", "token_o", "lead_o")
    vmem, dma = pltpu.VMEM, pltpu.SemaphoreType.DMA
    heads = cols // HEAD
    scratch = dict(
        qkv_v=vmem((width, 3 * cols), BF16), out_v=vmem((cols, width), BF16),
        up_v=vmem((width, hidden), BF16), down_v=vmem((hidden, width), BF16),
        hid_attn=vmem((LAYERS, row_len, width), BF16), hid_mlp=vmem((LAYERS, row_len, width), BF16),
        heads=vmem((LAYERS, 3 * heads, row_len, LANES), BF16),
        mixed=vmem((LAYERS, row_len, cols), BF16), log_sum=vmem((LAYERS, row_len, heads), F32),
        up=vmem((LAYERS, row_len, hidden), BF16), act=vmem((LAYERS, row_len, hidden), BF16),
        state=vmem((local, width), F32), middle=vmem((LAYERS, local, width), F32),
        branch=vmem((LAYERS, local, width), BF16), down=vmem((LAYERS, local, width), BF16),
        grad_hid=vmem((local, width), F32),
        grad_down=vmem((row_len, width), BF16), grad_branch=vmem((row_len, width), BF16),
        grad_up=vmem((row_len, hidden), BF16), grad_qkv=vmem((row_len, 3 * cols), BF16),
        grad_heads=vmem((heads, row_len, LANES), BF16),
        part=vmem((2, 2 * local, width), F32),
        core_tx=vmem((2, local, width), BF16), core_rx=vmem((2, local, width), BF16),
        side_tx=vmem((local, width), BF16), side_rx=vmem((local, width), BF16),
        ada_v=vmem((LAYERS, depth, mod_cols), BF16),
        lead=vmem((wide, 16, depth), BF16), lead_rx=vmem((wide, 16, depth), BF16),
        bias_rows=vmem((32, 3 * LANES), F32), bias_tx=vmem((32, 3 * LANES), BF16),
        bias_rx=vmem((wide, 32, 3 * LANES), BF16),
        ada_full=vmem((1, LAYERS, tiles * LANES), F32), qkv_full=vmem((1, LAYERS, 3 * width), F32),
        out_full=vmem((1, LAYERS, width), F32), up_full=vmem((1, LAYERS, narrow * hidden), F32),
        down_full=vmem((1, LAYERS, width), F32), seg_col=vmem((row_len, 1), jnp.int32),
        qkv_raw=vmem((LAYERS, 3, depth, 3 * LANES), BF16), up_raw=vmem((LAYERS, wide, depth, 2 * LANES), BF16),
        qkv_s=vmem((LAYERS, depth, 3 * cols), BF16), up_s=vmem((LAYERS, depth, hidden), BF16),
        lead_t=vmem((LAYERS, wide * LAYERS * SEGS, depth), F32),
        lead_tx=vmem((wide, SEGS, depth), F32), lead_back=vmem((wide, SEGS, depth), F32),
        bias_sum=vmem((4 * LAYERS, width), F32),
        mod_part=vmem((wide, LAYERS * SEGS, mod_cols), F32),
        mod_rx=vmem((wide, LAYERS * SEGS, mod_cols), F32),
        mod_q=vmem((narrow, LAYERS * SEGS, mod_cols), F32),
        mods=vmem((LAYERS * SEGS, tiles * LANES), F32),
        mod_grad=vmem((LAYERS * SEGS, tiles * LANES), F32),
        quarter_rx=vmem((3, LAYERS * SEGS, mod_cols), F32),
        quarter_sum=vmem((16, mod_cols // 2), BF16),
        quarter_all=vmem((wide, 16, mod_cols // 2), BF16),
        mod_all=vmem((wide * LAYERS * SEGS, mod_cols), BF16),
        bias_grad=vmem((4 * LAYERS, width), F32), bias_all=vmem((wide, 16, 5 * LANES), BF16),
        bias_half=vmem((16, 5 * LANES), BF16),
        bias_row=vmem((4 * LAYERS, width), F32),
        qkv_d=vmem((width, 3 * cols), BF16), out_d=vmem((cols, width), BF16),
        up_d=vmem((width, hidden), BF16), down_d=vmem((hidden, width), BF16),
        qkv_xr=vmem((PLANES, depth, 3 * cols), BF16), out_xr=vmem((1, depth, width), BF16),
        up_xr=vmem((PLANES, depth, hidden), BF16), down_xr=vmem((PLANES, hidden_own, width), BF16),
        qkv_zr=vmem((PLANES, depth, 3 * cols), BF16), out_zr=vmem((PLANES, depth, width), BF16),
        up_zr=vmem((PLANES, depth, hidden), BF16), down_zr=vmem((PLANES, hidden_own, width), BF16),
        qkv_f=vmem((depth, 3 * cols), BF16), out_f=vmem((depth, width), BF16),
        up_f=vmem((depth, hidden), BF16), down_f=vmem((hidden_own, width), BF16),
        wz_s=dma((8, 4)), wz_r=dma((8, 4)), wx_s=dma((8, 4)), wx_r=dma((8, 4)), w_own=dma((8,)),
        load_sem=dma((4,)), tok_s=dma((12,)), tok_r=dma((12,)), sum_s=dma((4,)), sum_r=dma((4,)),
        lead_sem_s=dma((wide - 1,)), lead_sem_r=dma((wide - 1,)),
        bias_sem_s=dma((wide - 1,)), bias_sem_r=dma((wide - 1,)),
        mod_sem_s=dma((wide - 1,)), mod_sem_r=dma((wide - 1,)),
        quarter_s=dma((3,)), quarter_r=dma((3,)), ada_sem=dma, raw_sem=dma((LAYERS, 3 + wide)), lead_own_sem=dma,
        lead_back_s=dma((wide - 1,)), lead_back_r=dma((wide - 1,)),
        lead_narrow_s=dma((3,)), lead_narrow_r=dma((3,)),
        dx_s=dma((4, 4)), dx_r=dma((4, 4)), dz_s=dma((4, 3)), dz_r=dma((4, 4)),
        e_s=dma((2, 3)), e_r=dma((2, 4)), ex_s=dma, ex_r=dma,
        down_e=vmem((hidden_own, width), BF16),
        spread_s=dma((8, 3)), spread_r=dma((8, 3)), spread_l=dma((8,)),
        back_s=dma((3,)), back_r=dma((3,)),
        wide_s=dma((wide - 1,)), wide_r=dma((wide - 1,)),
        bias_wide_s=dma((wide - 1,)), bias_wide_r=dma((wide - 1,)),
        bias_narrow_s=dma((3,)), bias_narrow_r=dma((3,)),
        mod_narrow_s=dma((3,)), mod_narrow_r=dma((3,)), mod_own_sem=dma, bias_own_sem=dma,
        credit_x=pltpu.SemaphoreType.REGULAR((4,)), credit_z=pltpu.SemaphoreType.REGULAR((4, 2)),
        credit_sum=pltpu.SemaphoreType.REGULAR((2,)),
    )
    cfg = SimpleNamespace(
        names=[*inputs, *outputs, *scratch], wide=wide, narrow=narrow, width=width, depth=depth,
        local=local, cols=cols, mod_cols=mod_cols, tiles=tiles,
    )

    def place(name, vmem_ok):
        return pl.BlockSpec(memory_space=pltpu.VMEM if vmem_ok else pl.ANY)

    results = pl.pallas_call(
        partial(block_kernel, cfg),
        out_shape=list(outputs.values()),
        in_specs=[place(name, name not in in_hbm) for name in inputs],
        out_specs=[place(name, name in out_vmem) for name in outputs],
        scratch_shapes=list(scratch.values()),
        compiler_params=pltpu.CompilerParams(
            collective_id=0, has_side_effects=True, vmem_limit_bytes=63 * 2**20
        ),
    )(*inputs.values())
    got = dict(zip(outputs, results))

    return finish(wide, narrow, got, cond[0], inputs["cond_index"], tiles, mod_cols, w)


def solution(mesh):
    matrix, vector = P(None, "wide", None), P(None, "wide")
    rows, cond_rows = P("wide", "narrow", None), P("wide", None, None)
    wide, narrow = mesh.shape["wide"], mesh.shape["narrow"]
    fused = wide == PLANES * PAIR and narrow == PLANES
    return jax.shard_map(
        partial(fused_device if fused else plain_device, wide, narrow),
        mesh=mesh,
        in_specs=(rows, cond_rows, P("wide", None), P("wide", None), rows) + (matrix, vector) * 5,
        out_specs=(rows, rows, cond_rows) + (matrix, vector) * 5,
        check_vma=False,
    )
```
